256 devices in a mesh: ctx: 32 (over z, y_lo, core), head: 8 (over x, y_hi).
Axes of the slice: x: 4, y: 4 (y_hi: 2, y_lo: 2; y = y_hi * 2 + y_lo), z: 8, core: 2. Of those that a mesh axis runs over, the one named last changes fastest.
Arguments:
- queries: bfloat16 [6144, 4096], P('ctx', 'head'), may hold values from -9 to 9
- keys: bfloat16 [6144, 1024], P('ctx', 'head'), may hold values from -9 to 9
- values: bfloat16 [6144, 1024], P('ctx', 'head'), may hold values from -6 to 6
- grad_out: bfloat16 [6144, 4096], P('ctx', 'head'), may hold values from -6 to 6
- out_weight: bfloat16 [4096, 4096], P('head'), may hold values from -0.09375 to 0.09375
- lengths: int32 [8], replicated, may hold values from 1 to 1536, 6144 in all
Outputs:
- grad_queries: bfloat16 [6144, 4096], P('ctx', 'head')
- grad_keys: bfloat16 [6144, 1024], P('ctx', 'head')
- grad_values: bfloat16 [6144, 1024], P('ctx', 'head')
The draws below stay inside these ranges and needn't reach their ends.
Inputs may be any that keep to these rules, and one draw needn't show every extreme that they name: `lengths`: the 8 documents fill all 6144 positions in order; each has at most 1536 tokens and one has exactly 1536.
All inputs are finite; a program needn't handle non-finite values.
Results may differ from the reference program's by a relative error of at most 0.0064.
Values may be sent and summed in bfloat16 or wider, within the bound.
No kernel may reach another device: no remote copies, remote signals or barrier semaphores. Data moves between devices by JAX's collectives and lax.ppermute only.
A program may use at most 64 MiB of HBM per device.

```python
import math
import jax
import jax.numpy as jnp
import numpy as np
from jax import lax

MODEL = 4096
Q_HEADS = 32
KV_HEADS = 8
HEAD_DIM = 128
TOKENS = 6144
MOST_DOC = 1536
DOCS = 8


def draw_queries(key, part):
    key = jax.random.fold_in(key, 5)
    return jnp.clip(jax.random.normal(key, (TOKENS, Q_HEADS * HEAD_DIM)), -4.5, 4.5).astype(jnp.bfloat16)


def draw_keys(key, part):
    key = jax.random.fold_in(key, 7)
    return jnp.clip(jax.random.normal(key, (TOKENS, KV_HEADS * HEAD_DIM)), -4.5, 4.5).astype(jnp.bfloat16)


def block_levels(key, extent, shards, least, top_value):
    loudness, own = 1.0, jax.random.fold_in(key, 6)
    for dim, parts in shards:
        steps = jnp.exp(jax.random.uniform(jax.random.fold_in(own, dim), (parts,), jnp.float32, least / len(shards), top_value / len(shards)))
        loudness = loudness * jnp.repeat(steps, extent[dim] // parts).reshape([-1 if axis == dim else 1 for axis in range(len(extent))])
    return loudness


def length_profile(count, total, bound, skew):
    loads = [(1 << 20) // math.isqrt(grade ** skew) + 1 for grade in range(2, count + 1)]
    surplus, holding = total - bound - (count - 1), [1] * (count - 1)
    while surplus > 0:
        candidates = [i for i in range(count - 1) if holding[i] < bound]
        whole, remaining = sum([loads[i] for i in candidates]), surplus
        for i in candidates:
            addition = min(bound - holding[i], max(1, remaining * loads[i] // whole), surplus)
            holding[i] = holding[i] + addition
            surplus = surplus - addition
    return np.array([bound] + holding)


def ragged_sizes(stream_key, amount, total, reach, skew):
    if amount == 2:
        one = jax.random.randint(stream_key, (), max(1, total - reach), min(reach, total - 1) + 1)
        return jnp.stack([one, total - one])
    sizes = jnp.asarray(length_profile(amount, total, reach, skew), jnp.int32)
    couples = (amount - 1) // 2
    giver, sink = sizes[1:1 + 2 * couples:2], sizes[2:2 + 2 * couples:2]
    room = jnp.minimum(giver - 1, reach - sink)
    passed = jax.random.randint(jax.random.fold_in(stream_key, 1), (couples,), 0, 1 << 20) % (room + 1)
    sizes = sizes.at[1:1 + 2 * couples:2].set(giver - passed).at[2:2 + 2 * couples:2].set(sink + passed)
    return sizes[jax.random.permutation(jax.random.fold_in(stream_key, 2), amount)]


def centred(own_key, dims, width, limit, cuts=(), kind=jnp.bfloat16):
    entries = jax.random.normal(own_key, dims, jnp.float32) * width
    if len(cuts) > 0:
        entries = block_levels(own_key, dims, cuts, -0.22, 0.18) * entries
    return jnp.clip(entries, min=-limit, max=limit).astype(kind)


def setup_inputs(seed: int = 0) -> dict:
    arg_keys = jax.random.split(jax.random.key(seed), 7)
    return {
        "queries": draw_queries(jax.random.fold_in(arg_keys[6], 71), 0),
        "keys": draw_keys(jax.random.fold_in(arg_keys[6], 71), 0),
        "values": centred(arg_keys[2], (TOKENS, KV_HEADS * HEAD_DIM), 1.0, 6.0, ((0, 32), (1, 8))),
        "grad_out": centred(arg_keys[3], (TOKENS, MODEL), 1.0, 6.0, ((0, 32), (1, 8))),
        "out_weight": centred(arg_keys[4], (Q_HEADS * HEAD_DIM, MODEL), MODEL ** -0.5, 0.09375, ((0, 8),)),
        "lengths": ragged_sizes(arg_keys[5], DOCS, TOKENS, MOST_DOC, 2).astype(jnp.int32),
    }


NEG = -1.0e30


def segment_of(lengths, positions):
    doc_ends = jnp.cumsum(lengths).astype(jnp.int32)
    return jnp.sum((doc_ends[None, :] <= positions[:, None]).astype(jnp.int32), axis=1).astype(jnp.int32)


def reference(queries, keys, values, grad_out, out_weight, lengths):
    scaling = HEAD_DIM ** -0.5
    group_size = Q_HEADS // KV_HEADS
    grad_attn = jnp.dot(grad_out, out_weight.T, preferred_element_type=jnp.float32).astype(jnp.bfloat16)
    block_rows = math.gcd(TOKENS, 512)
    margin = MOST_DOC
    window = margin + block_rows
    positions = jnp.arange(TOKENS, dtype=jnp.int32)
    document = segment_of(lengths, positions)
    doc_padded = jnp.concatenate([jnp.full((margin,), -1, jnp.int32), document])
    pos_padded = jnp.arange(TOKENS + margin, dtype=jnp.int32) - margin
    query_all = queries.astype(jnp.float32).reshape(TOKENS, KV_HEADS, group_size, HEAD_DIM).transpose(1, 0, 2, 3)
    grad_all = grad_attn.astype(jnp.float32).reshape(TOKENS, KV_HEADS, group_size, HEAD_DIM).transpose(1, 0, 2, 3)
    key_all = keys.astype(jnp.float32).reshape(TOKENS, KV_HEADS, HEAD_DIM).transpose(1, 0, 2)
    value_all = values.astype(jnp.float32).reshape(TOKENS, KV_HEADS, HEAD_DIM).transpose(1, 0, 2)
    key_all = jnp.pad(key_all, ((0, 0), (margin, 0), (0, 0)))
    value_all = jnp.pad(value_all, ((0, 0), (margin, 0), (0, 0)))

    def one_group(inputs):
        query_g, grad_g, key_g, value_g = inputs

        def one_block(carried, block_idx):
            key_acc, value_acc = carried
            offset = (block_idx * block_rows).astype(jnp.int32)
            query_rows = lax.dynamic_slice_in_dim(query_g, offset, block_rows, 0)
            grad_rows = lax.dynamic_slice_in_dim(grad_g, offset, block_rows, 0)
            doc_query = lax.dynamic_slice_in_dim(document, offset, block_rows, 0)
            pos_query = lax.dynamic_slice_in_dim(positions, offset, block_rows, 0)
            key_rows = lax.dynamic_slice_in_dim(key_g, offset, window, 0)
            value_rows = lax.dynamic_slice_in_dim(value_g, offset, window, 0)
            doc_keys = lax.dynamic_slice_in_dim(doc_padded, offset, window, 0)
            pos_keys = lax.dynamic_slice_in_dim(pos_padded, offset, window, 0)
            visible = (doc_query[:, None] == doc_keys[None, :]) & (pos_keys[None, :] <= pos_query[:, None])
            scores = jnp.einsum("qhd,kd->hqk", query_rows, key_rows) * scaling
            scores = jnp.where(visible[None], scores, NEG)
            row_max = jnp.max(scores, axis=-1, keepdims=True)
            log_total = row_max + jnp.log(jnp.sum(jnp.exp(scores - row_max), axis=-1, keepdims=True))
            probability = jnp.where(visible[None], jnp.exp(scores - log_total), 0.0)
            grad_prob = jnp.einsum("qhd,kd->hqk", grad_rows, value_rows)
            row_dot = jnp.sum(probability * grad_prob, axis=-1, keepdims=True)
            dscore = probability * (grad_prob - row_dot)
            prob_round = lax.optimization_barrier(probability.astype(jnp.bfloat16)).astype(jnp.float32)
            dscore_round = lax.optimization_barrier(dscore.astype(jnp.bfloat16)).astype(jnp.float32)
            value_add = jnp.einsum("hqk,qhd->kd", prob_round, grad_rows)
            key_add = jnp.einsum("hqk,qhd->kd", dscore_round, query_rows) * scaling
            query_part = jnp.einsum("hqk,kd->qhd", dscore_round, key_rows) * scaling
            key_acc = lax.dynamic_update_slice_in_dim(key_acc, lax.dynamic_slice_in_dim(key_acc, offset, window, 0) + key_add, offset, 0)
            value_acc = lax.dynamic_update_slice_in_dim(value_acc, lax.dynamic_slice_in_dim(value_acc, offset, window, 0) + value_add, offset, 0)
            return (key_acc, value_acc), query_part

        empty_acc = jnp.zeros((TOKENS + margin, HEAD_DIM), jnp.float32)
        (key_acc, value_acc), query_parts = lax.scan(one_block, (empty_acc, empty_acc), jnp.arange(TOKENS // block_rows, dtype=jnp.int32))
        return query_parts.reshape(TOKENS, group_size, HEAD_DIM), key_acc[margin:], value_acc[margin:]

    grad_q, grad_k, grad_v = lax.map(one_group, (query_all, grad_all, key_all, value_all))
    grad_queries = grad_q.transpose(1, 0, 2, 3).reshape(TOKENS, Q_HEADS * HEAD_DIM).astype(jnp.bfloat16)
    grad_keys = grad_k.transpose(1, 0, 2).reshape(TOKENS, KV_HEADS * HEAD_DIM).astype(jnp.bfloat16)
    grad_values = grad_v.transpose(1, 0, 2).reshape(TOKENS, KV_HEADS * HEAD_DIM).astype(jnp.bfloat16)
    return grad_queries, grad_keys, grad_values
```

```python
import functools

import jax
import jax.numpy as jnp
from jax import lax
from jax.experimental import pallas as pl
from jax.experimental.pallas import tpu as pltpu
from jax.sharding import PartitionSpec as P

D = 128
HEADS = 4
ROWS = 192
LANES = HEADS * ROWS
REACH = 4
SLOTS = REACH + 1
NEG = -1e30
SCALE = D**-0.5
LOG2E = 1.4426950408889634
MIB = 1 << 20


def dot(a, b, ca, cb):
    return lax.dot_general(a, b, (((ca,), (cb,)), ((), ())), preferred_element_type=jnp.float32)


def stack_heads(src, dst):
    for h in range(HEADS):
        dst[h * ROWS : (h + 1) * ROWS, :] = src[:, h * D : (h + 1) * D]


def first_kernel(place_ref, lengths_ref, q_ref, own_ref, par_ref, p_own_ref, p_par_ref, o_ref, q4, s_own, s_par):
    me = place_ref[0]
    core = lax.rem(me, 2)
    chip = me - core
    stack_heads(q_ref, q4)
    lane = lax.broadcasted_iota(jnp.int32, (1, LANES), 1)
    pos = lane + me * ROWS
    for h in range(1, HEADS):
        pos = pos - jnp.where(lane >= h * ROWS, ROWS, 0)
    start = jnp.zeros((1, LANES), jnp.int32)
    end = jnp.int32(0)
    for d in range(lengths_ref.shape[0]):
        end = end + lengths_ref[d]
        start = jnp.where(end <= pos, end, start)
    queries = q4[...]
    row = lax.broadcasted_iota(jnp.int32, (ROWS, LANES), 0)

    def score(kv_ref, slot, core_of, diagonal):
        keys = kv_ref[pl.ds(pl.multiple_of(slot * ROWS, ROWS), ROWS), :D]
        s = dot(keys, queries, 1, 1) * (SCALE * LOG2E)
        key = row + ((chip + core_of) + 2 * (slot - REACH)) * ROWS
        visible = key >= start
        if diagonal:
            visible = visible & (key <= pos)
        return jnp.where(visible, s, NEG)

    def online(s, state):
        top, total = state
        new = jnp.maximum(top, jnp.max(s, axis=0, keepdims=True))
        total = total * jnp.exp2(top - new) + jnp.sum(jnp.exp2(s - new), axis=0, keepdims=True)
        return new, total

    s = score(own_ref, REACH, core, True)
    s_own[REACH * ROWS :, :] = s
    top = jnp.max(s, axis=0, keepdims=True)
    state = (top, jnp.sum(jnp.exp2(s - top), axis=0, keepdims=True))

    def sweep(i, state):
        at = pl.ds(pl.multiple_of(i * ROWS, ROWS), ROWS)
        s = score(own_ref, i, core, False)
        s_own[at, :] = s
        state = online(s, state)
        s = score(par_ref, i + core, 1 - core, False)
        s_par[at, :] = s
        return online(s, state)

    top, total = lax.fori_loop(0, REACH, sweep, state)
    log_total = top + jnp.log2(total)

    def weigh(s_ref, p_ref, kv_ref, i, slot, state):
        acc, mass = state
        at = pl.ds(pl.multiple_of(i * ROWS, ROWS), ROWS)
        prob = jnp.exp2(s_ref[at, :] - log_total).astype(jnp.bfloat16)
        p_ref[at, :] = prob
        values = kv_ref[pl.ds(pl.multiple_of(slot * ROWS, ROWS), ROWS), D:]
        acc = acc + dot(values, prob, 0, 0)
        mass = mass + jnp.sum(prob.astype(jnp.float32), axis=0, keepdims=True)
        return acc, mass

    def second(i, state):
        state = weigh(s_own, p_own_ref, own_ref, i, i, state)
        return weigh(s_par, p_par_ref, par_ref, i, i + core, state)

    state = (jnp.zeros((D, LANES), jnp.float32), jnp.zeros((1, LANES), jnp.float32))
    state = lax.fori_loop(0, REACH, second, state)
    acc, mass = weigh(s_own, p_own_ref, own_ref, REACH, REACH, state)
    o_ref[...] = acc / mass


def back_block(kv_ref, slot, p_ref, i, g4, q4, rd):
    kv_at = pl.ds(pl.multiple_of(slot * ROWS, ROWS), ROWS)
    prob = p_ref[pl.ds(pl.multiple_of(i * ROWS, ROWS), ROWS), :]
    dprob = dot(kv_ref[kv_at, D:], g4, 1, 1)
    ds = (prob.astype(jnp.float32) * (dprob - rd)).astype(jnp.bfloat16)
    dv = dot(prob, g4, 1, 0)
    dk = dot(ds, q4, 1, 0) * SCALE
    dq = dot(kv_ref[kv_at, :D], ds, 0, 0)
    return dk, dv, dq


def second_kernel(place_ref, head_ref, *refs):
    pieces, (w_ref, q_ref, par_ref, p_ref, o_ref, out_ref, g_ref, rd_ref, dq_ref, q4) = refs[:8], refs[8:]
    me = place_ref[0]
    core = lax.rem(me, 2)
    head = head_ref[0]
    stack_heads(q_ref, q4)

    def flip(i):
        return i + 1 - 2 * lax.rem(i, 2)

    def ring(by):
        return lax.rem(head + by + 8, 8)

    sources = (head, flip(head), ring(-2), ring(2), flip(ring(-2)), flip(ring(2)), ring(4), flip(ring(4)))
    acc = jnp.zeros((ROWS, HEADS * D), jnp.float32)
    for piece, source in zip(pieces, sources):
        acc = acc + dot(piece[...], w_ref[:, pl.ds(pl.multiple_of(source * 512, 512), 512)], 1, 1)
    acc = acc.astype(jnp.bfloat16)
    for h in range(HEADS):
        g_ref[h * ROWS : (h + 1) * ROWS, :] = acc[:, h * D : (h + 1) * D]
    g4 = g_ref[...]
    gt = jnp.transpose(g4.astype(jnp.float32))
    rd = jnp.sum(gt * o_ref[...], axis=0, keepdims=True)
    rd_ref[...] = rd
    dq_ref[...] = jnp.zeros((D, LANES), jnp.float32)
    out_ref[...] = jnp.zeros(out_ref.shape, out_ref.dtype)

    def step(i, _):
        dk, dv, dq = back_block(par_ref, i + core, p_ref, i, g4, q4[...], rd)
        at = pl.ds(pl.multiple_of((i + core) * ROWS, ROWS), ROWS)
        out_ref[at, :D] = dk.astype(jnp.bfloat16)
        out_ref[at, D:] = dv.astype(jnp.bfloat16)
        dq_ref[...] += dq
        return 0

    lax.fori_loop(0, REACH, step, 0)


def third_kernel(q_ref, own_ref, p_ref, g_ref, rd_ref, dq_in_ref, out_ref, dq_out_ref, q4, acc):
    stack_heads(q_ref, q4)
    g4 = g_ref[...]
    rd = rd_ref[...]
    acc[...] = dq_in_ref[...]

    def step(i, _):
        dk, dv, dq = back_block(own_ref, i, p_ref, i, g4, q4[...], rd)
        at = pl.ds(pl.multiple_of(i * ROWS, ROWS), ROWS)
        out_ref[at, :D] = dk
        out_ref[at, D:] = dv
        acc[...] += dq
        return 0

    lax.fori_loop(0, SLOTS, step, 0)
    dq = jnp.transpose(acc[...]) * SCALE
    for h in range(HEADS):
        dq_out_ref[:, h * D : (h + 1) * D] = dq[h * ROWS : (h + 1) * ROWS, :].astype(jnp.bfloat16)


def vmem(n):
    return [pl.BlockSpec(memory_space=pltpu.VMEM)] * n


def smem(n):
    return [pl.BlockSpec(memory_space=pltpu.SMEM)] * n


def params(mib):
    return pltpu.CompilerParams(vmem_limit_bytes=mib * MIB)


def cost(flops, nbytes, exps=0):
    return pl.CostEstimate(flops=int(flops), bytes_accessed=int(nbytes), transcendentals=int(exps))


def moved(x, axis, to):
    return lax.ppermute(x, axis, [(i, to(i)) for i in range(lax.axis_size(axis))])


def turned(x, axis, by):
    count = lax.axis_size(axis)
    return moved(x, axis, lambda i: (i + by) % count)


def local(queries, keys, values, grad_out, out_weight, lengths):
    bf16, f32 = jnp.bfloat16, jnp.float32
    place = lax.axis_index("ctx").astype(jnp.int32).reshape(1)
    head = lax.axis_index("head").astype(jnp.int32).reshape(1)
    kv = jnp.concatenate([keys, values], axis=1)

    other = moved(grad_out, "head", lambda i: i ^ 1)
    right = turned(grad_out, "head", 2)
    left = turned(grad_out, "head", -2)
    earlier = [turned(kv, "ctx", 2 * k) for k in range(REACH, 0, -1)]
    other_right = turned(other, "head", 2)
    other_left = turned(other, "head", -2)
    far = turned(right, "head", 2)
    other_far = turned(other_left, "head", -2)
    pieces = (grad_out, other, right, left, other_right, other_left, far, other_far)

    own = jnp.concatenate(earlier + [kv], axis=0)
    par = moved(own, "ctx", lambda i: i ^ 1)

    pair = ROWS * LANES * D * 2
    p_own, p_par, out_t = pl.pallas_call(
        first_kernel,
        out_shape=(
            jax.ShapeDtypeStruct((SLOTS * ROWS, LANES), bf16),
            jax.ShapeDtypeStruct((REACH * ROWS, LANES), bf16),
            jax.ShapeDtypeStruct((D, LANES), f32),
        ),
        in_specs=smem(2) + vmem(3),
        out_specs=tuple(vmem(3)),
        scratch_shapes=[
            pltpu.VMEM((LANES, D), bf16),
            pltpu.VMEM((SLOTS * ROWS, LANES), f32),
            pltpu.VMEM((REACH * ROWS, LANES), f32),
        ],
        compiler_params=params(24),
        cost_estimate=cost(18 * pair, 5 * MIB, 18 * ROWS * LANES),
        name="softmax",
    )(place, lengths, queries, own, par)

    par_grad, g4, rd, dq = pl.pallas_call(
        second_kernel,
        out_shape=(
            jax.ShapeDtypeStruct((SLOTS * ROWS, 2 * D), bf16),
            jax.ShapeDtypeStruct((LANES, D), bf16),
            jax.ShapeDtypeStruct((1, LANES), f32),
            jax.ShapeDtypeStruct((D, LANES), f32),
        ),
        in_specs=smem(2) + vmem(8 + 5),
        out_specs=tuple(vmem(4)),
        scratch_shapes=[pltpu.VMEM((LANES, D), bf16)],
        compiler_params=params(24),
        cost_estimate=cost(16 * pair, 8 * MIB),
        name="partner_grads",
    )(place, head, *pieces, out_weight, queries, par, p_par, out_t)

    back = moved(par_grad, "ctx", lambda i: i ^ 1)

    own_grad, grad_queries = pl.pallas_call(
        third_kernel,
        out_shape=(
            jax.ShapeDtypeStruct((SLOTS * ROWS, 2 * D), f32),
            jax.ShapeDtypeStruct((ROWS, HEADS * D), bf16),
        ),
        in_specs=vmem(6),
        out_specs=tuple(vmem(2)),
        scratch_shapes=[pltpu.VMEM((LANES, D), bf16), pltpu.VMEM((D, LANES), f32)],
        compiler_params=params(24),
        cost_estimate=cost(20 * pair, 5 * MIB),
        name="own_grads",
    )(queries, own, p_own, g4, rd, dq)

    both = own_grad + back.astype(f32)
    total = both[REACH * ROWS :]
    for m in range(REACH):
        part = both[m * ROWS : (m + 1) * ROWS].astype(bf16)
        total = total + turned(part, "ctx", -2 * (REACH - m)).astype(f32)
    total = total.astype(bf16)
    return grad_queries, total[:, :D], total[:, D:]


def solution(mesh):
    return jax.shard_map(
        local,
        mesh=mesh,
        in_specs=(
            P("ctx", "head"),
            P("ctx", "head"),
            P("ctx", "head"),
            P("ctx", "head"),
            P("head", None),
            P(),
        ),
        out_specs=(P("ctx", "head"), P("ctx", "head"), P("ctx", "head")),
        check_vma=False,
    )
```

```python
import functools

import jax
import jax.numpy as jnp
from jax import lax
from jax.experimental import pallas as pl
from jax.experimental.pallas import tpu as pltpu
from jax.sharding import PartitionSpec as P

D = 128
HEADS = 4
ROWS = 192
LANES = HEADS * ROWS
REACH = 4
SLOTS = REACH + 1
PLANE = 4
NEG = -1e30
SCALE = D**-0.5
LOG2E = 1.4426950408889634
MIB = 1 << 20


def dot(a, b, ca, cb):
    return lax.dot_general(a, b, (((ca,), (cb,)), ((), ())), preferred_element_type=jnp.float32)


def stack_heads(src, dst):
    for h in range(HEADS):
        dst[h * ROWS : (h + 1) * ROWS, :] = src[:, h * D : (h + 1) * D]


def prepare(place_ref, len_ref, q_ref, q4_ref, bound_ref):
    stack_heads(q_ref, q4_ref)
    lane = lax.broadcasted_iota(jnp.int32, (1, LANES), 1)
    pos = lane + place_ref[0] * ROWS
    for h in range(1, HEADS):
        pos = pos - jnp.where(lane >= h * ROWS, ROWS, 0)
    start = jnp.zeros((1, LANES), jnp.int32)
    end = jnp.int32(0)
    for d in range(len_ref.shape[0]):
        end = end + len_ref[d]
        start = jnp.where(end <= pos, end, start)
    bound_ref[0:1, :] = pos
    bound_ref[1:2, :] = start


def pick_kernel(place_ref, z2_ref, z1_ref, z0_ref, *refs):
    out_ref = refs[-1]
    upper = lax.rem(lax.div(place_ref[0], 2), 2) == 1

    @pl.when(upper)
    def _():
        out_ref[:ROWS, :] = z2_ref[...]
        out_ref[ROWS:, :] = z1_ref[...]

    @pl.when(jnp.logical_not(upper))
    def _():
        out_ref[:ROWS, :] = z1_ref[...]
        out_ref[ROWS:, :] = z0_ref[...]


def join_kernel(z2_ref, z1_ref, z0_ref, side_ref, *refs):
    out_ref = refs[-1]
    parts = (z2_ref[...], side_ref[:ROWS, :], z1_ref[...], side_ref[ROWS:, :], z0_ref[...])
    for m, part in enumerate(parts):
        out_ref[m * ROWS : (m + 1) * ROWS, :] = part


def score(kv, queries, row, base, bound_ref, diagonal):
    s = dot(kv[:, :D], queries, 1, 1) * (SCALE * LOG2E)
    key = row + base * ROWS
    visible = key >= bound_ref[1:2, :]
    if diagonal:
        visible = visible & (key <= bound_ref[0:1, :])
    return jnp.where(visible, s, NEG)


def online(s, state):
    top, total = state
    new = jnp.maximum(top, jnp.max(s, axis=0, keepdims=True))
    total = total * jnp.exp2(top - new) + jnp.sum(jnp.exp2(s - new), axis=0, keepdims=True)
    return new, total


def near_kernel(place_ref, z2_ref, z1_ref, z0_ref, q4_ref, bound_ref, after, s_ref, stat_ref):
    me = place_ref[0]
    queries = q4_ref[...]
    row = lax.broadcasted_iota(jnp.int32, (ROWS, LANES), 0)
    s = score(z0_ref[...], queries, row, me, bound_ref, True)
    s_ref[2 * ROWS :, :] = s
    top = jnp.max(s, axis=0, keepdims=True)
    state = (top, jnp.sum(jnp.exp2(s - top), axis=0, keepdims=True))
    for i, ref in ((1, z1_ref), (0, z2_ref)):
        s = score(ref[...], queries, row, me - PLANE * (2 - i), bound_ref, False)
        s_ref[i * ROWS : (i + 1) * ROWS, :] = s
        state = online(s, state)
    stat_ref[0:1, :] = state[0]
    stat_ref[1:2, :] = state[1]


def rest_kernel(place_ref, own_ref, par_ref, q4_ref, bound_ref, s_ref, stat_ref, after, p_own_ref, p_par_ref, o_ref, s_side, s_par):
    me = place_ref[0]
    core = lax.rem(me, 2)
    chip = me - core
    queries = q4_ref[...]
    row = lax.broadcasted_iota(jnp.int32, (ROWS, LANES), 0)

    def rows(i):
        return pl.ds(pl.multiple_of(i * ROWS, ROWS), ROWS)

    def side(i, state):
        slot = 2 * i + 1
        s = score(own_ref[rows(slot), :], queries, row, me + 2 * (slot - REACH), bound_ref, False)
        s_side[rows(i), :] = s
        return online(s, state)

    def across(i, state):
        slot = i + core
        s = score(par_ref[rows(slot), :], queries, row, chip + 1 - core + 2 * (slot - REACH), bound_ref, False)
        s_par[rows(i), :] = s
        return online(s, state)

    state = (stat_ref[0:1, :], stat_ref[1:2, :])
    state = lax.fori_loop(0, 2, side, state)
    top, total = lax.fori_loop(0, REACH, across, state)
    log_total = top + jnp.log2(total)

    def weigh(s, kv_ref, slot, state):
        acc, mass = state
        prob = jnp.exp2(s - log_total).astype(jnp.bfloat16)
        acc = acc + dot(kv_ref[rows(slot), D:], prob, 0, 0)
        mass = mass + jnp.sum(prob.astype(jnp.float32), axis=0, keepdims=True)
        return prob, (acc, mass)

    def weigh_main(i, state):
        prob, state = weigh(s_ref[rows(i), :], own_ref, 2 * i, state)
        p_own_ref[rows(2 * i), :] = prob
        return state

    def weigh_side(i, state):
        prob, state = weigh(s_side[rows(i), :], own_ref, 2 * i + 1, state)
        p_own_ref[rows(2 * i + 1), :] = prob
        return state

    def weigh_across(i, state):
        prob, state = weigh(s_par[rows(i), :], par_ref, i + core, state)
        p_par_ref[rows(i), :] = prob
        return state

    state = (jnp.zeros((D, LANES), jnp.float32), jnp.zeros((1, LANES), jnp.float32))
    state = lax.fori_loop(0, 3, weigh_main, state)
    state = lax.fori_loop(0, 2, weigh_side, state)
    acc, mass = lax.fori_loop(0, REACH, weigh_across, state)
    o_ref[...] = acc / mass


def project(acc, pieces, sources, w_ref):
    for piece, source in zip(pieces, sources):
        part = dot(piece[...], w_ref[:, pl.ds(pl.multiple_of(source * 512, 512), 512)], 1, 1)
        acc = part if acc is None else acc + part
    return acc


def source_of(head, by, flip):
    at = lax.rem(head + by + 8, 8)
    return at + 1 - 2 * lax.rem(at, 2) if flip else at


def early_kernel(head_ref, a_ref, b_ref, c_ref, d_ref, e_ref, f_ref, w_ref, after, out_ref):
    head = head_ref[0]
    sources = (head, source_of(head, 0, True), source_of(head, -2, False), source_of(head, 2, False))
    sources += (source_of(head, -2, True), source_of(head, 2, True))
    out_ref[...] = project(None, (a_ref, b_ref, c_ref, d_ref, e_ref, f_ref), sources, w_ref)


def back_block(kv_ref, slot, p_ref, i, g4, q4, rd):
    kv_at = pl.ds(pl.multiple_of(slot * ROWS, ROWS), ROWS)
    prob = p_ref[pl.ds(pl.multiple_of(i * ROWS, ROWS), ROWS), :]
    dprob = dot(kv_ref[kv_at, D:], g4, 1, 1)
    ds = (prob.astype(jnp.float32) * (dprob - rd)).astype(jnp.bfloat16)
    dv = dot(prob, g4, 1, 0)
    dk = dot(ds, q4, 1, 0) * SCALE
    dq = dot(kv_ref[kv_at, :D], ds, 0, 0)
    return dk, dv, dq


def second_kernel(place_ref, head_ref, a_ref, b_ref, early_ref, w_ref, q4_ref, par_ref, p_ref, o_ref, out_ref, g_ref, rd_ref, dq_ref):
    me = place_ref[0]
    core = lax.rem(me, 2)
    head = head_ref[0]
    sources = (source_of(head, 4, False), source_of(head, 4, True))
    acc = project(early_ref[...], (a_ref, b_ref), sources, w_ref)
    acc = acc.astype(jnp.bfloat16)
    for h in range(HEADS):
        g_ref[h * ROWS : (h + 1) * ROWS, :] = acc[:, h * D : (h + 1) * D]
    g4 = g_ref[...]
    gt = jnp.transpose(g4.astype(jnp.float32))
    rd = jnp.sum(gt * o_ref[...], axis=0, keepdims=True)
    rd_ref[...] = rd
    dq_ref[...] = jnp.zeros((D, LANES), jnp.float32)
    out_ref[...] = jnp.zeros(out_ref.shape, out_ref.dtype)

    def step(i, _):
        dk, dv, dq = back_block(par_ref, i + core, p_ref, i, g4, q4_ref[...], rd)
        at = pl.ds(pl.multiple_of((i + core) * ROWS, ROWS), ROWS)
        out_ref[at, :D] = dk.astype(jnp.bfloat16)
        out_ref[at, D:] = dv.astype(jnp.bfloat16)
        dq_ref[...] += dq
        return 0

    lax.fori_loop(0, REACH, step, 0)


def third_kernel(q4_ref, own_ref, p_ref, g_ref, rd_ref, dq_in_ref, out_ref, dq_out_ref, acc):
    g4 = g_ref[...]
    rd = rd_ref[...]
    acc[...] = dq_in_ref[...]

    def step(i, _):
        dk, dv, dq = back_block(own_ref, i, p_ref, i, g4, q4_ref[...], rd)
        at = pl.ds(pl.multiple_of(i * ROWS, ROWS), ROWS)
        out_ref[at, :D] = dk
        out_ref[at, D:] = dv
        acc[...] += dq
        return 0

    lax.fori_loop(0, SLOTS, step, 0)
    dq = jnp.transpose(acc[...]) * SCALE
    for h in range(HEADS):
        dq_out_ref[:, h * D : (h + 1) * D] = dq[h * ROWS : (h + 1) * ROWS, :].astype(jnp.bfloat16)


def vmem(n):
    return [pl.BlockSpec(memory_space=pltpu.VMEM)] * n


def smem(n):
    return [pl.BlockSpec(memory_space=pltpu.SMEM)] * n


def hbm(n):
    return [pl.BlockSpec(memory_space=pltpu.HBM)] * n


def token(n):
    return [pl.BlockSpec(memory_space=pl.ANY)] * n


def params(mib):
    return pltpu.CompilerParams(vmem_limit_bytes=mib * MIB)


def cost(flops, nbytes, exps=0):
    return pl.CostEstimate(flops=int(flops), bytes_accessed=int(nbytes), transcendentals=int(exps))


def moved(x, axis, to):
    return lax.ppermute(x, axis, [(i, to(i)) for i in range(lax.axis_size(axis))])


def turned(x, axis, by):
    count = lax.axis_size(axis)
    return moved(x, axis, lambda i: (i + by) % count)


def shape(rows, cols, dtype):
    return jax.ShapeDtypeStruct((rows, cols), dtype)


def local(queries, keys, values, grad_out, out_weight, lengths):
    bf16, f32 = jnp.bfloat16, jnp.float32
    ctx = lax.axis_index("ctx").astype(jnp.int32)
    place = ctx.reshape(1)
    head = lax.axis_index("head").astype(jnp.int32).reshape(1)
    upper = lax.rem(ctx // 2, 2) == 1
    pair = ROWS * LANES * D * 2

    other = moved(grad_out, "head", lambda i: i ^ 1)
    right = turned(grad_out, "head", 2)
    left = turned(grad_out, "head", -2)

    kv = jnp.pad(keys, ((0, 0), (0, D))) + jnp.pad(values, ((0, 0), (D, 0)))
    q4, bound = pl.pallas_call(
        prepare,
        out_shape=(shape(LANES, D, bf16), shape(8, LANES, jnp.int32)),
        in_specs=smem(2) + vmem(1),
        out_specs=tuple(vmem(2)),
        compiler_params=params(8),
        cost_estimate=cost(1, 1),
        name="prepare",
    )(place, lengths, queries)

    z2 = turned(kv, "ctx", 2 * PLANE)
    z1 = turned(kv, "ctx", PLANE)

    other_right = turned(other, "head", 2)
    other_left = turned(other, "head", -2)
    far = turned(right, "head", 2)
    other_far = turned(other_left, "head", -2)

    picked = pl.pallas_call(
        pick_kernel,
        out_shape=shape(2 * ROWS, 2 * D, bf16),
        in_specs=smem(1) + vmem(3) + token(4),
        out_specs=vmem(1)[0],
        compiler_params=params(8),
        cost_estimate=cost(1, 1),
        name="pick_side",
    )(place, z2, z1, kv, other, right, left, q4)
    side = moved(picked, "ctx", lambda i: i ^ 2)

    s_near, stat = pl.pallas_call(
        near_kernel,
        out_shape=(shape(3 * ROWS, LANES, f32), shape(8, LANES, f32)),
        in_specs=smem(1) + vmem(5) + token(1),
        out_specs=tuple(vmem(2)),
        compiler_params=params(16),
        cost_estimate=cost(1, 1),
        name="near_scores",
    )(place, z2, z1, kv, q4, bound, picked)

    own = pl.pallas_call(
        join_kernel,
        out_shape=shape(SLOTS * ROWS, 2 * D, bf16),
        in_specs=vmem(4) + token(3),
        out_specs=vmem(1)[0],
        compiler_params=params(8),
        cost_estimate=cost(1, 1),
        name="join_slots",
    )(z2, z1, kv, side, stat, other_right, other_left)
    par = moved(own, "ctx", lambda i: i ^ 1)

    early = pl.pallas_call(
        early_kernel,
        out_shape=shape(ROWS, HEADS * D, f32),
        in_specs=smem(1) + vmem(7) + token(1),
        out_specs=vmem(1)[0],
        compiler_params=params(16),
        cost_estimate=cost(1, 1),
        name="early_projection",
    )(head, grad_out, other, right, left, other_right, other_left, out_weight, own)

    p_own, p_par, out_t = pl.pallas_call(
        rest_kernel,
        out_shape=(shape(SLOTS * ROWS, LANES, bf16), shape(REACH * ROWS, LANES, bf16), shape(D, LANES, f32)),
        in_specs=smem(1) + vmem(6) + token(1),
        out_specs=tuple(vmem(3)),
        scratch_shapes=[pltpu.VMEM((2 * ROWS, LANES), f32), pltpu.VMEM((REACH * ROWS, LANES), f32)],
        compiler_params=params(24),
        cost_estimate=cost(1, 1),
        name="softmax",
    )(place, own, par, q4, bound, s_near, stat, early)

    par_grad, g4, rd, dq = pl.pallas_call(
        second_kernel,
        out_shape=(shape(SLOTS * ROWS, 2 * D, bf16), shape(LANES, D, bf16), shape(1, LANES, f32), shape(D, LANES, f32)),
        in_specs=smem(2) + vmem(8),
        out_specs=tuple(vmem(4)),
        compiler_params=params(24),
        cost_estimate=cost(1, 1),
        name="partner_grads",
    )(place, head, far, other_far, early, out_weight, q4, par, p_par, out_t)

    back = moved(par_grad, "ctx", lambda i: i ^ 1)

    own_grad, grad_queries = pl.pallas_call(
        third_kernel,
        out_shape=(shape(SLOTS * ROWS, 2 * D, f32), shape(ROWS, HEADS * D, bf16)),
        in_specs=vmem(6),
        out_specs=tuple(vmem(2)),
        scratch_shapes=[pltpu.VMEM((D, LANES), f32)],
        compiler_params=params(24),
        cost_estimate=cost(1, 1),
        name="own_grads",
    )(q4, own, p_own, g4, rd, dq)

    both = own_grad + back.astype(f32)
    slots = [both[m * ROWS : (m + 1) * ROWS] for m in range(SLOTS)]
    crossed = moved(jnp.concatenate([slots[1], slots[3]]).astype(bf16), "ctx", lambda i: i ^ 2).astype(f32)
    first, second = crossed[:ROWS], crossed[ROWS:]
    zero = jnp.zeros_like(first)
    to_two = slots[0] + jnp.where(upper, first, zero)
    to_one = slots[2] + jnp.where(upper, second, first)
    total = slots[4] + jnp.where(upper, zero, second)
    got_two = turned(to_two.astype(bf16), "ctx", -2 * PLANE)
    got_one = turned(to_one.astype(bf16), "ctx", -PLANE)
    total = (total + got_one.astype(f32) + got_two.astype(f32)).astype(bf16)
    return grad_queries, total[:, :D], total[:, D:]


def solution(mesh):
    return jax.shard_map(
        local,
        mesh=mesh,
        in_specs=(
            P("ctx", "head"),
            P("ctx", "head"),
            P("ctx", "head"),
            P("ctx", "head"),
            P("head", None),
            P(),
        ),
        out_specs=(P("ctx", "head"), P("ctx", "head"), P("ctx", "head")),
        check_vma=False,
    )
```

```python
import functools

import jax
import jax.numpy as jnp
from jax import lax
from jax.experimental import pallas as pl
from jax.experimental.pallas import tpu as pltpu
from jax.sharding import PartitionSpec as P

D = 128
HEADS = 4
ROWS = 192
LANES = HEADS * ROWS
REACH = 4
SLOTS = REACH + 1
PLANE = 4
NEG = -1e30
SCALE = D**-0.5
LOG2E = 1.4426950408889634
MIB = 1 << 20


def dot(a, b, ca, cb):
    return lax.dot_general(a, b, (((ca,), (cb,)), ((), ())), preferred_element_type=jnp.float32)


def stack_heads(src, dst):
    for h in range(HEADS):
        dst[h * ROWS : (h + 1) * ROWS, :] = src[:, h * D : (h + 1) * D]


def prepare(place_ref, len_ref, q_ref, q4_ref, bound_ref):
    stack_heads(q_ref, q4_ref)
    lane = lax.broadcasted_iota(jnp.int32, (1, LANES), 1)
    pos = lane + place_ref[0] * ROWS
    for h in range(1, HEADS):
        pos = pos - jnp.where(lane >= h * ROWS, ROWS, 0)
    start = jnp.zeros((1, LANES), jnp.int32)
    end = jnp.int32(0)
    for d in range(len_ref.shape[0]):
        end = end + len_ref[d]
        start = jnp.where(end <= pos, end, start)
    bound_ref[0:1, :] = pos
    bound_ref[1:2, :] = start


def pick_kernel(place_ref, z2_ref, z1_ref, z0_ref, *refs):
    out_ref = refs[-1]
    upper = lax.rem(lax.div(place_ref[0], 2), 2) == 1

    @pl.when(upper)
    def _():
        out_ref[:ROWS, :] = z2_ref[...]
        out_ref[ROWS:, :] = z1_ref[...]

    @pl.when(jnp.logical_not(upper))
    def _():
        out_ref[:ROWS, :] = z1_ref[...]
        out_ref[ROWS:, :] = z0_ref[...]


def join_kernel(z2_ref, z1_ref, z0_ref, side_ref, *refs):
    out_ref = refs[-1]
    parts = (z2_ref[...], side_ref[:ROWS, :], z1_ref[...], side_ref[ROWS:, :], z0_ref[...])
    for m, part in enumerate(parts):
        out_ref[m * ROWS : (m + 1) * ROWS, :] = part


def score(kv, queries, row, base, bound_ref, diagonal):
    s = dot(kv[:, :D], queries, 1, 1) * (SCALE * LOG2E)
    key = row + base * ROWS
    visible = key >= bound_ref[1:2, :]
    if diagonal:
        visible = visible & (key <= bound_ref[0:1, :])
    return jnp.where(visible, s, NEG)


def online(s, state):
    top, total = state
    new = jnp.maximum(top, jnp.max(s, axis=0, keepdims=True))
    total = total * jnp.exp2(top - new) + jnp.sum(jnp.exp2(s - new), axis=0, keepdims=True)
    return new, total


def near_kernel(place_ref, z2_ref, z1_ref, z0_ref, q4_ref, bound_ref, *refs):
    s_ref, stat_ref = refs[-2:]
    me = place_ref[0]
    queries = q4_ref[...]
    row = lax.broadcasted_iota(jnp.int32, (ROWS, LANES), 0)
    s = score(z0_ref[...], queries, row, me, bound_ref, True)
    s_ref[2 * ROWS :, :] = s
    top = jnp.max(s, axis=0, keepdims=True)
    state = (top, jnp.sum(jnp.exp2(s - top), axis=0, keepdims=True))
    for i, ref in ((1, z1_ref), (0, z2_ref)):
        s = score(ref[...], queries, row, me - PLANE * (2 - i), bound_ref, False)
        s_ref[i * ROWS : (i + 1) * ROWS, :] = s
        state = online(s, state)
    stat_ref[0:1, :] = state[0]
    stat_ref[1:2, :] = state[1]


def rest_kernel(place_ref, own_ref, par_ref, q4_ref, bound_ref, s_ref, stat_ref, after, p_own_ref, p_par_ref, o_ref, s_side, s_par):
    me = place_ref[0]
    core = lax.rem(me, 2)
    chip = me - core
    queries = q4_ref[...]
    row = lax.broadcasted_iota(jnp.int32, (ROWS, LANES), 0)

    def rows(i):
        return pl.ds(pl.multiple_of(i * ROWS, ROWS), ROWS)

    def side(i, state):
        slot = 2 * i + 1
        s = score(own_ref[rows(slot), :], queries, row, me + 2 * (slot - REACH), bound_ref, False)
        s_side[rows(i), :] = s
        return online(s, state)

    def across(i, state):
        slot = i + core
        s = score(par_ref[rows(slot), :], queries, row, chip + 1 - core + 2 * (slot - REACH), bound_ref, False)
        s_par[rows(i), :] = s
        return online(s, state)

    state = (stat_ref[0:1, :], stat_ref[1:2, :])
    state = lax.fori_loop(0, 2, side, state)
    top, total = lax.fori_loop(0, REACH, across, state)
    log_total = top + jnp.log2(total)

    def weigh(s, kv_ref, slot, state):
        acc, mass = state
        prob = jnp.exp2(s - log_total).astype(jnp.bfloat16)
        acc = acc + dot(kv_ref[rows(slot), D:], prob, 0, 0)
        mass = mass + jnp.sum(prob.astype(jnp.float32), axis=0, keepdims=True)
        return prob, (acc, mass)

    def weigh_main(i, state):
        prob, state = weigh(s_ref[rows(i), :], own_ref, 2 * i, state)
        p_own_ref[rows(2 * i), :] = prob
        return state

    def weigh_side(i, state):
        prob, state = weigh(s_side[rows(i), :], own_ref, 2 * i + 1, state)
        p_own_ref[rows(2 * i + 1), :] = prob
        return state

    def weigh_across(i, state):
        prob, state = weigh(s_par[rows(i), :], par_ref, i + core, state)
        p_par_ref[rows(i), :] = prob
        return state

    state = (jnp.zeros((D, LANES), jnp.float32), jnp.zeros((1, LANES), jnp.float32))
    state = lax.fori_loop(0, 3, weigh_main, state)
    state = lax.fori_loop(0, 2, weigh_side, state)
    acc, mass = lax.fori_loop(0, REACH, weigh_across, state)
    o_ref[...] = acc / mass


def project(acc, pieces, sources, w_ref):
    for piece, source in zip(pieces, sources):
        part = dot(piece[...], w_ref[:, pl.ds(pl.multiple_of(source * 512, 512), 512)], 1, 1)
        acc = part if acc is None else acc + part
    return acc


def source_of(head, by, flip):
    at = lax.rem(head + by + 8, 8)
    return at + 1 - 2 * lax.rem(at, 2) if flip else at


def first_projection(head_ref, a_ref, w_ref, out_ref):
    out_ref[...] = project(None, (a_ref,), (head_ref[0],), w_ref)


def early_kernel(head_ref, acc_ref, b_ref, c_ref, d_ref, e_ref, f_ref, w_ref, after, out_ref):
    head = head_ref[0]
    sources = (source_of(head, 0, True), source_of(head, -2, False), source_of(head, 2, False))
    sources += (source_of(head, -2, True), source_of(head, 2, True))
    out_ref[...] = project(acc_ref[...], (b_ref, c_ref, d_ref, e_ref, f_ref), sources, w_ref)


def back_block(kv_ref, slot, p_ref, i, g4, q4, rd):
    kv_at = pl.ds(pl.multiple_of(slot * ROWS, ROWS), ROWS)
    prob = p_ref[pl.ds(pl.multiple_of(i * ROWS, ROWS), ROWS), :]
    dprob = dot(kv_ref[kv_at, D:], g4, 1, 1)
    ds = (prob.astype(jnp.float32) * (dprob - rd)).astype(jnp.bfloat16)
    dv = dot(prob, g4, 1, 0)
    dk = dot(ds, q4, 1, 0) * SCALE
    dq = dot(kv_ref[kv_at, :D], ds, 0, 0)
    return dk, dv, dq


def put(out_ref, slot, dk, dv):
    at = pl.ds(pl.multiple_of(slot * ROWS, ROWS), ROWS)
    out_ref[at, :D] = dk.astype(out_ref.dtype)
    out_ref[at, D:] = dv.astype(out_ref.dtype)


def cross_far(place_ref, head_ref, a_ref, b_ref, early_ref, w_ref, q4_ref, par_ref, p_ref, o_ref, out_ref, g_ref, rd_ref, dq_ref):
    core = lax.rem(place_ref[0], 2)
    head = head_ref[0]
    sources = (source_of(head, 4, False), source_of(head, 4, True))
    acc = project(early_ref[...], (a_ref, b_ref), sources, w_ref)
    acc = acc.astype(jnp.bfloat16)
    for h in range(HEADS):
        g_ref[h * ROWS : (h + 1) * ROWS, :] = acc[:, h * D : (h + 1) * D]
    g4 = g_ref[...]
    gt = jnp.transpose(g4.astype(jnp.float32))
    rd = jnp.sum(gt * o_ref[...], axis=0, keepdims=True)
    rd_ref[...] = rd
    dq_ref[...] = jnp.zeros((D, LANES), jnp.float32)

    @pl.when(core == 1)
    def _():
        out_ref[:ROWS, :] = jnp.zeros((ROWS, 2 * D), out_ref.dtype)

    def step(slot, _):
        dk, dv, dq = back_block(par_ref, slot, p_ref, slot - core, g4, q4_ref[...], rd)
        put(out_ref, slot, dk, dv)
        dq_ref[...] += dq
        return 0

    lax.fori_loop(core, 2, step, 0)


def cross_near(place_ref, q4_ref, par_ref, p_ref, g_ref, rd_ref, dq_in_ref, out_ref, dq_ref):
    core = lax.rem(place_ref[0], 2)
    g4 = g_ref[...]
    rd = rd_ref[...]
    dq_ref[...] = dq_in_ref[...]

    @pl.when(core == 0)
    def _():
        out_ref[2 * ROWS :, :] = jnp.zeros((ROWS, 2 * D), out_ref.dtype)

    def step(slot, _):
        dk, dv, dq = back_block(par_ref, slot, p_ref, slot - core, g4, q4_ref[...], rd)
        put(out_ref, slot - 2, dk, dv)
        dq_ref[...] += dq
        return 0

    lax.fori_loop(2, REACH + core, step, 0)


def own_far(q4_ref, own_ref, p_ref, g_ref, rd_ref, dq_in_ref, out_ref, dq_ref):
    g4 = g_ref[...]
    rd = rd_ref[...]
    dq_ref[...] = dq_in_ref[...]

    def step(slot, _):
        dk, dv, dq = back_block(own_ref, slot, p_ref, slot, g4, q4_ref[...], rd)
        put(out_ref, slot, dk, dv)
        dq_ref[...] += dq
        return 0

    lax.fori_loop(0, 2, step, 0)


def own_near(q4_ref, own_ref, p_ref, g_ref, rd_ref, dq_in_ref, after, out_ref, dq_out_ref, acc):
    g4 = g_ref[...]
    rd = rd_ref[...]
    acc[...] = dq_in_ref[...]

    def step(slot, _):
        dk, dv, dq = back_block(own_ref, slot, p_ref, slot, g4, q4_ref[...], rd)
        put(out_ref, slot - 2, dk, dv)
        acc[...] += dq
        return 0

    lax.fori_loop(2, SLOTS, step, 0)
    dq = jnp.transpose(acc[...]) * SCALE
    for h in range(HEADS):
        dq_out_ref[:, h * D : (h + 1) * D] = dq[h * ROWS : (h + 1) * ROWS, :].astype(jnp.bfloat16)


def settle_kernel(own_ref, back_ref, after, both_ref, side_ref):
    both = own_ref[...] + back_ref[...].astype(jnp.float32)
    both_ref[...] = both
    side_ref[...] = both[ROWS : 2 * ROWS].astype(jnp.bfloat16)


def vmem(n):
    return [pl.BlockSpec(memory_space=pltpu.VMEM)] * n


def smem(n):
    return [pl.BlockSpec(memory_space=pltpu.SMEM)] * n


def hbm(n):
    return [pl.BlockSpec(memory_space=pltpu.HBM)] * n


def token(n):
    return [pl.BlockSpec(memory_space=pl.ANY)] * n


def params(mib):
    return pltpu.CompilerParams(vmem_limit_bytes=mib * MIB)


def cost(flops, nbytes, exps=0):
    return pl.CostEstimate(flops=int(flops), bytes_accessed=int(nbytes), transcendentals=int(exps))


def moved(x, axis, to):
    return lax.ppermute(x, axis, [(i, to(i)) for i in range(lax.axis_size(axis))])


def turned(x, axis, by):
    count = lax.axis_size(axis)
    return moved(x, axis, lambda i: (i + by) % count)


def shape(rows, cols, dtype):
    return jax.ShapeDtypeStruct((rows, cols), dtype)


def local(queries, keys, values, grad_out, out_weight, lengths):
    bf16, f32 = jnp.bfloat16, jnp.float32
    ctx = lax.axis_index("ctx").astype(jnp.int32)
    place = ctx.reshape(1)
    head = lax.axis_index("head").astype(jnp.int32).reshape(1)
    upper = lax.rem(ctx // 2, 2) == 1
    pair = ROWS * LANES * D * 2

    other = moved(grad_out, "head", lambda i: i ^ 1)
    right = turned(grad_out, "head", 2)
    left = turned(grad_out, "head", -2)

    kv = jnp.pad(keys, ((0, 0), (0, D))) + jnp.pad(values, ((0, 0), (D, 0)))
    q4, bound = pl.pallas_call(
        prepare,
        out_shape=(shape(LANES, D, bf16), shape(8, LANES, jnp.int32)),
        in_specs=smem(2) + vmem(1),
        out_specs=tuple(vmem(2)),
        compiler_params=params(8),
        cost_estimate=cost(1, 1),
        name="prepare",
    )(place, lengths, queries)

    begun = pl.pallas_call(
        first_projection,
        out_shape=shape(ROWS, HEADS * D, f32),
        in_specs=smem(1) + vmem(2),
        out_specs=vmem(1)[0],
        compiler_params=params(8),
        cost_estimate=cost(1, 1),
        name="first_projection",
    )(head, grad_out, out_weight)

    z2 = turned(kv, "ctx", 2 * PLANE)
    z1 = turned(kv, "ctx", PLANE)

    other_right = turned(other, "head", 2)
    other_left = turned(other, "head", -2)
    far = turned(right, "head", 2)
    other_far = turned(other_left, "head", -2)

    picked = pl.pallas_call(
        pick_kernel,
        out_shape=shape(2 * ROWS, 2 * D, bf16),
        in_specs=smem(1) + vmem(3) + token(2),
        out_specs=vmem(1)[0],
        compiler_params=params(8),
        cost_estimate=cost(1, 1),
        name="pick_side",
    )(place, z2, z1, kv, q4, begun)
    side = moved(picked, "ctx", lambda i: i ^ 2)

    s_near, stat = pl.pallas_call(
        near_kernel,
        out_shape=(shape(3 * ROWS, LANES, f32), shape(8, LANES, f32)),
        in_specs=smem(1) + vmem(5) + token(3),
        out_specs=tuple(vmem(2)),
        compiler_params=params(10),
        cost_estimate=cost(1, 1),
        name="near_scores",
    )(place, z2, z1, kv, q4, bound, picked, right, left)

    own = pl.pallas_call(
        join_kernel,
        out_shape=shape(SLOTS * ROWS, 2 * D, bf16),
        in_specs=vmem(4) + token(3),
        out_specs=vmem(1)[0],
        compiler_params=params(8),
        cost_estimate=cost(1, 1),
        name="join_slots",
    )(z2, z1, kv, side, stat, other_right, other_left)
    par = moved(own, "ctx", lambda i: i ^ 1)

    early = pl.pallas_call(
        early_kernel,
        out_shape=shape(ROWS, HEADS * D, f32),
        in_specs=smem(1) + vmem(7) + token(1),
        out_specs=vmem(1)[0],
        compiler_params=params(10),
        cost_estimate=cost(1, 1),
        name="early_projection",
    )(head, begun, other, right, left, other_right, other_left, out_weight, own)

    p_own, p_par, out_t = pl.pallas_call(
        rest_kernel,
        out_shape=(shape(SLOTS * ROWS, LANES, bf16), shape(REACH * ROWS, LANES, bf16), shape(D, LANES, f32)),
        in_specs=smem(1) + vmem(6) + token(1),
        out_specs=tuple(vmem(3)),
        scratch_shapes=[pltpu.VMEM((2 * ROWS, LANES), f32), pltpu.VMEM((REACH * ROWS, LANES), f32)],
        compiler_params=params(12),
        cost_estimate=cost(1, 1),
        name="softmax",
    )(place, own, par, q4, bound, s_near, stat, early)

    far_cross, g4, rd, dq = pl.pallas_call(
        cross_far,
        out_shape=(shape(2 * ROWS, 2 * D, bf16), shape(LANES, D, bf16), shape(1, LANES, f32), shape(D, LANES, f32)),
        in_specs=smem(2) + vmem(8),
        out_specs=tuple(vmem(4)),
        compiler_params=params(10),
        cost_estimate=cost(1, 1),
        name="cross_far",
    )(place, head, far, other_far, early, out_weight, q4, par, p_par, out_t)
    far_back = moved(far_cross, "ctx", lambda i: i ^ 1)

    near_cross, dq = pl.pallas_call(
        cross_near,
        out_shape=(shape(3 * ROWS, 2 * D, bf16), shape(D, LANES, f32)),
        in_specs=smem(1) + vmem(6),
        out_specs=tuple(vmem(2)),
        compiler_params=params(10),
        cost_estimate=cost(1, 1),
        name="cross_near",
    )(place, q4, par, p_par, g4, rd, dq)
    near_back = moved(near_cross, "ctx", lambda i: i ^ 1)

    far_own, dq = pl.pallas_call(
        own_far,
        out_shape=(shape(2 * ROWS, 2 * D, f32), shape(D, LANES, f32)),
        in_specs=vmem(6),
        out_specs=tuple(vmem(2)),
        compiler_params=params(10),
        cost_estimate=cost(1, 1),
        name="own_far",
    )(q4, own, p_own, g4, rd, dq)
    far_both = far_own + far_back.astype(f32)
    far_side = moved(far_both[ROWS:].astype(bf16), "ctx", lambda i: i ^ 2)

    near_own, grad_queries = pl.pallas_call(
        own_near,
        out_shape=(shape(3 * ROWS, 2 * D, f32), shape(ROWS, HEADS * D, bf16)),
        in_specs=vmem(6) + token(1),
        out_specs=tuple(vmem(2)),
        scratch_shapes=[pltpu.VMEM((D, LANES), f32)],
        compiler_params=params(10),
        cost_estimate=cost(1, 1),
        name="own_near",
    )(q4, own, p_own, g4, rd, dq, far_back)
    zero = jnp.zeros((ROWS, 2 * D), f32)
    far_side = far_side.astype(f32)
    to_two = (far_both[:ROWS] + jnp.where(upper, far_side, zero)).astype(bf16)
    got_two = turned(to_two, "ctx", -2 * PLANE)

    near_both, near_side = pl.pallas_call(
        settle_kernel,
        out_shape=(shape(3 * ROWS, 2 * D, f32), shape(ROWS, 2 * D, bf16)),
        in_specs=vmem(2) + token(1),
        out_specs=tuple(vmem(2)),
        compiler_params=params(8),
        cost_estimate=cost(1, 1),
        name="settle",
    )(near_own, near_back, to_two)
    near_side = moved(near_side, "ctx", lambda i: i ^ 2).astype(f32)

    to_one = near_both[:ROWS] + jnp.where(upper, near_side, far_side)
    got_one = turned(to_one.astype(bf16), "ctx", -PLANE)
    total = near_both[2 * ROWS :] + jnp.where(upper, zero, near_side)
    total = (total + got_one.astype(f32) + got_two.astype(f32)).astype(bf16)
    return grad_queries, total[:, :D], total[:, D:]


def solution(mesh):
    return jax.shard_map(
        local,
        mesh=mesh,
        in_specs=(
            P("ctx", "head"),
            P("ctx", "head"),
            P("ctx", "head"),
            P("ctx", "head"),
            P("head", None),
            P(),
        ),
        out_specs=(P("ctx", "head"), P("ctx", "head"), P("ctx", "head")),
        check_vma=False,
    )
```

```python
import functools

import jax
import jax.numpy as jnp
from jax import lax
from jax.experimental import pallas as pl
from jax.experimental.pallas import tpu as pltpu
from jax.sharding import PartitionSpec as P

D = 128
HEADS = 4
ROWS = 192
LANES = HEADS * ROWS
REACH = 4
SLOTS = REACH + 1
PLANE = 4
BLOCK = 512
NEG = -1e30
FLOOR = -1e20
SCALE = D**-0.5
LOG2E = 1.4426950408889634
MIB = 1 << 20


def dot(a, b, ca, cb):
    return lax.dot_general(a, b, (((ca,), (cb,)), ((), ())), preferred_element_type=jnp.float32)


def stack_heads(src, dst):
    for h in range(HEADS):
        dst[h * ROWS : (h + 1) * ROWS, :] = src[:, h * D : (h + 1) * D]


def prepare(place_ref, len_hbm, q_hbm, q4_ref, bound_ref, len_ref, sems):
    copies = [pltpu.make_async_copy(len_hbm, len_ref, sems.at[0])]
    for h in range(HEADS):
        rows, cols = pl.ds(h * ROWS, ROWS), pl.ds(h * D, D)
        copies.append(pltpu.make_async_copy(q_hbm.at[:, cols], q4_ref.at[rows, :], sems.at[1 + h]))
    for copy in copies:
        copy.start()
    lane = lax.broadcasted_iota(jnp.int32, (1, LANES), 1)
    pos = lane + place_ref[0] * ROWS
    for h in range(1, HEADS):
        pos = pos - jnp.where(lane >= h * ROWS, ROWS, 0)
    start = jnp.zeros((1, LANES), jnp.int32)
    end = jnp.int32(0)
    copies[0].wait()
    for d in range(len_ref.shape[0]):
        end = end + len_ref[d]
        start = jnp.where(end <= pos, end, start)
    bound_ref[0:1, :] = pos
    bound_ref[1:2, :] = start
    for copy in copies[1:]:
        copy.wait()


def pick_kernel(place_ref, z2_ref, z1_ref, z0_ref, *refs):
    out_ref = refs[-1]
    upper = lax.rem(lax.div(place_ref[0], 2), 2) == 1

    @pl.when(upper)
    def _():
        out_ref[:ROWS, :] = z2_ref[...]
        out_ref[ROWS:, :] = z1_ref[...]

    @pl.when(jnp.logical_not(upper))
    def _():
        out_ref[:ROWS, :] = z1_ref[...]
        out_ref[ROWS:, :] = z0_ref[...]


def join_kernel(z2_ref, z1_ref, z0_ref, side_ref, *refs):
    out_ref = refs[-1]
    parts = (z2_ref[...], side_ref[:ROWS, :], z1_ref[...], side_ref[ROWS:, :], z0_ref[...])
    for m, part in enumerate(parts):
        out_ref[m * ROWS : (m + 1) * ROWS, :] = part


def score(kv, queries, row, base, bound_ref, diagonal):
    s = dot(kv[:, :D], queries, 1, 1) * (SCALE * LOG2E)
    key = row + base * ROWS
    visible = key >= bound_ref[1:2, :]
    if diagonal:
        visible = visible & (key <= bound_ref[0:1, :])
    return jnp.where(visible, s, NEG)


def online(s, state):
    top, total = state
    new = jnp.maximum(top, jnp.max(s, axis=0, keepdims=True))
    total = total * jnp.exp2(top - new) + jnp.sum(jnp.exp2(s - new), axis=0, keepdims=True)
    return new, total


def near_kernel(place_ref, z2_ref, z1_ref, z0_ref, q4_ref, bound_ref, *refs):
    s_ref, stat_ref = refs[-2:]
    me = place_ref[0]
    queries = q4_ref[...]
    row = lax.broadcasted_iota(jnp.int32, (ROWS, LANES), 0)
    s = score(z0_ref[...], queries, row, me, bound_ref, True)
    s_ref[2 * ROWS :, :] = s
    top = jnp.max(s, axis=0, keepdims=True)
    state = (top, jnp.sum(jnp.exp2(s - top), axis=0, keepdims=True))
    for i, ref in ((1, z1_ref), (0, z2_ref)):
        s = score(ref[...], queries, row, me - PLANE * (2 - i), bound_ref, False)
        s_ref[i * ROWS : (i + 1) * ROWS, :] = s
        state = online(s, state)
    stat_ref[0:1, :] = state[0]
    stat_ref[1:2, :] = state[1]


def rows(i):
    return pl.ds(pl.multiple_of(i * ROWS, ROWS), ROWS)


def close(state):
    top, total = state
    return top + jnp.log2(jnp.maximum(total, 1e-30))


def weigh(s, log_total, values, state):
    acc, mass = state
    prob = jnp.exp2(s - log_total).astype(jnp.bfloat16)
    acc = acc + dot(values, prob, 0, 0)
    mass = mass + jnp.sum(prob.astype(jnp.float32), axis=0, keepdims=True)
    return prob, (acc, mass)


def no_weight():
    return jnp.zeros((D, LANES), jnp.float32), jnp.zeros((1, LANES), jnp.float32)


def project(acc, pieces, sources, w_ref):
    for piece, source in zip(pieces, sources):
        part = dot(piece[...], w_ref[:, pl.ds(pl.multiple_of(source * BLOCK, BLOCK), BLOCK)], 1, 1)
        acc = part if acc is None else acc + part
    return acc


def source_of(head, by, flip):
    at = lax.rem(head + by + 8, 8)
    return at + 1 - 2 * lax.rem(at, 2) if flip else at


def middle_kernel(place_ref, head_ref, own_ref, q4_ref, bound_ref, s_ref, stat_ref, g_hbm, w_hbm, y_ref, r_ref, l_ref, or_ref, ol_ref, p_ref, o_ref, log_ref, acc_ref, tail_ref, s_side, g_ref, w_ref, sems):
    head = head_ref[0]
    tails = (source_of(head, 4, False), source_of(head, 4, True))
    copies = [pltpu.make_async_copy(w_hbm, w_ref, sems.at[0]), pltpu.make_async_copy(g_hbm, g_ref, sems.at[1])]
    for i, source in enumerate(tails):
        cols = pl.ds(pl.multiple_of(source * BLOCK, BLOCK), BLOCK)
        copies.append(pltpu.make_async_copy(w_hbm.at[:, cols], tail_ref.at[:, pl.ds(i * BLOCK, BLOCK)], sems.at[2 + i]))
    for copy in copies:
        copy.start()

    queries = q4_ref[...]
    row = lax.broadcasted_iota(jnp.int32, (ROWS, LANES), 0)

    def side(i, state):
        slot = 2 * i + 1
        s = score(own_ref[rows(slot), :], queries, row, place_ref[0] + 2 * (slot - REACH), bound_ref, False)
        s_side[rows(i), :] = s
        return online(s, state)

    log_total = close(lax.fori_loop(0, 2, side, (stat_ref[0:1, :], stat_ref[1:2, :])))
    log_ref[0:1, :] = log_total

    def weigh_main(i, state):
        prob, state = weigh(s_ref[rows(i), :], log_total, own_ref[rows(2 * i), D:], state)
        p_ref[rows(2 * i), :] = prob
        return state

    def weigh_side(i, state):
        prob, state = weigh(s_side[rows(i), :], log_total, own_ref[rows(2 * i + 1), D:], state)
        p_ref[rows(2 * i + 1), :] = prob
        return state

    acc, mass = lax.fori_loop(0, 2, weigh_side, lax.fori_loop(0, 3, weigh_main, no_weight()))
    o_ref[...] = acc / mass
    for copy in copies:
        copy.wait()
    sources = (head, source_of(head, 0, True), source_of(head, -2, False), source_of(head, 2, False))
    sources += (source_of(head, -2, True), source_of(head, 2, True))
    acc_ref[...] = project(None, (g_ref, y_ref, r_ref, l_ref, or_ref, ol_ref), sources, w_ref)


def across_kernel(place_ref, par_ref, q4_ref, bound_ref, o_own_ref, log_ref, p_ref, o_ref, f_ref, s_par):
    me = place_ref[0]
    core = lax.rem(me, 2)
    chip = me - core
    queries = q4_ref[...]
    row = lax.broadcasted_iota(jnp.int32, (ROWS, LANES), 0)

    def across(i, state):
        slot = i + core
        s = score(par_ref[rows(slot), :], queries, row, chip + 1 - core + 2 * (slot - REACH), bound_ref, False)
        s_par[rows(i), :] = s
        return online(s, state)

    state = (jnp.full((1, LANES), FLOOR, jnp.float32), jnp.zeros((1, LANES), jnp.float32))
    log_par = close(lax.fori_loop(0, REACH, across, state))

    def weigh_across(i, state):
        prob, state = weigh(s_par[rows(i), :], log_par, par_ref[rows(i + core), D:], state)
        p_ref[rows(i), :] = prob
        return state

    acc, mass = lax.fori_loop(0, REACH, weigh_across, no_weight())
    log_own = log_ref[0:1, :]
    top = jnp.maximum(log_own, log_par)
    own, par = jnp.exp2(log_own - top), jnp.exp2(log_par - top)
    both = own + par
    own, par = own / both, par / both
    f_ref[0:1, :] = own
    f_ref[1:2, :] = par
    o_ref[...] = o_own_ref[...] * own + acc * (par / jnp.maximum(mass, 0.5))


def back_block(kv_ref, slot, p_ref, i, g4, q4, rd, share):
    prob = p_ref[rows(i), :].astype(jnp.float32) * share
    dprob = dot(kv_ref[rows(slot), D:], g4, 1, 1)
    ds = (prob * (dprob - rd)).astype(jnp.bfloat16)
    dv = dot(prob.astype(jnp.bfloat16), g4, 1, 0)
    dk = dot(ds, q4, 1, 0) * SCALE
    dq = dot(kv_ref[rows(slot), :D], ds, 0, 0)
    return dk, dv, dq


def put(out_ref, slot, dk, dv):
    at = pl.ds(pl.multiple_of(slot * ROWS, ROWS), ROWS)
    out_ref[at, :D] = dk.astype(out_ref.dtype)
    out_ref[at, D:] = dv.astype(out_ref.dtype)


def cross_far(place_ref, a_ref, b_ref, early_ref, w_ref, q4_ref, par_ref, p_ref, o_ref, f_ref, out_ref, g_ref, rd_ref, dq_ref):
    core = lax.rem(place_ref[0], 2)
    acc = project(early_ref[...], (a_ref, b_ref), (0, 1), w_ref)
    acc = acc.astype(jnp.bfloat16)
    for h in range(HEADS):
        g_ref[h * ROWS : (h + 1) * ROWS, :] = acc[:, h * D : (h + 1) * D]
    g4 = g_ref[...]
    gt = jnp.transpose(g4.astype(jnp.float32))
    rd = jnp.sum(gt * o_ref[...], axis=0, keepdims=True)
    rd_ref[...] = rd
    dq_ref[...] = jnp.zeros((D, LANES), jnp.float32)

    @pl.when(core == 1)
    def _():
        out_ref[:ROWS, :] = jnp.zeros((ROWS, 2 * D), out_ref.dtype)

    def step(slot, _):
        dk, dv, dq = back_block(par_ref, slot, p_ref, slot - core, g4, q4_ref[...], rd, f_ref[1:2, :])
        put(out_ref, slot, dk, dv)
        dq_ref[...] += dq
        return 0

    lax.fori_loop(core, 2, step, 0)


def cross_near(place_ref, q4_ref, par_ref, p_ref, g_ref, rd_ref, f_ref, dq_in_ref, out_ref, dq_ref):
    core = lax.rem(place_ref[0], 2)
    g4 = g_ref[...]
    rd = rd_ref[...]
    dq_ref[...] = dq_in_ref[...]

    @pl.when(core == 0)
    def _():
        out_ref[2 * ROWS :, :] = jnp.zeros((ROWS, 2 * D), out_ref.dtype)

    def step(slot, _):
        dk, dv, dq = back_block(par_ref, slot, p_ref, slot - core, g4, q4_ref[...], rd, f_ref[1:2, :])
        put(out_ref, slot - 2, dk, dv)
        dq_ref[...] += dq
        return 0

    lax.fori_loop(2, REACH + core, step, 0)


def own_far(q4_ref, own_ref, p_ref, g_ref, rd_ref, f_ref, dq_in_ref, out_ref, dq_ref):
    g4 = g_ref[...]
    rd = rd_ref[...]
    dq_ref[...] = dq_in_ref[...]

    def step(slot, _):
        dk, dv, dq = back_block(own_ref, slot, p_ref, slot, g4, q4_ref[...], rd, f_ref[0:1, :])
        put(out_ref, slot, dk, dv)
        dq_ref[...] += dq
        return 0

    lax.fori_loop(0, 2, step, 0)


def own_near(q4_ref, own_ref, p_ref, g_ref, rd_ref, f_ref, dq_in_ref, after, out_ref, dq_out_ref, acc):
    g4 = g_ref[...]
    rd = rd_ref[...]
    acc[...] = dq_in_ref[...]

    def step(slot, _):
        dk, dv, dq = back_block(own_ref, slot, p_ref, slot, g4, q4_ref[...], rd, f_ref[0:1, :])
        put(out_ref, slot - 2, dk, dv)
        acc[...] += dq
        return 0

    lax.fori_loop(2, SLOTS, step, 0)
    dq = jnp.transpose(acc[...]) * SCALE
    for h in range(HEADS):
        dq_out_ref[:, h * D : (h + 1) * D] = dq[h * ROWS : (h + 1) * ROWS, :].astype(jnp.bfloat16)


def is_upper(place_ref):
    return (lax.rem(lax.div(place_ref[0], 2), 2) == 1).astype(jnp.float32)


def settle_far(own_ref, back_ref, keep_ref, side_ref):
    both = own_ref[...] + back_ref[...].astype(jnp.float32)
    keep_ref[...] = both[:ROWS]
    side_ref[...] = both[ROWS:].astype(jnp.bfloat16)


def relay_far(place_ref, keep_ref, side_ref, out_ref):
    out_ref[...] = (keep_ref[...] + side_ref[...].astype(jnp.float32) * is_upper(place_ref)).astype(jnp.bfloat16)


def settle_near(own_ref, back_ref, after, both_ref, side_ref):
    both = own_ref[...] + back_ref[...].astype(jnp.float32)
    both_ref[...] = both
    side_ref[...] = both[ROWS : 2 * ROWS].astype(jnp.bfloat16)


def relay_near(place_ref, both_ref, near_ref, far_ref, out_ref, keep_ref):
    upper = is_upper(place_ref)
    near, far = near_ref[...].astype(jnp.float32), far_ref[...].astype(jnp.float32)
    out_ref[...] = (both_ref[:ROWS, :] + near * upper + far * (1 - upper)).astype(jnp.bfloat16)
    keep_ref[...] = both_ref[2 * ROWS :, :] + near * (1 - upper)


def vmem(n):
    return [pl.BlockSpec(memory_space=pltpu.VMEM)] * n


def smem(n):
    return [pl.BlockSpec(memory_space=pltpu.SMEM)] * n


def hbm(n):
    return [pl.BlockSpec(memory_space=pltpu.HBM)] * n


def token(n):
    return [pl.BlockSpec(memory_space=pl.ANY)] * n


def params(mib):
    return pltpu.CompilerParams(vmem_limit_bytes=mib * MIB)


def moved(x, axis, to):
    return lax.ppermute(x, axis, [(i, to(i)) for i in range(lax.axis_size(axis))])


def turned(x, axis, by):
    count = lax.axis_size(axis)
    return moved(x, axis, lambda i: (i + by) % count)


def shape(rows, cols, dtype):
    return jax.ShapeDtypeStruct((rows, cols), dtype)


def call(name, kernel, outs, ins, mib, args, scratch=()):
    one = not isinstance(outs, tuple)
    return pl.pallas_call(
        kernel,
        out_shape=outs,
        in_specs=ins,
        out_specs=vmem(1)[0] if one else tuple(vmem(len(outs))),
        scratch_shapes=list(scratch),
        compiler_params=params(mib),
        cost_estimate=pl.CostEstimate(flops=1, bytes_accessed=1, transcendentals=0),
        name=name,
    )(*args)


def local(queries, keys, values, grad_out, out_weight, lengths):
    bf16, f32 = jnp.bfloat16, jnp.float32
    place = lax.axis_index("ctx").astype(jnp.int32).reshape(1)
    head = lax.axis_index("head").astype(jnp.int32).reshape(1)
    dma = pltpu.SemaphoreType.DMA
    pinned = functools.partial(pltpu.with_memory_space_constraint, memory_space=pltpu.HBM)

    other = moved(grad_out, "head", lambda i: i ^ 1)
    right = turned(grad_out, "head", 2)
    left = turned(grad_out, "head", -2)
    kv = jnp.pad(keys, ((0, 0), (0, D))) + jnp.pad(values, ((0, 0), (D, 0)))
    z2 = turned(kv, "ctx", 2 * PLANE)
    z1 = turned(kv, "ctx", PLANE)
    other_right = turned(other, "head", 2)
    other_left = turned(other, "head", -2)
    far = turned(right, "head", 2)
    other_far = turned(other_left, "head", -2)

    q4, bound = call(
        "prepare",
        prepare,
        (shape(LANES, D, bf16), shape(8, LANES, jnp.int32)),
        smem(1) + hbm(2),
        4,
        (place, pinned(lengths), pinned(queries)),
        [pltpu.SMEM((lengths.shape[0],), jnp.int32), dma((1 + HEADS,))],
    )
    picked = call("pick_side", pick_kernel, shape(2 * ROWS, 2 * D, bf16), smem(1) + vmem(3) + token(1), 4, (place, z2, z1, kv, q4))
    side = moved(picked, "ctx", lambda i: i ^ 2)
    s_near, stat = call(
        "near_scores",
        near_kernel,
        (shape(3 * ROWS, LANES, f32), shape(8, LANES, f32)),
        smem(1) + vmem(5) + token(4),
        8,
        (place, z2, z1, kv, q4, bound, picked, other, right, left),
    )
    own = call("join_slots", join_kernel, shape(SLOTS * ROWS, 2 * D, bf16), vmem(4) + token(3), 4, (z2, z1, kv, side, stat, other_right, other_left))
    par = moved(own, "ctx", lambda i: i ^ 1)

    p_own, o_own, log_own, early, tail = call(
        "middle",
        middle_kernel,
        (
            shape(SLOTS * ROWS, LANES, bf16),
            shape(D, LANES, f32),
            shape(8, LANES, f32),
            shape(ROWS, HEADS * D, f32),
            shape(HEADS * D, 2 * BLOCK, bf16),
        ),
        smem(2) + vmem(5) + hbm(2) + vmem(5),
        16,
        (place, head, own, q4, bound, s_near, stat, pinned(grad_out), pinned(out_weight), other, right, left, other_right, other_left),
        [
            pltpu.VMEM((2 * ROWS, LANES), f32),
            pltpu.VMEM((ROWS, BLOCK), bf16),
            pltpu.VMEM((HEADS * D, 8 * BLOCK), bf16),
            dma((4,)),
        ],
    )
    p_par, out_t, share = call(
        "across",
        across_kernel,
        (shape(REACH * ROWS, LANES, bf16), shape(D, LANES, f32), shape(8, LANES, f32)),
        smem(1) + vmem(5),
        12,
        (place, par, q4, bound, o_own, log_own),
        [pltpu.VMEM((REACH * ROWS, LANES), f32)],
    )

    far_cross, g4, rd, dq = call(
        "cross_far",
        cross_far,
        (shape(2 * ROWS, 2 * D, bf16), shape(LANES, D, bf16), shape(1, LANES, f32), shape(D, LANES, f32)),
        smem(1) + vmem(9),
        10,
        (place, far, other_far, early, tail, q4, par, p_par, out_t, share),
    )
    far_back = moved(far_cross, "ctx", lambda i: i ^ 1)
    near_cross, dq = call(
        "cross_near",
        cross_near,
        (shape(3 * ROWS, 2 * D, bf16), shape(D, LANES, f32)),
        smem(1) + vmem(7),
        10,
        (place, q4, par, p_par, g4, rd, share, dq),
    )
    near_back = moved(near_cross, "ctx", lambda i: i ^ 1)
    far_own, dq = call(
        "own_far",
        own_far,
        (shape(2 * ROWS, 2 * D, f32), shape(D, LANES, f32)),
        vmem(7),
        10,
        (q4, own, p_own, g4, rd, share, dq),
    )
    far_keep, far_side = call(
        "settle_far", settle_far, (shape(ROWS, 2 * D, f32), shape(ROWS, 2 * D, bf16)), vmem(2), 4, (far_own, far_back)
    )
    far_side = moved(far_side, "ctx", lambda i: i ^ 2)
    near_own, grad_queries = call(
        "own_near",
        own_near,
        (shape(3 * ROWS, 2 * D, f32), shape(ROWS, HEADS * D, bf16)),
        vmem(7) + token(1),
        10,
        (q4, own, p_own, g4, rd, share, dq, far_keep),
        [pltpu.VMEM((D, LANES), f32)],
    )
    to_two = call("relay_far", relay_far, shape(ROWS, 2 * D, bf16), smem(1) + vmem(2), 4, (place, far_keep, far_side))
    got_two = turned(to_two, "ctx", -2 * PLANE)
    near_both, near_side = call(
        "settle_near",
        settle_near,
        (shape(3 * ROWS, 2 * D, f32), shape(ROWS, 2 * D, bf16)),
        vmem(2) + token(1),
        4,
        (near_own, near_back, to_two),
    )
    near_side = moved(near_side, "ctx", lambda i: i ^ 2)
    to_one, keep = call(
        "relay_near",
        relay_near,
        (shape(ROWS, 2 * D, bf16), shape(ROWS, 2 * D, f32)),
        smem(1) + vmem(3),
        4,
        (place, near_both, near_side, far_side),
    )
    got_one = turned(to_one, "ctx", -PLANE)
    total = (keep + got_one.astype(f32) + got_two.astype(f32)).astype(bf16)
    return grad_queries, total[:, :D], total[:, D:]


def solution(mesh):
    return jax.shard_map(
        local,
        mesh=mesh,
        in_specs=(
            P("ctx", "head"),
            P("ctx", "head"),
            P("ctx", "head"),
            P("ctx", "head"),
            P("head", None),
            P(),
        ),
        out_specs=(P("ctx", "head"), P("ctx", "head"), P("ctx", "head")),
        check_vma=False,
    )
```

```python
import functools

import jax
import jax.numpy as jnp
from jax import lax
from jax.experimental import pallas as pl
from jax.experimental.pallas import tpu as pltpu
from jax.sharding import PartitionSpec as P

D = 128
HEADS = 4
ROWS = 192
LANES = HEADS * ROWS
REACH = 4
SLOTS = REACH + 1
PLANE = 4
BLOCK = 512
NEG = -1e30
FLOOR = -1e20
SCALE = D**-0.5
LOG2E = 1.4426950408889634
MIB = 1 << 20


def dot(a, b, ca, cb):
    return lax.dot_general(a, b, (((ca,), (cb,)), ((), ())), preferred_element_type=jnp.float32)


def stack_heads(src, dst):
    for h in range(HEADS):
        dst[h * ROWS : (h + 1) * ROWS, :] = src[:, h * D : (h + 1) * D]


def prepare(place_ref, len_hbm, q_hbm, q4_ref, bound_ref, len_ref, sems):
    copies = [pltpu.make_async_copy(len_hbm, len_ref, sems.at[0])]
    for h in range(HEADS):
        rows, cols = pl.ds(h * ROWS, ROWS), pl.ds(h * D, D)
        copies.append(pltpu.make_async_copy(q_hbm.at[:, cols], q4_ref.at[rows, :], sems.at[1 + h]))
    for copy in copies:
        copy.start()
    lane = lax.broadcasted_iota(jnp.int32, (1, LANES), 1)
    pos = lane + place_ref[0] * ROWS
    for h in range(1, HEADS):
        pos = pos - jnp.where(lane >= h * ROWS, ROWS, 0)
    start = jnp.zeros((1, LANES), jnp.int32)
    end = jnp.int32(0)
    copies[0].wait()
    for d in range(len_ref.shape[0]):
        end = end + len_ref[d]
        start = jnp.where(end <= pos, end, start)
    bound_ref[0:1, :] = pos
    bound_ref[1:2, :] = start
    for copy in copies[1:]:
        copy.wait()


def pick_kernel(place_ref, z2_ref, z1_ref, z0_ref, *refs):
    out_ref = refs[-1]
    upper = lax.rem(lax.div(place_ref[0], 2), 2) == 1

    @pl.when(upper)
    def _():
        out_ref[:ROWS, :] = z2_ref[...]
        out_ref[ROWS:, :] = z1_ref[...]

    @pl.when(jnp.logical_not(upper))
    def _():
        out_ref[:ROWS, :] = z1_ref[...]
        out_ref[ROWS:, :] = z0_ref[...]


def join_kernel(z2_ref, z1_ref, z0_ref, side_ref, *refs):
    out_ref = refs[-1]
    parts = (z2_ref[...], side_ref[:ROWS, :], z1_ref[...], side_ref[ROWS:, :], z0_ref[...])
    for m, part in enumerate(parts):
        out_ref[m * ROWS : (m + 1) * ROWS, :] = part


def score(kv, queries, row, base, bound_ref, diagonal):
    s = dot(kv[:, :D], queries, 1, 1) * (SCALE * LOG2E)
    key = row + base * ROWS
    visible = key >= bound_ref[1:2, :]
    if diagonal:
        visible = visible & (key <= bound_ref[0:1, :])
    return jnp.where(visible, s, NEG)


def online(s, state):
    top, total = state
    new = jnp.maximum(top, jnp.max(s, axis=0, keepdims=True))
    total = total * jnp.exp2(top - new) + jnp.sum(jnp.exp2(s - new), axis=0, keepdims=True)
    return new, total


def near_kernel(place_ref, z2_ref, z1_ref, z0_ref, q4_ref, bound_ref, *refs):
    s_ref, stat_ref = refs[-2:]
    me = place_ref[0]
    queries = q4_ref[...]
    row = lax.broadcasted_iota(jnp.int32, (ROWS, LANES), 0)
    s = score(z0_ref[...], queries, row, me, bound_ref, True)
    s_ref[2 * ROWS :, :] = s
    top = jnp.max(s, axis=0, keepdims=True)
    state = (top, jnp.sum(jnp.exp2(s - top), axis=0, keepdims=True))
    for i, ref in ((1, z1_ref), (0, z2_ref)):
        s = score(ref[...], queries, row, me - PLANE * (2 - i), bound_ref, False)
        s_ref[i * ROWS : (i + 1) * ROWS, :] = s
        state = online(s, state)
    stat_ref[0:1, :] = state[0]
    stat_ref[1:2, :] = state[1]


def rows(i):
    return pl.ds(pl.multiple_of(i * ROWS, ROWS), ROWS)


def close(state):
    top, total = state
    return top + jnp.log2(jnp.maximum(total, 1e-30))


def weigh(s, log_total, values, state):
    acc, mass = state
    prob = jnp.exp2(s - log_total).astype(jnp.bfloat16)
    acc = acc + dot(values, prob, 0, 0)
    mass = mass + jnp.sum(prob.astype(jnp.float32), axis=0, keepdims=True)
    return prob, (acc, mass)


def no_weight():
    return jnp.zeros((D, LANES), jnp.float32), jnp.zeros((1, LANES), jnp.float32)


def project(acc, pieces, sources, w_ref):
    for piece, source in zip(pieces, sources):
        part = dot(piece[...], w_ref[:, pl.ds(pl.multiple_of(source * BLOCK, BLOCK), BLOCK)], 1, 1)
        acc = part if acc is None else acc + part
    return acc


def source_of(head, by, flip):
    at = lax.rem(head + by + 8, 8)
    return at + 1 - 2 * lax.rem(at, 2) if flip else at


def middle_kernel(place_ref, head_ref, own_ref, q4_ref, bound_ref, s_ref, stat_ref, g_hbm, w_hbm, y_ref, r_ref, l_ref, or_ref, ol_ref, p_ref, o_ref, log_ref, acc_ref, tail_ref, s_side, g_ref, w_ref, sems):
    head = head_ref[0]
    tails = (source_of(head, 4, False), source_of(head, 4, True))
    copies = [pltpu.make_async_copy(w_hbm, w_ref, sems.at[0]), pltpu.make_async_copy(g_hbm, g_ref, sems.at[1])]
    for i, source in enumerate(tails):
        cols = pl.ds(pl.multiple_of(source * BLOCK, BLOCK), BLOCK)
        copies.append(pltpu.make_async_copy(w_hbm.at[:, cols], tail_ref.at[:, pl.ds(i * BLOCK, BLOCK)], sems.at[2 + i]))
    for copy in copies:
        copy.start()

    queries = q4_ref[...]
    row = lax.broadcasted_iota(jnp.int32, (ROWS, LANES), 0)

    def side(i, state):
        slot = 2 * i + 1
        s = score(own_ref[rows(slot), :], queries, row, place_ref[0] + 2 * (slot - REACH), bound_ref, False)
        s_side[rows(i), :] = s
        return online(s, state)

    log_total = close(lax.fori_loop(0, 2, side, (stat_ref[0:1, :], stat_ref[1:2, :])))
    log_ref[0:1, :] = log_total

    def weigh_main(i, state):
        prob, state = weigh(s_ref[rows(i), :], log_total, own_ref[rows(2 * i), D:], state)
        p_ref[rows(2 * i), :] = prob
        return state

    def weigh_side(i, state):
        prob, state = weigh(s_side[rows(i), :], log_total, own_ref[rows(2 * i + 1), D:], state)
        p_ref[rows(2 * i + 1), :] = prob
        return state

    acc, mass = lax.fori_loop(0, 2, weigh_side, lax.fori_loop(0, 3, weigh_main, no_weight()))
    o_ref[...] = acc / mass
    for copy in copies:
        copy.wait()
    sources = (head, source_of(head, 0, True), source_of(head, -2, False), source_of(head, 2, False))
    sources += (source_of(head, -2, True), source_of(head, 2, True))
    acc_ref[...] = project(None, (g_ref, y_ref, r_ref, l_ref, or_ref, ol_ref), sources, w_ref)


def across_kernel(place_ref, par_ref, q4_ref, bound_ref, o_own_ref, log_ref, p_ref, o_ref, f_ref, s_par):
    me = place_ref[0]
    core = lax.rem(me, 2)
    chip = me - core
    queries = q4_ref[...]
    row = lax.broadcasted_iota(jnp.int32, (ROWS, LANES), 0)

    def across(i, state):
        slot = i + core
        s = score(par_ref[rows(slot), :], queries, row, chip + 1 - core + 2 * (slot - REACH), bound_ref, False)
        s_par[rows(i), :] = s
        return online(s, state)

    state = (jnp.full((1, LANES), FLOOR, jnp.float32), jnp.zeros((1, LANES), jnp.float32))
    log_par = close(lax.fori_loop(0, REACH, across, state))

    def weigh_across(i, state):
        prob, state = weigh(s_par[rows(i), :], log_par, par_ref[rows(i + core), D:], state)
        p_ref[rows(i), :] = prob
        return state

    acc, mass = lax.fori_loop(0, REACH, weigh_across, no_weight())
    log_own = log_ref[0:1, :]
    top = jnp.maximum(log_own, log_par)
    own, par = jnp.exp2(log_own - top), jnp.exp2(log_par - top)
    both = own + par
    own, par = own / both, par / both
    f_ref[0:1, :] = own
    f_ref[1:2, :] = par
    o_ref[...] = o_own_ref[...] * own + acc * (par / jnp.maximum(mass, 0.5))


def back_block(kv_ref, slot, p_ref, i, g4, q4, rd, share):
    prob = p_ref[rows(i), :].astype(jnp.float32) * share
    dprob = dot(kv_ref[rows(slot), D:], g4, 1, 1)
    ds = (prob * (dprob - rd)).astype(jnp.bfloat16)
    dv = dot(prob.astype(jnp.bfloat16), g4, 1, 0)
    dk = dot(ds, q4, 1, 0) * SCALE
    dq = dot(kv_ref[rows(slot), :D], ds, 0, 0)
    return dk, dv, dq


def put(out_ref, slot, dk, dv):
    at = pl.ds(pl.multiple_of(slot * ROWS, ROWS), ROWS)
    out_ref[at, :D] = dk.astype(out_ref.dtype)
    out_ref[at, D:] = dv.astype(out_ref.dtype)


def cross_far(place_ref, a_ref, b_ref, early_ref, w_ref, q4_ref, par_ref, p_ref, o_ref, f_ref, out_ref, g_ref, rd_ref, dq_ref):
    core = lax.rem(place_ref[0], 2)
    acc = project(early_ref[...], (a_ref, b_ref), (0, 1), w_ref)
    acc = acc.astype(jnp.bfloat16)
    for h in range(HEADS):
        g_ref[h * ROWS : (h + 1) * ROWS, :] = acc[:, h * D : (h + 1) * D]
    g4 = g_ref[...]
    gt = jnp.transpose(g4.astype(jnp.float32))
    rd = jnp.sum(gt * o_ref[...], axis=0, keepdims=True)
    rd_ref[...] = rd
    dq_ref[...] = jnp.zeros((D, LANES), jnp.float32)

    @pl.when(core == 1)
    def _():
        out_ref[:ROWS, :] = jnp.zeros((ROWS, 2 * D), out_ref.dtype)

    def step(slot, _):
        dk, dv, dq = back_block(par_ref, slot, p_ref, slot - core, g4, q4_ref[...], rd, f_ref[1:2, :])
        put(out_ref, slot, dk, dv)
        dq_ref[...] += dq
        return 0

    lax.fori_loop(core, 2, step, 0)


def cross_near(place_ref, q4_ref, par_ref, p_ref, g_ref, rd_ref, f_ref, dq_in_ref, out_ref, dq_ref):
    core = lax.rem(place_ref[0], 2)
    g4 = g_ref[...]
    rd = rd_ref[...]
    dq_ref[...] = dq_in_ref[...]

    @pl.when(core == 0)
    def _():
        out_ref[2 * ROWS :, :] = jnp.zeros((ROWS, 2 * D), out_ref.dtype)

    def step(slot, _):
        dk, dv, dq = back_block(par_ref, slot, p_ref, slot - core, g4, q4_ref[...], rd, f_ref[1:2, :])
        put(out_ref, slot - 2, dk, dv)
        dq_ref[...] += dq
        return 0

    lax.fori_loop(2, REACH + core, step, 0)


def own_far(q4_ref, own_ref, p_ref, g_ref, rd_ref, f_ref, dq_in_ref, out_ref, dq_ref):
    g4 = g_ref[...]
    rd = rd_ref[...]
    dq_ref[...] = dq_in_ref[...]

    def step(slot, _):
        dk, dv, dq = back_block(own_ref, slot, p_ref, slot, g4, q4_ref[...], rd, f_ref[0:1, :])
        put(out_ref, slot, dk, dv)
        dq_ref[...] += dq
        return 0

    lax.fori_loop(0, 2, step, 0)


def own_near(q4_ref, own_ref, p_ref, g_ref, rd_ref, f_ref, dq_in_ref, after, out_ref, dq_out_ref, acc):
    g4 = g_ref[...]
    rd = rd_ref[...]
    acc[...] = dq_in_ref[...]

    def step(slot, _):
        dk, dv, dq = back_block(own_ref, slot, p_ref, slot, g4, q4_ref[...], rd, f_ref[0:1, :])
        put(out_ref, slot - 2, dk, dv)
        acc[...] += dq
        return 0

    lax.fori_loop(2, SLOTS, step, 0)
    dq = jnp.transpose(acc[...]) * SCALE
    for h in range(HEADS):
        dq_out_ref[:, h * D : (h + 1) * D] = dq[h * ROWS : (h + 1) * ROWS, :].astype(jnp.bfloat16)


def is_upper(place_ref):
    return (lax.rem(lax.div(place_ref[0], 2), 2) == 1).astype(jnp.float32)


def settle_far(own_ref, back_ref, keep_ref, side_ref):
    both = own_ref[...] + back_ref[...].astype(jnp.float32)
    keep_ref[...] = both[:ROWS]
    side_ref[...] = both[ROWS:].astype(jnp.bfloat16)


def relay_far(place_ref, keep_ref, side_ref, out_ref):
    out_ref[...] = (keep_ref[...] + side_ref[...].astype(jnp.float32) * is_upper(place_ref)).astype(jnp.bfloat16)


def settle_near(own_ref, back_ref, after, both_ref, side_ref):
    both = own_ref[...] + back_ref[...].astype(jnp.float32)
    both_ref[...] = both
    side_ref[...] = both[ROWS : 2 * ROWS].astype(jnp.bfloat16)


def relay_near(place_ref, both_ref, near_ref, far_ref, out_ref, keep_ref):
    upper = is_upper(place_ref)
    near, far = near_ref[...].astype(jnp.float32), far_ref[...].astype(jnp.float32)
    out_ref[...] = (both_ref[:ROWS, :] + near * upper + far * (1 - upper)).astype(jnp.bfloat16)
    keep_ref[...] = both_ref[2 * ROWS :, :] + near * (1 - upper)


def vmem(n):
    return [pl.BlockSpec(memory_space=pltpu.VMEM)] * n


def smem(n):
    return [pl.BlockSpec(memory_space=pltpu.SMEM)] * n


def hbm(n):
    return [pl.BlockSpec(memory_space=pltpu.HBM)] * n


def token(n):
    return [pl.BlockSpec(memory_space=pl.ANY)] * n


def params(mib):
    return pltpu.CompilerParams(vmem_limit_bytes=max(mib, 16) * MIB)


def moved(x, axis, to):
    return lax.ppermute(x, axis, [(i, to(i)) for i in range(lax.axis_size(axis))])


def turned(x, axis, by):
    count = lax.axis_size(axis)
    return moved(x, axis, lambda i: (i + by) % count)


def shape(rows, cols, dtype):
    return jax.ShapeDtypeStruct((rows, cols), dtype)


def call(name, kernel, outs, ins, mib, args, scratch=(), flops=1):
    one = not isinstance(outs, tuple)
    return pl.pallas_call(
        kernel,
        out_shape=outs,
        in_specs=ins,
        out_specs=vmem(1)[0] if one else tuple(vmem(len(outs))),
        scratch_shapes=list(scratch),
        compiler_params=params(mib),
        cost_estimate=pl.CostEstimate(flops=flops, bytes_accessed=1, transcendentals=0),
        name=name,
    )(*args)


def local(queries, keys, values, grad_out, out_weight, lengths):
    bf16, f32 = jnp.bfloat16, jnp.float32
    place = lax.axis_index("ctx").astype(jnp.int32).reshape(1)
    head = lax.axis_index("head").astype(jnp.int32).reshape(1)
    dma = pltpu.SemaphoreType.DMA
    pinned = functools.partial(pltpu.with_memory_space_constraint, memory_space=pltpu.HBM)

    other = moved(grad_out, "head", lambda i: i ^ 1)
    right = turned(grad_out, "head", 2)
    left = turned(grad_out, "head", -2)
    kv = jnp.pad(keys, ((0, 0), (0, D))) + jnp.pad(values, ((0, 0), (D, 0)))
    z2 = turned(kv, "ctx", 2 * PLANE)
    z1 = turned(kv, "ctx", PLANE)
    other_right = turned(other, "head", 2)
    other_left = turned(other, "head", -2)
    far = turned(right, "head", 2)
    other_far = turned(other_left, "head", -2)

    q4, bound = call(
        "prepare",
        prepare,
        (shape(LANES, D, bf16), shape(8, LANES, jnp.int32)),
        smem(1) + hbm(2),
        4,
        (place, pinned(lengths), pinned(queries)),
        [pltpu.SMEM((lengths.shape[0],), jnp.int32), dma((1 + HEADS,))],
    )
    picked = call("pick_side", pick_kernel, shape(2 * ROWS, 2 * D, bf16), smem(1) + vmem(3) + token(1), 4, (place, z2, z1, kv, q4))
    side = moved(picked, "ctx", lambda i: i ^ 2)
    s_near, stat = call(
        "near_scores",
        near_kernel,
        (shape(3 * ROWS, LANES, f32), shape(8, LANES, f32)),
        smem(1) + vmem(5) + token(6),
        8,
        (place, z2, z1, kv, q4, bound, picked, other, right, left, other_right, other_left),
        flops=10**10,
    )
    own = call("join_slots", join_kernel, shape(SLOTS * ROWS, 2 * D, bf16), vmem(4) + token(1), 4, (z2, z1, kv, side, stat))
    par = moved(own, "ctx", lambda i: i ^ 1)

    p_own, o_own, log_own, early, tail = call(
        "middle",
        middle_kernel,
        (
            shape(SLOTS * ROWS, LANES, bf16),
            shape(D, LANES, f32),
            shape(8, LANES, f32),
            shape(ROWS, HEADS * D, f32),
            shape(HEADS * D, 2 * BLOCK, bf16),
        ),
        smem(2) + vmem(5) + hbm(2) + vmem(5),
        16,
        (place, head, own, q4, bound, s_near, stat, pinned(grad_out), pinned(out_weight), other, right, left, other_right, other_left),
        [
            pltpu.VMEM((2 * ROWS, LANES), f32),
            pltpu.VMEM((ROWS, BLOCK), bf16),
            pltpu.VMEM((HEADS * D, 8 * BLOCK), bf16),
            dma((4,)),
        ],
    )
    p_par, out_t, share = call(
        "across",
        across_kernel,
        (shape(REACH * ROWS, LANES, bf16), shape(D, LANES, f32), shape(8, LANES, f32)),
        smem(1) + vmem(5),
        12,
        (place, par, q4, bound, o_own, log_own),
        [pltpu.VMEM((REACH * ROWS, LANES), f32)],
    )

    far_cross, g4, rd, dq = call(
        "cross_far",
        cross_far,
        (shape(2 * ROWS, 2 * D, bf16), shape(LANES, D, bf16), shape(1, LANES, f32), shape(D, LANES, f32)),
        smem(1) + vmem(9),
        10,
        (place, far, other_far, early, tail, q4, par, p_par, out_t, share),
    )
    far_back = moved(far_cross, "ctx", lambda i: i ^ 1)
    near_cross, dq = call(
        "cross_near",
        cross_near,
        (shape(3 * ROWS, 2 * D, bf16), shape(D, LANES, f32)),
        smem(1) + vmem(7),
        10,
        (place, q4, par, p_par, g4, rd, share, dq),
    )
    near_back = moved(near_cross, "ctx", lambda i: i ^ 1)
    far_own, dq = call(
        "own_far",
        own_far,
        (shape(2 * ROWS, 2 * D, f32), shape(D, LANES, f32)),
        vmem(7),
        10,
        (q4, own, p_own, g4, rd, share, dq),
    )
    far_keep, far_side = call(
        "settle_far", settle_far, (shape(ROWS, 2 * D, f32), shape(ROWS, 2 * D, bf16)), vmem(2), 4, (far_own, far_back)
    )
    far_side = moved(far_side, "ctx", lambda i: i ^ 2)
    near_own, grad_queries = call(
        "own_near",
        own_near,
        (shape(3 * ROWS, 2 * D, f32), shape(ROWS, HEADS * D, bf16)),
        vmem(7) + token(1),
        10,
        (q4, own, p_own, g4, rd, share, dq, far_keep),
        [pltpu.VMEM((D, LANES), f32)],
    )
    to_two = call("relay_far", relay_far, shape(ROWS, 2 * D, bf16), smem(1) + vmem(2), 4, (place, far_keep, far_side))
    got_two = turned(to_two, "ctx", -2 * PLANE)
    near_both, near_side = call(
        "settle_near",
        settle_near,
        (shape(3 * ROWS, 2 * D, f32), shape(ROWS, 2 * D, bf16)),
        vmem(2) + token(1),
        4,
        (near_own, near_back, to_two),
    )
    near_side = moved(near_side, "ctx", lambda i: i ^ 2)
    to_one, keep = call(
        "relay_near",
        relay_near,
        (shape(ROWS, 2 * D, bf16), shape(ROWS, 2 * D, f32)),
        smem(1) + vmem(3),
        4,
        (place, near_both, near_side, far_side),
    )
    got_one = turned(to_one, "ctx", -PLANE)
    total = (keep + got_one.astype(f32) + got_two.astype(f32)).astype(bf16)
    return grad_queries, total[:, :D], total[:, D:]


def solution(mesh):
    return jax.shard_map(
        local,
        mesh=mesh,
        in_specs=(
            P("ctx", "head"),
            P("ctx", "head"),
            P("ctx", "head"),
            P("ctx", "head"),
            P("head", None),
            P(),
        ),
        out_specs=(P("ctx", "head"), P("ctx", "head"), P("ctx", "head")),
        check_vma=False,
    )
```

```python
import functools

import jax
import jax.numpy as jnp
from jax import lax
from jax.experimental import pallas as pl
from jax.experimental.pallas import tpu as pltpu
from jax.sharding import PartitionSpec as P

D = 128
HEADS = 4
ROWS = 192
LANES = HEADS * ROWS
REACH = 4
SLOTS = REACH + 1
PLANE = 4
BLOCK = 512
STAT = 3 * ROWS
NEG = -1e30
FLOOR = -1e20
SCALE = D**-0.5
LOG2E = 1.4426950408889634
MIB = 1 << 20


def dot(a, b, ca, cb):
    return lax.dot_general(a, b, (((ca,), (cb,)), ((), ())), preferred_element_type=jnp.float32)


def stack_heads(src, dst):
    for h in range(HEADS):
        dst[h * ROWS : (h + 1) * ROWS, :] = src[:, h * D : (h + 1) * D]


def prepare(place_ref, len_hbm, q_hbm, *refs):
    q4_ref, bound_ref, len_ref, sems = refs[-4:]
    copies = [pltpu.make_async_copy(len_hbm, len_ref, sems.at[0])]
    for h in range(HEADS):
        rows, cols = pl.ds(h * ROWS, ROWS), pl.ds(h * D, D)
        copies.append(pltpu.make_async_copy(q_hbm.at[:, cols], q4_ref.at[rows, :], sems.at[1 + h]))
    for copy in copies:
        copy.start()
    lane = lax.broadcasted_iota(jnp.int32, (1, LANES), 1)
    pos = lane + place_ref[0] * ROWS
    for h in range(1, HEADS):
        pos = pos - jnp.where(lane >= h * ROWS, ROWS, 0)
    start = jnp.zeros((1, LANES), jnp.int32)
    end = jnp.int32(0)
    copies[0].wait()
    for d in range(len_ref.shape[0]):
        end = end + len_ref[d]
        start = jnp.where(end <= pos, end, start)
    bound_ref[0:1, :] = pos.astype(jnp.float32)
    bound_ref[1:2, :] = start.astype(jnp.float32)
    for copy in copies[1:]:
        copy.wait()


def pick_kernel(place_ref, z2_ref, z1_ref, z0_ref, *refs):
    out_ref = refs[-1]
    upper = lax.rem(lax.div(place_ref[0], 2), 2) == 1

    @pl.when(upper)
    def _():
        out_ref[:ROWS, :] = z2_ref[...]
        out_ref[ROWS:, :] = z1_ref[...]

    @pl.when(jnp.logical_not(upper))
    def _():
        out_ref[:ROWS, :] = z1_ref[...]
        out_ref[ROWS:, :] = z0_ref[...]


def join_kernel(z2_ref, z1_ref, z0_ref, side_ref, *refs):
    out_ref = refs[-1]
    parts = (z2_ref[...], side_ref[:ROWS, :], z1_ref[...], side_ref[ROWS:, :], z0_ref[...])
    for m, part in enumerate(parts):
        out_ref[m * ROWS : (m + 1) * ROWS, :] = part


def score(kv, queries, row, base, start, pos=None):
    s = dot(kv[:, :D], queries, 1, 1) * (SCALE * LOG2E)
    visible = row >= start - base * ROWS
    if pos is not None:
        visible = visible & (row <= pos - base * ROWS)
    return jnp.where(visible, s, NEG)


def online(s, state):
    top, total = state
    new = jnp.maximum(top, jnp.max(s, axis=0, keepdims=True))
    total = total * jnp.exp2(top - new) + jnp.sum(jnp.exp2(s - new), axis=0, keepdims=True)
    return new, total


def near_kernel(place_ref, z2_ref, z1_ref, z0_ref, q4_ref, bound_ref, *refs):
    s_ref = refs[-1]
    me = place_ref[0]
    queries = q4_ref[...]
    row = lax.broadcasted_iota(jnp.int32, (ROWS, LANES), 0)
    pos, start = bound_ref[0:1, :].astype(jnp.int32), bound_ref[1:2, :].astype(jnp.int32)
    s = score(z0_ref[...], queries, row, me, start, pos)
    s_ref[2 * ROWS : 3 * ROWS, :] = s
    top = jnp.max(s, axis=0, keepdims=True)
    state = (top, jnp.sum(jnp.exp2(s - top), axis=0, keepdims=True))
    for i, ref in ((1, z1_ref), (0, z2_ref)):
        s = score(ref[...], queries, row, me - PLANE * (2 - i), start)
        s_ref[i * ROWS : (i + 1) * ROWS, :] = s
        state = online(s, state)
    s_ref[STAT : STAT + 1, :] = state[0]
    s_ref[STAT + 1 : STAT + 2, :] = state[1]
    s_ref[STAT + 2 : STAT + 3, :] = bound_ref[1:2, :]


def rows(i):
    return pl.ds(pl.multiple_of(i * ROWS, ROWS), ROWS)


def close(state):
    top, total = state
    return top + jnp.log2(jnp.maximum(total, 1e-30))


def weigh(s, log_total, values, state):
    acc, mass = state
    prob = jnp.exp2(s - log_total).astype(jnp.bfloat16)
    acc = acc + dot(values, prob, 0, 0)
    mass = mass + jnp.sum(prob.astype(jnp.float32), axis=0, keepdims=True)
    return prob, (acc, mass)


def no_weight():
    return jnp.zeros((D, LANES), jnp.float32), jnp.zeros((1, LANES), jnp.float32)


def project(acc, pieces, sources, w_ref):
    for piece, source in zip(pieces, sources):
        part = dot(piece[...], w_ref[:, pl.ds(pl.multiple_of(source * BLOCK, BLOCK), BLOCK)], 1, 1)
        acc = part if acc is None else acc + part
    return acc


def source_of(head, by, flip):
    at = lax.rem(head + by + 8, 8)
    return at + 1 - 2 * lax.rem(at, 2) if flip else at


def middle_kernel(place_ref, head_ref, own_ref, q4_ref, s_ref, g_hbm, w_hbm, y_hbm, l_hbm, r_ref, or_ref, ol_ref, p_ref, o_ref, acc_ref, tail_ref, s_side, g_ref, y_ref, l_ref, w_ref, sems):
    head = head_ref[0]
    tails = (source_of(head, 4, False), source_of(head, 4, True))
    copies = [pltpu.make_async_copy(w_hbm, w_ref, sems.at[0]), pltpu.make_async_copy(g_hbm, g_ref, sems.at[1])]
    copies += [pltpu.make_async_copy(y_hbm, y_ref, sems.at[2]), pltpu.make_async_copy(l_hbm, l_ref, sems.at[3])]
    for i, source in enumerate(tails):
        cols = pl.ds(pl.multiple_of(source * BLOCK, BLOCK), BLOCK)
        copies.append(pltpu.make_async_copy(w_hbm.at[:, cols], tail_ref.at[:, pl.ds(i * BLOCK, BLOCK)], sems.at[4 + i]))
    for copy in copies:
        copy.start()

    queries = q4_ref[...]
    row = lax.broadcasted_iota(jnp.int32, (ROWS, LANES), 0)

    start = s_ref[STAT + 2 : STAT + 3, :].astype(jnp.int32)

    def side(i, state):
        slot = 2 * i + 1
        s = score(own_ref[rows(slot), :], queries, row, place_ref[0] + 2 * (slot - REACH), start)
        s_side[rows(i), :] = s
        return online(s, state)

    log_total = close(lax.fori_loop(0, 2, side, (s_ref[STAT : STAT + 1, :], s_ref[STAT + 1 : STAT + 2, :])))
    o_ref[D : D + 1, :] = log_total
    o_ref[D + 1 : D + 2, :] = s_ref[STAT + 2 : STAT + 3, :]

    def weigh_main(i, state):
        prob, state = weigh(s_ref[rows(i), :], log_total, own_ref[rows(2 * i), D:], state)
        p_ref[rows(2 * i), :] = prob
        return state

    def weigh_side(i, state):
        prob, state = weigh(s_side[rows(i), :], log_total, own_ref[rows(2 * i + 1), D:], state)
        p_ref[rows(2 * i + 1), :] = prob
        return state

    acc, mass = lax.fori_loop(0, 2, weigh_side, lax.fori_loop(0, 3, weigh_main, no_weight()))
    o_ref[:D, :] = acc / mass
    for copy in copies:
        copy.wait()
    sources = (head, source_of(head, 0, True), source_of(head, -2, False), source_of(head, 2, False))
    sources += (source_of(head, -2, True), source_of(head, 2, True))
    acc_ref[...] = project(None, (g_ref, y_ref, r_ref, l_ref, or_ref, ol_ref), sources, w_ref)


def across_kernel(place_ref, par_ref, q4_ref, o_own_ref, p_ref, o_ref, s_par):
    me = place_ref[0]
    core = lax.rem(me, 2)
    chip = me - core
    queries = q4_ref[...]
    row = lax.broadcasted_iota(jnp.int32, (ROWS, LANES), 0)

    start = o_own_ref[D + 1 : D + 2, :].astype(jnp.int32)

    def across(i, state):
        slot = i + core
        s = score(par_ref[rows(slot), :], queries, row, chip + 1 - core + 2 * (slot - REACH), start)
        s_par[rows(i), :] = s
        return online(s, state)

    state = (jnp.full((1, LANES), FLOOR, jnp.float32), jnp.zeros((1, LANES), jnp.float32))
    log_par = close(lax.fori_loop(0, REACH, across, state))

    def weigh_across(i, state):
        prob, state = weigh(s_par[rows(i), :], log_par, par_ref[rows(i + core), D:], state)
        p_ref[rows(i), :] = prob
        return state

    acc, mass = lax.fori_loop(0, REACH, weigh_across, no_weight())
    log_own = o_own_ref[D : D + 1, :]
    top = jnp.maximum(log_own, log_par)
    own, par = jnp.exp2(log_own - top), jnp.exp2(log_par - top)
    both = own + par
    own, par = own / both, par / both
    o_ref[D : D + 1, :] = own
    o_ref[D + 1 : D + 2, :] = par
    o_ref[:D, :] = o_own_ref[:D, :] * own + acc * (par / jnp.maximum(mass, 0.5))


def back_block(kv_ref, slot, p_ref, i, g4, q4, rd, share):
    prob = p_ref[rows(i), :].astype(jnp.float32) * share
    dprob = dot(kv_ref[rows(slot), D:], g4, 1, 1)
    ds = (prob * (dprob - rd)).astype(jnp.bfloat16)
    dv = dot(prob.astype(jnp.bfloat16), g4, 1, 0)
    dk = dot(ds, q4, 1, 0) * SCALE
    dq = dot(kv_ref[rows(slot), :D], ds, 0, 0)
    return dk, dv, dq


def put(out_ref, slot, dk, dv):
    at = pl.ds(pl.multiple_of(slot * ROWS, ROWS), ROWS)
    out_ref[at, :D] = dk.astype(out_ref.dtype)
    out_ref[at, D:] = dv.astype(out_ref.dtype)


def cross_far(place_ref, a_ref, b_ref, early_ref, w_ref, q4_ref, par_ref, p_ref, o_ref, out_ref, g_ref, dq_ref):
    core = lax.rem(place_ref[0], 2)
    acc = project(early_ref[...], (a_ref, b_ref), (0, 1), w_ref)
    acc = acc.astype(jnp.bfloat16)
    for h in range(HEADS):
        g_ref[h * ROWS : (h + 1) * ROWS, :] = acc[:, h * D : (h + 1) * D]
    g4 = g_ref[...]
    gt = jnp.transpose(g4.astype(jnp.float32))
    rd = jnp.sum(gt * o_ref[:D, :], axis=0, keepdims=True)
    dq_ref[:D, :] = jnp.zeros((D, LANES), jnp.float32)
    dq_ref[D : D + 1, :] = o_ref[D : D + 1, :]
    dq_ref[D + 1 : D + 2, :] = o_ref[D + 1 : D + 2, :]
    dq_ref[D + 2 : D + 3, :] = rd

    @pl.when(core == 1)
    def _():
        out_ref[:ROWS, :] = jnp.zeros((ROWS, 2 * D), out_ref.dtype)

    def step(slot, _):
        dk, dv, dq = back_block(par_ref, slot, p_ref, slot - core, g4, q4_ref[...], rd, dq_ref[D + 1 : D + 2, :])
        put(out_ref, slot, dk, dv)
        dq_ref[:D, :] += dq
        return 0

    lax.fori_loop(core, 2, step, 0)


def cross_near(place_ref, q4_ref, par_ref, p_ref, g_ref, dq_in_ref, out_ref, dq_ref):
    core = lax.rem(place_ref[0], 2)
    g4 = g_ref[...]
    rd = dq_in_ref[D + 2 : D + 3, :]
    dq_ref[...] = dq_in_ref[...]

    @pl.when(core == 0)
    def _():
        out_ref[2 * ROWS :, :] = jnp.zeros((ROWS, 2 * D), out_ref.dtype)

    def step(slot, _):
        dk, dv, dq = back_block(par_ref, slot, p_ref, slot - core, g4, q4_ref[...], rd, dq_ref[D + 1 : D + 2, :])
        put(out_ref, slot - 2, dk, dv)
        dq_ref[:D, :] += dq
        return 0

    lax.fori_loop(2, REACH + core, step, 0)


def own_far(q4_ref, own_ref, p_ref, g_ref, dq_in_ref, out_ref, dq_ref):
    g4 = g_ref[...]
    rd = dq_in_ref[D + 2 : D + 3, :]
    dq_ref[...] = dq_in_ref[...]

    def step(slot, _):
        dk, dv, dq = back_block(own_ref, slot, p_ref, slot, g4, q4_ref[...], rd, dq_ref[D : D + 1, :])
        put(out_ref, slot, dk, dv)
        dq_ref[:D, :] += dq
        return 0

    lax.fori_loop(0, 2, step, 0)


def own_near(q4_ref, own_ref, p_ref, g_ref, dq_in_ref, after, out_ref, dq_out_ref, acc):
    g4 = g_ref[...]
    rd = dq_in_ref[D + 2 : D + 3, :]
    acc[...] = dq_in_ref[:D, :]

    def step(slot, _):
        dk, dv, dq = back_block(own_ref, slot, p_ref, slot, g4, q4_ref[...], rd, dq_in_ref[D : D + 1, :])
        put(out_ref, slot - 2, dk, dv)
        acc[...] += dq
        return 0

    lax.fori_loop(2, SLOTS, step, 0)
    dq = jnp.transpose(acc[...]) * SCALE
    for h in range(HEADS):
        dq_out_ref[:, h * D : (h + 1) * D] = dq[h * ROWS : (h + 1) * ROWS, :].astype(jnp.bfloat16)


def is_upper(place_ref):
    return (lax.rem(lax.div(place_ref[0], 2), 2) == 1).astype(jnp.float32)


def settle_far(own_ref, back_ref, keep_ref, side_ref):
    both = own_ref[...] + back_ref[...].astype(jnp.float32)
    keep_ref[...] = both[:ROWS]
    side_ref[...] = both[ROWS:].astype(jnp.bfloat16)


def relay_far(place_ref, keep_ref, side_ref, out_ref):
    out_ref[...] = (keep_ref[...] + side_ref[...].astype(jnp.float32) * is_upper(place_ref)).astype(jnp.bfloat16)


def settle_near(own_ref, back_ref, after, both_ref, side_ref):
    both = own_ref[...] + back_ref[...].astype(jnp.float32)
    both_ref[...] = both
    side_ref[...] = both[ROWS : 2 * ROWS].astype(jnp.bfloat16)


def relay_near(place_ref, both_ref, near_ref, far_ref, out_ref, keep_ref):
    upper = is_upper(place_ref)
    near, far = near_ref[...].astype(jnp.float32), far_ref[...].astype(jnp.float32)
    out_ref[...] = (both_ref[:ROWS, :] + near * upper + far * (1 - upper)).astype(jnp.bfloat16)
    keep_ref[...] = both_ref[2 * ROWS :, :] + near * (1 - upper)


def vmem(n):
    return [pl.BlockSpec(memory_space=pltpu.VMEM)] * n


def smem(n):
    return [pl.BlockSpec(memory_space=pltpu.SMEM)] * n


def hbm(n):
    return [pl.BlockSpec(memory_space=pltpu.HBM)] * n


def token(n):
    return [pl.BlockSpec(memory_space=pl.ANY)] * n


def params(mib):
    return pltpu.CompilerParams(vmem_limit_bytes=10 * MIB)


def moved(x, axis, to):
    return lax.ppermute(x, axis, [(i, to(i)) for i in range(lax.axis_size(axis))])


def turned(x, axis, by):
    count = lax.axis_size(axis)
    return moved(x, axis, lambda i: (i + by) % count)


def shape(rows, cols, dtype):
    return jax.ShapeDtypeStruct((rows, cols), dtype)


def call(name, kernel, outs, ins, mib, args, scratch=()):
    one = not isinstance(outs, tuple)
    return pl.pallas_call(
        kernel,
        out_shape=outs,
        in_specs=ins,
        out_specs=vmem(1)[0] if one else tuple(vmem(len(outs))),
        scratch_shapes=list(scratch),
        compiler_params=params(mib),
        cost_estimate=pl.CostEstimate(flops=1, bytes_accessed=1, transcendentals=0),
        name=name,
    )(*args)


def local(queries, keys, values, grad_out, out_weight, lengths):
    bf16, f32 = jnp.bfloat16, jnp.float32
    place = lax.axis_index("ctx").astype(jnp.int32).reshape(1)
    head = lax.axis_index("head").astype(jnp.int32).reshape(1)
    dma = pltpu.SemaphoreType.DMA
    pinned = functools.partial(pltpu.with_memory_space_constraint, memory_space=pltpu.HBM)

    other = moved(grad_out, "head", lambda i: i ^ 1)
    right = turned(grad_out, "head", 2)
    left = turned(grad_out, "head", -2)
    kv = jnp.pad(keys, ((0, 0), (0, D))) + jnp.pad(values, ((0, 0), (D, 0)))
    z2 = turned(kv, "ctx", 2 * PLANE)
    z1 = turned(kv, "ctx", PLANE)
    other_right = turned(other, "head", 2)
    other_left = turned(other, "head", -2)
    far = turned(right, "head", 2)
    other_far = turned(other_left, "head", -2)

    q4, bound = call(
        "prepare",
        prepare,
        (shape(LANES, D, bf16), shape(8, LANES, f32)),
        smem(1) + hbm(2) + token(3),
        4,
        (place, pinned(lengths), pinned(queries), other, right, left),
        [pltpu.SMEM((lengths.shape[0],), jnp.int32), dma((1 + HEADS,))],
    )
    picked = call("pick_side", pick_kernel, shape(2 * ROWS, 2 * D, bf16), smem(1) + vmem(3) + token(1), 4, (place, z2, z1, kv, q4))
    side = moved(picked, "ctx", lambda i: i ^ 2)
    s_near = call(
        "near_scores",
        near_kernel,
        shape(STAT + 8, LANES, f32),
        smem(1) + vmem(5) + token(3),
        8,
        (place, z2, z1, kv, q4, bound, picked, other_right, other_left),
    )
    own = call("join_slots", join_kernel, shape(SLOTS * ROWS, 2 * D, bf16), vmem(4) + token(1), 4, (z2, z1, kv, side, s_near))
    par = moved(own, "ctx", lambda i: i ^ 1)

    p_own, o_own, early, tail = call(
        "middle",
        middle_kernel,
        (
            shape(SLOTS * ROWS, LANES, bf16),
            shape(D + 8, LANES, f32),
            shape(ROWS, HEADS * D, f32),
            shape(HEADS * D, 2 * BLOCK, bf16),
        ),
        smem(2) + vmem(3) + hbm(4) + vmem(3),
        16,
        (place, head, own, q4, s_near, pinned(grad_out), pinned(out_weight), pinned(other), pinned(left), right, other_right, other_left),
        [
            pltpu.VMEM((2 * ROWS, LANES), f32),
            pltpu.VMEM((ROWS, BLOCK), bf16),
            pltpu.VMEM((ROWS, BLOCK), bf16),
            pltpu.VMEM((ROWS, BLOCK), bf16),
            pltpu.VMEM((HEADS * D, 8 * BLOCK), bf16),
            dma((6,)),
        ],
    )
    p_par, out_t = call(
        "across",
        across_kernel,
        (shape(REACH * ROWS, LANES, bf16), shape(D + 8, LANES, f32)),
        smem(1) + vmem(3),
        12,
        (place, par, q4, o_own),
        [pltpu.VMEM((REACH * ROWS, LANES), f32)],
    )

    far_cross, g4, dq = call(
        "cross_far",
        cross_far,
        (shape(2 * ROWS, 2 * D, bf16), shape(LANES, D, bf16), shape(D + 8, LANES, f32)),
        smem(1) + vmem(8),
        10,
        (place, far, other_far, early, tail, q4, par, p_par, out_t),
    )
    far_back = moved(far_cross, "ctx", lambda i: i ^ 1)
    near_cross, dq = call(
        "cross_near",
        cross_near,
        (shape(3 * ROWS, 2 * D, bf16), shape(D + 8, LANES, f32)),
        smem(1) + vmem(5),
        10,
        (place, q4, par, p_par, g4, dq),
    )
    near_back = moved(near_cross, "ctx", lambda i: i ^ 1)
    far_own, dq = call(
        "own_far",
        own_far,
        (shape(2 * ROWS, 2 * D, f32), shape(D + 8, LANES, f32)),
        vmem(5),
        10,
        (q4, own, p_own, g4, dq),
    )
    far_keep, far_side = call(
        "settle_far", settle_far, (shape(ROWS, 2 * D, f32), shape(ROWS, 2 * D, bf16)), vmem(2), 4, (far_own, far_back)
    )
    far_side = moved(far_side, "ctx", lambda i: i ^ 2)
    near_own, grad_queries = call(
        "own_near",
        own_near,
        (shape(3 * ROWS, 2 * D, f32), shape(ROWS, HEADS * D, bf16)),
        vmem(5) + token(1),
        10,
        (q4, own, p_own, g4, dq, far_keep),
        [pltpu.VMEM((D, LANES), f32)],
    )
    to_two = call("relay_far", relay_far, shape(ROWS, 2 * D, bf16), smem(1) + vmem(2), 4, (place, far_keep, far_side))
    got_two = turned(to_two, "ctx", -2 * PLANE)
    near_both, near_side = call(
        "settle_near",
        settle_near,
        (shape(3 * ROWS, 2 * D, f32), shape(ROWS, 2 * D, bf16)),
        vmem(2) + token(1),
        4,
        (near_own, near_back, to_two),
    )
    near_side = moved(near_side, "ctx", lambda i: i ^ 2)
    to_one, keep = call(
        "relay_near",
        relay_near,
        (shape(ROWS, 2 * D, bf16), shape(ROWS, 2 * D, f32)),
        smem(1) + vmem(3),
        4,
        (place, near_both, near_side, far_side),
    )
    got_one = turned(to_one, "ctx", -PLANE)
    total = (keep + got_one.astype(f32) + got_two.astype(f32)).astype(bf16)
    return grad_queries, total[:, :D], total[:, D:]


def solution(mesh):
    return jax.shard_map(
        local,
        mesh=mesh,
        in_specs=(
            P("ctx", "head"),
            P("ctx", "head"),
            P("ctx", "head"),
            P("ctx", "head"),
            P("head", None),
            P(),
        ),
        out_specs=(P("ctx", "head"), P("ctx", "head"), P("ctx", "head")),
        check_vma=False,
    )
```

```python
import functools

import jax
import jax.numpy as jnp
from jax import lax
from jax.experimental import pallas as pl
from jax.experimental.pallas import tpu as pltpu
from jax.sharding import PartitionSpec as P

D = 128
HEADS = 4
ROWS = 192
LANES = HEADS * ROWS
REACH = 4
SLOTS = REACH + 1
PLANE = 4
BLOCK = 512
MASS, TOP, START, DOT = D, D + 1, D + 2, D + 3
PEAK = D + 8
STATE = PEAK + 16
NEG = -1e30
FLOOR = -1e20
SCALE = D**-0.5
LOG2E = 1.4426950408889634
MIB = 1 << 20
FL = 10**9


def dot(a, b, ca, cb):
    return lax.dot_general(a, b, (((ca,), (cb,)), ((), ())), preferred_element_type=jnp.float32)


def stack_heads(src, dst):
    for h in range(HEADS):
        dst[h * ROWS : (h + 1) * ROWS, :] = src[:, h * D : (h + 1) * D]


def load_kernel(place_ref, len_hbm, q_hbm, q4_ref, bound_ref, len_ref, sems):
    copies = [pltpu.make_async_copy(len_hbm, len_ref, sems.at[0])]
    for h in range(HEADS):
        across, along = pl.ds(h * ROWS, ROWS), pl.ds(h * D, D)
        copies.append(pltpu.make_async_copy(q_hbm.at[:, along], q4_ref.at[across, :], sems.at[1 + h]))
    for copy in copies:
        copy.start()
    lane = lax.broadcasted_iota(jnp.int32, (1, LANES), 1)
    pos = lane + place_ref[0] * ROWS
    for h in range(1, HEADS):
        pos = pos - jnp.where(lane >= h * ROWS, ROWS, 0)
    start = jnp.zeros((1, LANES), jnp.int32)
    end = jnp.int32(0)
    copies[0].wait()
    for d in range(len_ref.shape[0]):
        end = end + len_ref[d]
        start = jnp.where(end <= pos, end, start)
    bound_ref[0:1, :] = pos.astype(jnp.float32)
    bound_ref[1:2, :] = start.astype(jnp.float32)
    for copy in copies[1:]:
        copy.wait()


def gate_kernel(*refs):
    refs[-1][...] = jnp.zeros(refs[-1].shape, refs[-1].dtype)


def pick_kernel(place_ref, z2_ref, z1_ref, z0_ref, *refs):
    out_ref = refs[-1]
    upper = lax.rem(lax.div(place_ref[0], 2), 2) == 1

    @pl.when(upper)
    def _():
        out_ref[:ROWS, :] = z2_ref[...]
        out_ref[ROWS:, :] = z1_ref[...]

    @pl.when(jnp.logical_not(upper))
    def _():
        out_ref[:ROWS, :] = z1_ref[...]
        out_ref[ROWS:, :] = z0_ref[...]


def join_kernel(z2_ref, z1_ref, z0_ref, side_ref, *refs):
    out_ref = refs[-1]
    parts = (z2_ref[...], side_ref[:ROWS, :], z1_ref[...], side_ref[ROWS:, :], z0_ref[...])
    for m, part in enumerate(parts):
        out_ref[m * ROWS : (m + 1) * ROWS, :] = part


def absorb(block, queries, row, base, start, state, pos=None):
    s = dot(block[:, :D], queries, 1, 1) * (SCALE * LOG2E)
    visible = row >= start - base * ROWS
    if pos is not None:
        visible = visible & (row <= pos - base * ROWS)
    s = jnp.where(visible, s, NEG)
    peak = jnp.maximum(jnp.max(s, axis=0, keepdims=True), FLOOR)
    prob = jnp.exp2(s - peak).astype(jnp.bfloat16)
    mass = jnp.sum(prob.astype(jnp.float32), axis=0, keepdims=True)
    out = dot(block[:, D:], prob, 0, 0)
    if state is None:
        return prob, peak, (out, mass, peak)
    old_out, old_mass, old_peak = state
    top = jnp.maximum(old_peak, peak)
    before, now = jnp.exp2(old_peak - top), jnp.exp2(peak - top)
    return prob, peak, (old_out * before + out * now, old_mass * before + mass * now, top)


def read_state(ref):
    return ref[:D, :], ref[MASS : MASS + 1, :], ref[TOP : TOP + 1, :]


def write_state(ref, state):
    ref[:D, :], ref[MASS : MASS + 1, :], ref[TOP : TOP + 1, :] = state


def put_row(ref, at, value):
    ref[at : at + 1, :] = value


def near_kernel(place_ref, head_ref, z2_ref, z1_ref, z0_ref, q4_ref, bound_ref, g_hbm, w_hbm, y_ref, r_ref, l_ref, or_ref, ol_ref, after, p_ref, st_ref, acc_ref, tail_ref, g_ref, w_ref, sems):
    head = head_ref[0]
    copies = [pltpu.make_async_copy(g_hbm, g_ref, sems.at[0])]
    for i, source in enumerate((source_of(head, 4, False), source_of(head, 4, True))):
        cols = pl.ds(pl.multiple_of(source * BLOCK, BLOCK), BLOCK)
        copies.append(pltpu.make_async_copy(w_hbm.at[:, cols], tail_ref.at[:, pl.ds(i * BLOCK, BLOCK)], sems.at[1 + i]))
    sources = (head, source_of(head, 0, True), source_of(head, -2, False), source_of(head, 2, False))
    sources += (source_of(head, -2, True), source_of(head, 2, True))
    for i, source in enumerate(sources):
        cols = pl.ds(pl.multiple_of(source * BLOCK, BLOCK), BLOCK)
        copies.append(pltpu.make_async_copy(w_hbm.at[:, cols], w_ref.at[:, pl.ds(i * BLOCK, BLOCK)], sems.at[3 + i]))
    for copy in copies:
        copy.start()
    me = place_ref[0]
    queries = q4_ref[...]
    row = lax.broadcasted_iota(jnp.int32, (ROWS, LANES), 0)
    pos, start = bound_ref[0:1, :].astype(jnp.int32), bound_ref[1:2, :].astype(jnp.int32)
    state = None
    for i, ref in ((2, z0_ref), (1, z1_ref), (0, z2_ref)):
        at = pos if i == 2 else None
        prob, peak, state = absorb(ref[...], queries, row, me - PLANE * (2 - i), start, state, at)
        p_ref[i * ROWS : (i + 1) * ROWS, :] = prob
        put_row(st_ref, PEAK + 2 * i, peak)
    write_state(st_ref, state)
    put_row(st_ref, START, bound_ref[1:2, :])
    for copy in copies:
        copy.wait()
    acc_ref[...] = project(None, (g_ref, y_ref, r_ref, l_ref, or_ref, ol_ref), range(6), w_ref)


def rows(i):
    return pl.ds(pl.multiple_of(i * ROWS, ROWS), ROWS)


def project(acc, pieces, sources, w_ref):
    for piece, source in zip(pieces, sources):
        part = dot(piece[...], w_ref[:, source * BLOCK : (source + 1) * BLOCK], 1, 1)
        acc = part if acc is None else acc + part
    return acc


def source_of(head, by, flip):
    at = lax.rem(head + by + 8, 8)
    return at + 1 - 2 * lax.rem(at, 2) if flip else at


def middle_kernel(place_ref, own_ref, q4_ref, st_in_ref, p_ref, st_ref):
    queries = q4_ref[...]
    row = lax.broadcasted_iota(jnp.int32, (ROWS, LANES), 0)
    start = st_in_ref[START : START + 1, :].astype(jnp.int32)
    state = read_state(st_in_ref)
    st_ref[PEAK:, :] = st_in_ref[PEAK:, :]
    for i in range(2):
        slot = 2 * i + 1
        block = own_ref[slot * ROWS : (slot + 1) * ROWS, :]
        prob, peak, state = absorb(block, queries, row, place_ref[0] + 2 * (slot - REACH), start, state)
        p_ref[i * ROWS : (i + 1) * ROWS, :] = prob
        put_row(st_ref, PEAK + slot, peak)
    write_state(st_ref, state)
    put_row(st_ref, START, st_in_ref[START : START + 1, :])


def across_kernel(place_ref, par_ref, q4_ref, st_in_ref, p_ref, st_ref):
    me = place_ref[0]
    core = lax.rem(me, 2)
    chip = me - core
    queries = q4_ref[...]
    row = lax.broadcasted_iota(jnp.int32, (ROWS, LANES), 0)
    start = st_in_ref[START : START + 1, :].astype(jnp.int32)
    state = read_state(st_in_ref)
    peaks = [st_in_ref[PEAK + m : PEAK + m + 1, :] for m in range(SLOTS)]
    for i in range(REACH):
        slot = i + core
        prob, peak, state = absorb(par_ref[rows(slot), :], queries, row, chip + 1 - core + 2 * (slot - REACH), start, state)
        p_ref[i * ROWS : (i + 1) * ROWS, :] = prob
        peaks.append(peak)
    out, mass, top = state
    st_ref[:D, :] = out / mass
    log_total = top + jnp.log2(mass)
    for i, peak in enumerate(peaks):
        put_row(st_ref, PEAK + i, jnp.exp2(peak - log_total))


def back_block(block, prob, share, g4, q4, rd):
    prob = prob.astype(jnp.float32) * share
    dprob = dot(block[:, D:], g4, 1, 1)
    ds = (prob * (dprob - rd)).astype(jnp.bfloat16)
    dv = dot(prob.astype(jnp.bfloat16), g4, 1, 0)
    dk = dot(ds, q4, 1, 0) * SCALE
    dq = dot(block[:, :D], ds, 0, 0)
    return dk, dv, dq


def put(out_ref, slot, dk, dv):
    at = pl.ds(pl.multiple_of(slot * ROWS, ROWS), ROWS)
    out_ref[at, :D] = dk.astype(out_ref.dtype)
    out_ref[at, D:] = dv.astype(out_ref.dtype)


def cross_step(slot, core, par_ref, p_ref, st_ref, g4, q4_ref, rd):
    share = st_ref[pl.ds(PEAK + SLOTS + slot - core, 1), :]
    return back_block(par_ref[rows(slot), :], p_ref[rows(slot - core), :], share, g4, q4_ref[...], rd)


def cross_far(place_ref, a_ref, b_ref, early_ref, w_ref, q4_ref, par_ref, p_ref, st_in_ref, out_ref, g_ref, st_ref):
    core = lax.rem(place_ref[0], 2)
    acc = project(early_ref[...], (a_ref, b_ref), range(2), w_ref)
    acc = acc.astype(jnp.bfloat16)
    for h in range(HEADS):
        g_ref[h * ROWS : (h + 1) * ROWS, :] = acc[:, h * D : (h + 1) * D]
    g4 = g_ref[...]
    gt = jnp.transpose(g4.astype(jnp.float32))
    rd = jnp.sum(gt * st_in_ref[:D, :], axis=0, keepdims=True)
    st_ref[PEAK:, :] = st_in_ref[PEAK:, :]
    put_row(st_ref, DOT, rd)

    dk, dv, dq = cross_step(1, core, par_ref, p_ref, st_ref, g4, q4_ref, rd)
    put(out_ref, 1, dk, dv)
    st_ref[:D, :] = dq

    @pl.when(core == 1)
    def _():
        out_ref[:ROWS, :] = jnp.zeros((ROWS, 2 * D), out_ref.dtype)

    @pl.when(core == 0)
    def _():
        dk, dv, dq = cross_step(0, core, par_ref, p_ref, st_ref, g4, q4_ref, rd)
        put(out_ref, 0, dk, dv)
        st_ref[:D, :] += dq


def cross_near(place_ref, q4_ref, par_ref, p_ref, g_ref, st_in_ref, out_ref, st_ref):
    core = lax.rem(place_ref[0], 2)
    g4 = g_ref[...]
    rd = st_in_ref[DOT : DOT + 1, :]
    st_ref[DOT : DOT + 1, :] = rd
    st_ref[PEAK:, :] = st_in_ref[PEAK:, :]
    total = st_in_ref[:D, :]
    for slot in (2, 3):
        dk, dv, dq = cross_step(slot, core, par_ref, p_ref, st_ref, g4, q4_ref, rd)
        put(out_ref, slot - 2, dk, dv)
        total = total + dq
    st_ref[:D, :] = total

    @pl.when(core == 0)
    def _():
        out_ref[2 * ROWS :, :] = jnp.zeros((ROWS, 2 * D), out_ref.dtype)

    @pl.when(core == 1)
    def _():
        dk, dv, dq = cross_step(4, core, par_ref, p_ref, st_ref, g4, q4_ref, rd)
        put(out_ref, 2, dk, dv)
        st_ref[:D, :] += dq


def own_kernel(slots, q4_ref, own_ref, near_ref, side_ref, g_ref, st_in_ref, *refs):
    out_ref, st_ref = refs[-2:]
    g4 = g_ref[...]
    rd = st_in_ref[DOT : DOT + 1, :]
    total = st_in_ref[:D, :]
    for i, slot in enumerate(slots):
        at = slot // 2 * ROWS
        prob = (side_ref if slot % 2 else near_ref)[at : at + ROWS, :]
        share = st_in_ref[PEAK + slot : PEAK + slot + 1, :]
        dk, dv, dq = back_block(own_ref[slot * ROWS : (slot + 1) * ROWS, :], prob, share, g4, q4_ref[...], rd)
        out_ref[i * ROWS : (i + 1) * ROWS, :D] = dk
        out_ref[i * ROWS : (i + 1) * ROWS, D:] = dv
        total = total + dq
    if slots[-1] < REACH:
        st_ref[DOT : DOT + 1, :] = rd
        st_ref[PEAK:, :] = st_in_ref[PEAK:, :]
        st_ref[:D, :] = total
    else:
        dq = jnp.transpose(total) * SCALE
        for h in range(HEADS):
            st_ref[:, h * D : (h + 1) * D] = dq[h * ROWS : (h + 1) * ROWS, :].astype(jnp.bfloat16)


def is_upper(place_ref):
    return (lax.rem(lax.div(place_ref[0], 2), 2) == 1).astype(jnp.float32)


def settle_far(own_ref, back_ref, keep_ref, side_ref):
    both = own_ref[...] + back_ref[...].astype(jnp.float32)
    keep_ref[...] = both[:ROWS]
    side_ref[...] = both[ROWS:].astype(jnp.bfloat16)


def relay_far(place_ref, keep_ref, side_ref, out_ref):
    out_ref[...] = (keep_ref[...] + side_ref[...].astype(jnp.float32) * is_upper(place_ref)).astype(jnp.bfloat16)


def settle_near(own_ref, back_ref, keep_ref, side_ref):
    both = own_ref[...] + back_ref[: 2 * ROWS, :].astype(jnp.float32)
    keep_ref[...] = both[:ROWS]
    side_ref[...] = both[ROWS:].astype(jnp.bfloat16)


def relay_near(place_ref, keep_ref, near_ref, far_ref, *refs):
    out_ref = refs[-1]
    upper = is_upper(place_ref)
    near, far = near_ref[...].astype(jnp.float32), far_ref[...].astype(jnp.float32)
    out_ref[...] = (keep_ref[...] + near * upper + far * (1 - upper)).astype(jnp.bfloat16)


def finish_kernel(place_ref, own_ref, back_ref, near_ref, one_ref, two_ref, k_ref, v_ref):
    def wide(x):
        return x.astype(jnp.float32)

    total = own_ref[...] + wide(back_ref[2 * ROWS :, :]) + wide(near_ref[...]) * (1 - is_upper(place_ref))
    total = (total + wide(one_ref[...]) + wide(two_ref[...])).astype(jnp.bfloat16)
    k_ref[...] = total[:, :D]
    v_ref[...] = total[:, D:]


def vmem(n):
    return [pl.BlockSpec(memory_space=pltpu.VMEM)] * n


def smem(n):
    return [pl.BlockSpec(memory_space=pltpu.SMEM)] * n


def hbm(n):
    return [pl.BlockSpec(memory_space=pltpu.HBM)] * n


def token(n):
    return [pl.BlockSpec(memory_space=pl.ANY)] * n


def moved(x, axis, to):
    return lax.ppermute(x, axis, [(i, to(i)) for i in range(lax.axis_size(axis))])


def turned(x, axis, by):
    count = lax.axis_size(axis)
    return moved(x, axis, lambda i: (i + by) % count)


def shape(rows, cols, dtype):
    return jax.ShapeDtypeStruct((rows, cols), dtype)


def call(name, kernel, outs, ins, args, scratch=(), flops=1):
    one = not isinstance(outs, tuple)
    return pl.pallas_call(
        kernel,
        out_shape=outs,
        in_specs=ins,
        out_specs=vmem(1)[0] if one else tuple(vmem(len(outs))),
        scratch_shapes=list(scratch),
        compiler_params=pltpu.CompilerParams(vmem_limit_bytes=8 * MIB),
        cost_estimate=pl.CostEstimate(flops=flops, bytes_accessed=1, transcendentals=0),
        name=name,
    )(*args)


def local(queries, keys, values, grad_out, out_weight, lengths):
    bf16, f32 = jnp.bfloat16, jnp.float32
    place = lax.axis_index("ctx").astype(jnp.int32).reshape(1)
    head = lax.axis_index("head").astype(jnp.int32).reshape(1)
    dma = pltpu.SemaphoreType.DMA
    pinned = functools.partial(pltpu.with_memory_space_constraint, memory_space=pltpu.HBM)
    state = shape(STATE, LANES, f32)

    first = moved(grad_out, "head", lambda i: i ^ 1)
    right = turned(grad_out, "head", 2)
    left = turned(grad_out, "head", -2)
    kv = jnp.pad(keys, ((0, 0), (0, D))) + jnp.pad(values, ((0, 0), (D, 0)))
    z2 = turned(kv, "ctx", 2 * PLANE)
    z1 = turned(kv, "ctx", PLANE)
    q4, bound = call(
        "load",
        load_kernel,
        (shape(LANES, D, bf16), shape(8, LANES, f32)),
        smem(1) + hbm(2),
        (place, pinned(lengths), pinned(queries)),
        [pltpu.SMEM((lengths.shape[0],), jnp.int32), dma((1 + HEADS,))],
    )
    other = first
    other_right = turned(other, "head", 2)
    other_left = turned(other, "head", -2)
    far = turned(right, "head", 2)
    other_far = turned(other_left, "head", -2)

    gate = call("gate", gate_kernel, shape(8, D, f32), token(4), (other, right, left, q4))
    picked = call(
        "pick_side", pick_kernel, shape(2 * ROWS, 2 * D, bf16), smem(1) + vmem(3) + token(1), (place, z2, z1, kv, gate)
    )
    side = moved(picked, "ctx", lambda i: i ^ 2)
    p_near, st, early, tail = call(
        "near",
        near_kernel,
        (shape(3 * ROWS, LANES, bf16), state, shape(ROWS, HEADS * D, f32), shape(HEADS * D, 2 * BLOCK, bf16)),
        smem(2) + vmem(5) + hbm(2) + vmem(5) + token(1),
        (place, head, z2, z1, kv, q4, bound, pinned(grad_out), pinned(out_weight), other, right, left, other_right, other_left, picked),
        [pltpu.VMEM((ROWS, BLOCK), bf16), pltpu.VMEM((HEADS * D, 6 * BLOCK), bf16), dma((9,))],
    )
    own = call("join_slots", join_kernel, shape(SLOTS * ROWS, 2 * D, bf16), vmem(4) + token(1), (z2, z1, kv, side, st))
    par = moved(own, "ctx", lambda i: i ^ 1)

    p_side, st = call(
        "middle", middle_kernel, (shape(2 * ROWS, LANES, bf16), state), smem(1) + vmem(3), (place, own, q4, st)
    )
    p_par, st = call(
        "across", across_kernel, (shape(REACH * ROWS, LANES, bf16), state), smem(1) + vmem(3), (place, par, q4, st)
    )

    far_cross, g4, st = call(
        "cross_far",
        cross_far,
        (shape(2 * ROWS, 2 * D, bf16), shape(LANES, D, bf16), state),
        smem(1) + vmem(8),
        (place, far, other_far, early, tail, q4, par, p_par, st),
    )
    far_back = moved(far_cross, "ctx", lambda i: i ^ 1)
    near_cross, st = call(
        "cross_near", cross_near, (shape(3 * ROWS, 2 * D, bf16), state), smem(1) + vmem(5), (place, q4, par, p_par, g4, st), flops=FL
    )
    near_back = moved(near_cross, "ctx", lambda i: i ^ 1)
    far_own, st = call(
        "own_far",
        functools.partial(own_kernel, (0, 1)),
        (shape(2 * ROWS, 2 * D, f32), state),
        vmem(6),
        (q4, own, p_near, p_side, g4, st),
        flops=FL,
    )
    far_keep, far_side = call(
        "settle_far", settle_far, (shape(ROWS, 2 * D, f32), shape(ROWS, 2 * D, bf16)), vmem(2), (far_own, far_back)
    )
    far_side = moved(far_side, "ctx", lambda i: i ^ 2)
    near_own, st = call(
        "own_near",
        functools.partial(own_kernel, (2, 3)),
        (shape(2 * ROWS, 2 * D, f32), state),
        vmem(6) + token(1),
        (q4, own, p_near, p_side, g4, st, far_keep),
        flops=FL,
    )
    near_keep, near_side = call(
        "settle_near", settle_near, (shape(ROWS, 2 * D, f32), shape(ROWS, 2 * D, bf16)), vmem(2), (near_own, near_back)
    )
    near_side = moved(near_side, "ctx", lambda i: i ^ 2)
    last_own, grad_queries = call(
        "own_last",
        functools.partial(own_kernel, (4,)),
        (shape(ROWS, 2 * D, f32), shape(ROWS, HEADS * D, bf16)),
        vmem(6) + token(1),
        (q4, own, p_near, p_side, g4, st, near_keep),
    )
    to_two = call("relay_far", relay_far, shape(ROWS, 2 * D, bf16), smem(1) + vmem(2), (place, far_keep, far_side))
    got_two = turned(to_two, "ctx", -2 * PLANE)
    to_one = call(
        "relay_near",
        relay_near,
        shape(ROWS, 2 * D, bf16),
        smem(1) + vmem(3) + token(2),
        (place, near_keep, near_side, far_side, to_two, last_own),
    )
    got_one = turned(to_one, "ctx", -PLANE)
    grad_keys, grad_values = call(
        "finish",
        finish_kernel,
        (shape(ROWS, D, bf16), shape(ROWS, D, bf16)),
        smem(1) + vmem(5),
        (place, last_own, near_back, near_side, got_one, got_two),
    )
    return grad_queries, grad_keys, grad_values


def solution(mesh):
    return jax.shard_map(
        local,
        mesh=mesh,
        in_specs=(
            P("ctx", "head"),
            P("ctx", "head"),
            P("ctx", "head"),
            P("ctx", "head"),
            P("head", None),
            P(),
        ),
        out_specs=(P("ctx", "head"), P("ctx", "head"), P("ctx", "head")),
        check_vma=False,
    )
```

```python
import functools

import jax
import jax.numpy as jnp
from jax import lax
from jax.experimental import pallas as pl
from jax.experimental.pallas import tpu as pltpu
from jax.sharding import PartitionSpec as P

D = 128
HEADS = 4
ROWS = 192
LANES = HEADS * ROWS
REACH = 4
SLOTS = REACH + 1
PLANE = 4
BLOCK = 512
MASS, TOP, START, DOT = D, D + 1, D + 2, D + 3
PEAK = D + 8
STATE = PEAK + 16
NEG = -1e30
FLOOR = -1e20
SCALE = D**-0.5
LOG2E = 1.4426950408889634
MIB = 1 << 20
FL = 4 * 10**9


def dot(a, b, ca, cb):
    return lax.dot_general(a, b, (((ca,), (cb,)), ((), ())), preferred_element_type=jnp.float32)


def stack_heads(src, dst):
    for h in range(HEADS):
        dst[h * ROWS : (h + 1) * ROWS, :] = src[:, h * D : (h + 1) * D]


def load_kernel(place_ref, len_hbm, q_hbm, q4_ref, bound_ref, len_ref, sems):
    copies = [pltpu.make_async_copy(len_hbm, len_ref, sems.at[0])]
    for h in range(HEADS):
        across, along = pl.ds(h * ROWS, ROWS), pl.ds(h * D, D)
        copies.append(pltpu.make_async_copy(q_hbm.at[:, along], q4_ref.at[across, :], sems.at[1 + h]))
    for copy in copies:
        copy.start()
    lane = lax.broadcasted_iota(jnp.int32, (1, LANES), 1)
    pos = lane + place_ref[0] * ROWS
    for h in range(1, HEADS):
        pos = pos - jnp.where(lane >= h * ROWS, ROWS, 0)
    start = jnp.zeros((1, LANES), jnp.int32)
    end = jnp.int32(0)
    copies[0].wait()
    for d in range(len_ref.shape[0]):
        end = end + len_ref[d]
        start = jnp.where(end <= pos, end, start)
    bound_ref[0:1, :] = pos.astype(jnp.float32)
    bound_ref[1:2, :] = start.astype(jnp.float32)
    for copy in copies[1:]:
        copy.wait()


def gate_kernel(*refs):
    refs[-1][...] = jnp.zeros(refs[-1].shape, refs[-1].dtype)


def pick_kernel(place_ref, z2_ref, z1_ref, z0_ref, *refs):
    out_ref = refs[-1]
    upper = lax.rem(lax.div(place_ref[0], 2), 2) == 1

    @pl.when(upper)
    def _():
        out_ref[:ROWS, :] = z2_ref[...]
        out_ref[ROWS:, :] = z1_ref[...]

    @pl.when(jnp.logical_not(upper))
    def _():
        out_ref[:ROWS, :] = z1_ref[...]
        out_ref[ROWS:, :] = z0_ref[...]


def join_kernel(z2_ref, z1_ref, z0_ref, side_ref, *refs):
    out_ref = refs[-1]
    parts = (z2_ref[...], side_ref[:ROWS, :], z1_ref[...], side_ref[ROWS:, :], z0_ref[...])
    for m, part in enumerate(parts):
        out_ref[m * ROWS : (m + 1) * ROWS, :] = part


def absorb(block, queries, row, base, start, state, pos=None):
    s = dot(block[:, :D], queries, 1, 1) * (SCALE * LOG2E)
    visible = row >= start - base * ROWS
    if pos is not None:
        visible = visible & (row <= pos - base * ROWS)
    s = jnp.where(visible, s, NEG)
    peak = jnp.maximum(jnp.max(s, axis=0, keepdims=True), FLOOR)
    prob = jnp.exp2(s - peak).astype(jnp.bfloat16)
    mass = jnp.sum(prob.astype(jnp.float32), axis=0, keepdims=True)
    out = dot(block[:, D:], prob, 0, 0)
    if state is None:
        return prob, peak, (out, mass, peak)
    old_out, old_mass, old_peak = state
    top = jnp.maximum(old_peak, peak)
    before, now = jnp.exp2(old_peak - top), jnp.exp2(peak - top)
    return prob, peak, (old_out * before + out * now, old_mass * before + mass * now, top)


def read_state(ref):
    return ref[:D, :], ref[MASS : MASS + 1, :], ref[TOP : TOP + 1, :]


def write_state(ref, state):
    ref[:D, :], ref[MASS : MASS + 1, :], ref[TOP : TOP + 1, :] = state


def put_row(ref, at, value):
    ref[at : at + 1, :] = value


def near_kernel(place_ref, head_ref, z2_ref, z1_ref, z0_ref, q4_ref, bound_ref, w_hbm, *refs):
    p_ref, st_ref, w_ref, tail_ref, sems = refs[-5:]
    head = head_ref[0]
    sources = (head, source_of(head, 0, True), source_of(head, -2, False), source_of(head, 2, False))
    sources += (source_of(head, -2, True), source_of(head, 2, True), source_of(head, 4, False), source_of(head, 4, True))
    copies = []
    for i, source in enumerate(sources):
        cols = pl.ds(pl.multiple_of(source * BLOCK, BLOCK), BLOCK)
        target = w_ref.at[:, pl.ds(i * BLOCK, BLOCK)] if i < 6 else tail_ref.at[:, pl.ds((i - 6) * BLOCK, BLOCK)]
        copies.append(pltpu.make_async_copy(w_hbm.at[:, cols], target, sems.at[i]))
    for copy in copies:
        copy.start()
    me = place_ref[0]
    queries = q4_ref[...]
    row = lax.broadcasted_iota(jnp.int32, (ROWS, LANES), 0)
    pos, start = bound_ref[0:1, :].astype(jnp.int32), bound_ref[1:2, :].astype(jnp.int32)
    state = None
    for i, ref in ((2, z0_ref), (1, z1_ref), (0, z2_ref)):
        at = pos if i == 2 else None
        prob, peak, state = absorb(ref[...], queries, row, me - PLANE * (2 - i), start, state, at)
        p_ref[i * ROWS : (i + 1) * ROWS, :] = prob
        put_row(st_ref, PEAK + 2 * i, peak)
    write_state(st_ref, state)
    put_row(st_ref, START, bound_ref[1:2, :])
    for copy in copies:
        copy.wait()


def early_kernel(g_ref, y_ref, r_ref, l_ref, or_ref, ol_ref, w_ref, after, acc_ref):
    acc_ref[...] = project(None, (g_ref, y_ref, r_ref, l_ref, or_ref, ol_ref), range(6), w_ref)


def rows(i):
    return pl.ds(pl.multiple_of(i * ROWS, ROWS), ROWS)


def project(acc, pieces, sources, w_ref):
    for piece, source in zip(pieces, sources):
        part = dot(piece[...], w_ref[:, source * BLOCK : (source + 1) * BLOCK], 1, 1)
        acc = part if acc is None else acc + part
    return acc


def source_of(head, by, flip):
    at = lax.rem(head + by + 8, 8)
    return at + 1 - 2 * lax.rem(at, 2) if flip else at


def middle_kernel(place_ref, own_ref, q4_ref, st_in_ref, after, p_ref, st_ref):
    queries = q4_ref[...]
    row = lax.broadcasted_iota(jnp.int32, (ROWS, LANES), 0)
    start = st_in_ref[START : START + 1, :].astype(jnp.int32)
    state = read_state(st_in_ref)
    st_ref[PEAK:, :] = st_in_ref[PEAK:, :]
    for i in range(2):
        slot = 2 * i + 1
        block = own_ref[slot * ROWS : (slot + 1) * ROWS, :]
        prob, peak, state = absorb(block, queries, row, place_ref[0] + 2 * (slot - REACH), start, state)
        p_ref[i * ROWS : (i + 1) * ROWS, :] = prob
        put_row(st_ref, PEAK + slot, peak)
    write_state(st_ref, state)
    put_row(st_ref, START, st_in_ref[START : START + 1, :])


def across_kernel(place_ref, par_ref, q4_ref, st_in_ref, p_ref, st_ref):
    me = place_ref[0]
    core = lax.rem(me, 2)
    chip = me - core
    queries = q4_ref[...]
    row = lax.broadcasted_iota(jnp.int32, (ROWS, LANES), 0)
    start = st_in_ref[START : START + 1, :].astype(jnp.int32)
    state = read_state(st_in_ref)
    peaks = [st_in_ref[PEAK + m : PEAK + m + 1, :] for m in range(SLOTS)]
    for i in range(REACH):
        slot = i + core
        prob, peak, state = absorb(par_ref[rows(slot), :], queries, row, chip + 1 - core + 2 * (slot - REACH), start, state)
        p_ref[i * ROWS : (i + 1) * ROWS, :] = prob
        peaks.append(peak)
    out, mass, top = state
    st_ref[:D, :] = out / mass
    log_total = top + jnp.log2(mass)
    for i, peak in enumerate(peaks):
        put_row(st_ref, PEAK + i, jnp.exp2(peak - log_total))


def back_block(block, prob, share, g4, q4, rd):
    prob = prob.astype(jnp.float32) * share
    dprob = dot(block[:, D:], g4, 1, 1)
    ds = (prob * (dprob - rd)).astype(jnp.bfloat16)
    dv = dot(prob.astype(jnp.bfloat16), g4, 1, 0)
    dk = dot(ds, q4, 1, 0) * SCALE
    dq = dot(block[:, :D], ds, 0, 0)
    return dk, dv, dq


def put(out_ref, slot, dk, dv):
    at = pl.ds(pl.multiple_of(slot * ROWS, ROWS), ROWS)
    out_ref[at, :D] = dk.astype(out_ref.dtype)
    out_ref[at, D:] = dv.astype(out_ref.dtype)


def cross_step(slot, core, par_ref, p_ref, st_ref, g4, q4_ref, rd):
    share = st_ref[pl.ds(PEAK + SLOTS + slot - core, 1), :]
    return back_block(par_ref[rows(slot), :], p_ref[rows(slot - core), :], share, g4, q4_ref[...], rd)


def cross_far(place_ref, a_ref, b_ref, early_ref, w_ref, q4_ref, par_ref, p_ref, st_in_ref, out_ref, g_ref, st_ref):
    core = lax.rem(place_ref[0], 2)
    acc = project(early_ref[...], (a_ref, b_ref), range(2), w_ref)
    acc = acc.astype(jnp.bfloat16)
    for h in range(HEADS):
        g_ref[h * ROWS : (h + 1) * ROWS, :] = acc[:, h * D : (h + 1) * D]
    g4 = g_ref[...]
    gt = jnp.transpose(g4.astype(jnp.float32))
    rd = jnp.sum(gt * st_in_ref[:D, :], axis=0, keepdims=True)
    st_ref[PEAK:, :] = st_in_ref[PEAK:, :]
    put_row(st_ref, DOT, rd)

    dk, dv, dq = cross_step(1, core, par_ref, p_ref, st_ref, g4, q4_ref, rd)
    put(out_ref, 1, dk, dv)
    st_ref[:D, :] = dq

    @pl.when(core == 1)
    def _():
        out_ref[:ROWS, :] = jnp.zeros((ROWS, 2 * D), out_ref.dtype)

    @pl.when(core == 0)
    def _():
        dk, dv, dq = cross_step(0, core, par_ref, p_ref, st_ref, g4, q4_ref, rd)
        put(out_ref, 0, dk, dv)
        st_ref[:D, :] += dq


def cross_near(place_ref, q4_ref, par_ref, p_ref, g_ref, st_in_ref, out_ref, st_ref):
    core = lax.rem(place_ref[0], 2)
    g4 = g_ref[...]
    rd = st_in_ref[DOT : DOT + 1, :]
    st_ref[DOT : DOT + 1, :] = rd
    st_ref[PEAK:, :] = st_in_ref[PEAK:, :]
    total = st_in_ref[:D, :]
    for slot in (2, 3):
        dk, dv, dq = cross_step(slot, core, par_ref, p_ref, st_ref, g4, q4_ref, rd)
        put(out_ref, slot - 2, dk, dv)
        total = total + dq
    st_ref[:D, :] = total

    @pl.when(core == 0)
    def _():
        out_ref[2 * ROWS :, :] = jnp.zeros((ROWS, 2 * D), out_ref.dtype)

    @pl.when(core == 1)
    def _():
        dk, dv, dq = cross_step(4, core, par_ref, p_ref, st_ref, g4, q4_ref, rd)
        put(out_ref, 2, dk, dv)
        st_ref[:D, :] += dq


def own_kernel(slots, q4_ref, own_ref, near_ref, side_ref, g_ref, st_in_ref, *refs):
    out_ref, st_ref = refs[-2:]
    g4 = g_ref[...]
    rd = st_in_ref[DOT : DOT + 1, :]
    total = st_in_ref[:D, :]
    for i, slot in enumerate(slots):
        at = slot // 2 * ROWS
        prob = (side_ref if slot % 2 else near_ref)[at : at + ROWS, :]
        share = st_in_ref[PEAK + slot : PEAK + slot + 1, :]
        dk, dv, dq = back_block(own_ref[slot * ROWS : (slot + 1) * ROWS, :], prob, share, g4, q4_ref[...], rd)
        out_ref[i * ROWS : (i + 1) * ROWS, :D] = dk
        out_ref[i * ROWS : (i + 1) * ROWS, D:] = dv
        total = total + dq
    if slots[-1] < REACH:
        st_ref[DOT : DOT + 1, :] = rd
        st_ref[PEAK:, :] = st_in_ref[PEAK:, :]
        st_ref[:D, :] = total
    else:
        dq = jnp.transpose(total) * SCALE
        for h in range(HEADS):
            st_ref[:, h * D : (h + 1) * D] = dq[h * ROWS : (h + 1) * ROWS, :].astype(jnp.bfloat16)


def is_upper(place_ref):
    return (lax.rem(lax.div(place_ref[0], 2), 2) == 1).astype(jnp.float32)


def settle_far(own_ref, back_ref, keep_ref, side_ref):
    both = own_ref[...] + back_ref[...].astype(jnp.float32)
    keep_ref[...] = both[:ROWS]
    side_ref[...] = both[ROWS:].astype(jnp.bfloat16)


def relay_far(place_ref, keep_ref, side_ref, out_ref):
    out_ref[...] = (keep_ref[...] + side_ref[...].astype(jnp.float32) * is_upper(place_ref)).astype(jnp.bfloat16)


def settle_near(own_ref, back_ref, keep_ref, side_ref):
    both = own_ref[...] + back_ref[: 2 * ROWS, :].astype(jnp.float32)
    keep_ref[...] = both[:ROWS]
    side_ref[...] = both[ROWS:].astype(jnp.bfloat16)


def relay_near(place_ref, keep_ref, near_ref, far_ref, *refs):
    out_ref = refs[-1]
    upper = is_upper(place_ref)
    near, far = near_ref[...].astype(jnp.float32), far_ref[...].astype(jnp.float32)
    out_ref[...] = (keep_ref[...] + near * upper + far * (1 - upper)).astype(jnp.bfloat16)


def finish_kernel(place_ref, own_ref, back_ref, near_ref, one_ref, two_ref, k_ref, v_ref):
    def wide(x):
        return x.astype(jnp.float32)

    total = own_ref[...] + wide(back_ref[2 * ROWS :, :]) + wide(near_ref[...]) * (1 - is_upper(place_ref))
    total = (total + wide(one_ref[...]) + wide(two_ref[...])).astype(jnp.bfloat16)
    k_ref[...] = total[:, :D]
    v_ref[...] = total[:, D:]


def vmem(n):
    return [pl.BlockSpec(memory_space=pltpu.VMEM)] * n


def smem(n):
    return [pl.BlockSpec(memory_space=pltpu.SMEM)] * n


def hbm(n):
    return [pl.BlockSpec(memory_space=pltpu.HBM)] * n


def token(n):
    return [pl.BlockSpec(memory_space=pl.ANY)] * n


def moved(x, axis, to):
    return lax.ppermute(x, axis, [(i, to(i)) for i in range(lax.axis_size(axis))])


def turned(x, axis, by):
    count = lax.axis_size(axis)
    return moved(x, axis, lambda i: (i + by) % count)


def shape(rows, cols, dtype):
    return jax.ShapeDtypeStruct((rows, cols), dtype)


def call(name, kernel, outs, ins, args, scratch=(), flops=1):
    one = not isinstance(outs, tuple)
    return pl.pallas_call(
        kernel,
        out_shape=outs,
        in_specs=ins,
        out_specs=vmem(1)[0] if one else tuple(vmem(len(outs))),
        scratch_shapes=list(scratch),
        compiler_params=pltpu.CompilerParams(vmem_limit_bytes=8 * MIB),
        cost_estimate=pl.CostEstimate(flops=flops, bytes_accessed=1, transcendentals=0),
        name=name,
    )(*args)


def local(queries, keys, values, grad_out, out_weight, lengths):
    bf16, f32 = jnp.bfloat16, jnp.float32
    place = lax.axis_index("ctx").astype(jnp.int32).reshape(1)
    head = lax.axis_index("head").astype(jnp.int32).reshape(1)
    dma = pltpu.SemaphoreType.DMA
    pinned = functools.partial(pltpu.with_memory_space_constraint, memory_space=pltpu.HBM)
    state = shape(STATE, LANES, f32)

    first = moved(grad_out, "head", lambda i: i ^ 1)
    right = turned(grad_out, "head", 2)
    left = turned(grad_out, "head", -2)
    kv = jnp.pad(keys, ((0, 0), (0, D))) + jnp.pad(values, ((0, 0), (D, 0)))
    z2 = turned(kv, "ctx", 2 * PLANE)
    z1 = turned(kv, "ctx", PLANE)
    q4, bound = call(
        "load",
        load_kernel,
        (shape(LANES, D, bf16), shape(8, LANES, f32)),
        smem(1) + hbm(2),
        (place, pinned(lengths), pinned(queries)),
        [pltpu.SMEM((lengths.shape[0],), jnp.int32), dma((1 + HEADS,))],
    )
    other = first
    other_right = turned(other, "head", 2)
    other_left = turned(other, "head", -2)
    far = turned(right, "head", 2)
    other_far = turned(other_left, "head", -2)

    gate = call("gate", gate_kernel, shape(8, D, f32), token(4), (other, right, left, q4))
    picked = call(
        "pick_side", pick_kernel, shape(2 * ROWS, 2 * D, bf16), smem(1) + vmem(3) + token(1), (place, z2, z1, kv, gate)
    )
    side = moved(picked, "ctx", lambda i: i ^ 2)
    p_near, st, weight, tail = call(
        "near",
        near_kernel,
        (
            shape(3 * ROWS, LANES, bf16),
            state,
            shape(HEADS * D, 6 * BLOCK, bf16),
            shape(HEADS * D, 2 * BLOCK, bf16),
        ),
        smem(2) + vmem(5) + hbm(1) + token(3),
        (place, head, z2, z1, kv, q4, bound, pinned(out_weight), picked, other_right, other_left),
        [dma((8,))],
    )
    own = call("join_slots", join_kernel, shape(SLOTS * ROWS, 2 * D, bf16), vmem(4) + token(1), (z2, z1, kv, side, st))
    par = moved(own, "ctx", lambda i: i ^ 1)

    early = call(
        "early",
        early_kernel,
        shape(ROWS, HEADS * D, f32),
        vmem(7) + token(1),
        (grad_out, other, right, left, other_right, other_left, weight, own),
    )
    p_side, st = call(
        "middle", middle_kernel, (shape(2 * ROWS, LANES, bf16), state), smem(1) + vmem(3) + token(1), (place, own, q4, st, early)
    )
    p_par, st = call(
        "across", across_kernel, (shape(REACH * ROWS, LANES, bf16), state), smem(1) + vmem(3), (place, par, q4, st)
    )

    far_cross, g4, st = call(
        "cross_far",
        cross_far,
        (shape(2 * ROWS, 2 * D, bf16), shape(LANES, D, bf16), state),
        smem(1) + vmem(8),
        (place, far, other_far, early, tail, q4, par, p_par, st),
    )
    far_back = moved(far_cross, "ctx", lambda i: i ^ 1)
    near_cross, st = call(
        "cross_near", cross_near, (shape(3 * ROWS, 2 * D, bf16), state), smem(1) + vmem(5), (place, q4, par, p_par, g4, st), flops=FL
    )
    near_back = moved(near_cross, "ctx", lambda i: i ^ 1)
    far_own, st = call(
        "own_far",
        functools.partial(own_kernel, (0, 1)),
        (shape(2 * ROWS, 2 * D, f32), state),
        vmem(6),
        (q4, own, p_near, p_side, g4, st),
        flops=FL,
    )
    far_keep, far_side = call(
        "settle_far", settle_far, (shape(ROWS, 2 * D, f32), shape(ROWS, 2 * D, bf16)), vmem(2), (far_own, far_back)
    )
    far_side = moved(far_side, "ctx", lambda i: i ^ 2)
    near_own, st = call(
        "own_near",
        functools.partial(own_kernel, (2, 3)),
        (shape(2 * ROWS, 2 * D, f32), state),
        vmem(6) + token(1),
        (q4, own, p_near, p_side, g4, st, far_keep),
        flops=FL,
    )
    near_keep, near_side = call(
        "settle_near", settle_near, (shape(ROWS, 2 * D, f32), shape(ROWS, 2 * D, bf16)), vmem(2), (near_own, near_back)
    )
    near_side = moved(near_side, "ctx", lambda i: i ^ 2)
    last_own, grad_queries = call(
        "own_last",
        functools.partial(own_kernel, (4,)),
        (shape(ROWS, 2 * D, f32), shape(ROWS, HEADS * D, bf16)),
        vmem(6) + token(1),
        (q4, own, p_near, p_side, g4, st, near_keep),
    )
    to_two = call("relay_far", relay_far, shape(ROWS, 2 * D, bf16), smem(1) + vmem(2), (place, far_keep, far_side))
    got_two = turned(to_two, "ctx", -2 * PLANE)
    to_one = call(
        "relay_near",
        relay_near,
        shape(ROWS, 2 * D, bf16),
        smem(1) + vmem(3) + token(2),
        (place, near_keep, near_side, far_side, to_two, last_own),
    )
    got_one = turned(to_one, "ctx", -PLANE)
    grad_keys, grad_values = call(
        "finish",
        finish_kernel,
        (shape(ROWS, D, bf16), shape(ROWS, D, bf16)),
        smem(1) + vmem(5),
        (place, last_own, near_back, near_side, got_one, got_two),
    )
    return grad_queries, grad_keys, grad_values


def solution(mesh):
    return jax.shard_map(
        local,
        mesh=mesh,
        in_specs=(
            P("ctx", "head"),
            P("ctx", "head"),
            P("ctx", "head"),
            P("ctx", "head"),
            P("head", None),
            P(),
        ),
        out_specs=(P("ctx", "head"), P("ctx", "head"), P("ctx", "head")),
        check_vma=False,
    )
```

```python
import functools

import jax
import jax.numpy as jnp
from jax import lax
from jax.experimental import pallas as pl
from jax.experimental.pallas import tpu as pltpu
from jax.sharding import PartitionSpec as P

D = 128
HEADS = 4
ROWS = 192
LANES = HEADS * ROWS
REACH = 4
SLOTS = REACH + 1
PLANE = 4
BLOCK = 512
MASS, TOP, START, DOT = D, D + 1, D + 2, D + 3
PEAK = D + 8
STATE = PEAK + 16
NEG = -1e30
FLOOR = -1e20
SCALE = D**-0.5
LOG2E = 1.4426950408889634
MIB = 1 << 20
FL = 4 * 10**9


def dot(a, b, ca, cb):
    return lax.dot_general(a, b, (((ca,), (cb,)), ((), ())), preferred_element_type=jnp.float32)


def stack_heads(src, dst):
    for h in range(HEADS):
        dst[h * ROWS : (h + 1) * ROWS, :] = src[:, h * D : (h + 1) * D]


def load_kernel(place_ref, len_hbm, q_hbm, q4_ref, bound_ref, len_ref, sems):
    copies = [pltpu.make_async_copy(len_hbm, len_ref, sems.at[0])]
    for h in range(HEADS):
        across, along = pl.ds(h * ROWS, ROWS), pl.ds(h * D, D)
        copies.append(pltpu.make_async_copy(q_hbm.at[:, along], q4_ref.at[across, :], sems.at[1 + h]))
    for copy in copies:
        copy.start()
    lane = lax.broadcasted_iota(jnp.int32, (1, LANES), 1)
    pos = lane + place_ref[0] * ROWS
    for h in range(1, HEADS):
        pos = pos - jnp.where(lane >= h * ROWS, ROWS, 0)
    start = jnp.zeros((1, LANES), jnp.int32)
    end = jnp.int32(0)
    copies[0].wait()
    for d in range(len_ref.shape[0]):
        end = end + len_ref[d]
        start = jnp.where(end <= pos, end, start)
    bound_ref[0:1, :] = pos.astype(jnp.float32)
    bound_ref[1:2, :] = start.astype(jnp.float32)
    for copy in copies[1:]:
        copy.wait()


def gate_kernel(*refs):
    refs[-1][...] = jnp.zeros(refs[-1].shape, refs[-1].dtype)


def pick_kernel(place_ref, z2_ref, z1_ref, z0_ref, *refs):
    out_ref = refs[-1]
    upper = lax.rem(lax.div(place_ref[0], 2), 2) == 1

    @pl.when(upper)
    def _():
        out_ref[:ROWS, :] = z2_ref[...]
        out_ref[ROWS:, :] = z1_ref[...]

    @pl.when(jnp.logical_not(upper))
    def _():
        out_ref[:ROWS, :] = z1_ref[...]
        out_ref[ROWS:, :] = z0_ref[...]


def join_kernel(z2_ref, z1_ref, z0_ref, side_ref, *refs):
    out_ref = refs[-1]
    parts = (z2_ref[...], side_ref[:ROWS, :], z1_ref[...], side_ref[ROWS:, :], z0_ref[...])
    for m, part in enumerate(parts):
        out_ref[m * ROWS : (m + 1) * ROWS, :] = part


def absorb(block, queries, row, base, start, state, pos=None):
    s = dot(block[:, :D], queries, 1, 1) * (SCALE * LOG2E)
    visible = row >= start - base * ROWS
    if pos is not None:
        visible = visible & (row <= pos - base * ROWS)
    s = jnp.where(visible, s, NEG)
    peak = jnp.maximum(jnp.max(s, axis=0, keepdims=True), FLOOR)
    prob = jnp.exp2(s - peak).astype(jnp.bfloat16)
    mass = jnp.sum(prob.astype(jnp.float32), axis=0, keepdims=True)
    out = dot(block[:, D:], prob, 0, 0)
    if state is None:
        return prob, peak, (out, mass, peak)
    old_out, old_mass, old_peak = state
    top = jnp.maximum(old_peak, peak)
    before, now = jnp.exp2(old_peak - top), jnp.exp2(peak - top)
    return prob, peak, (old_out * before + out * now, old_mass * before + mass * now, top)


def read_state(ref):
    return ref[:D, :], ref[MASS : MASS + 1, :], ref[TOP : TOP + 1, :]


def write_state(ref, state):
    ref[:D, :], ref[MASS : MASS + 1, :], ref[TOP : TOP + 1, :] = state


def put_row(ref, at, value):
    ref[at : at + 1, :] = value


def near_kernel(place_ref, head_ref, z2_ref, z1_ref, z0_ref, q4_ref, bound_ref, w_hbm, *refs):
    p_ref, st_ref, w_ref, sems = refs[-4:]
    head = head_ref[0]
    sources = (head, source_of(head, 0, True), source_of(head, -2, False), source_of(head, 2, False))
    sources += (source_of(head, -2, True), source_of(head, 2, True), source_of(head, 4, False), source_of(head, 4, True))
    copies = []
    for i, source in enumerate(sources):
        cols = pl.ds(pl.multiple_of(source * BLOCK, BLOCK), BLOCK)
        copies.append(pltpu.make_async_copy(w_hbm.at[:, cols], w_ref.at[:, pl.ds(i * BLOCK, BLOCK)], sems.at[i]))
    for copy in copies:
        copy.start()
    me = place_ref[0]
    queries = q4_ref[...]
    row = lax.broadcasted_iota(jnp.int32, (ROWS, LANES), 0)
    pos, start = bound_ref[0:1, :].astype(jnp.int32), bound_ref[1:2, :].astype(jnp.int32)
    state = None
    for i, ref in ((2, z0_ref), (1, z1_ref), (0, z2_ref)):
        at = pos if i == 2 else None
        prob, peak, state = absorb(ref[...], queries, row, me - PLANE * (2 - i), start, state, at)
        p_ref[i * ROWS : (i + 1) * ROWS, :] = prob
        put_row(st_ref, PEAK + 2 * i, peak)
    write_state(st_ref, state)
    put_row(st_ref, START, bound_ref[1:2, :])
    for copy in copies:
        copy.wait()


def project_kernel(*refs):
    pieces, (w_ref, after, g4_ref, gt_ref) = refs[:8], refs[8:]
    acc = None
    for i, piece in enumerate(pieces):
        part = dot(piece[...], w_ref[:, i * BLOCK : (i + 1) * BLOCK], 1, 1)
        acc = part if acc is None else acc + part
    acc = acc.astype(jnp.bfloat16)
    for h in range(HEADS):
        g4_ref[h * ROWS : (h + 1) * ROWS, :] = acc[:, h * D : (h + 1) * D]
    gt_ref[...] = jnp.transpose(g4_ref[...].astype(jnp.float32))


def rows(i):
    return pl.ds(pl.multiple_of(i * ROWS, ROWS), ROWS)


def source_of(head, by, flip):
    at = lax.rem(head + by + 8, 8)
    return at + 1 - 2 * lax.rem(at, 2) if flip else at


def middle_kernel(place_ref, own_ref, q4_ref, st_in_ref, after, p_ref, st_ref):
    queries = q4_ref[...]
    row = lax.broadcasted_iota(jnp.int32, (ROWS, LANES), 0)
    start = st_in_ref[START : START + 1, :].astype(jnp.int32)
    state = read_state(st_in_ref)
    st_ref[PEAK:, :] = st_in_ref[PEAK:, :]
    for i in range(2):
        slot = 2 * i + 1
        block = own_ref[slot * ROWS : (slot + 1) * ROWS, :]
        prob, peak, state = absorb(block, queries, row, place_ref[0] + 2 * (slot - REACH), start, state)
        p_ref[i * ROWS : (i + 1) * ROWS, :] = prob
        put_row(st_ref, PEAK + slot, peak)
    write_state(st_ref, state)
    put_row(st_ref, START, st_in_ref[START : START + 1, :])


def across_kernel(place_ref, par_ref, q4_ref, gt_ref, st_in_ref, p_ref, st_ref):
    me = place_ref[0]
    core = lax.rem(me, 2)
    chip = me - core
    queries = q4_ref[...]
    row = lax.broadcasted_iota(jnp.int32, (ROWS, LANES), 0)
    start = st_in_ref[START : START + 1, :].astype(jnp.int32)
    state = read_state(st_in_ref)
    peaks = [st_in_ref[PEAK + m : PEAK + m + 1, :] for m in range(SLOTS)]
    for i in range(REACH):
        slot = i + core
        prob, peak, state = absorb(par_ref[rows(slot), :], queries, row, chip + 1 - core + 2 * (slot - REACH), start, state)
        p_ref[i * ROWS : (i + 1) * ROWS, :] = prob
        peaks.append(peak)
    out, mass, top = state
    put_row(st_ref, DOT, jnp.sum(gt_ref[...] * out, axis=0, keepdims=True) / mass)
    log_total = top + jnp.log2(mass)
    for i, peak in enumerate(peaks):
        put_row(st_ref, PEAK + i, jnp.exp2(peak - log_total))


def back_block(block, prob, share, g4, q4, rd):
    prob = prob.astype(jnp.float32) * share
    dprob = dot(block[:, D:], g4, 1, 1)
    ds = (prob * (dprob - rd)).astype(jnp.bfloat16)
    dv = dot(prob.astype(jnp.bfloat16), g4, 1, 0)
    dk = dot(ds, q4, 1, 0) * SCALE
    dq = dot(block[:, :D], ds, 0, 0)
    return dk, dv, dq


def put(out_ref, slot, dk, dv):
    at = pl.ds(pl.multiple_of(slot * ROWS, ROWS), ROWS)
    out_ref[at, :D] = dk.astype(out_ref.dtype)
    out_ref[at, D:] = dv.astype(out_ref.dtype)


def cross_step(slot, core, par_ref, p_ref, st_ref, g4, q4_ref, rd):
    share = st_ref[pl.ds(PEAK + SLOTS + slot - core, 1), :]
    return back_block(par_ref[rows(slot), :], p_ref[rows(slot - core), :], share, g4, q4_ref[...], rd)


def cross_far(place_ref, q4_ref, par_ref, p_ref, g_ref, st_in_ref, out_ref, st_ref):
    core = lax.rem(place_ref[0], 2)
    g4 = g_ref[...]
    rd = st_in_ref[DOT : DOT + 1, :]
    st_ref[DOT : DOT + 1, :] = rd
    st_ref[PEAK:, :] = st_in_ref[PEAK:, :]
    dk, dv, dq = cross_step(1, core, par_ref, p_ref, st_ref, g4, q4_ref, rd)
    put(out_ref, 1, dk, dv)
    st_ref[:D, :] = dq

    @pl.when(core == 1)
    def _():
        out_ref[:ROWS, :] = jnp.zeros((ROWS, 2 * D), out_ref.dtype)

    @pl.when(core == 0)
    def _():
        dk, dv, dq = cross_step(0, core, par_ref, p_ref, st_ref, g4, q4_ref, rd)
        put(out_ref, 0, dk, dv)
        st_ref[:D, :] += dq


def cross_near(place_ref, q4_ref, par_ref, p_ref, g_ref, st_in_ref, out_ref, st_ref):
    core = lax.rem(place_ref[0], 2)
    g4 = g_ref[...]
    rd = st_in_ref[DOT : DOT + 1, :]
    st_ref[DOT : DOT + 1, :] = rd
    st_ref[PEAK:, :] = st_in_ref[PEAK:, :]
    total = st_in_ref[:D, :]
    for slot in (2, 3):
        dk, dv, dq = cross_step(slot, core, par_ref, p_ref, st_ref, g4, q4_ref, rd)
        put(out_ref, slot - 2, dk, dv)
        total = total + dq
    st_ref[:D, :] = total

    @pl.when(core == 0)
    def _():
        out_ref[2 * ROWS :, :] = jnp.zeros((ROWS, 2 * D), out_ref.dtype)

    @pl.when(core == 1)
    def _():
        dk, dv, dq = cross_step(4, core, par_ref, p_ref, st_ref, g4, q4_ref, rd)
        put(out_ref, 2, dk, dv)
        st_ref[:D, :] += dq


def own_kernel(slots, q4_ref, own_ref, near_ref, side_ref, g_ref, st_in_ref, *refs):
    out_ref, st_ref = refs[-2:]
    g4 = g_ref[...]
    rd = st_in_ref[DOT : DOT + 1, :]
    total = st_in_ref[:D, :]
    for i, slot in enumerate(slots):
        at = slot // 2 * ROWS
        prob = (side_ref if slot % 2 else near_ref)[at : at + ROWS, :]
        share = st_in_ref[PEAK + slot : PEAK + slot + 1, :]
        dk, dv, dq = back_block(own_ref[slot * ROWS : (slot + 1) * ROWS, :], prob, share, g4, q4_ref[...], rd)
        out_ref[i * ROWS : (i + 1) * ROWS, :D] = dk
        out_ref[i * ROWS : (i + 1) * ROWS, D:] = dv
        total = total + dq
    if slots[-1] < REACH:
        st_ref[DOT : DOT + 1, :] = rd
        st_ref[PEAK:, :] = st_in_ref[PEAK:, :]
        st_ref[:D, :] = total
    else:
        dq = jnp.transpose(total) * SCALE
        for h in range(HEADS):
            st_ref[:, h * D : (h + 1) * D] = dq[h * ROWS : (h + 1) * ROWS, :].astype(jnp.bfloat16)


def is_upper(place_ref):
    return (lax.rem(lax.div(place_ref[0], 2), 2) == 1).astype(jnp.float32)


def settle_far(own_ref, back_ref, keep_ref, side_ref):
    both = own_ref[...] + back_ref[...].astype(jnp.float32)
    keep_ref[...] = both[:ROWS]
    side_ref[...] = both[ROWS:].astype(jnp.bfloat16)


def relay_far(place_ref, keep_ref, side_ref, out_ref):
    out_ref[...] = (keep_ref[...] + side_ref[...].astype(jnp.float32) * is_upper(place_ref)).astype(jnp.bfloat16)


def settle_near(own_ref, back_ref, keep_ref, side_ref):
    both = own_ref[...] + back_ref[: 2 * ROWS, :].astype(jnp.float32)
    keep_ref[...] = both[:ROWS]
    side_ref[...] = both[ROWS:].astype(jnp.bfloat16)


def relay_near(place_ref, keep_ref, near_ref, far_ref, *refs):
    out_ref = refs[-1]
    upper = is_upper(place_ref)
    near, far = near_ref[...].astype(jnp.float32), far_ref[...].astype(jnp.float32)
    out_ref[...] = (keep_ref[...] + near * upper + far * (1 - upper)).astype(jnp.bfloat16)


def finish_kernel(place_ref, own_ref, back_ref, near_ref, one_ref, two_ref, k_ref, v_ref):
    def wide(x):
        return x.astype(jnp.float32)

    total = own_ref[...] + wide(back_ref[2 * ROWS :, :]) + wide(near_ref[...]) * (1 - is_upper(place_ref))
    total = (total + wide(one_ref[...]) + wide(two_ref[...])).astype(jnp.bfloat16)
    k_ref[...] = total[:, :D]
    v_ref[...] = total[:, D:]


def vmem(n):
    return [pl.BlockSpec(memory_space=pltpu.VMEM)] * n


def smem(n):
    return [pl.BlockSpec(memory_space=pltpu.SMEM)] * n


def hbm(n):
    return [pl.BlockSpec(memory_space=pltpu.HBM)] * n


def token(n):
    return [pl.BlockSpec(memory_space=pl.ANY)] * n


def moved(x, axis, to):
    return lax.ppermute(x, axis, [(i, to(i)) for i in range(lax.axis_size(axis))])


def turned(x, axis, by):
    count = lax.axis_size(axis)
    return moved(x, axis, lambda i: (i + by) % count)


def shape(rows, cols, dtype):
    return jax.ShapeDtypeStruct((rows, cols), dtype)


def call(name, kernel, outs, ins, args, scratch=(), flops=1):
    one = not isinstance(outs, tuple)
    return pl.pallas_call(
        kernel,
        out_shape=outs,
        in_specs=ins,
        out_specs=vmem(1)[0] if one else tuple(vmem(len(outs))),
        scratch_shapes=list(scratch),
        compiler_params=pltpu.CompilerParams(vmem_limit_bytes=8 * MIB),
        cost_estimate=pl.CostEstimate(flops=flops, bytes_accessed=1, transcendentals=0),
        name=name,
    )(*args)


def local(queries, keys, values, grad_out, out_weight, lengths):
    bf16, f32 = jnp.bfloat16, jnp.float32
    place = lax.axis_index("ctx").astype(jnp.int32).reshape(1)
    head = lax.axis_index("head").astype(jnp.int32).reshape(1)
    dma = pltpu.SemaphoreType.DMA
    pinned = functools.partial(pltpu.with_memory_space_constraint, memory_space=pltpu.HBM)
    state = shape(STATE, LANES, f32)

    first = moved(grad_out, "head", lambda i: i ^ 1)
    right = turned(grad_out, "head", 2)
    left = turned(grad_out, "head", -2)
    kv = jnp.pad(keys, ((0, 0), (0, D))) + jnp.pad(values, ((0, 0), (D, 0)))
    z2 = turned(kv, "ctx", 2 * PLANE)
    z1 = turned(kv, "ctx", PLANE)
    q4, bound = call(
        "load",
        load_kernel,
        (shape(LANES, D, bf16), shape(8, LANES, f32)),
        smem(1) + hbm(2),
        (place, pinned(lengths), pinned(queries)),
        [pltpu.SMEM((lengths.shape[0],), jnp.int32), dma((1 + HEADS,))],
    )
    other = first
    other_right = turned(other, "head", 2)
    other_left = turned(other, "head", -2)
    far = turned(right, "head", 2)
    other_far = turned(other_left, "head", -2)

    gate = call("gate", gate_kernel, shape(8, D, f32), token(4), (other, right, left, q4))
    picked = call(
        "pick_side", pick_kernel, shape(2 * ROWS, 2 * D, bf16), smem(1) + vmem(3) + token(1), (place, z2, z1, kv, gate)
    )
    side = moved(picked, "ctx", lambda i: i ^ 2)
    p_near, st, weight = call(
        "near",
        near_kernel,
        (
            shape(3 * ROWS, LANES, bf16),
            state,
            shape(HEADS * D, 8 * BLOCK, bf16),
        ),
        smem(2) + vmem(5) + hbm(1) + token(3),
        (place, head, z2, z1, kv, q4, bound, pinned(out_weight), picked, other_right, other_left),
        [dma((8,))],
    )
    own = call("join_slots", join_kernel, shape(SLOTS * ROWS, 2 * D, bf16), vmem(4) + token(1), (z2, z1, kv, side, st))
    par = moved(own, "ctx", lambda i: i ^ 1)

    g4, gt = call(
        "project",
        project_kernel,
        (shape(LANES, D, bf16), shape(D, LANES, f32)),
        vmem(9) + token(1),
        (grad_out, other, right, left, other_right, other_left, far, other_far, weight, own),
    )
    p_side, st = call(
        "middle", middle_kernel, (shape(2 * ROWS, LANES, bf16), state), smem(1) + vmem(3) + token(1), (place, own, q4, st, gt), flops=4 * 10**9
    )
    p_par, st = call(
        "across", across_kernel, (shape(REACH * ROWS, LANES, bf16), state), smem(1) + vmem(4), (place, par, q4, gt, st)
    )

    far_cross, st = call(
        "cross_far", cross_far, (shape(2 * ROWS, 2 * D, bf16), state), smem(1) + vmem(5), (place, q4, par, p_par, g4, st)
    )
    far_back = moved(far_cross, "ctx", lambda i: i ^ 1)
    near_cross, st = call(
        "cross_near", cross_near, (shape(3 * ROWS, 2 * D, bf16), state), smem(1) + vmem(5), (place, q4, par, p_par, g4, st), flops=FL
    )
    near_back = moved(near_cross, "ctx", lambda i: i ^ 1)
    far_own, st = call(
        "own_far",
        functools.partial(own_kernel, (0, 1)),
        (shape(2 * ROWS, 2 * D, f32), state),
        vmem(6),
        (q4, own, p_near, p_side, g4, st),
        flops=FL,
    )
    far_keep, far_side = call(
        "settle_far", settle_far, (shape(ROWS, 2 * D, f32), shape(ROWS, 2 * D, bf16)), vmem(2), (far_own, far_back)
    )
    far_side = moved(far_side, "ctx", lambda i: i ^ 2)
    near_own, st = call(
        "own_near",
        functools.partial(own_kernel, (2, 3)),
        (shape(2 * ROWS, 2 * D, f32), state),
        vmem(6) + token(1),
        (q4, own, p_near, p_side, g4, st, far_keep),
        flops=FL,
    )
    near_keep, near_side = call(
        "settle_near", settle_near, (shape(ROWS, 2 * D, f32), shape(ROWS, 2 * D, bf16)), vmem(2), (near_own, near_back)
    )
    near_side = moved(near_side, "ctx", lambda i: i ^ 2)
    last_own, grad_queries = call(
        "own_last",
        functools.partial(own_kernel, (4,)),
        (shape(ROWS, 2 * D, f32), shape(ROWS, HEADS * D, bf16)),
        vmem(6) + token(1),
        (q4, own, p_near, p_side, g4, st, near_keep),
    )
    to_two = call("relay_far", relay_far, shape(ROWS, 2 * D, bf16), smem(1) + vmem(2), (place, far_keep, far_side))
    got_two = turned(to_two, "ctx", -2 * PLANE)
    to_one = call(
        "relay_near",
        relay_near,
        shape(ROWS, 2 * D, bf16),
        smem(1) + vmem(3) + token(2),
        (place, near_keep, near_side, far_side, to_two, last_own),
    )
    got_one = turned(to_one, "ctx", -PLANE)
    grad_keys, grad_values = call(
        "finish",
        finish_kernel,
        (shape(ROWS, D, bf16), shape(ROWS, D, bf16)),
        smem(1) + vmem(5),
        (place, last_own, near_back, near_side, got_one, got_two),
    )
    return grad_queries, grad_keys, grad_values


def solution(mesh):
    return jax.shard_map(
        local,
        mesh=mesh,
        in_specs=(
            P("ctx", "head"),
            P("ctx", "head"),
            P("ctx", "head"),
            P("ctx", "head"),
            P("head", None),
            P(),
        ),
        out_specs=(P("ctx", "head"), P("ctx", "head"), P("ctx", "head")),
        check_vma=False,
    )
```

```python
import functools

import jax
import jax.numpy as jnp
from jax import lax
from jax.experimental import pallas as pl
from jax.experimental.pallas import tpu as pltpu
from jax.sharding import PartitionSpec as P

D = 128
HEADS = 4
ROWS = 192
LANES = HEADS * ROWS
REACH = 4
SLOTS = REACH + 1
PLANE = 4
BLOCK = 512
MASS, TOP, START, DOT = D, D + 1, D + 2, D + 3
PEAK = D + 8
STATE = PEAK + 16
NEG = -1e30
FLOOR = -1e20
SCALE = D**-0.5
LOG2E = 1.4426950408889634
MIB = 1 << 20
FL = 4 * 10**9


def dot(a, b, ca, cb):
    return lax.dot_general(a, b, (((ca,), (cb,)), ((), ())), preferred_element_type=jnp.float32)


def stack_heads(src, dst):
    for h in range(HEADS):
        dst[h * ROWS : (h + 1) * ROWS, :] = src[:, h * D : (h + 1) * D]


def load_kernel(place_ref, head_ref, len_hbm, q_hbm, w_hbm, q4_ref, bound_ref, w_ref, len_ref, sems):
    head = head_ref[0]
    copies = [pltpu.make_async_copy(len_hbm, len_ref, sems.at[0])]
    sources = (head, source_of(head, 0, True), source_of(head, -2, False), source_of(head, 2, False))
    sources += (source_of(head, -2, True), source_of(head, 2, True), source_of(head, 4, False), source_of(head, 4, True))
    for i, source in enumerate(sources):
        cols = pl.ds(pl.multiple_of(source * BLOCK, BLOCK), BLOCK)
        copies.append(pltpu.make_async_copy(w_hbm.at[:, cols], w_ref.at[:, pl.ds(i * BLOCK, BLOCK)], sems.at[1 + HEADS + i]))
    for h in range(HEADS):
        across, along = pl.ds(h * ROWS, ROWS), pl.ds(h * D, D)
        copies.append(pltpu.make_async_copy(q_hbm.at[:, along], q4_ref.at[across, :], sems.at[1 + h]))
    for copy in copies:
        copy.start()
    lane = lax.broadcasted_iota(jnp.int32, (1, LANES), 1)
    pos = lane + place_ref[0] * ROWS
    for h in range(1, HEADS):
        pos = pos - jnp.where(lane >= h * ROWS, ROWS, 0)
    start = jnp.zeros((1, LANES), jnp.int32)
    end = jnp.int32(0)
    copies[0].wait()
    for d in range(len_ref.shape[0]):
        end = end + len_ref[d]
        start = jnp.where(end <= pos, end, start)
    bound_ref[0:1, :] = pos.astype(jnp.float32)
    bound_ref[1:2, :] = start.astype(jnp.float32)
    for copy in copies[1:]:
        copy.wait()


def stage_kernel(piece_ref, after, out_ref):
    out_ref[...] = piece_ref[...]


def gate_kernel(*refs):
    refs[-1][...] = jnp.zeros(refs[-1].shape, refs[-1].dtype)


def pick_kernel(place_ref, z2_ref, z1_ref, z0_ref, *refs):
    out_ref = refs[-1]
    upper = lax.rem(lax.div(place_ref[0], 2), 2) == 1

    @pl.when(upper)
    def _():
        out_ref[:ROWS, :] = z2_ref[...]
        out_ref[ROWS:, :] = z1_ref[...]

    @pl.when(jnp.logical_not(upper))
    def _():
        out_ref[:ROWS, :] = z1_ref[...]
        out_ref[ROWS:, :] = z0_ref[...]


def join_kernel(z2_ref, z1_ref, z0_ref, side_ref, *refs):
    out_ref = refs[-1]
    parts = (z2_ref[...], side_ref[:ROWS, :], z1_ref[...], side_ref[ROWS:, :], z0_ref[...])
    for m, part in enumerate(parts):
        out_ref[m * ROWS : (m + 1) * ROWS, :] = part


def absorb(block, queries, row, base, start, state, pos=None):
    s = dot(block[:, :D], queries, 1, 1) * (SCALE * LOG2E)
    visible = row >= start - base * ROWS
    if pos is not None:
        visible = visible & (row <= pos - base * ROWS)
    s = jnp.where(visible, s, NEG)
    peak = jnp.maximum(jnp.max(s, axis=0, keepdims=True), FLOOR)
    prob = jnp.exp2(s - peak).astype(jnp.bfloat16)
    mass = jnp.sum(prob.astype(jnp.float32), axis=0, keepdims=True)
    out = dot(block[:, D:], prob, 0, 0)
    if state is None:
        return prob, peak, (out, mass, peak)
    old_out, old_mass, old_peak = state
    top = jnp.maximum(old_peak, peak)
    before, now = jnp.exp2(old_peak - top), jnp.exp2(peak - top)
    return prob, peak, (old_out * before + out * now, old_mass * before + mass * now, top)


def read_state(ref):
    return ref[:D, :], ref[MASS : MASS + 1, :], ref[TOP : TOP + 1, :]


def write_state(ref, state):
    ref[:D, :], ref[MASS : MASS + 1, :], ref[TOP : TOP + 1, :] = state


def put_row(ref, at, value):
    ref[at : at + 1, :] = value


def near_kernel(place_ref, z2_ref, z1_ref, z0_ref, q4_ref, bound_ref, *refs):
    p_ref, st_ref = refs[-2:]
    me = place_ref[0]
    queries = q4_ref[...]
    row = lax.broadcasted_iota(jnp.int32, (ROWS, LANES), 0)
    pos, start = bound_ref[0:1, :].astype(jnp.int32), bound_ref[1:2, :].astype(jnp.int32)
    state = None
    for i, ref in ((2, z0_ref), (1, z1_ref), (0, z2_ref)):
        at = pos if i == 2 else None
        prob, peak, state = absorb(ref[...], queries, row, me - PLANE * (2 - i), start, state, at)
        p_ref[i * ROWS : (i + 1) * ROWS, :] = prob
        put_row(st_ref, PEAK + 2 * i, peak)
    write_state(st_ref, state)
    put_row(st_ref, START, bound_ref[1:2, :])


def project_kernel(*refs):
    pieces, (w_ref, after, g4_ref, gt_ref) = refs[:8], refs[8:]
    acc = None
    for i, piece in enumerate(pieces):
        part = dot(piece[...], w_ref[:, i * BLOCK : (i + 1) * BLOCK], 1, 1)
        acc = part if acc is None else acc + part
    acc = acc.astype(jnp.bfloat16)
    for h in range(HEADS):
        g4_ref[h * ROWS : (h + 1) * ROWS, :] = acc[:, h * D : (h + 1) * D]
    gt_ref[...] = jnp.transpose(g4_ref[...].astype(jnp.float32))


def rows(i):
    return pl.ds(pl.multiple_of(i * ROWS, ROWS), ROWS)


def source_of(head, by, flip):
    at = lax.rem(head + by + 8, 8)
    return at + 1 - 2 * lax.rem(at, 2) if flip else at


def middle_kernel(place_ref, own_ref, q4_ref, st_in_ref, after, p_ref, st_ref):
    queries = q4_ref[...]
    row = lax.broadcasted_iota(jnp.int32, (ROWS, LANES), 0)
    start = st_in_ref[START : START + 1, :].astype(jnp.int32)
    state = read_state(st_in_ref)
    st_ref[PEAK:, :] = st_in_ref[PEAK:, :]
    for i in range(2):
        slot = 2 * i + 1
        block = own_ref[slot * ROWS : (slot + 1) * ROWS, :]
        prob, peak, state = absorb(block, queries, row, place_ref[0] + 2 * (slot - REACH), start, state)
        p_ref[i * ROWS : (i + 1) * ROWS, :] = prob
        put_row(st_ref, PEAK + slot, peak)
    write_state(st_ref, state)
    put_row(st_ref, START, st_in_ref[START : START + 1, :])


def across_kernel(place_ref, par_ref, q4_ref, gt_ref, st_in_ref, p_ref, st_ref):
    me = place_ref[0]
    core = lax.rem(me, 2)
    chip = me - core
    queries = q4_ref[...]
    row = lax.broadcasted_iota(jnp.int32, (ROWS, LANES), 0)
    start = st_in_ref[START : START + 1, :].astype(jnp.int32)
    state = read_state(st_in_ref)
    peaks = [st_in_ref[PEAK + m : PEAK + m + 1, :] for m in range(SLOTS)]
    for i in range(REACH):
        slot = i + core
        prob, peak, state = absorb(par_ref[rows(slot), :], queries, row, chip + 1 - core + 2 * (slot - REACH), start, state)
        p_ref[i * ROWS : (i + 1) * ROWS, :] = prob
        peaks.append(peak)
    out, mass, top = state
    put_row(st_ref, DOT, jnp.sum(gt_ref[...] * out, axis=0, keepdims=True) / mass)
    log_total = top + jnp.log2(mass)
    for i, peak in enumerate(peaks):
        put_row(st_ref, PEAK + i, jnp.exp2(peak - log_total))


def back_block(block, prob, share, g4, q4, rd):
    prob = prob.astype(jnp.float32) * share
    dprob = dot(block[:, D:], g4, 1, 1)
    ds = (prob * (dprob - rd)).astype(jnp.bfloat16)
    dv = dot(prob.astype(jnp.bfloat16), g4, 1, 0)
    dk = dot(ds, q4, 1, 0) * SCALE
    dq = dot(block[:, :D], ds, 0, 0)
    return dk, dv, dq


def put(out_ref, slot, dk, dv):
    at = pl.ds(pl.multiple_of(slot * ROWS, ROWS), ROWS)
    out_ref[at, :D] = dk.astype(out_ref.dtype)
    out_ref[at, D:] = dv.astype(out_ref.dtype)


def cross_step(slot, core, par_ref, p_ref, st_ref, g4, q4_ref, rd):
    share = st_ref[pl.ds(PEAK + SLOTS + slot - core, 1), :]
    return back_block(par_ref[rows(slot), :], p_ref[rows(slot - core), :], share, g4, q4_ref[...], rd)


def cross_far(place_ref, q4_ref, par_ref, p_ref, g_ref, st_in_ref, out_ref, st_ref):
    core = lax.rem(place_ref[0], 2)
    g4 = g_ref[...]
    rd = st_in_ref[DOT : DOT + 1, :]
    st_ref[DOT : DOT + 1, :] = rd
    st_ref[PEAK:, :] = st_in_ref[PEAK:, :]
    dk, dv, dq = cross_step(1, core, par_ref, p_ref, st_ref, g4, q4_ref, rd)
    put(out_ref, 1, dk, dv)
    st_ref[:D, :] = dq

    @pl.when(core == 1)
    def _():
        out_ref[:ROWS, :] = jnp.zeros((ROWS, 2 * D), out_ref.dtype)

    @pl.when(core == 0)
    def _():
        dk, dv, dq = cross_step(0, core, par_ref, p_ref, st_ref, g4, q4_ref, rd)
        put(out_ref, 0, dk, dv)
        st_ref[:D, :] += dq


def cross_near(place_ref, q4_ref, par_ref, p_ref, g_ref, st_in_ref, out_ref, st_ref):
    core = lax.rem(place_ref[0], 2)
    g4 = g_ref[...]
    rd = st_in_ref[DOT : DOT + 1, :]
    st_ref[DOT : DOT + 1, :] = rd
    st_ref[PEAK:, :] = st_in_ref[PEAK:, :]
    total = st_in_ref[:D, :]
    for slot in (2, 3):
        dk, dv, dq = cross_step(slot, core, par_ref, p_ref, st_ref, g4, q4_ref, rd)
        put(out_ref, slot - 2, dk, dv)
        total = total + dq
    st_ref[:D, :] = total

    @pl.when(core == 0)
    def _():
        out_ref[2 * ROWS :, :] = jnp.zeros((ROWS, 2 * D), out_ref.dtype)

    @pl.when(core == 1)
    def _():
        dk, dv, dq = cross_step(4, core, par_ref, p_ref, st_ref, g4, q4_ref, rd)
        put(out_ref, 2, dk, dv)
        st_ref[:D, :] += dq


def own_kernel(slots, q4_ref, own_ref, near_ref, side_ref, g_ref, st_in_ref, *refs):
    out_ref, st_ref = refs[-2:]
    g4 = g_ref[...]
    rd = st_in_ref[DOT : DOT + 1, :]
    total = st_in_ref[:D, :]
    for i, slot in enumerate(slots):
        at = slot // 2 * ROWS
        prob = (side_ref if slot % 2 else near_ref)[at : at + ROWS, :]
        share = st_in_ref[PEAK + slot : PEAK + slot + 1, :]
        dk, dv, dq = back_block(own_ref[slot * ROWS : (slot + 1) * ROWS, :], prob, share, g4, q4_ref[...], rd)
        out_ref[i * ROWS : (i + 1) * ROWS, :D] = dk
        out_ref[i * ROWS : (i + 1) * ROWS, D:] = dv
        total = total + dq
    if slots[-1] < REACH:
        st_ref[DOT : DOT + 1, :] = rd
        st_ref[PEAK:, :] = st_in_ref[PEAK:, :]
        st_ref[:D, :] = total
    else:
        dq = jnp.transpose(total) * SCALE
        for h in range(HEADS):
            st_ref[:, h * D : (h + 1) * D] = dq[h * ROWS : (h + 1) * ROWS, :].astype(jnp.bfloat16)


def is_upper(place_ref):
    return (lax.rem(lax.div(place_ref[0], 2), 2) == 1).astype(jnp.float32)


def settle_kernel(own_ref, back_ref, low_ref, high_ref):
    both = own_ref[...] + back_ref[: 2 * ROWS, :].astype(jnp.float32)
    low_ref[...] = both[:ROWS].astype(low_ref.dtype)
    high_ref[...] = both[ROWS:].astype(jnp.bfloat16)


def relay_far(place_ref, keep_ref, side_ref, out_ref):
    out_ref[...] = (keep_ref[...] + side_ref[...].astype(jnp.float32) * is_upper(place_ref)).astype(jnp.bfloat16)


def finish_kernel(place_ref, own_ref, back_ref, side_ref, two_ref, four_ref, eight_ref, k_ref, v_ref):
    def wide(x):
        return x.astype(jnp.float32)

    total = own_ref[...] + wide(back_ref[2 * ROWS :, :]) + wide(side_ref[...]) * (1 - is_upper(place_ref))
    total = (total + wide(two_ref[...]) + wide(four_ref[...]) + wide(eight_ref[...])).astype(jnp.bfloat16)
    k_ref[...] = total[:, :D]
    v_ref[...] = total[:, D:]


def vmem(n):
    return [pl.BlockSpec(memory_space=pltpu.VMEM)] * n


def smem(n):
    return [pl.BlockSpec(memory_space=pltpu.SMEM)] * n


def hbm(n):
    return [pl.BlockSpec(memory_space=pltpu.HBM)] * n


def token(n):
    return [pl.BlockSpec(memory_space=pl.ANY)] * n


def moved(x, axis, to):
    return lax.ppermute(x, axis, [(i, to(i)) for i in range(lax.axis_size(axis))])


def turned(x, axis, by):
    count = lax.axis_size(axis)
    return moved(x, axis, lambda i: (i + by) % count)


def shape(rows, cols, dtype):
    return jax.ShapeDtypeStruct((rows, cols), dtype)


def call(name, kernel, outs, ins, args, scratch=(), flops=1):
    one = not isinstance(outs, tuple)
    return pl.pallas_call(
        kernel,
        out_shape=outs,
        in_specs=ins,
        out_specs=vmem(1)[0] if one else tuple(vmem(len(outs))),
        scratch_shapes=list(scratch),
        compiler_params=pltpu.CompilerParams(vmem_limit_bytes=8 * MIB),
        cost_estimate=pl.CostEstimate(flops=flops, bytes_accessed=1, transcendentals=0),
        name=name,
    )(*args)


def local(queries, keys, values, grad_out, out_weight, lengths):
    bf16, f32 = jnp.bfloat16, jnp.float32
    place = lax.axis_index("ctx").astype(jnp.int32).reshape(1)
    head = lax.axis_index("head").astype(jnp.int32).reshape(1)
    dma = pltpu.SemaphoreType.DMA
    pinned = functools.partial(pltpu.with_memory_space_constraint, memory_space=pltpu.HBM)
    state = shape(STATE, LANES, f32)

    first = moved(grad_out, "head", lambda i: i ^ 1)
    right = turned(grad_out, "head", 2)
    left = turned(grad_out, "head", -2)
    kv = jnp.pad(keys, ((0, 0), (0, D))) + jnp.pad(values, ((0, 0), (D, 0)))
    z2 = turned(kv, "ctx", 2 * PLANE)
    z1 = turned(kv, "ctx", PLANE)
    q4, bound, weight = call(
        "load",
        load_kernel,
        (shape(LANES, D, bf16), shape(8, LANES, f32), shape(HEADS * D, 8 * BLOCK, bf16)),
        smem(2) + hbm(3),
        (place, head, pinned(lengths), pinned(queries), pinned(out_weight)),
        [pltpu.SMEM((lengths.shape[0],), jnp.int32), dma((9 + HEADS,))],
    )
    other = call("stage", stage_kernel, shape(ROWS, BLOCK, bf16), vmem(1) + token(1), (first, q4))
    other_right = turned(other, "head", 2)
    other_left = turned(other, "head", -2)
    far = turned(right, "head", 2)
    other_far = turned(other_left, "head", -2)

    gate = call("gate", gate_kernel, shape(8, D, f32), token(4), (other, right, left, q4))
    picked = call(
        "pick_side", pick_kernel, shape(2 * ROWS, 2 * D, bf16), smem(1) + vmem(3) + token(1), (place, z2, z1, kv, gate)
    )
    side = moved(picked, "ctx", lambda i: i ^ 2)
    p_near, st = call(
        "near",
        near_kernel,
        (shape(3 * ROWS, LANES, bf16), state),
        smem(1) + vmem(5) + token(3),
        (place, z2, z1, kv, q4, bound, picked, other_right, other_left),
    )
    own = call("join_slots", join_kernel, shape(SLOTS * ROWS, 2 * D, bf16), vmem(4) + token(1), (z2, z1, kv, side, st))
    par = moved(own, "ctx", lambda i: i ^ 1)

    g4, gt = call(
        "project",
        project_kernel,
        (shape(LANES, D, bf16), shape(D, LANES, f32)),
        vmem(9) + token(1),
        (grad_out, other, right, left, other_right, other_left, far, other_far, weight, own),
    )
    p_side, st = call(
        "middle", middle_kernel, (shape(2 * ROWS, LANES, bf16), state), smem(1) + vmem(3) + token(1), (place, own, q4, st, gt), flops=4 * 10**9
    )
    p_par, st = call(
        "across", across_kernel, (shape(REACH * ROWS, LANES, bf16), state), smem(1) + vmem(4), (place, par, q4, gt, st)
    )

    far_cross, st = call(
        "cross_far", cross_far, (shape(2 * ROWS, 2 * D, bf16), state), smem(1) + vmem(5), (place, q4, par, p_par, g4, st)
    )
    far_back = moved(far_cross, "ctx", lambda i: i ^ 1)
    near_cross, st = call(
        "cross_near", cross_near, (shape(3 * ROWS, 2 * D, bf16), state), smem(1) + vmem(5), (place, q4, par, p_par, g4, st), flops=FL
    )
    near_back = moved(near_cross, "ctx", lambda i: i ^ 1)
    far_own, st = call(
        "own_far",
        functools.partial(own_kernel, (0, 1)),
        (shape(2 * ROWS, 2 * D, f32), state),
        vmem(6),
        (q4, own, p_near, p_side, g4, st),
        flops=FL,
    )
    far_keep, far_side = call(
        "settle_far", settle_kernel, (shape(ROWS, 2 * D, f32), shape(ROWS, 2 * D, bf16)), vmem(2), (far_own, far_back)
    )
    count = lax.axis_size("ctx")
    far_side = moved(far_side, "ctx", lambda i: (i + 2 if i // 2 % 2 == 0 else i - 6) % count)
    near_own, st = call(
        "own_near",
        functools.partial(own_kernel, (2, 3)),
        (shape(2 * ROWS, 2 * D, f32), state),
        vmem(6) + token(1),
        (q4, own, p_near, p_side, g4, st, far_keep),
        flops=FL,
    )
    by_four, by_two = call(
        "settle_near", settle_kernel, (shape(ROWS, 2 * D, bf16), shape(ROWS, 2 * D, bf16)), vmem(2), (near_own, near_back)
    )
    by_four = turned(by_four, "ctx", -4)
    by_two = turned(by_two, "ctx", -2)
    to_eight = call("relay_far", relay_far, shape(ROWS, 2 * D, bf16), smem(1) + vmem(2), (place, far_keep, far_side))
    by_eight = turned(to_eight, "ctx", -8)
    last_own, grad_queries = call(
        "own_last",
        functools.partial(own_kernel, (4,)),
        (shape(ROWS, 2 * D, f32), shape(ROWS, HEADS * D, bf16)),
        vmem(6) + token(3),
        (q4, own, p_near, p_side, g4, st, to_eight, by_four, by_two),
        flops=FL,
    )
    grad_keys, grad_values = call(
        "finish",
        finish_kernel,
        (shape(ROWS, D, bf16), shape(ROWS, D, bf16)),
        smem(1) + vmem(6),
        (place, last_own, near_back, far_side, by_two, by_four, by_eight),
    )
    return grad_queries, grad_keys, grad_values


def solution(mesh):
    return jax.shard_map(
        local,
        mesh=mesh,
        in_specs=(
            P("ctx", "head"),
            P("ctx", "head"),
            P("ctx", "head"),
            P("ctx", "head"),
            P("head", None),
            P(),
        ),
        out_specs=(P("ctx", "head"), P("ctx", "head"), P("ctx", "head")),
        check_vma=False,
    )
```

```python
import functools

import jax
import jax.numpy as jnp
from jax import lax
from jax.experimental import pallas as pl
from jax.experimental.pallas import tpu as pltpu
from jax.sharding import PartitionSpec as P

D = 128
HEADS = 4
ROWS = 192
LANES = HEADS * ROWS
REACH = 4
SLOTS = REACH + 1
PLANE = 4
BLOCK = 512
MASS, TOP, START, DOT = D, D + 1, D + 2, D + 3
PEAK = D + 8
STATE = PEAK + 16
NEG = -1e30
FLOOR = -1e20
SCALE = D**-0.5
LOG2E = 1.4426950408889634
MIB = 1 << 20
FL = 4 * 10**9
COSTLY = 4 * 10**9


def dot(a, b, ca, cb):
    return lax.dot_general(a, b, (((ca,), (cb,)), ((), ())), preferred_element_type=jnp.float32)


def stack_heads(src, dst):
    for h in range(HEADS):
        dst[h * ROWS : (h + 1) * ROWS, :] = src[:, h * D : (h + 1) * D]


def load_kernel(place_ref, head_ref, len_hbm, q_hbm, w_hbm, q4_ref, bound_ref, w_ref, len_ref, sems):
    head = head_ref[0]
    copies = [pltpu.make_async_copy(len_hbm, len_ref, sems.at[0])]
    sources = (head, source_of(head, 0, True), source_of(head, -2, False), source_of(head, 2, False))
    sources += (source_of(head, -2, True), source_of(head, 2, True), source_of(head, 4, False), source_of(head, 4, True))
    for i, source in enumerate(sources):
        cols = pl.ds(pl.multiple_of(source * BLOCK, BLOCK), BLOCK)
        copies.append(pltpu.make_async_copy(w_hbm.at[:, cols], w_ref.at[:, pl.ds(i * BLOCK, BLOCK)], sems.at[1 + HEADS + i]))
    for h in range(HEADS):
        across, along = pl.ds(h * ROWS, ROWS), pl.ds(h * D, D)
        copies.append(pltpu.make_async_copy(q_hbm.at[:, along], q4_ref.at[across, :], sems.at[1 + h]))
    for copy in copies:
        copy.start()
    lane = lax.broadcasted_iota(jnp.int32, (1, LANES), 1)
    pos = lane + place_ref[0] * ROWS
    for h in range(1, HEADS):
        pos = pos - jnp.where(lane >= h * ROWS, ROWS, 0)
    start = jnp.zeros((1, LANES), jnp.int32)
    end = jnp.int32(0)
    copies[0].wait()
    for d in range(len_ref.shape[0]):
        end = end + len_ref[d]
        start = jnp.where(end <= pos, end, start)
    bound_ref[0:1, :] = pos.astype(jnp.float32)
    bound_ref[1:2, :] = start.astype(jnp.float32)
    for copy in copies[1:]:
        copy.wait()


def stage_kernel(piece_ref, after, out_ref):
    out_ref[...] = piece_ref[...]


def gate_kernel(*refs):
    refs[-1][...] = jnp.zeros(refs[-1].shape, refs[-1].dtype)


def pick_kernel(place_ref, z2_ref, z1_ref, z0_ref, *refs):
    out_ref = refs[-1]
    upper = lax.rem(lax.div(place_ref[0], 2), 2) == 1

    @pl.when(upper)
    def _():
        out_ref[:ROWS, :] = z2_ref[...]
        out_ref[ROWS:, :] = z1_ref[...]

    @pl.when(jnp.logical_not(upper))
    def _():
        out_ref[:ROWS, :] = z1_ref[...]
        out_ref[ROWS:, :] = z0_ref[...]


def join_kernel(z2_ref, z1_ref, z0_ref, side_ref, *refs):
    out_ref = refs[-1]
    parts = (z2_ref[...], side_ref[:ROWS, :], z1_ref[...], side_ref[ROWS:, :], z0_ref[...])
    for m, part in enumerate(parts):
        out_ref[m * ROWS : (m + 1) * ROWS, :] = part


def absorb(block, queries, row, base, start, state, pos=None):
    s = dot(block[:, :D], queries, 1, 1) * (SCALE * LOG2E)
    visible = row >= start - base * ROWS
    if pos is not None:
        visible = visible & (row <= pos - base * ROWS)
    s = jnp.where(visible, s, NEG)
    peak = jnp.maximum(jnp.max(s, axis=0, keepdims=True), FLOOR)
    prob = jnp.exp2(s - peak).astype(jnp.bfloat16)
    mass = jnp.sum(prob.astype(jnp.float32), axis=0, keepdims=True)
    out = dot(block[:, D:], prob, 0, 0)
    if state is None:
        return prob, peak, (out, mass, peak)
    old_out, old_mass, old_peak = state
    top = jnp.maximum(old_peak, peak)
    before, now = jnp.exp2(old_peak - top), jnp.exp2(peak - top)
    return prob, peak, (old_out * before + out * now, old_mass * before + mass * now, top)


def read_state(ref):
    return ref[:D, :], ref[MASS : MASS + 1, :], ref[TOP : TOP + 1, :]


def write_state(ref, state):
    ref[:D, :], ref[MASS : MASS + 1, :], ref[TOP : TOP + 1, :] = state


def put_row(ref, at, value):
    ref[at : at + 1, :] = value


def near_kernel(place_ref, z2_ref, z1_ref, z0_ref, q4_ref, bound_ref, *refs):
    p_ref, st_ref = refs[-2:]
    me = place_ref[0]
    queries = q4_ref[...]
    row = lax.broadcasted_iota(jnp.int32, (ROWS, LANES), 0)
    pos, start = bound_ref[0:1, :].astype(jnp.int32), bound_ref[1:2, :].astype(jnp.int32)
    state = None
    for i, ref in ((2, z0_ref), (1, z1_ref), (0, z2_ref)):
        at = pos if i == 2 else None
        prob, peak, state = absorb(ref[...], queries, row, me - PLANE * (2 - i), start, state, at)
        p_ref[i * ROWS : (i + 1) * ROWS, :] = prob
        put_row(st_ref, PEAK + 2 * i, peak)
    write_state(st_ref, state)
    put_row(st_ref, START, bound_ref[1:2, :])


def project_kernel(*refs):
    pieces, (w_ref, after, acc_ref) = refs[:7], refs[7:]
    acc = None
    for i, piece in enumerate(pieces):
        part = dot(piece[...], w_ref[:, i * BLOCK : (i + 1) * BLOCK], 1, 1)
        acc = part if acc is None else acc + part
    acc_ref[...] = acc


def last_projection(piece_ref, w_ref, acc_ref, after, g4_ref, gt_ref):
    acc = (acc_ref[...] + dot(piece_ref[...], w_ref[:, 7 * BLOCK :], 1, 1)).astype(jnp.bfloat16)
    for h in range(HEADS):
        g4_ref[h * ROWS : (h + 1) * ROWS, :] = acc[:, h * D : (h + 1) * D]
    gt_ref[...] = jnp.transpose(g4_ref[...].astype(jnp.float32))


def rows(i):
    return pl.ds(pl.multiple_of(i * ROWS, ROWS), ROWS)


def source_of(head, by, flip):
    at = lax.rem(head + by + 8, 8)
    return at + 1 - 2 * lax.rem(at, 2) if flip else at


def middle_kernel(place_ref, own_ref, q4_ref, st_in_ref, after, p_ref, st_ref):
    queries = q4_ref[...]
    row = lax.broadcasted_iota(jnp.int32, (ROWS, LANES), 0)
    start = st_in_ref[START : START + 1, :].astype(jnp.int32)
    state = read_state(st_in_ref)
    st_ref[PEAK:, :] = st_in_ref[PEAK:, :]
    for i in range(2):
        slot = 2 * i + 1
        block = own_ref[slot * ROWS : (slot + 1) * ROWS, :]
        prob, peak, state = absorb(block, queries, row, place_ref[0] + 2 * (slot - REACH), start, state)
        p_ref[i * ROWS : (i + 1) * ROWS, :] = prob
        put_row(st_ref, PEAK + slot, peak)
    write_state(st_ref, state)
    put_row(st_ref, START, st_in_ref[START : START + 1, :])


def across_kernel(place_ref, par_ref, q4_ref, gt_ref, st_in_ref, p_ref, st_ref):
    me = place_ref[0]
    core = lax.rem(me, 2)
    chip = me - core
    queries = q4_ref[...]
    row = lax.broadcasted_iota(jnp.int32, (ROWS, LANES), 0)
    start = st_in_ref[START : START + 1, :].astype(jnp.int32)
    state = read_state(st_in_ref)
    peaks = [st_in_ref[PEAK + m : PEAK + m + 1, :] for m in range(SLOTS)]
    for i in range(REACH):
        slot = i + core
        prob, peak, state = absorb(par_ref[rows(slot), :], queries, row, chip + 1 - core + 2 * (slot - REACH), start, state)
        p_ref[i * ROWS : (i + 1) * ROWS, :] = prob
        peaks.append(peak)
    out, mass, top = state
    put_row(st_ref, DOT, jnp.sum(gt_ref[...] * out, axis=0, keepdims=True) / mass)
    log_total = top + jnp.log2(mass)
    for i, peak in enumerate(peaks):
        put_row(st_ref, PEAK + i, jnp.exp2(peak - log_total))


def back_block(block, prob, share, g4, q4, rd):
    prob = prob.astype(jnp.float32) * share
    dprob = dot(block[:, D:], g4, 1, 1)
    ds = (prob * (dprob - rd)).astype(jnp.bfloat16)
    dv = dot(prob.astype(jnp.bfloat16), g4, 1, 0)
    dk = dot(ds, q4, 1, 0) * SCALE
    dq = dot(block[:, :D], ds, 0, 0)
    return dk, dv, dq


def put(out_ref, slot, dk, dv):
    at = pl.ds(pl.multiple_of(slot * ROWS, ROWS), ROWS)
    out_ref[at, :D] = dk.astype(out_ref.dtype)
    out_ref[at, D:] = dv.astype(out_ref.dtype)


def cross_step(slot, core, par_ref, p_ref, st_ref, g4, q4_ref, rd):
    share = st_ref[pl.ds(PEAK + SLOTS + slot - core, 1), :]
    return back_block(par_ref[rows(slot), :], p_ref[rows(slot - core), :], share, g4, q4_ref[...], rd)


def cross_far(place_ref, q4_ref, par_ref, p_ref, g_ref, st_in_ref, out_ref, st_ref):
    core = lax.rem(place_ref[0], 2)
    g4 = g_ref[...]
    rd = st_in_ref[DOT : DOT + 1, :]
    st_ref[DOT : DOT + 1, :] = rd
    st_ref[PEAK:, :] = st_in_ref[PEAK:, :]
    dk, dv, dq = cross_step(1, core, par_ref, p_ref, st_ref, g4, q4_ref, rd)
    put(out_ref, 1, dk, dv)
    st_ref[:D, :] = dq

    @pl.when(core == 1)
    def _():
        out_ref[:ROWS, :] = jnp.zeros((ROWS, 2 * D), out_ref.dtype)

    @pl.when(core == 0)
    def _():
        dk, dv, dq = cross_step(0, core, par_ref, p_ref, st_ref, g4, q4_ref, rd)
        put(out_ref, 0, dk, dv)
        st_ref[:D, :] += dq


def cross_near(place_ref, q4_ref, par_ref, p_ref, g_ref, st_in_ref, out_ref, st_ref):
    core = lax.rem(place_ref[0], 2)
    g4 = g_ref[...]
    rd = st_in_ref[DOT : DOT + 1, :]
    st_ref[DOT : DOT + 1, :] = rd
    st_ref[PEAK:, :] = st_in_ref[PEAK:, :]
    total = st_in_ref[:D, :]
    for slot in (2, 3):
        dk, dv, dq = cross_step(slot, core, par_ref, p_ref, st_ref, g4, q4_ref, rd)
        put(out_ref, slot - 2, dk, dv)
        total = total + dq
    st_ref[:D, :] = total

    @pl.when(core == 0)
    def _():
        out_ref[2 * ROWS :, :] = jnp.zeros((ROWS, 2 * D), out_ref.dtype)

    @pl.when(core == 1)
    def _():
        dk, dv, dq = cross_step(4, core, par_ref, p_ref, st_ref, g4, q4_ref, rd)
        put(out_ref, 2, dk, dv)
        st_ref[:D, :] += dq


def own_kernel(slots, q4_ref, own_ref, near_ref, side_ref, g_ref, st_in_ref, *refs):
    out_ref, st_ref = refs[-2:]
    g4 = g_ref[...]
    rd = st_in_ref[DOT : DOT + 1, :]
    total = st_in_ref[:D, :]
    for i, slot in enumerate(slots):
        at = slot // 2 * ROWS
        prob = (side_ref if slot % 2 else near_ref)[at : at + ROWS, :]
        share = st_in_ref[PEAK + slot : PEAK + slot + 1, :]
        dk, dv, dq = back_block(own_ref[slot * ROWS : (slot + 1) * ROWS, :], prob, share, g4, q4_ref[...], rd)
        out_ref[i * ROWS : (i + 1) * ROWS, :D] = dk
        out_ref[i * ROWS : (i + 1) * ROWS, D:] = dv
        total = total + dq
    if slots[-1] < REACH:
        st_ref[DOT : DOT + 1, :] = rd
        st_ref[PEAK:, :] = st_in_ref[PEAK:, :]
        st_ref[:D, :] = total
    else:
        dq = jnp.transpose(total) * SCALE
        for h in range(HEADS):
            st_ref[:, h * D : (h + 1) * D] = dq[h * ROWS : (h + 1) * ROWS, :].astype(jnp.bfloat16)


def is_upper(place_ref):
    return (lax.rem(lax.div(place_ref[0], 2), 2) == 1).astype(jnp.float32)


def settle_kernel(own_ref, back_ref, low_ref, high_ref):
    both = own_ref[...] + back_ref[: 2 * ROWS, :].astype(jnp.float32)
    low_ref[...] = both[:ROWS].astype(low_ref.dtype)
    high_ref[...] = both[ROWS:].astype(jnp.bfloat16)


def relay_far(place_ref, keep_ref, side_ref, out_ref):
    out_ref[...] = (keep_ref[...] + side_ref[...].astype(jnp.float32) * is_upper(place_ref)).astype(jnp.bfloat16)


def finish_kernel(place_ref, own_ref, back_ref, side_ref, two_ref, four_ref, eight_ref, k_ref, v_ref):
    def wide(x):
        return x.astype(jnp.float32)

    total = own_ref[...] + wide(back_ref[2 * ROWS :, :]) + wide(side_ref[...]) * (1 - is_upper(place_ref))
    total = (total + wide(two_ref[...]) + wide(four_ref[...]) + wide(eight_ref[...])).astype(jnp.bfloat16)
    k_ref[...] = total[:, :D]
    v_ref[...] = total[:, D:]


def vmem(n):
    return [pl.BlockSpec(memory_space=pltpu.VMEM)] * n


def smem(n):
    return [pl.BlockSpec(memory_space=pltpu.SMEM)] * n


def hbm(n):
    return [pl.BlockSpec(memory_space=pltpu.HBM)] * n


def token(n):
    return [pl.BlockSpec(memory_space=pl.ANY)] * n


def moved(x, axis, to):
    return lax.ppermute(x, axis, [(i, to(i)) for i in range(lax.axis_size(axis))])


def turned(x, axis, by):
    count = lax.axis_size(axis)
    return moved(x, axis, lambda i: (i + by) % count)


def shape(rows, cols, dtype):
    return jax.ShapeDtypeStruct((rows, cols), dtype)


def call(name, kernel, outs, ins, args, scratch=(), flops=1):
    one = not isinstance(outs, tuple)
    return pl.pallas_call(
        kernel,
        out_shape=outs,
        in_specs=ins,
        out_specs=vmem(1)[0] if one else tuple(vmem(len(outs))),
        scratch_shapes=list(scratch),
        compiler_params=pltpu.CompilerParams(vmem_limit_bytes=8 * MIB),
        cost_estimate=pl.CostEstimate(flops=flops, bytes_accessed=1, transcendentals=0),
        name=name,
    )(*args)


def local(queries, keys, values, grad_out, out_weight, lengths):
    bf16, f32 = jnp.bfloat16, jnp.float32
    place = lax.axis_index("ctx").astype(jnp.int32).reshape(1)
    head = lax.axis_index("head").astype(jnp.int32).reshape(1)
    dma = pltpu.SemaphoreType.DMA
    pinned = functools.partial(pltpu.with_memory_space_constraint, memory_space=pltpu.HBM)
    state = shape(STATE, LANES, f32)

    first = moved(grad_out, "head", lambda i: i ^ 1)
    right = turned(grad_out, "head", 2)
    left = turned(grad_out, "head", -2)
    kv = jnp.pad(keys, ((0, 0), (0, D))) + jnp.pad(values, ((0, 0), (D, 0)))
    z2 = turned(kv, "ctx", 2 * PLANE)
    z1 = turned(kv, "ctx", PLANE)
    q4, bound, weight = call(
        "load",
        load_kernel,
        (shape(LANES, D, bf16), shape(8, LANES, f32), shape(HEADS * D, 8 * BLOCK, bf16)),
        smem(2) + hbm(3),
        (place, head, pinned(lengths), pinned(queries), pinned(out_weight)),
        [pltpu.SMEM((lengths.shape[0],), jnp.int32), dma((9 + HEADS,))],
    )
    other = call("stage", stage_kernel, shape(ROWS, BLOCK, bf16), vmem(1) + token(1), (first, q4))
    other_right = turned(other, "head", 2)
    other_left = turned(other, "head", -2)
    far = turned(right, "head", 2)
    other_far = turned(other_left, "head", -2)

    gate = call("gate", gate_kernel, shape(8, D, f32), token(4), (other, right, left, q4))
    picked = call(
        "pick_side", pick_kernel, shape(2 * ROWS, 2 * D, bf16), smem(1) + vmem(3) + token(1), (place, z2, z1, kv, gate)
    )
    side = moved(picked, "ctx", lambda i: i ^ 2)
    p_near, st = call(
        "near",
        near_kernel,
        (shape(3 * ROWS, LANES, bf16), state),
        smem(1) + vmem(5) + token(3),
        (place, z2, z1, kv, q4, bound, picked, other_right, other_left),
    )
    own = call("join_slots", join_kernel, shape(SLOTS * ROWS, 2 * D, bf16), vmem(4) + token(1), (z2, z1, kv, side, st))
    par = moved(own, "ctx", lambda i: i ^ 1)

    early = call(
        "project",
        project_kernel,
        shape(ROWS, HEADS * D, f32),
        vmem(8) + token(1),
        (grad_out, other, right, left, other_right, other_left, far, weight, own),
    )
    p_side, st = call(
        "middle",
        middle_kernel,
        (shape(2 * ROWS, LANES, bf16), state),
        smem(1) + vmem(3) + token(1),
        (place, own, q4, st, early),
    )
    g4, gt = call(
        "last_projection",
        last_projection,
        (shape(LANES, D, bf16), shape(D, LANES, f32)),
        vmem(3) + token(1),
        (other_far, weight, early, st),
        flops=COSTLY,
    )
    p_par, st = call(
        "across", across_kernel, (shape(REACH * ROWS, LANES, bf16), state), smem(1) + vmem(4), (place, par, q4, gt, st)
    )

    far_cross, st = call(
        "cross_far", cross_far, (shape(2 * ROWS, 2 * D, bf16), state), smem(1) + vmem(5), (place, q4, par, p_par, g4, st)
    )
    far_back = moved(far_cross, "ctx", lambda i: i ^ 1)
    near_cross, st = call(
        "cross_near", cross_near, (shape(3 * ROWS, 2 * D, bf16), state), smem(1) + vmem(5), (place, q4, par, p_par, g4, st), flops=FL
    )
    near_back = moved(near_cross, "ctx", lambda i: i ^ 1)
    far_own, st = call(
        "own_far",
        functools.partial(own_kernel, (0, 1)),
        (shape(2 * ROWS, 2 * D, f32), state),
        vmem(6),
        (q4, own, p_near, p_side, g4, st),
        flops=FL,
    )
    far_keep, far_side = call(
        "settle_far", settle_kernel, (shape(ROWS, 2 * D, f32), shape(ROWS, 2 * D, bf16)), vmem(2), (far_own, far_back)
    )
    count = lax.axis_size("ctx")
    far_side = moved(far_side, "ctx", lambda i: (i + 2 if i // 2 % 2 == 0 else i - 6) % count)
    near_own, st = call(
        "own_near",
        functools.partial(own_kernel, (2, 3)),
        (shape(2 * ROWS, 2 * D, f32), state),
        vmem(6) + token(1),
        (q4, own, p_near, p_side, g4, st, far_keep),
        flops=FL,
    )
    by_four, by_two = call(
        "settle_near", settle_kernel, (shape(ROWS, 2 * D, bf16), shape(ROWS, 2 * D, bf16)), vmem(2), (near_own, near_back)
    )
    by_four = turned(by_four, "ctx", -4)
    by_two = turned(by_two, "ctx", -2)
    to_eight = call("relay_far", relay_far, shape(ROWS, 2 * D, bf16), smem(1) + vmem(2), (place, far_keep, far_side))
    by_eight = turned(to_eight, "ctx", -8)
    last_own, grad_queries = call(
        "own_last",
        functools.partial(own_kernel, (4,)),
        (shape(ROWS, 2 * D, f32), shape(ROWS, HEADS * D, bf16)),
        vmem(6) + token(3),
        (q4, own, p_near, p_side, g4, st, to_eight, by_four, by_two),
        flops=FL,
    )
    grad_keys, grad_values = call(
        "finish",
        finish_kernel,
        (shape(ROWS, D, bf16), shape(ROWS, D, bf16)),
        smem(1) + vmem(6),
        (place, last_own, near_back, far_side, by_two, by_four, by_eight),
    )
    return grad_queries, grad_keys, grad_values


def solution(mesh):
    return jax.shard_map(
        local,
        mesh=mesh,
        in_specs=(
            P("ctx", "head"),
            P("ctx", "head"),
            P("ctx", "head"),
            P("ctx", "head"),
            P("head", None),
            P(),
        ),
        out_specs=(P("ctx", "head"), P("ctx", "head"), P("ctx", "head")),
        check_vma=False,
    )
```

```python
import functools

import jax
import jax.numpy as jnp
from jax import lax
from jax.experimental import pallas as pl
from jax.experimental.pallas import tpu as pltpu
from jax.sharding import PartitionSpec as P

D = 128
HEADS = 4
ROWS = 192
LANES = HEADS * ROWS
REACH = 4
SLOTS = REACH + 1
PLANE = 4
BLOCK = 512
MASS, TOP, START, DOT = D, D + 1, D + 2, D + 3
PEAK = D + 8
STATE = PEAK + 16
NEG = -1e30
FLOOR = -1e20
SCALE = D**-0.5
LOG2E = 1.4426950408889634
MIB = 1 << 20
FL = 4 * 10**9
COSTLY = 4 * 10**9


def dot(a, b, ca, cb):
    return lax.dot_general(a, b, (((ca,), (cb,)), ((), ())), preferred_element_type=jnp.float32)


def stack_heads(src, dst):
    for h in range(HEADS):
        dst[h * ROWS : (h + 1) * ROWS, :] = src[:, h * D : (h + 1) * D]


def load_kernel(place_ref, head_ref, len_hbm, q_hbm, w_hbm, q4_ref, bound_ref, w_ref, len_ref, sems):
    head = head_ref[0]
    copies = [pltpu.make_async_copy(len_hbm, len_ref, sems.at[0])]
    sources = (head, source_of(head, 0, True), source_of(head, -2, False), source_of(head, 2, False))
    sources += (source_of(head, -2, True), source_of(head, 2, True), source_of(head, 4, False), source_of(head, 4, True))
    for i, source in enumerate(sources):
        cols = pl.ds(pl.multiple_of(source * BLOCK, BLOCK), BLOCK)
        copies.append(pltpu.make_async_copy(w_hbm.at[:, cols], w_ref.at[:, pl.ds(i * BLOCK, BLOCK)], sems.at[1 + HEADS + i]))
    for h in range(HEADS):
        across, along = pl.ds(h * ROWS, ROWS), pl.ds(h * D, D)
        copies.append(pltpu.make_async_copy(q_hbm.at[:, along], q4_ref.at[across, :], sems.at[1 + h]))
    for copy in copies:
        copy.start()
    lane = lax.broadcasted_iota(jnp.int32, (1, LANES), 1)
    pos = lane + place_ref[0] * ROWS
    for h in range(1, HEADS):
        pos = pos - jnp.where(lane >= h * ROWS, ROWS, 0)
    start = jnp.zeros((1, LANES), jnp.int32)
    end = jnp.int32(0)
    copies[0].wait()
    for d in range(len_ref.shape[0]):
        end = end + len_ref[d]
        start = jnp.where(end <= pos, end, start)
    bound_ref[0:1, :] = pos.astype(jnp.float32)
    bound_ref[1:2, :] = start.astype(jnp.float32)
    for copy in copies[1:]:
        copy.wait()


def stage_kernel(piece_ref, after, out_ref):
    out_ref[...] = piece_ref[...]


def gate_kernel(*refs):
    refs[-1][...] = jnp.zeros(refs[-1].shape, refs[-1].dtype)


def pick_kernel(place_ref, z2_ref, z1_ref, z0_ref, *refs):
    out_ref = refs[-1]
    upper = lax.rem(lax.div(place_ref[0], 2), 2) == 1

    @pl.when(upper)
    def _():
        out_ref[:ROWS, :] = z2_ref[...]
        out_ref[ROWS:, :] = z1_ref[...]

    @pl.when(jnp.logical_not(upper))
    def _():
        out_ref[:ROWS, :] = z1_ref[...]
        out_ref[ROWS:, :] = z0_ref[...]


def join_kernel(z2_ref, z1_ref, z0_ref, side_ref, *refs):
    out_ref = refs[-1]
    parts = (z2_ref[...], side_ref[:ROWS, :], z1_ref[...], side_ref[ROWS:, :], z0_ref[...])
    for m, part in enumerate(parts):
        out_ref[m * ROWS : (m + 1) * ROWS, :] = part


def absorb(block, queries, row, base, start, state, pos=None):
    s = dot(block[:, :D], queries, 1, 1) * (SCALE * LOG2E)
    visible = row >= start - base * ROWS
    if pos is not None:
        visible = visible & (row <= pos - base * ROWS)
    s = jnp.where(visible, s, NEG)
    peak = jnp.maximum(jnp.max(s, axis=0, keepdims=True), FLOOR)
    prob = jnp.exp2(s - peak).astype(jnp.bfloat16)
    mass = jnp.sum(prob.astype(jnp.float32), axis=0, keepdims=True)
    out = dot(block[:, D:], prob, 0, 0)
    if state is None:
        return prob, peak, (out, mass, peak)
    old_out, old_mass, old_peak = state
    top = jnp.maximum(old_peak, peak)
    before, now = jnp.exp2(old_peak - top), jnp.exp2(peak - top)
    return prob, peak, (old_out * before + out * now, old_mass * before + mass * now, top)


def read_state(ref):
    return ref[:D, :], ref[MASS : MASS + 1, :], ref[TOP : TOP + 1, :]


def write_state(ref, state):
    ref[:D, :], ref[MASS : MASS + 1, :], ref[TOP : TOP + 1, :] = state


def put_row(ref, at, value):
    ref[at : at + 1, :] = value


def near_kernel(place_ref, z2_ref, z1_ref, z0_ref, q4_ref, bound_ref, *refs):
    p_ref, st_ref = refs[-2:]
    me = place_ref[0]
    queries = q4_ref[...]
    row = lax.broadcasted_iota(jnp.int32, (ROWS, LANES), 0)
    pos, start = bound_ref[0:1, :].astype(jnp.int32), bound_ref[1:2, :].astype(jnp.int32)
    state = None
    for i, ref in ((2, z0_ref), (1, z1_ref), (0, z2_ref)):
        at = pos if i == 2 else None
        prob, peak, state = absorb(ref[...], queries, row, me - PLANE * (2 - i), start, state, at)
        p_ref[i * ROWS : (i + 1) * ROWS, :] = prob
        put_row(st_ref, PEAK + 2 * i, peak)
    write_state(st_ref, state)
    put_row(st_ref, START, bound_ref[1:2, :])


def project_kernel(*refs):
    pieces, (w_ref, after, acc_ref) = refs[:7], refs[7:]
    acc = None
    for i, piece in enumerate(pieces):
        part = dot(piece[...], w_ref[:, i * BLOCK : (i + 1) * BLOCK], 1, 1)
        acc = part if acc is None else acc + part
    acc_ref[...] = acc


def last_projection(piece_ref, w_ref, acc_ref, after, g4_ref, gt_ref):
    acc = (acc_ref[...] + dot(piece_ref[...], w_ref[:, 7 * BLOCK :], 1, 1)).astype(jnp.bfloat16)
    for h in range(HEADS):
        g4_ref[h * ROWS : (h + 1) * ROWS, :] = acc[:, h * D : (h + 1) * D]
    gt_ref[...] = jnp.transpose(g4_ref[...].astype(jnp.float32))


def rows(i):
    return pl.ds(pl.multiple_of(i * ROWS, ROWS), ROWS)


def source_of(head, by, flip):
    at = lax.rem(head + by + 8, 8)
    return at + 1 - 2 * lax.rem(at, 2) if flip else at


def middle_kernel(place_ref, own_ref, q4_ref, st_in_ref, after, p_ref, st_ref):
    queries = q4_ref[...]
    row = lax.broadcasted_iota(jnp.int32, (ROWS, LANES), 0)
    start = st_in_ref[START : START + 1, :].astype(jnp.int32)
    state = read_state(st_in_ref)
    st_ref[PEAK:, :] = st_in_ref[PEAK:, :]
    for i in range(2):
        slot = 2 * i + 1
        block = own_ref[slot * ROWS : (slot + 1) * ROWS, :]
        prob, peak, state = absorb(block, queries, row, place_ref[0] + 2 * (slot - REACH), start, state)
        p_ref[i * ROWS : (i + 1) * ROWS, :] = prob
        put_row(st_ref, PEAK + slot, peak)
    write_state(st_ref, state)
    put_row(st_ref, START, st_in_ref[START : START + 1, :])


def across_kernel(place_ref, par_ref, q4_ref, gt_ref, st_in_ref, p_ref, st_ref):
    me = place_ref[0]
    core = lax.rem(me, 2)
    chip = me - core
    queries = q4_ref[...]
    row = lax.broadcasted_iota(jnp.int32, (ROWS, LANES), 0)
    start = st_in_ref[START : START + 1, :].astype(jnp.int32)
    state = read_state(st_in_ref)
    peaks = [st_in_ref[PEAK + m : PEAK + m + 1, :] for m in range(SLOTS)]
    for i in range(REACH):
        slot = i + core
        prob, peak, state = absorb(par_ref[rows(slot), :], queries, row, chip + 1 - core + 2 * (slot - REACH), start, state)
        p_ref[i * ROWS : (i + 1) * ROWS, :] = prob
        peaks.append(peak)
    out, mass, top = state
    put_row(st_ref, DOT, jnp.sum(gt_ref[...] * out, axis=0, keepdims=True) / mass)
    log_total = top + jnp.log2(mass)
    for i, peak in enumerate(peaks):
        put_row(st_ref, PEAK + i, jnp.exp2(peak - log_total))


def back_block(block, prob, share, g4, q4, rd):
    prob = prob.astype(jnp.float32) * share
    dprob = dot(block[:, D:], g4, 1, 1)
    ds = (prob * (dprob - rd)).astype(jnp.bfloat16)
    dv = dot(prob.astype(jnp.bfloat16), g4, 1, 0)
    dk = dot(ds, q4, 1, 0) * SCALE
    dq = dot(block[:, :D], ds, 0, 0)
    return dk, dv, dq


def put(out_ref, slot, dk, dv):
    at = pl.ds(pl.multiple_of(slot * ROWS, ROWS), ROWS)
    out_ref[at, :D] = dk.astype(out_ref.dtype)
    out_ref[at, D:] = dv.astype(out_ref.dtype)


def cross_step(slot, core, par_ref, p_ref, st_ref, g4, q4_ref, rd):
    share = st_ref[pl.ds(PEAK + SLOTS + slot - core, 1), :]
    return back_block(par_ref[rows(slot), :], p_ref[rows(slot - core), :], share, g4, q4_ref[...], rd)


def cross_far(place_ref, q4_ref, par_ref, p_ref, g_ref, st_in_ref, out_ref, st_ref):
    core = lax.rem(place_ref[0], 2)
    g4 = g_ref[...]
    rd = st_in_ref[DOT : DOT + 1, :]
    st_ref[DOT : DOT + 1, :] = rd
    st_ref[PEAK:, :] = st_in_ref[PEAK:, :]
    dk, dv, dq = cross_step(1, core, par_ref, p_ref, st_ref, g4, q4_ref, rd)
    put(out_ref, 1, dk, dv)
    st_ref[:D, :] = dq

    @pl.when(core == 1)
    def _():
        out_ref[:ROWS, :] = jnp.zeros((ROWS, 2 * D), out_ref.dtype)

    @pl.when(core == 0)
    def _():
        dk, dv, dq = cross_step(0, core, par_ref, p_ref, st_ref, g4, q4_ref, rd)
        put(out_ref, 0, dk, dv)
        st_ref[:D, :] += dq


def cross_near(place_ref, q4_ref, par_ref, p_ref, g_ref, st_in_ref, out_ref, st_ref):
    core = lax.rem(place_ref[0], 2)
    g4 = g_ref[...]
    rd = st_in_ref[DOT : DOT + 1, :]
    st_ref[DOT : DOT + 1, :] = rd
    st_ref[PEAK:, :] = st_in_ref[PEAK:, :]
    total = st_in_ref[:D, :]
    for slot in (2, 3):
        dk, dv, dq = cross_step(slot, core, par_ref, p_ref, st_ref, g4, q4_ref, rd)
        put(out_ref, slot - 2, dk, dv)
        total = total + dq
    st_ref[:D, :] = total

    @pl.when(core == 0)
    def _():
        out_ref[2 * ROWS :, :] = jnp.zeros((ROWS, 2 * D), out_ref.dtype)

    @pl.when(core == 1)
    def _():
        dk, dv, dq = cross_step(4, core, par_ref, p_ref, st_ref, g4, q4_ref, rd)
        put(out_ref, 2, dk, dv)
        st_ref[:D, :] += dq


def own_kernel(slots, q4_ref, own_ref, near_ref, side_ref, g_ref, st_in_ref, *refs):
    out_ref, st_ref = refs[-2:]
    g4 = g_ref[...]
    rd = st_in_ref[DOT : DOT + 1, :]
    total = st_in_ref[:D, :]
    for i, slot in enumerate(slots):
        at = slot // 2 * ROWS
        prob = (side_ref if slot % 2 else near_ref)[at : at + ROWS, :]
        share = st_in_ref[PEAK + slot : PEAK + slot + 1, :]
        dk, dv, dq = back_block(own_ref[slot * ROWS : (slot + 1) * ROWS, :], prob, share, g4, q4_ref[...], rd)
        out_ref[i * ROWS : (i + 1) * ROWS, :D] = dk
        out_ref[i * ROWS : (i + 1) * ROWS, D:] = dv
        total = total + dq
    if slots[-1] < REACH:
        st_ref[DOT : DOT + 1, :] = rd
        st_ref[PEAK:, :] = st_in_ref[PEAK:, :]
        st_ref[:D, :] = total
    else:
        dq = jnp.transpose(total) * SCALE
        for h in range(HEADS):
            st_ref[:, h * D : (h + 1) * D] = dq[h * ROWS : (h + 1) * ROWS, :].astype(jnp.bfloat16)


def settle_kernel(own_ref, back_ref, low_ref, high_ref):
    both = own_ref[...] + back_ref[: 2 * ROWS, :].astype(jnp.float32)
    low_ref[...] = both[:ROWS].astype(low_ref.dtype)
    high_ref[...] = both[ROWS:].astype(jnp.bfloat16)


def relay_far(keep_ref, side_ref, out_ref):
    out_ref[...] = (keep_ref[...] + side_ref[...].astype(jnp.float32)).astype(jnp.bfloat16)


def gather_kernel(own_ref, back_ref, side_ref, two_ref, four_ref, out_ref):
    total = own_ref[...] + back_ref[2 * ROWS :, :].astype(jnp.float32) + side_ref[...].astype(jnp.float32)
    out_ref[...] = total + two_ref[...].astype(jnp.float32) + four_ref[...].astype(jnp.float32)


def finish_kernel(sum_ref, eight_ref, k_ref, v_ref):
    total = (sum_ref[...] + eight_ref[...].astype(jnp.float32)).astype(jnp.bfloat16)
    k_ref[...] = total[:, :D]
    v_ref[...] = total[:, D:]


def vmem(n):
    return [pl.BlockSpec(memory_space=pltpu.VMEM)] * n


def smem(n):
    return [pl.BlockSpec(memory_space=pltpu.SMEM)] * n


def hbm(n):
    return [pl.BlockSpec(memory_space=pltpu.HBM)] * n


def token(n):
    return [pl.BlockSpec(memory_space=pl.ANY)] * n


def moved(x, axis, to):
    return lax.ppermute(x, axis, [(i, to(i)) for i in range(lax.axis_size(axis))])


def turned(x, axis, by):
    count = lax.axis_size(axis)
    return moved(x, axis, lambda i: (i + by) % count)


def shape(rows, cols, dtype):
    return jax.ShapeDtypeStruct((rows, cols), dtype)


def call(name, kernel, outs, ins, args, scratch=(), flops=1):
    one = not isinstance(outs, tuple)
    return pl.pallas_call(
        kernel,
        out_shape=outs,
        in_specs=ins,
        out_specs=vmem(1)[0] if one else tuple(vmem(len(outs))),
        scratch_shapes=list(scratch),
        compiler_params=pltpu.CompilerParams(vmem_limit_bytes=8 * MIB),
        cost_estimate=pl.CostEstimate(flops=flops, bytes_accessed=1, transcendentals=0),
        name=name,
    )(*args)


def local(queries, keys, values, grad_out, out_weight, lengths):
    bf16, f32 = jnp.bfloat16, jnp.float32
    place = lax.axis_index("ctx").astype(jnp.int32).reshape(1)
    head = lax.axis_index("head").astype(jnp.int32).reshape(1)
    dma = pltpu.SemaphoreType.DMA
    pinned = functools.partial(pltpu.with_memory_space_constraint, memory_space=pltpu.HBM)
    state = shape(STATE, LANES, f32)

    first = moved(grad_out, "head", lambda i: i ^ 1)
    right = turned(grad_out, "head", 2)
    left = turned(grad_out, "head", -2)
    kv = jnp.pad(keys, ((0, 0), (0, D))) + jnp.pad(values, ((0, 0), (D, 0)))
    z2 = turned(kv, "ctx", 2 * PLANE)
    z1 = turned(kv, "ctx", PLANE)
    q4, bound, weight = call(
        "load",
        load_kernel,
        (shape(LANES, D, bf16), shape(8, LANES, f32), shape(HEADS * D, 8 * BLOCK, bf16)),
        smem(2) + hbm(3),
        (place, head, pinned(lengths), pinned(queries), pinned(out_weight)),
        [pltpu.SMEM((lengths.shape[0],), jnp.int32), dma((9 + HEADS,))],
    )
    other = call("stage", stage_kernel, shape(ROWS, BLOCK, bf16), vmem(1) + token(1), (first, q4))
    other_right = turned(other, "head", 2)
    other_left = turned(other, "head", -2)
    far = turned(right, "head", 2)
    other_far = turned(other_left, "head", -2)

    gate = call("gate", gate_kernel, shape(8, D, f32), token(4), (other, right, left, q4))
    picked = call(
        "pick_side", pick_kernel, shape(2 * ROWS, 2 * D, bf16), smem(1) + vmem(3) + token(1), (place, z2, z1, kv, gate)
    )
    side = moved(picked, "ctx", lambda i: i ^ 2)
    p_near, st = call(
        "near",
        near_kernel,
        (shape(3 * ROWS, LANES, bf16), state),
        smem(1) + vmem(5) + token(3),
        (place, z2, z1, kv, q4, bound, picked, other_right, other_left),
    )
    own = call("join_slots", join_kernel, shape(SLOTS * ROWS, 2 * D, bf16), vmem(4) + token(1), (z2, z1, kv, side, st))
    par = moved(own, "ctx", lambda i: i ^ 1)

    early = call(
        "project",
        project_kernel,
        shape(ROWS, HEADS * D, f32),
        vmem(8) + token(1),
        (grad_out, other, right, left, other_right, other_left, far, weight, own),
    )
    p_side, st = call(
        "middle",
        middle_kernel,
        (shape(2 * ROWS, LANES, bf16), state),
        smem(1) + vmem(3) + token(1),
        (place, own, q4, st, early),
    )
    g4, gt = call(
        "last_projection",
        last_projection,
        (shape(LANES, D, bf16), shape(D, LANES, f32)),
        vmem(3) + token(1),
        (other_far, weight, early, st),
        flops=COSTLY,
    )
    p_par, st = call(
        "across", across_kernel, (shape(REACH * ROWS, LANES, bf16), state), smem(1) + vmem(4), (place, par, q4, gt, st)
    )

    far_cross, st = call(
        "cross_far", cross_far, (shape(2 * ROWS, 2 * D, bf16), state), smem(1) + vmem(5), (place, q4, par, p_par, g4, st)
    )
    far_back = moved(far_cross, "ctx", lambda i: i ^ 1)
    near_cross, st = call(
        "cross_near", cross_near, (shape(3 * ROWS, 2 * D, bf16), state), smem(1) + vmem(5), (place, q4, par, p_par, g4, st), flops=FL
    )
    near_back = moved(near_cross, "ctx", lambda i: i ^ 1)
    far_own, st = call(
        "own_far",
        functools.partial(own_kernel, (0, 1)),
        (shape(2 * ROWS, 2 * D, f32), state),
        vmem(6),
        (q4, own, p_near, p_side, g4, st),
        flops=FL,
    )
    far_keep, far_side = call(
        "settle_far", settle_kernel, (shape(ROWS, 2 * D, f32), shape(ROWS, 2 * D, bf16)), vmem(2), (far_own, far_back)
    )
    count = lax.axis_size("ctx")
    lower = [i for i in range(count) if i // 2 % 2 == 0]
    upper = [i for i in range(count) if i // 2 % 2 == 1]
    far_up = lax.ppermute(far_side, "ctx", [(i, i + 2) for i in lower])
    far_down = lax.ppermute(far_side, "ctx", [(i, (i - 6) % count) for i in upper])
    near_own, st = call(
        "own_near",
        functools.partial(own_kernel, (2, 3)),
        (shape(2 * ROWS, 2 * D, f32), state),
        vmem(6) + token(1),
        (q4, own, p_near, p_side, g4, st, far_keep),
        flops=FL,
    )
    by_four, by_two = call(
        "settle_near", settle_kernel, (shape(ROWS, 2 * D, bf16), shape(ROWS, 2 * D, bf16)), vmem(2), (near_own, near_back)
    )
    by_four = turned(by_four, "ctx", -4)
    by_two = turned(by_two, "ctx", -2)
    to_eight = call("relay_far", relay_far, shape(ROWS, 2 * D, bf16), vmem(2), (far_keep, far_up))
    by_eight = turned(to_eight, "ctx", -8)
    last_own, grad_queries = call(
        "own_last",
        functools.partial(own_kernel, (4,)),
        (shape(ROWS, 2 * D, f32), shape(ROWS, HEADS * D, bf16)),
        vmem(6) + token(1),
        (q4, own, p_near, p_side, g4, st, to_eight),
    )
    partial_sum = call(
        "gather_near",
        gather_kernel,
        shape(ROWS, 2 * D, f32),
        vmem(5),
        (last_own, near_back, far_down, by_two, by_four),
        flops=COSTLY,
    )
    grad_keys, grad_values = call(
        "finish", finish_kernel, (shape(ROWS, D, bf16), shape(ROWS, D, bf16)), vmem(2), (partial_sum, by_eight)
    )
    return grad_queries, grad_keys, grad_values


def solution(mesh):
    return jax.shard_map(
        local,
        mesh=mesh,
        in_specs=(
            P("ctx", "head"),
            P("ctx", "head"),
            P("ctx", "head"),
            P("ctx", "head"),
            P("head", None),
            P(),
        ),
        out_specs=(P("ctx", "head"), P("ctx", "head"), P("ctx", "head")),
        check_vma=False,
    )
```

```python
import functools

import jax
import jax.numpy as jnp
from jax import lax
from jax.experimental import pallas as pl
from jax.experimental.pallas import tpu as pltpu
from jax.sharding import PartitionSpec as P

D = 128
HEADS = 4
ROWS = 192
LANES = HEADS * ROWS
REACH = 4
SLOTS = REACH + 1
PLANE = 4
BLOCK = 512
MASS, TOP, START, DOT = D, D + 1, D + 2, D + 3
PEAK = D + 8
STATE = PEAK + 16
NEG = -1e30
FLOOR = -1e20
SCALE = D**-0.5
LOG2E = 1.4426950408889634
MIB = 1 << 20
COSTLY = 4 * 10**9


def dot(a, b, ca, cb):
    return lax.dot_general(a, b, (((ca,), (cb,)), ((), ())), preferred_element_type=jnp.float32)


def stack_heads(src, dst):
    for h in range(HEADS):
        dst[h * ROWS : (h + 1) * ROWS, :] = src[:, h * D : (h + 1) * D]


def load_kernel(place_ref, head_ref, len_hbm, q_hbm, w_hbm, q4_ref, bound_ref, w_ref, len_ref, sems):
    head = head_ref[0]
    copies = [pltpu.make_async_copy(len_hbm, len_ref, sems.at[0])]
    sources = (head, source_of(head, 0, True), source_of(head, -2, False), source_of(head, 2, False))
    sources += (source_of(head, -2, True), source_of(head, 2, True), source_of(head, 4, False), source_of(head, 4, True))
    for i, source in enumerate(sources):
        cols = pl.ds(pl.multiple_of(source * BLOCK, BLOCK), BLOCK)
        copies.append(pltpu.make_async_copy(w_hbm.at[:, cols], w_ref.at[:, pl.ds(i * BLOCK, BLOCK)], sems.at[1 + HEADS + i]))
    for h in range(HEADS):
        across, along = pl.ds(h * ROWS, ROWS), pl.ds(h * D, D)
        copies.append(pltpu.make_async_copy(q_hbm.at[:, along], q4_ref.at[across, :], sems.at[1 + h]))
    for copy in copies:
        copy.start()
    lane = lax.broadcasted_iota(jnp.int32, (1, LANES), 1)
    pos = lane + place_ref[0] * ROWS
    for h in range(1, HEADS):
        pos = pos - jnp.where(lane >= h * ROWS, ROWS, 0)
    start = jnp.zeros((1, LANES), jnp.int32)
    end = jnp.int32(0)
    copies[0].wait()
    for d in range(len_ref.shape[0]):
        end = end + len_ref[d]
        start = jnp.where(end <= pos, end, start)
    bound_ref[0:1, :] = pos.astype(jnp.float32)
    bound_ref[1:2, :] = start.astype(jnp.float32)
    for copy in copies[1:]:
        copy.wait()


def stage_kernel(piece_ref, after, out_ref):
    out_ref[...] = piece_ref[...]


def gate_kernel(*refs):
    refs[-1][...] = jnp.zeros(refs[-1].shape, refs[-1].dtype)


def pick_kernel(place_ref, z2_ref, z1_ref, z0_ref, *refs):
    out_ref = refs[-1]
    upper = lax.rem(lax.div(place_ref[0], 2), 2) == 1

    @pl.when(upper)
    def _():
        out_ref[:ROWS, :] = z2_ref[...]
        out_ref[ROWS:, :] = z1_ref[...]

    @pl.when(jnp.logical_not(upper))
    def _():
        out_ref[:ROWS, :] = z1_ref[...]
        out_ref[ROWS:, :] = z0_ref[...]


def join_kernel(z2_ref, z1_ref, z0_ref, side_ref, *refs):
    out_ref = refs[-1]
    parts = (z2_ref[...], side_ref[:ROWS, :], z1_ref[...], side_ref[ROWS:, :], z0_ref[...])
    for m, part in enumerate(parts):
        out_ref[m * ROWS : (m + 1) * ROWS, :] = part


def absorb(block, queries, row, base, start, state, pos=None):
    s = dot(block[:, :D], queries, 1, 1) * (SCALE * LOG2E)
    visible = row >= start - base * ROWS
    if pos is not None:
        visible = visible & (row <= pos - base * ROWS)
    s = jnp.where(visible, s, NEG)
    peak = jnp.maximum(jnp.max(s, axis=0, keepdims=True), FLOOR)
    prob = jnp.exp2(s - peak).astype(jnp.bfloat16)
    mass = jnp.sum(prob.astype(jnp.float32), axis=0, keepdims=True)
    out = dot(block[:, D:], prob, 0, 0)
    if state is None:
        return prob, peak, (out, mass, peak)
    old_out, old_mass, old_peak = state
    top = jnp.maximum(old_peak, peak)
    before, now = jnp.exp2(old_peak - top), jnp.exp2(peak - top)
    return prob, peak, (old_out * before + out * now, old_mass * before + mass * now, top)


def read_state(ref):
    return ref[:D, :], ref[MASS : MASS + 1, :], ref[TOP : TOP + 1, :]


def write_state(ref, state):
    ref[:D, :], ref[MASS : MASS + 1, :], ref[TOP : TOP + 1, :] = state


def put_row(ref, at, value):
    ref[at : at + 1, :] = value


def near_kernel(place_ref, z2_ref, z1_ref, z0_ref, q4_ref, bound_ref, *refs):
    p_ref, st_ref = refs[-2:]
    me = place_ref[0]
    queries = q4_ref[...]
    row = lax.broadcasted_iota(jnp.int32, (ROWS, LANES), 0)
    pos, start = bound_ref[0:1, :].astype(jnp.int32), bound_ref[1:2, :].astype(jnp.int32)
    state = None
    for i, ref in ((2, z0_ref), (1, z1_ref), (0, z2_ref)):
        at = pos if i == 2 else None
        prob, peak, state = absorb(ref[...], queries, row, me - PLANE * (2 - i), start, state, at)
        p_ref[i * ROWS : (i + 1) * ROWS, :] = prob
        put_row(st_ref, PEAK + 2 * i, peak)
    write_state(st_ref, state)
    put_row(st_ref, START, bound_ref[1:2, :])


def project_kernel(*refs):
    pieces, (w_ref, after, acc_ref) = refs[:7], refs[7:]
    acc = None
    for i, piece in enumerate(pieces):
        part = dot(piece[...], w_ref[:, i * BLOCK : (i + 1) * BLOCK], 1, 1)
        acc = part if acc is None else acc + part
    acc_ref[...] = acc


def last_projection(piece_ref, w_ref, acc_ref, after, g4_ref, gt_ref):
    acc = (acc_ref[...] + dot(piece_ref[...], w_ref[:, 7 * BLOCK :], 1, 1)).astype(jnp.bfloat16)
    for h in range(HEADS):
        g4_ref[h * ROWS : (h + 1) * ROWS, :] = acc[:, h * D : (h + 1) * D]
    gt_ref[...] = jnp.transpose(g4_ref[...].astype(jnp.float32))


def rows(i):
    return pl.ds(pl.multiple_of(i * ROWS, ROWS), ROWS)


def source_of(head, by, flip):
    at = lax.rem(head + by + 8, 8)
    return at + 1 - 2 * lax.rem(at, 2) if flip else at


def middle_kernel(place_ref, own_ref, q4_ref, st_in_ref, after, p_ref, st_ref):
    queries = q4_ref[...]
    row = lax.broadcasted_iota(jnp.int32, (ROWS, LANES), 0)
    start = st_in_ref[START : START + 1, :].astype(jnp.int32)
    state = read_state(st_in_ref)
    st_ref[PEAK:, :] = st_in_ref[PEAK:, :]
    for i in range(2):
        slot = 2 * i + 1
        block = own_ref[slot * ROWS : (slot + 1) * ROWS, :]
        prob, peak, state = absorb(block, queries, row, place_ref[0] + 2 * (slot - REACH), start, state)
        p_ref[i * ROWS : (i + 1) * ROWS, :] = prob
        put_row(st_ref, PEAK + slot, peak)
    write_state(st_ref, state)
    put_row(st_ref, START, st_in_ref[START : START + 1, :])


def across_kernel(place_ref, par_ref, q4_ref, gt_ref, st_in_ref, p_ref, st_ref):
    me = place_ref[0]
    core = lax.rem(me, 2)
    chip = me - core
    queries = q4_ref[...]
    row = lax.broadcasted_iota(jnp.int32, (ROWS, LANES), 0)
    start = st_in_ref[START : START + 1, :].astype(jnp.int32)
    state = read_state(st_in_ref)
    peaks = [st_in_ref[PEAK + m : PEAK + m + 1, :] for m in range(SLOTS)]
    for i in range(REACH):
        slot = i + core
        prob, peak, state = absorb(par_ref[rows(slot), :], queries, row, chip + 1 - core + 2 * (slot - REACH), start, state)
        p_ref[i * ROWS : (i + 1) * ROWS, :] = prob
        peaks.append(peak)
    out, mass, top = state
    put_row(st_ref, DOT, jnp.sum(gt_ref[...] * out, axis=0, keepdims=True) / mass)
    log_total = top + jnp.log2(mass)
    for i, peak in enumerate(peaks):
        put_row(st_ref, PEAK + i, jnp.exp2(peak - log_total))


def back_block(block, prob, share, g4, q4, rd):
    prob = prob.astype(jnp.float32) * share
    dprob = dot(block[:, D:], g4, 1, 1)
    ds = (prob * (dprob - rd)).astype(jnp.bfloat16)
    dv = dot(prob.astype(jnp.bfloat16), g4, 1, 0)
    dk = dot(ds, q4, 1, 0) * SCALE
    dq = dot(block[:, :D], ds, 0, 0)
    return dk, dv, dq


def cross_kernel(place_ref, q4_ref, par_ref, p_ref, g_ref, st_in_ref, out_ref, st_ref):
    core = lax.rem(place_ref[0], 2)
    g4 = g_ref[...]
    rd = st_in_ref[DOT : DOT + 1, :]
    st_ref[DOT : DOT + 1, :] = rd
    st_ref[PEAK:, :] = st_in_ref[PEAK:, :]
    total = None
    for i in range(REACH):
        share = st_in_ref[PEAK + SLOTS + i : PEAK + SLOTS + i + 1, :]
        prob = p_ref[i * ROWS : (i + 1) * ROWS, :]
        dk, dv, dq = back_block(par_ref[rows(i + core), :], prob, share, g4, q4_ref[...], rd)
        out_ref[i * ROWS : (i + 1) * ROWS, :D] = dk.astype(out_ref.dtype)
        out_ref[i * ROWS : (i + 1) * ROWS, D:] = dv.astype(out_ref.dtype)
        total = dq if total is None else total + dq
    st_ref[:D, :] = total


def returned(back_ref, place_ref, slot):
    odd = lax.rem(place_ref[0], 2).astype(jnp.float32)
    value = None
    for i, share in ((slot, odd), (slot - 1, 1 - odd)):
        if 0 <= i < REACH:
            part = back_ref[i * ROWS : (i + 1) * ROWS, :].astype(jnp.float32) * share
            value = part if value is None else value + part
    return value


def own_kernel(slots, q4_ref, own_ref, near_ref, side_ref, g_ref, st_in_ref, *refs):
    out_ref, st_ref = refs[-2:]
    g4 = g_ref[...]
    rd = st_in_ref[DOT : DOT + 1, :]
    total = st_in_ref[:D, :]
    for i, slot in enumerate(slots):
        at = slot // 2 * ROWS
        prob = (side_ref if slot % 2 else near_ref)[at : at + ROWS, :]
        share = st_in_ref[PEAK + slot : PEAK + slot + 1, :]
        dk, dv, dq = back_block(own_ref[slot * ROWS : (slot + 1) * ROWS, :], prob, share, g4, q4_ref[...], rd)
        out_ref[i * ROWS : (i + 1) * ROWS, :D] = dk
        out_ref[i * ROWS : (i + 1) * ROWS, D:] = dv
        total = total + dq
    if slots[-1] < REACH:
        st_ref[DOT : DOT + 1, :] = rd
        st_ref[PEAK:, :] = st_in_ref[PEAK:, :]
        st_ref[:D, :] = total
    else:
        dq = jnp.transpose(total) * SCALE
        for h in range(HEADS):
            st_ref[:, h * D : (h + 1) * D] = dq[h * ROWS : (h + 1) * ROWS, :].astype(jnp.bfloat16)


def settle_kernel(place_ref, own_ref, back_ref, keep_ref, side_ref):
    for slot in range(REACH):
        both = own_ref[slot * ROWS : (slot + 1) * ROWS, :] + returned(back_ref, place_ref, slot)
        target = pl.ds(slot // 2 * ROWS, ROWS)
        if slot % 2:
            side_ref[target, :] = both.astype(jnp.bfloat16)
        else:
            keep_ref[target, :] = both


def relay_kernel(place_ref, keep_ref, side_ref, after, two_ref, one_ref):
    upper = (lax.rem(lax.div(place_ref[0], 2), 2) == 1).astype(jnp.float32)
    first, second = side_ref[:ROWS, :].astype(jnp.float32), side_ref[ROWS:, :].astype(jnp.float32)
    two_ref[...] = (keep_ref[:ROWS, :] + first * upper).astype(jnp.bfloat16)
    one_ref[...] = (keep_ref[ROWS:, :] + second * upper + first * (1 - upper)).astype(jnp.bfloat16)


def finish_kernel(place_ref, own_ref, back_ref, side_ref, two_ref, one_ref, k_ref, v_ref):
    def wide(x):
        return x.astype(jnp.float32)

    upper = (lax.rem(lax.div(place_ref[0], 2), 2) == 1).astype(jnp.float32)
    total = own_ref[...] + returned(back_ref, place_ref, REACH) + wide(side_ref[ROWS:, :]) * (1 - upper)
    total = (total + wide(one_ref[...]) + wide(two_ref[...])).astype(jnp.bfloat16)
    k_ref[...] = total[:, :D]
    v_ref[...] = total[:, D:]


def vmem(n):
    return [pl.BlockSpec(memory_space=pltpu.VMEM)] * n


def smem(n):
    return [pl.BlockSpec(memory_space=pltpu.SMEM)] * n


def hbm(n):
    return [pl.BlockSpec(memory_space=pltpu.HBM)] * n


def token(n):
    return [pl.BlockSpec(memory_space=pl.ANY)] * n


def moved(x, axis, to):
    return lax.ppermute(x, axis, [(i, to(i)) for i in range(lax.axis_size(axis))])


def turned(x, axis, by):
    count = lax.axis_size(axis)
    return moved(x, axis, lambda i: (i + by) % count)


def shape(rows, cols, dtype):
    return jax.ShapeDtypeStruct((rows, cols), dtype)


def call(name, kernel, outs, ins, args, scratch=(), flops=1):
    one = not isinstance(outs, tuple)
    return pl.pallas_call(
        kernel,
        out_shape=outs,
        in_specs=ins,
        out_specs=vmem(1)[0] if one else tuple(vmem(len(outs))),
        scratch_shapes=list(scratch),
        compiler_params=pltpu.CompilerParams(vmem_limit_bytes=8 * MIB),
        cost_estimate=pl.CostEstimate(flops=flops, bytes_accessed=1, transcendentals=0),
        name=name,
    )(*args)


def local(queries, keys, values, grad_out, out_weight, lengths):
    bf16, f32 = jnp.bfloat16, jnp.float32
    place = lax.axis_index("ctx").astype(jnp.int32).reshape(1)
    head = lax.axis_index("head").astype(jnp.int32).reshape(1)
    dma = pltpu.SemaphoreType.DMA
    pinned = functools.partial(pltpu.with_memory_space_constraint, memory_space=pltpu.HBM)
    state = shape(STATE, LANES, f32)

    first = moved(grad_out, "head", lambda i: i ^ 1)
    right = turned(grad_out, "head", 2)
    left = turned(grad_out, "head", -2)
    kv = jnp.pad(keys, ((0, 0), (0, D))) + jnp.pad(values, ((0, 0), (D, 0)))
    z2 = turned(kv, "ctx", 2 * PLANE)
    z1 = turned(kv, "ctx", PLANE)
    q4, bound, weight = call(
        "load",
        load_kernel,
        (shape(LANES, D, bf16), shape(8, LANES, f32), shape(HEADS * D, 8 * BLOCK, bf16)),
        smem(2) + hbm(3),
        (place, head, pinned(lengths), pinned(queries), pinned(out_weight)),
        [pltpu.SMEM((lengths.shape[0],), jnp.int32), dma((9 + HEADS,))],
    )
    other = call("stage", stage_kernel, shape(ROWS, BLOCK, bf16), vmem(1) + token(1), (first, q4))
    other_right = turned(other, "head", 2)
    other_left = turned(other, "head", -2)
    far = turned(right, "head", 2)
    other_far = turned(other_left, "head", -2)

    gate = call("gate", gate_kernel, shape(8, D, f32), token(4), (other, right, left, q4))
    picked = call(
        "pick_side", pick_kernel, shape(2 * ROWS, 2 * D, bf16), smem(1) + vmem(3) + token(1), (place, z2, z1, kv, gate)
    )
    side = moved(picked, "ctx", lambda i: i ^ 2)
    p_near, st = call(
        "near",
        near_kernel,
        (shape(3 * ROWS, LANES, bf16), state),
        smem(1) + vmem(5) + token(3),
        (place, z2, z1, kv, q4, bound, picked, other_right, other_left),
    )
    own = call("join_slots", join_kernel, shape(SLOTS * ROWS, 2 * D, bf16), vmem(4) + token(1), (z2, z1, kv, side, st))
    par = moved(own, "ctx", lambda i: i ^ 1)

    early = call(
        "project",
        project_kernel,
        shape(ROWS, HEADS * D, f32),
        vmem(8) + token(1),
        (grad_out, other, right, left, other_right, other_left, far, weight, own),
    )
    p_side, st = call(
        "middle",
        middle_kernel,
        (shape(2 * ROWS, LANES, bf16), state),
        smem(1) + vmem(3) + token(1),
        (place, own, q4, st, early),
    )
    g4, gt = call(
        "last_projection",
        last_projection,
        (shape(LANES, D, bf16), shape(D, LANES, f32)),
        vmem(3) + token(1),
        (other_far, weight, early, st),
        flops=COSTLY,
    )
    p_par, st = call(
        "across", across_kernel, (shape(REACH * ROWS, LANES, bf16), state), smem(1) + vmem(4), (place, par, q4, gt, st)
    )

    cross, st = call(
        "cross", cross_kernel, (shape(REACH * ROWS, 2 * D, bf16), state), smem(1) + vmem(5), (place, q4, par, p_par, g4, st)
    )
    back = moved(cross, "ctx", lambda i: i ^ 1)
    mine, st = call(
        "own_earlier",
        functools.partial(own_kernel, (0, 1, 2, 3)),
        (shape(REACH * ROWS, 2 * D, f32), state),
        vmem(6),
        (q4, own, p_near, p_side, g4, st),
    )
    keep, side_out = call(
        "settle", settle_kernel, (shape(2 * ROWS, 2 * D, f32), shape(2 * ROWS, 2 * D, bf16)), smem(1) + vmem(2), (place, mine, back)
    )
    crossed = moved(side_out, "ctx", lambda i: i ^ 2)
    last, grad_queries = call(
        "own_last",
        functools.partial(own_kernel, (4,)),
        (shape(ROWS, 2 * D, f32), shape(ROWS, HEADS * D, bf16)),
        vmem(6) + token(1),
        (q4, own, p_near, p_side, g4, st, keep),
    )
    to_two, to_one = call(
        "relay",
        relay_kernel,
        (shape(ROWS, 2 * D, bf16), shape(ROWS, 2 * D, bf16)),
        smem(1) + vmem(2) + token(1),
        (place, keep, crossed, last),
    )
    got_two = turned(to_two, "ctx", -2 * PLANE)
    got_one = turned(to_one, "ctx", -PLANE)
    grad_keys, grad_values = call(
        "finish",
        finish_kernel,
        (shape(ROWS, D, bf16), shape(ROWS, D, bf16)),
        smem(1) + vmem(5),
        (place, last, back, crossed, got_two, got_one),
    )
    return grad_queries, grad_keys, grad_values


def solution(mesh):
    return jax.shard_map(
        local,
        mesh=mesh,
        in_specs=(
            P("ctx", "head"),
            P("ctx", "head"),
            P("ctx", "head"),
            P("ctx", "head"),
            P("head", None),
            P(),
        ),
        out_specs=(P("ctx", "head"), P("ctx", "head"), P("ctx", "head")),
        check_vma=False,
    )
```

```python
import functools

import jax
import jax.numpy as jnp
from jax import lax
from jax.experimental import pallas as pl
from jax.experimental.pallas import tpu as pltpu
from jax.sharding import PartitionSpec as P

D = 128
HEADS = 4
ROWS = 192
LANES = HEADS * ROWS
REACH = 4
SLOTS = REACH + 1
PLANE = 4
BLOCK = 512
MASS, TOP, START, DOT = D, D + 1, D + 2, D + 3
PEAK = D + 8
STATE = PEAK + 16
NEG = -1e30
FLOOR = -1e20
SCALE = D**-0.5
LOG2E = 1.4426950408889634
MIB = 1 << 20
FL = 4 * 10**9
COSTLY = 4 * 10**9


def dot(a, b, ca, cb):
    return lax.dot_general(a, b, (((ca,), (cb,)), ((), ())), preferred_element_type=jnp.float32)


def stack_heads(src, dst):
    for h in range(HEADS):
        dst[h * ROWS : (h + 1) * ROWS, :] = src[:, h * D : (h + 1) * D]


def load_kernel(place_ref, head_ref, len_hbm, q_hbm, w_hbm, q4_ref, bound_ref, w_ref, len_ref, sems):
    head = head_ref[0]
    copies = [pltpu.make_async_copy(len_hbm, len_ref, sems.at[0])]
    sources = (head, source_of(head, 0, True), source_of(head, -2, False), source_of(head, 2, False))
    sources += (source_of(head, -2, True), source_of(head, 2, True), source_of(head, 4, False), source_of(head, 4, True))
    for i, source in enumerate(sources):
        cols = pl.ds(pl.multiple_of(source * BLOCK, BLOCK), BLOCK)
        copies.append(pltpu.make_async_copy(w_hbm.at[:, cols], w_ref.at[:, pl.ds(i * BLOCK, BLOCK)], sems.at[1 + HEADS + i]))
    for h in range(HEADS):
        across, along = pl.ds(h * ROWS, ROWS), pl.ds(h * D, D)
        copies.append(pltpu.make_async_copy(q_hbm.at[:, along], q4_ref.at[across, :], sems.at[1 + h]))
    for copy in copies:
        copy.start()
    lane = lax.broadcasted_iota(jnp.int32, (1, LANES), 1)
    pos = lane + place_ref[0] * ROWS
    for h in range(1, HEADS):
        pos = pos - jnp.where(lane >= h * ROWS, ROWS, 0)
    start = jnp.zeros((1, LANES), jnp.int32)
    end = jnp.int32(0)
    copies[0].wait()
    for d in range(len_ref.shape[0]):
        end = end + len_ref[d]
        start = jnp.where(end <= pos, end, start)
    bound_ref[0:1, :] = pos.astype(jnp.float32)
    bound_ref[1:2, :] = start.astype(jnp.float32)
    for copy in copies[1:]:
        copy.wait()


def stage_kernel(piece_ref, after, out_ref):
    out_ref[...] = piece_ref[...]


def gate_kernel(*refs):
    refs[-1][...] = jnp.zeros(refs[-1].shape, refs[-1].dtype)


def pick_kernel(place_ref, z2_ref, z1_ref, z0_ref, *refs):
    out_ref = refs[-1]
    upper = lax.rem(lax.div(place_ref[0], 2), 2) == 1

    @pl.when(upper)
    def _():
        out_ref[:ROWS, :] = z2_ref[...]
        out_ref[ROWS:, :] = z1_ref[...]

    @pl.when(jnp.logical_not(upper))
    def _():
        out_ref[:ROWS, :] = z1_ref[...]
        out_ref[ROWS:, :] = z0_ref[...]


def join_kernel(z2_ref, z1_ref, z0_ref, side_ref, *refs):
    out_ref = refs[-1]
    parts = (z2_ref[...], side_ref[:ROWS, :], z1_ref[...], side_ref[ROWS:, :], z0_ref[...])
    for m, part in enumerate(parts):
        out_ref[m * ROWS : (m + 1) * ROWS, :] = part


def absorb(block, queries, row, base, start, state, pos=None):
    s = dot(block[:, :D], queries, 1, 1) * (SCALE * LOG2E)
    visible = row >= start - base * ROWS
    if pos is not None:
        visible = visible & (row <= pos - base * ROWS)
    s = jnp.where(visible, s, NEG)
    peak = jnp.maximum(jnp.max(s, axis=0, keepdims=True), FLOOR)
    prob = jnp.exp2(s - peak).astype(jnp.bfloat16)
    mass = jnp.sum(prob.astype(jnp.float32), axis=0, keepdims=True)
    out = dot(block[:, D:], prob, 0, 0)
    if state is None:
        return prob, peak, (out, mass, peak)
    old_out, old_mass, old_peak = state
    top = jnp.maximum(old_peak, peak)
    before, now = jnp.exp2(old_peak - top), jnp.exp2(peak - top)
    return prob, peak, (old_out * before + out * now, old_mass * before + mass * now, top)


def read_state(ref):
    return ref[:D, :], ref[MASS : MASS + 1, :], ref[TOP : TOP + 1, :]


def write_state(ref, state):
    ref[:D, :], ref[MASS : MASS + 1, :], ref[TOP : TOP + 1, :] = state


def put_row(ref, at, value):
    ref[at : at + 1, :] = value


def near_kernel(place_ref, z2_ref, z1_ref, z0_ref, q4_ref, bound_ref, *refs):
    p_ref, st_ref = refs[-2:]
    me = place_ref[0]
    queries = q4_ref[...]
    row = lax.broadcasted_iota(jnp.int32, (ROWS, LANES), 0)
    pos, start = bound_ref[0:1, :].astype(jnp.int32), bound_ref[1:2, :].astype(jnp.int32)
    state = None
    for i, ref in ((2, z0_ref), (1, z1_ref), (0, z2_ref)):
        at = pos if i == 2 else None
        prob, peak, state = absorb(ref[...], queries, row, me - PLANE * (2 - i), start, state, at)
        p_ref[i * ROWS : (i + 1) * ROWS, :] = prob
        put_row(st_ref, PEAK + 2 * i, peak)
    write_state(st_ref, state)
    put_row(st_ref, START, bound_ref[1:2, :])


def project_kernel(*refs):
    pieces, (w_ref, after, acc_ref) = refs[:7], refs[7:]
    acc = None
    for i, piece in enumerate(pieces):
        part = dot(piece[...], w_ref[:, i * BLOCK : (i + 1) * BLOCK], 1, 1)
        acc = part if acc is None else acc + part
    acc_ref[...] = acc


def last_projection(piece_ref, w_ref, acc_ref, g4_ref, gt_ref):
    acc = (acc_ref[...] + dot(piece_ref[...], w_ref[:, 7 * BLOCK :], 1, 1)).astype(jnp.bfloat16)
    for h in range(HEADS):
        g4_ref[h * ROWS : (h + 1) * ROWS, :] = acc[:, h * D : (h + 1) * D]
    gt_ref[...] = jnp.transpose(g4_ref[...].astype(jnp.float32))


def rows(i):
    return pl.ds(pl.multiple_of(i * ROWS, ROWS), ROWS)


def source_of(head, by, flip):
    at = lax.rem(head + by + 8, 8)
    return at + 1 - 2 * lax.rem(at, 2) if flip else at


def middle_kernel(place_ref, own_ref, q4_ref, st_in_ref, p_ref, st_ref):
    queries = q4_ref[...]
    row = lax.broadcasted_iota(jnp.int32, (ROWS, LANES), 0)
    start = st_in_ref[START : START + 1, :].astype(jnp.int32)
    state = read_state(st_in_ref)
    st_ref[PEAK:, :] = st_in_ref[PEAK:, :]
    for i in range(2):
        slot = 2 * i + 1
        block = own_ref[slot * ROWS : (slot + 1) * ROWS, :]
        prob, peak, state = absorb(block, queries, row, place_ref[0] + 2 * (slot - REACH), start, state)
        p_ref[i * ROWS : (i + 1) * ROWS, :] = prob
        put_row(st_ref, PEAK + slot, peak)
    write_state(st_ref, state)
    put_row(st_ref, START, st_in_ref[START : START + 1, :])


def across_kernel(place_ref, par_ref, q4_ref, gt_ref, st_in_ref, p_ref, st_ref):
    me = place_ref[0]
    core = lax.rem(me, 2)
    chip = me - core
    queries = q4_ref[...]
    row = lax.broadcasted_iota(jnp.int32, (ROWS, LANES), 0)
    start = st_in_ref[START : START + 1, :].astype(jnp.int32)
    state = read_state(st_in_ref)
    peaks = [st_in_ref[PEAK + m : PEAK + m + 1, :] for m in range(SLOTS)]
    for i in range(REACH):
        slot = i + core
        prob, peak, state = absorb(par_ref[rows(slot), :], queries, row, chip + 1 - core + 2 * (slot - REACH), start, state)
        p_ref[i * ROWS : (i + 1) * ROWS, :] = prob
        peaks.append(peak)
    out, mass, top = state
    put_row(st_ref, DOT, jnp.sum(gt_ref[...] * out, axis=0, keepdims=True) / mass)
    log_total = top + jnp.log2(mass)
    for i, peak in enumerate(peaks):
        put_row(st_ref, PEAK + i, jnp.exp2(peak - log_total))


def back_block(block, prob, share, g4, q4, rd):
    prob = prob.astype(jnp.float32) * share
    dprob = dot(block[:, D:], g4, 1, 1)
    ds = (prob * (dprob - rd)).astype(jnp.bfloat16)
    dv = dot(prob.astype(jnp.bfloat16), g4, 1, 0)
    dk = dot(ds, q4, 1, 0) * SCALE
    dq = dot(block[:, :D], ds, 0, 0)
    return dk, dv, dq


def put(out_ref, slot, dk, dv):
    at = pl.ds(pl.multiple_of(slot * ROWS, ROWS), ROWS)
    out_ref[at, :D] = dk.astype(out_ref.dtype)
    out_ref[at, D:] = dv.astype(out_ref.dtype)


def cross_step(slot, core, par_ref, p_ref, st_ref, g4, q4_ref, rd):
    share = st_ref[pl.ds(PEAK + SLOTS + slot - core, 1), :]
    return back_block(par_ref[rows(slot), :], p_ref[rows(slot - core), :], share, g4, q4_ref[...], rd)


def cross_far(place_ref, q4_ref, par_ref, p_ref, g_ref, st_in_ref, out_ref, st_ref):
    core = lax.rem(place_ref[0], 2)
    g4 = g_ref[...]
    rd = st_in_ref[DOT : DOT + 1, :]
    st_ref[DOT : DOT + 1, :] = rd
    st_ref[PEAK:, :] = st_in_ref[PEAK:, :]
    dk, dv, dq = cross_step(1, core, par_ref, p_ref, st_ref, g4, q4_ref, rd)
    put(out_ref, 1, dk, dv)
    st_ref[:D, :] = dq

    @pl.when(core == 1)
    def _():
        out_ref[:ROWS, :] = jnp.zeros((ROWS, 2 * D), out_ref.dtype)

    @pl.when(core == 0)
    def _():
        dk, dv, dq = cross_step(0, core, par_ref, p_ref, st_ref, g4, q4_ref, rd)
        put(out_ref, 0, dk, dv)
        st_ref[:D, :] += dq


def cross_near(place_ref, q4_ref, par_ref, p_ref, g_ref, st_in_ref, out_ref, st_ref):
    core = lax.rem(place_ref[0], 2)
    g4 = g_ref[...]
    rd = st_in_ref[DOT : DOT + 1, :]
    st_ref[DOT : DOT + 1, :] = rd
    st_ref[PEAK:, :] = st_in_ref[PEAK:, :]
    total = st_in_ref[:D, :]
    for slot in (2, 3):
        dk, dv, dq = cross_step(slot, core, par_ref, p_ref, st_ref, g4, q4_ref, rd)
        put(out_ref, slot - 2, dk, dv)
        total = total + dq
    st_ref[:D, :] = total

    @pl.when(core == 0)
    def _():
        out_ref[2 * ROWS :, :] = jnp.zeros((ROWS, 2 * D), out_ref.dtype)

    @pl.when(core == 1)
    def _():
        dk, dv, dq = cross_step(4, core, par_ref, p_ref, st_ref, g4, q4_ref, rd)
        put(out_ref, 2, dk, dv)
        st_ref[:D, :] += dq


def own_kernel(slots, q4_ref, own_ref, near_ref, side_ref, g_ref, st_in_ref, *refs):
    out_ref, st_ref = refs[-2:]
    g4 = g_ref[...]
    rd = st_in_ref[DOT : DOT + 1, :]
    total = st_in_ref[:D, :]
    for i, slot in enumerate(slots):
        at = slot // 2 * ROWS
        prob = (side_ref if slot % 2 else near_ref)[at : at + ROWS, :]
        share = st_in_ref[PEAK + slot : PEAK + slot + 1, :]
        dk, dv, dq = back_block(own_ref[slot * ROWS : (slot + 1) * ROWS, :], prob, share, g4, q4_ref[...], rd)
        out_ref[i * ROWS : (i + 1) * ROWS, :D] = dk
        out_ref[i * ROWS : (i + 1) * ROWS, D:] = dv
        total = total + dq
    if slots[-1] < REACH:
        st_ref[DOT : DOT + 1, :] = rd
        st_ref[PEAK:, :] = st_in_ref[PEAK:, :]
        st_ref[:D, :] = total
    else:
        dq = jnp.transpose(total) * SCALE
        for h in range(HEADS):
            st_ref[:, h * D : (h + 1) * D] = dq[h * ROWS : (h + 1) * ROWS, :].astype(jnp.bfloat16)


def is_upper(place_ref):
    return (lax.rem(lax.div(place_ref[0], 2), 2) == 1).astype(jnp.float32)


def settle_kernel(own_ref, back_ref, low_ref, high_ref):
    both = own_ref[...] + back_ref[: 2 * ROWS, :].astype(jnp.float32)
    low_ref[...] = both[:ROWS].astype(low_ref.dtype)
    high_ref[...] = both[ROWS:].astype(jnp.bfloat16)


def relay_far(place_ref, keep_ref, side_ref, out_ref):
    out_ref[...] = (keep_ref[...] + side_ref[...].astype(jnp.float32) * is_upper(place_ref)).astype(jnp.bfloat16)


def gather_kernel(place_ref, own_ref, back_ref, side_ref, two_ref, four_ref, out_ref):
    total = own_ref[...] + back_ref[2 * ROWS :, :].astype(jnp.float32)
    total = total + side_ref[...].astype(jnp.float32) * (1 - is_upper(place_ref))
    out_ref[...] = total + two_ref[...].astype(jnp.float32) + four_ref[...].astype(jnp.float32)


def finish_kernel(sum_ref, eight_ref, k_ref, v_ref):
    total = (sum_ref[...] + eight_ref[...].astype(jnp.float32)).astype(jnp.bfloat16)
    k_ref[...] = total[:, :D]
    v_ref[...] = total[:, D:]


def vmem(n):
    return [pl.BlockSpec(memory_space=pltpu.VMEM)] * n


def smem(n):
    return [pl.BlockSpec(memory_space=pltpu.SMEM)] * n


def hbm(n):
    return [pl.BlockSpec(memory_space=pltpu.HBM)] * n


def token(n):
    return [pl.BlockSpec(memory_space=pl.ANY)] * n


def moved(x, axis, to):
    return lax.ppermute(x, axis, [(i, to(i)) for i in range(lax.axis_size(axis))])


def turned(x, axis, by):
    count = lax.axis_size(axis)
    return moved(x, axis, lambda i: (i + by) % count)


def shape(rows, cols, dtype):
    return jax.ShapeDtypeStruct((rows, cols), dtype)


def call(name, kernel, outs, ins, args, scratch=(), flops=1):
    one = not isinstance(outs, tuple)
    return pl.pallas_call(
        kernel,
        out_shape=outs,
        in_specs=ins,
        out_specs=vmem(1)[0] if one else tuple(vmem(len(outs))),
        scratch_shapes=list(scratch),
        compiler_params=pltpu.CompilerParams(vmem_limit_bytes=8 * MIB),
        cost_estimate=pl.CostEstimate(flops=flops, bytes_accessed=1, transcendentals=0),
        name=name,
    )(*args)


def local(queries, keys, values, grad_out, out_weight, lengths):
    bf16, f32 = jnp.bfloat16, jnp.float32
    place = lax.axis_index("ctx").astype(jnp.int32).reshape(1)
    head = lax.axis_index("head").astype(jnp.int32).reshape(1)
    dma = pltpu.SemaphoreType.DMA
    pinned = functools.partial(pltpu.with_memory_space_constraint, memory_space=pltpu.HBM)
    state = shape(STATE, LANES, f32)

    first = moved(grad_out, "head", lambda i: i ^ 1)
    right = turned(grad_out, "head", 2)
    left = turned(grad_out, "head", -2)
    kv = jnp.pad(keys, ((0, 0), (0, D))) + jnp.pad(values, ((0, 0), (D, 0)))
    z2 = turned(kv, "ctx", 2 * PLANE)
    z1 = turned(kv, "ctx", PLANE)
    q4, bound, weight = call(
        "load",
        load_kernel,
        (shape(LANES, D, bf16), shape(8, LANES, f32), shape(HEADS * D, 8 * BLOCK, bf16)),
        smem(2) + hbm(3),
        (place, head, pinned(lengths), pinned(queries), pinned(out_weight)),
        [pltpu.SMEM((lengths.shape[0],), jnp.int32), dma((9 + HEADS,))],
    )
    other = call("stage", stage_kernel, shape(ROWS, BLOCK, bf16), vmem(1) + token(1), (first, q4))
    other_right = turned(other, "head", 2)
    other_left = turned(other, "head", -2)
    far = turned(right, "head", 2)
    other_far = turned(other_left, "head", -2)

    gate = call("gate", gate_kernel, shape(8, D, f32), token(4), (other, right, left, q4))
    picked = call(
        "pick_side", pick_kernel, shape(2 * ROWS, 2 * D, bf16), smem(1) + vmem(3) + token(1), (place, z2, z1, kv, gate)
    )
    side = moved(picked, "ctx", lambda i: i ^ 2)
    p_near, st = call(
        "near",
        near_kernel,
        (shape(3 * ROWS, LANES, bf16), state),
        smem(1) + vmem(5) + token(3),
        (place, z2, z1, kv, q4, bound, picked, other_right, other_left),
    )
    own = call("join_slots", join_kernel, shape(SLOTS * ROWS, 2 * D, bf16), vmem(4) + token(1), (z2, z1, kv, side, st))
    par = moved(own, "ctx", lambda i: i ^ 1)

    p_side, st = call(
        "middle",
        middle_kernel,
        (shape(2 * ROWS, LANES, bf16), state),
        smem(1) + vmem(3),
        (place, own, q4, st),
    )
    early = call(
        "project",
        project_kernel,
        shape(ROWS, HEADS * D, f32),
        vmem(8) + token(1),
        (grad_out, other, right, left, other_right, other_left, far, weight, st),
    )
    g4, gt = call(
        "last_projection",
        last_projection,
        (shape(LANES, D, bf16), shape(D, LANES, f32)),
        vmem(3),
        (other_far, weight, early),
        flops=COSTLY,
    )
    p_par, st = call(
        "across", across_kernel, (shape(REACH * ROWS, LANES, bf16), state), smem(1) + vmem(4), (place, par, q4, gt, st)
    )

    far_cross, st = call(
        "cross_far", cross_far, (shape(2 * ROWS, 2 * D, bf16), state), smem(1) + vmem(5), (place, q4, par, p_par, g4, st)
    )
    far_back = moved(far_cross, "ctx", lambda i: i ^ 1)
    near_cross, st = call(
        "cross_near", cross_near, (shape(3 * ROWS, 2 * D, bf16), state), smem(1) + vmem(5), (place, q4, par, p_par, g4, st), flops=FL
    )
    near_back = moved(near_cross, "ctx", lambda i: i ^ 1)
    far_own, st = call(
        "own_far",
        functools.partial(own_kernel, (0, 1)),
        (shape(2 * ROWS, 2 * D, f32), state),
        vmem(6),
        (q4, own, p_near, p_side, g4, st),
        flops=FL,
    )
    far_keep, far_side = call(
        "settle_far", settle_kernel, (shape(ROWS, 2 * D, f32), shape(ROWS, 2 * D, bf16)), vmem(2), (far_own, far_back)
    )
    count = lax.axis_size("ctx")
    far_side = moved(far_side, "ctx", lambda i: (i + 2 if i // 2 % 2 == 0 else i - 6) % count)
    near_own, st = call(
        "own_near",
        functools.partial(own_kernel, (2, 3)),
        (shape(2 * ROWS, 2 * D, f32), state),
        vmem(6) + token(1),
        (q4, own, p_near, p_side, g4, st, far_keep),
        flops=FL,
    )
    by_four, by_two = call(
        "settle_near", settle_kernel, (shape(ROWS, 2 * D, bf16), shape(ROWS, 2 * D, bf16)), vmem(2), (near_own, near_back)
    )
    by_four = turned(by_four, "ctx", -4)
    by_two = turned(by_two, "ctx", -2)
    to_eight = call("relay_far", relay_far, shape(ROWS, 2 * D, bf16), smem(1) + vmem(2), (place, far_keep, far_side))
    by_eight = turned(to_eight, "ctx", -8)
    last_own, grad_queries = call(
        "own_last",
        functools.partial(own_kernel, (4,)),
        (shape(ROWS, 2 * D, f32), shape(ROWS, HEADS * D, bf16)),
        vmem(6) + token(1),
        (q4, own, p_near, p_side, g4, st, to_eight),
    )
    partial_sum = call(
        "gather_near",
        gather_kernel,
        shape(ROWS, 2 * D, f32),
        smem(1) + vmem(5),
        (place, last_own, near_back, far_side, by_two, by_four),
        flops=COSTLY,
    )
    grad_keys, grad_values = call(
        "finish", finish_kernel, (shape(ROWS, D, bf16), shape(ROWS, D, bf16)), vmem(2), (partial_sum, by_eight)
    )
    return grad_queries, grad_keys, grad_values


def solution(mesh):
    return jax.shard_map(
        local,
        mesh=mesh,
        in_specs=(
            P("ctx", "head"),
            P("ctx", "head"),
            P("ctx", "head"),
            P("ctx", "head"),
            P("head", None),
            P(),
        ),
        out_specs=(P("ctx", "head"), P("ctx", "head"), P("ctx", "head")),
        check_vma=False,
    )
```

```python
import functools

import jax
import jax.numpy as jnp
from jax import lax
from jax.experimental import pallas as pl
from jax.experimental.pallas import tpu as pltpu
from jax.sharding import PartitionSpec as P

D = 128
HEADS = 4
ROWS = 192
LANES = HEADS * ROWS
REACH = 4
SLOTS = REACH + 1
PLANE = 4
BLOCK = 512
MASS, TOP, START, DOT = D, D + 1, D + 2, D + 3
PEAK = D + 8
STATE = PEAK + 16
NEG = -1e30
FLOOR = -1e20
SCALE = D**-0.5
LOG2E = 1.4426950408889634
MIB = 1 << 20
FL = 4 * 10**9
COSTLY = 4 * 10**9


def dot(a, b, ca, cb):
    return lax.dot_general(a, b, (((ca,), (cb,)), ((), ())), preferred_element_type=jnp.float32)


def stack_heads(src, dst):
    for h in range(HEADS):
        dst[h * ROWS : (h + 1) * ROWS, :] = src[:, h * D : (h + 1) * D]


def load_kernel(place_ref, head_ref, len_hbm, q_hbm, w_hbm, q4_ref, bound_ref, w_ref, len_ref, sems):
    head = head_ref[0]
    copies = [pltpu.make_async_copy(len_hbm, len_ref, sems.at[0])]
    sources = (head, source_of(head, 0, True), source_of(head, -2, False), source_of(head, 2, False))
    sources += (source_of(head, -2, True), source_of(head, 2, True), source_of(head, 4, False), source_of(head, 4, True))
    for i, source in enumerate(sources):
        cols = pl.ds(pl.multiple_of(source * BLOCK, BLOCK), BLOCK)
        copies.append(pltpu.make_async_copy(w_hbm.at[:, cols], w_ref.at[:, pl.ds(i * BLOCK, BLOCK)], sems.at[1 + HEADS + i]))
    for h in range(HEADS):
        across, along = pl.ds(h * ROWS, ROWS), pl.ds(h * D, D)
        copies.append(pltpu.make_async_copy(q_hbm.at[:, along], q4_ref.at[across, :], sems.at[1 + h]))
    for copy in copies:
        copy.start()
    lane = lax.broadcasted_iota(jnp.int32, (1, LANES), 1)
    pos = lane + place_ref[0] * ROWS
    for h in range(1, HEADS):
        pos = pos - jnp.where(lane >= h * ROWS, ROWS, 0)
    start = jnp.zeros((1, LANES), jnp.int32)
    end = jnp.int32(0)
    copies[0].wait()
    for d in range(len_ref.shape[0]):
        end = end + len_ref[d]
        start = jnp.where(end <= pos, end, start)
    bound_ref[0:1, :] = pos.astype(jnp.float32)
    bound_ref[1:2, :] = start.astype(jnp.float32)
    for copy in copies[1:]:
        copy.wait()


def stage_kernel(piece_ref, after, out_ref):
    out_ref[...] = piece_ref[...]


def gate_kernel(*refs):
    refs[-1][...] = jnp.zeros(refs[-1].shape, refs[-1].dtype)


def pick_kernel(place_ref, z2_ref, z1_ref, z0_ref, *refs):
    out_ref = refs[-1]
    upper = lax.rem(lax.div(place_ref[0], 2), 2) == 1

    @pl.when(upper)
    def _():
        out_ref[:ROWS, :] = z2_ref[...]
        out_ref[ROWS:, :] = z1_ref[...]

    @pl.when(jnp.logical_not(upper))
    def _():
        out_ref[:ROWS, :] = z1_ref[...]
        out_ref[ROWS:, :] = z0_ref[...]


def join_kernel(z2_ref, z1_ref, z0_ref, side_ref, *refs):
    out_ref = refs[-1]
    parts = (z2_ref[...], side_ref[:ROWS, :], z1_ref[...], side_ref[ROWS:, :], z0_ref[...])
    for m, part in enumerate(parts):
        out_ref[m * ROWS : (m + 1) * ROWS, :] = part


def absorb(block, queries, row, base, start, state, pos=None):
    s = dot(block[:, :D], queries, 1, 1) * (SCALE * LOG2E)
    visible = row >= start - base * ROWS
    if pos is not None:
        visible = visible & (row <= pos - base * ROWS)
    s = jnp.where(visible, s, NEG)
    peak = jnp.maximum(jnp.max(s, axis=0, keepdims=True), FLOOR)
    prob = jnp.exp2(s - peak).astype(jnp.bfloat16)
    mass = jnp.sum(prob.astype(jnp.float32), axis=0, keepdims=True)
    out = dot(block[:, D:], prob, 0, 0)
    if state is None:
        return prob, peak, (out, mass, peak)
    old_out, old_mass, old_peak = state
    top = jnp.maximum(old_peak, peak)
    before, now = jnp.exp2(old_peak - top), jnp.exp2(peak - top)
    return prob, peak, (old_out * before + out * now, old_mass * before + mass * now, top)


def read_state(ref):
    return ref[:D, :], ref[MASS : MASS + 1, :], ref[TOP : TOP + 1, :]


def write_state(ref, state):
    ref[:D, :], ref[MASS : MASS + 1, :], ref[TOP : TOP + 1, :] = state


def put_row(ref, at, value):
    ref[at : at + 1, :] = value


def near_kernel(place_ref, z2_ref, z1_ref, z0_ref, q4_ref, bound_ref, *refs):
    p_ref, st_ref = refs[-2:]
    me = place_ref[0]
    queries = q4_ref[...]
    row = lax.broadcasted_iota(jnp.int32, (ROWS, LANES), 0)
    pos, start = bound_ref[0:1, :].astype(jnp.int32), bound_ref[1:2, :].astype(jnp.int32)
    state = None
    for i, ref in ((2, z0_ref), (1, z1_ref), (0, z2_ref)):
        at = pos if i == 2 else None
        prob, peak, state = absorb(ref[...], queries, row, me - PLANE * (2 - i), start, state, at)
        p_ref[i * ROWS : (i + 1) * ROWS, :] = prob
        put_row(st_ref, PEAK + 2 * i, peak)
    write_state(st_ref, state)
    put_row(st_ref, START, bound_ref[1:2, :])


def project_kernel(*refs):
    pieces, (w_ref, after, acc_ref) = refs[:7], refs[7:]
    acc = None
    for i, piece in enumerate(pieces):
        part = dot(piece[...], w_ref[:, i * BLOCK : (i + 1) * BLOCK], 1, 1)
        acc = part if acc is None else acc + part
    acc_ref[...] = acc


def last_projection(piece_ref, w_ref, acc_ref, g4_ref, gt_ref):
    acc = (acc_ref[...] + dot(piece_ref[...], w_ref[:, 7 * BLOCK :], 1, 1)).astype(jnp.bfloat16)
    for h in range(HEADS):
        g4_ref[h * ROWS : (h + 1) * ROWS, :] = acc[:, h * D : (h + 1) * D]
    gt_ref[...] = jnp.transpose(g4_ref[...].astype(jnp.float32))


def rows(i):
    return pl.ds(pl.multiple_of(i * ROWS, ROWS), ROWS)


def source_of(head, by, flip):
    at = lax.rem(head + by + 8, 8)
    return at + 1 - 2 * lax.rem(at, 2) if flip else at


def middle_kernel(place_ref, own_ref, q4_ref, st_in_ref, p_ref, st_ref):
    queries = q4_ref[...]
    row = lax.broadcasted_iota(jnp.int32, (ROWS, LANES), 0)
    start = st_in_ref[START : START + 1, :].astype(jnp.int32)
    state = read_state(st_in_ref)
    st_ref[PEAK:, :] = st_in_ref[PEAK:, :]
    for i in range(2):
        slot = 2 * i + 1
        block = own_ref[slot * ROWS : (slot + 1) * ROWS, :]
        prob, peak, state = absorb(block, queries, row, place_ref[0] + 2 * (slot - REACH), start, state)
        p_ref[i * ROWS : (i + 1) * ROWS, :] = prob
        put_row(st_ref, PEAK + slot, peak)
    write_state(st_ref, state)
    put_row(st_ref, START, st_in_ref[START : START + 1, :])


def across_kernel(place_ref, par_ref, q4_ref, gt_ref, st_in_ref, p_ref, st_ref):
    me = place_ref[0]
    core = lax.rem(me, 2)
    chip = me - core
    queries = q4_ref[...]
    row = lax.broadcasted_iota(jnp.int32, (ROWS, LANES), 0)
    start = st_in_ref[START : START + 1, :].astype(jnp.int32)
    state = read_state(st_in_ref)
    peaks = [st_in_ref[PEAK + m : PEAK + m + 1, :] for m in range(SLOTS)]
    for i in range(REACH):
        slot = i + core
        prob, peak, state = absorb(par_ref[rows(slot), :], queries, row, chip + 1 - core + 2 * (slot - REACH), start, state)
        p_ref[i * ROWS : (i + 1) * ROWS, :] = prob
        peaks.append(peak)
    out, mass, top = state
    put_row(st_ref, DOT, jnp.sum(gt_ref[...] * out, axis=0, keepdims=True) / mass)
    log_total = top + jnp.log2(mass)
    for i, peak in enumerate(peaks):
        put_row(st_ref, PEAK + i, jnp.exp2(peak - log_total))


def back_block(block, prob, share, g4, q4, rd):
    prob = prob.astype(jnp.float32) * share
    dprob = dot(block[:, D:], g4, 1, 1)
    ds = (prob * (dprob - rd)).astype(jnp.bfloat16)
    dv = dot(prob.astype(jnp.bfloat16), g4, 1, 0)
    dk = dot(ds, q4, 1, 0) * SCALE
    dq = dot(block[:, :D], ds, 0, 0)
    return dk, dv, dq


def put(out_ref, slot, dk, dv):
    at = pl.ds(pl.multiple_of(slot * ROWS, ROWS), ROWS)
    out_ref[at, :D] = dk.astype(out_ref.dtype)
    out_ref[at, D:] = dv.astype(out_ref.dtype)


def cross_step(slot, core, par_ref, p_ref, st_ref, g4, q4_ref, rd):
    share = st_ref[pl.ds(PEAK + SLOTS + slot - core, 1), :]
    return back_block(par_ref[rows(slot), :], p_ref[rows(slot - core), :], share, g4, q4_ref[...], rd)


def cross_far(place_ref, q4_ref, par_ref, p_ref, g_ref, st_in_ref, out_ref, st_ref):
    core = lax.rem(place_ref[0], 2)
    g4 = g_ref[...]
    rd = st_in_ref[DOT : DOT + 1, :]
    st_ref[DOT : DOT + 1, :] = rd
    st_ref[PEAK:, :] = st_in_ref[PEAK:, :]
    dk, dv, dq = cross_step(1, core, par_ref, p_ref, st_ref, g4, q4_ref, rd)
    put(out_ref, 1, dk, dv)
    st_ref[:D, :] = dq

    @pl.when(core == 1)
    def _():
        out_ref[:ROWS, :] = jnp.zeros((ROWS, 2 * D), out_ref.dtype)

    @pl.when(core == 0)
    def _():
        dk, dv, dq = cross_step(0, core, par_ref, p_ref, st_ref, g4, q4_ref, rd)
        put(out_ref, 0, dk, dv)
        st_ref[:D, :] += dq


def cross_near(place_ref, q4_ref, par_ref, p_ref, g_ref, st_in_ref, out_ref, st_ref):
    core = lax.rem(place_ref[0], 2)
    g4 = g_ref[...]
    rd = st_in_ref[DOT : DOT + 1, :]
    st_ref[DOT : DOT + 1, :] = rd
    st_ref[PEAK:, :] = st_in_ref[PEAK:, :]
    total = st_in_ref[:D, :]
    for slot in (2, 3):
        dk, dv, dq = cross_step(slot, core, par_ref, p_ref, st_ref, g4, q4_ref, rd)
        put(out_ref, slot - 2, dk, dv)
        total = total + dq
    st_ref[:D, :] = total

    @pl.when(core == 0)
    def _():
        out_ref[2 * ROWS :, :] = jnp.zeros((ROWS, 2 * D), out_ref.dtype)

    @pl.when(core == 1)
    def _():
        dk, dv, dq = cross_step(4, core, par_ref, p_ref, st_ref, g4, q4_ref, rd)
        put(out_ref, 2, dk, dv)
        st_ref[:D, :] += dq


def own_kernel(slots, q4_ref, own_ref, near_ref, side_ref, g_ref, st_in_ref, *refs):
    out_ref, st_ref = refs[-2:]
    g4 = g_ref[...]
    rd = st_in_ref[DOT : DOT + 1, :]
    total = st_in_ref[:D, :]
    for i, slot in enumerate(slots):
        at = slot // 2 * ROWS
        prob = (side_ref if slot % 2 else near_ref)[at : at + ROWS, :]
        share = st_in_ref[PEAK + slot : PEAK + slot + 1, :]
        dk, dv, dq = back_block(own_ref[slot * ROWS : (slot + 1) * ROWS, :], prob, share, g4, q4_ref[...], rd)
        out_ref[i * ROWS : (i + 1) * ROWS, :D] = dk
        out_ref[i * ROWS : (i + 1) * ROWS, D:] = dv
        total = total + dq
    if slots[-1] < REACH:
        st_ref[DOT : DOT + 1, :] = rd
        st_ref[PEAK:, :] = st_in_ref[PEAK:, :]
        st_ref[:D, :] = total
    else:
        dq = jnp.transpose(total) * SCALE
        for h in range(HEADS):
            st_ref[:, h * D : (h + 1) * D] = dq[h * ROWS : (h + 1) * ROWS, :].astype(jnp.bfloat16)


def is_upper(place_ref):
    return (lax.rem(lax.div(place_ref[0], 2), 2) == 1).astype(jnp.float32)


def settle_kernel(own_ref, back_ref, keep_ref, send_ref):
    both = own_ref[...] + back_ref[: 2 * ROWS, :].astype(jnp.float32)
    keep_ref[...] = both[:ROWS]
    send_ref[...] = both[ROWS:].astype(jnp.bfloat16)


def relay_kernel(place_ref, far_ref, near_ref, side_ref, eight_ref, four_ref):
    side = side_ref[...].astype(jnp.float32)
    upper = is_upper(place_ref)
    eight_ref[...] = (far_ref[...] + side * upper).astype(jnp.bfloat16)
    four_ref[...] = (near_ref[...] + side * (1 - upper)).astype(jnp.bfloat16)


def gather_kernel(own_ref, back_ref, two_ref, out_ref):
    total = own_ref[...] + back_ref[2 * ROWS :, :].astype(jnp.float32)
    out_ref[...] = total + two_ref[...].astype(jnp.float32)


def finish_kernel(sum_ref, four_ref, eight_ref, k_ref, v_ref):
    total = sum_ref[...] + four_ref[...].astype(jnp.float32) + eight_ref[...].astype(jnp.float32)
    total = total.astype(jnp.bfloat16)
    k_ref[...] = total[:, :D]
    v_ref[...] = total[:, D:]


def vmem(n):
    return [pl.BlockSpec(memory_space=pltpu.VMEM)] * n


def smem(n):
    return [pl.BlockSpec(memory_space=pltpu.SMEM)] * n


def hbm(n):
    return [pl.BlockSpec(memory_space=pltpu.HBM)] * n


def token(n):
    return [pl.BlockSpec(memory_space=pl.ANY)] * n


def moved(x, axis, to):
    return lax.ppermute(x, axis, [(i, to(i)) for i in range(lax.axis_size(axis))])


def turned(x, axis, by):
    count = lax.axis_size(axis)
    return moved(x, axis, lambda i: (i + by) % count)


def shape(rows, cols, dtype):
    return jax.ShapeDtypeStruct((rows, cols), dtype)


def call(name, kernel, outs, ins, args, scratch=(), flops=1):
    one = not isinstance(outs, tuple)
    return pl.pallas_call(
        kernel,
        out_shape=outs,
        in_specs=ins,
        out_specs=vmem(1)[0] if one else tuple(vmem(len(outs))),
        scratch_shapes=list(scratch),
        compiler_params=pltpu.CompilerParams(vmem_limit_bytes=8 * MIB),
        cost_estimate=pl.CostEstimate(flops=flops, bytes_accessed=1, transcendentals=0),
        name=name,
    )(*args)


def local(queries, keys, values, grad_out, out_weight, lengths):
    bf16, f32 = jnp.bfloat16, jnp.float32
    place = lax.axis_index("ctx").astype(jnp.int32).reshape(1)
    head = lax.axis_index("head").astype(jnp.int32).reshape(1)
    dma = pltpu.SemaphoreType.DMA
    pinned = functools.partial(pltpu.with_memory_space_constraint, memory_space=pltpu.HBM)
    state = shape(STATE, LANES, f32)

    first = moved(grad_out, "head", lambda i: i ^ 1)
    right = turned(grad_out, "head", 2)
    left = turned(grad_out, "head", -2)
    kv = jnp.pad(keys, ((0, 0), (0, D))) + jnp.pad(values, ((0, 0), (D, 0)))
    z2 = turned(kv, "ctx", 2 * PLANE)
    z1 = turned(kv, "ctx", PLANE)
    q4, bound, weight = call(
        "load",
        load_kernel,
        (shape(LANES, D, bf16), shape(8, LANES, f32), shape(HEADS * D, 8 * BLOCK, bf16)),
        smem(2) + hbm(3),
        (place, head, pinned(lengths), pinned(queries), pinned(out_weight)),
        [pltpu.SMEM((lengths.shape[0],), jnp.int32), dma((9 + HEADS,))],
    )
    other = call("stage", stage_kernel, shape(ROWS, BLOCK, bf16), vmem(1) + token(1), (first, q4))
    other_right = turned(other, "head", 2)
    other_left = turned(other, "head", -2)
    far = turned(right, "head", 2)
    other_far = turned(other_left, "head", -2)

    gate = call("gate", gate_kernel, shape(8, D, f32), token(4), (other, right, left, q4))
    picked = call(
        "pick_side", pick_kernel, shape(2 * ROWS, 2 * D, bf16), smem(1) + vmem(3) + token(1), (place, z2, z1, kv, gate)
    )
    side = moved(picked, "ctx", lambda i: i ^ 2)
    p_near, st = call(
        "near",
        near_kernel,
        (shape(3 * ROWS, LANES, bf16), state),
        smem(1) + vmem(5) + token(3),
        (place, z2, z1, kv, q4, bound, picked, other_right, other_left),
    )
    own = call("join_slots", join_kernel, shape(SLOTS * ROWS, 2 * D, bf16), vmem(4) + token(1), (z2, z1, kv, side, st))
    par = moved(own, "ctx", lambda i: i ^ 1)

    p_side, st = call(
        "middle",
        middle_kernel,
        (shape(2 * ROWS, LANES, bf16), state),
        smem(1) + vmem(3),
        (place, own, q4, st),
    )
    early = call(
        "project",
        project_kernel,
        shape(ROWS, HEADS * D, f32),
        vmem(8) + token(1),
        (grad_out, other, right, left, other_right, other_left, far, weight, st),
    )
    g4, gt = call(
        "last_projection",
        last_projection,
        (shape(LANES, D, bf16), shape(D, LANES, f32)),
        vmem(3),
        (other_far, weight, early),
        flops=COSTLY,
    )
    p_par, st = call(
        "across", across_kernel, (shape(REACH * ROWS, LANES, bf16), state), smem(1) + vmem(4), (place, par, q4, gt, st)
    )

    far_cross, st = call(
        "cross_far", cross_far, (shape(2 * ROWS, 2 * D, bf16), state), smem(1) + vmem(5), (place, q4, par, p_par, g4, st)
    )
    far_back = moved(far_cross, "ctx", lambda i: i ^ 1)
    near_cross, st = call(
        "cross_near", cross_near, (shape(3 * ROWS, 2 * D, bf16), state), smem(1) + vmem(5), (place, q4, par, p_par, g4, st), flops=FL
    )
    near_back = moved(near_cross, "ctx", lambda i: i ^ 1)
    far_own, st = call(
        "own_far",
        functools.partial(own_kernel, (0, 1)),
        (shape(2 * ROWS, 2 * D, f32), state),
        vmem(6),
        (q4, own, p_near, p_side, g4, st),
        flops=FL,
    )
    far_keep, far_side = call(
        "settle_far", settle_kernel, (shape(ROWS, 2 * D, f32), shape(ROWS, 2 * D, bf16)), vmem(2), (far_own, far_back)
    )
    far_side = moved(far_side, "ctx", lambda i: i ^ 2)
    near_own, st = call(
        "own_near",
        functools.partial(own_kernel, (2, 3)),
        (shape(2 * ROWS, 2 * D, f32), state),
        vmem(6) + token(1),
        (q4, own, p_near, p_side, g4, st, far_keep),
        flops=FL,
    )
    near_keep, by_two = call(
        "settle_near", settle_kernel, (shape(ROWS, 2 * D, f32), shape(ROWS, 2 * D, bf16)), vmem(2), (near_own, near_back)
    )
    by_two = turned(by_two, "ctx", -2)
    to_eight, to_four = call(
        "relay",
        relay_kernel,
        (shape(ROWS, 2 * D, bf16), shape(ROWS, 2 * D, bf16)),
        smem(1) + vmem(3),
        (place, far_keep, near_keep, far_side),
    )
    by_eight = turned(to_eight, "ctx", -2 * PLANE)
    by_four = turned(to_four, "ctx", -PLANE)
    last_own, grad_queries = call(
        "own_last",
        functools.partial(own_kernel, (4,)),
        (shape(ROWS, 2 * D, f32), shape(ROWS, HEADS * D, bf16)),
        vmem(6) + token(1),
        (q4, own, p_near, p_side, g4, st, to_eight),
    )
    partial_sum = call(
        "gather_near", gather_kernel, shape(ROWS, 2 * D, f32), vmem(3), (last_own, near_back, by_two), flops=COSTLY
    )
    grad_keys, grad_values = call(
        "finish", finish_kernel, (shape(ROWS, D, bf16), shape(ROWS, D, bf16)), vmem(3), (partial_sum, by_four, by_eight)
    )
    return grad_queries, grad_keys, grad_values


def solution(mesh):
    return jax.shard_map(
        local,
        mesh=mesh,
        in_specs=(
            P("ctx", "head"),
            P("ctx", "head"),
            P("ctx", "head"),
            P("ctx", "head"),
            P("head", None),
            P(),
        ),
        out_specs=(P("ctx", "head"), P("ctx", "head"), P("ctx", "head")),
        check_vma=False,
    )
```

```python
import functools

import jax
import jax.numpy as jnp
from jax import lax
from jax.experimental import pallas as pl
from jax.experimental.pallas import tpu as pltpu
from jax.sharding import PartitionSpec as P

D = 128
HEADS = 4
ROWS = 192
LANES = HEADS * ROWS
REACH = 4
SLOTS = REACH + 1
PLANE = 4
BLOCK = 512
MASS, TOP, START, DOT = D, D + 1, D + 2, D + 3
PEAK = D + 8
STATE = PEAK + 16
NEG = -1e30
FLOOR = -1e20
SCALE = D**-0.5
LOG2E = 1.4426950408889634
MIB = 1 << 20
FL = 4 * 10**9
COSTLY = 4 * 10**9


def dot(a, b, ca, cb):
    return lax.dot_general(a, b, (((ca,), (cb,)), ((), ())), preferred_element_type=jnp.float32)


def stack_heads(src, dst):
    for h in range(HEADS):
        dst[h * ROWS : (h + 1) * ROWS, :] = src[:, h * D : (h + 1) * D]


def load_kernel(place_ref, head_ref, len_hbm, q_hbm, w_hbm, q4_ref, bound_ref, w_ref, len_ref, sems):
    head = head_ref[0]
    copies = [pltpu.make_async_copy(len_hbm, len_ref, sems.at[0])]
    sources = (head, source_of(head, 0, True), source_of(head, -2, False), source_of(head, 2, False))
    sources += (source_of(head, -2, True), source_of(head, 2, True), source_of(head, 4, False), source_of(head, 4, True))
    for i, source in enumerate(sources):
        cols = pl.ds(pl.multiple_of(source * BLOCK, BLOCK), BLOCK)
        copies.append(pltpu.make_async_copy(w_hbm.at[:, cols], w_ref.at[:, pl.ds(i * BLOCK, BLOCK)], sems.at[1 + HEADS + i]))
    for h in range(HEADS):
        across, along = pl.ds(h * ROWS, ROWS), pl.ds(h * D, D)
        copies.append(pltpu.make_async_copy(q_hbm.at[:, along], q4_ref.at[across, :], sems.at[1 + h]))
    for copy in copies:
        copy.start()
    lane = lax.broadcasted_iota(jnp.int32, (1, LANES), 1)
    pos = lane + place_ref[0] * ROWS
    for h in range(1, HEADS):
        pos = pos - jnp.where(lane >= h * ROWS, ROWS, 0)
    start = jnp.zeros((1, LANES), jnp.int32)
    end = jnp.int32(0)
    copies[0].wait()
    for d in range(len_ref.shape[0]):
        end = end + len_ref[d]
        start = jnp.where(end <= pos, end, start)
    bound_ref[0:1, :] = pos.astype(jnp.float32)
    bound_ref[1:2, :] = start.astype(jnp.float32)
    for copy in copies[1:]:
        copy.wait()


def stage_kernel(piece_ref, after, out_ref):
    out_ref[...] = piece_ref[...]


def gate_kernel(*refs):
    refs[-1][...] = jnp.zeros(refs[-1].shape, refs[-1].dtype)


def pick_kernel(place_ref, z2_ref, z1_ref, z0_ref, *refs):
    out_ref = refs[-1]
    upper = lax.rem(lax.div(place_ref[0], 2), 2) == 1

    @pl.when(upper)
    def _():
        out_ref[:ROWS, :] = z2_ref[...]
        out_ref[ROWS:, :] = z1_ref[...]

    @pl.when(jnp.logical_not(upper))
    def _():
        out_ref[:ROWS, :] = z1_ref[...]
        out_ref[ROWS:, :] = z0_ref[...]


def join_kernel(z2_ref, z1_ref, z0_ref, side_ref, *refs):
    out_ref = refs[-1]
    parts = (z2_ref[...], side_ref[:ROWS, :], z1_ref[...], side_ref[ROWS:, :], z0_ref[...])
    for m, part in enumerate(parts):
        out_ref[m * ROWS : (m + 1) * ROWS, :] = part


def absorb(block, queries, row, base, start, state, pos=None):
    s = dot(block[:, :D], queries, 1, 1) * (SCALE * LOG2E)
    visible = row >= start - base * ROWS
    if pos is not None:
        visible = visible & (row <= pos - base * ROWS)
    s = jnp.where(visible, s, NEG)
    peak = jnp.maximum(jnp.max(s, axis=0, keepdims=True), FLOOR)
    prob = jnp.exp2(s - peak).astype(jnp.bfloat16)
    mass = jnp.sum(prob.astype(jnp.float32), axis=0, keepdims=True)
    out = dot(block[:, D:], prob, 0, 0)
    if state is None:
        return prob, peak, (out, mass, peak)
    old_out, old_mass, old_peak = state
    top = jnp.maximum(old_peak, peak)
    before, now = jnp.exp2(old_peak - top), jnp.exp2(peak - top)
    return prob, peak, (old_out * before + out * now, old_mass * before + mass * now, top)


def read_state(ref):
    return ref[:D, :], ref[MASS : MASS + 1, :], ref[TOP : TOP + 1, :]


def write_state(ref, state):
    ref[:D, :], ref[MASS : MASS + 1, :], ref[TOP : TOP + 1, :] = state


def put_row(ref, at, value):
    ref[at : at + 1, :] = value


def near_kernel(place_ref, z2_ref, z1_ref, z0_ref, q4_ref, bound_ref, *refs):
    p_ref, st_ref = refs[-2:]
    me = place_ref[0]
    queries = q4_ref[...]
    row = lax.broadcasted_iota(jnp.int32, (ROWS, LANES), 0)
    pos, start = bound_ref[0:1, :].astype(jnp.int32), bound_ref[1:2, :].astype(jnp.int32)
    state = None
    for i, ref in ((2, z0_ref), (1, z1_ref), (0, z2_ref)):
        at = pos if i == 2 else None
        prob, peak, state = absorb(ref[...], queries, row, me - PLANE * (2 - i), start, state, at)
        p_ref[i * ROWS : (i + 1) * ROWS, :] = prob
        put_row(st_ref, PEAK + 2 * i, peak)
    write_state(st_ref, state)
    put_row(st_ref, START, bound_ref[1:2, :])


def project_kernel(*refs):
    pieces, (w_ref, after, acc_ref) = refs[:7], refs[7:]
    acc = None
    for i, piece in enumerate(pieces):
        part = dot(piece[...], w_ref[:, i * BLOCK : (i + 1) * BLOCK], 1, 1)
        acc = part if acc is None else acc + part
    acc_ref[...] = acc


def last_projection(piece_ref, w_ref, acc_ref, g4_ref, gt_ref):
    acc = (acc_ref[...] + dot(piece_ref[...], w_ref[:, 7 * BLOCK :], 1, 1)).astype(jnp.bfloat16)
    for h in range(HEADS):
        g4_ref[h * ROWS : (h + 1) * ROWS, :] = acc[:, h * D : (h + 1) * D]
    gt_ref[...] = jnp.transpose(g4_ref[...].astype(jnp.float32))


def rows(i):
    return pl.ds(pl.multiple_of(i * ROWS, ROWS), ROWS)


def source_of(head, by, flip):
    at = lax.rem(head + by + 8, 8)
    return at + 1 - 2 * lax.rem(at, 2) if flip else at


def middle_kernel(place_ref, own_ref, q4_ref, st_in_ref, p_ref, st_ref):
    queries = q4_ref[...]
    row = lax.broadcasted_iota(jnp.int32, (ROWS, LANES), 0)
    start = st_in_ref[START : START + 1, :].astype(jnp.int32)
    state = read_state(st_in_ref)
    st_ref[PEAK:, :] = st_in_ref[PEAK:, :]
    for i in range(2):
        slot = 2 * i + 1
        block = own_ref[slot * ROWS : (slot + 1) * ROWS, :]
        prob, peak, state = absorb(block, queries, row, place_ref[0] + 2 * (slot - REACH), start, state)
        p_ref[i * ROWS : (i + 1) * ROWS, :] = prob
        put_row(st_ref, PEAK + slot, peak)
    write_state(st_ref, state)
    put_row(st_ref, START, st_in_ref[START : START + 1, :])


def across_kernel(place_ref, par_ref, q4_ref, gt_ref, st_in_ref, p_ref, st_ref):
    me = place_ref[0]
    core = lax.rem(me, 2)
    chip = me - core
    queries = q4_ref[...]
    row = lax.broadcasted_iota(jnp.int32, (ROWS, LANES), 0)
    start = st_in_ref[START : START + 1, :].astype(jnp.int32)
    state = read_state(st_in_ref)
    peaks = [st_in_ref[PEAK + m : PEAK + m + 1, :] for m in range(SLOTS)]
    for i in range(REACH):
        slot = i + core
        prob, peak, state = absorb(par_ref[rows(slot), :], queries, row, chip + 1 - core + 2 * (slot - REACH), start, state)
        p_ref[i * ROWS : (i + 1) * ROWS, :] = prob
        peaks.append(peak)
    out, mass, top = state
    put_row(st_ref, DOT, jnp.sum(gt_ref[...] * out, axis=0, keepdims=True) / mass)
    log_total = top + jnp.log2(mass)
    for i, peak in enumerate(peaks):
        put_row(st_ref, PEAK + i, jnp.exp2(peak - log_total))


def back_block(block, prob, share, g4, q4, rd):
    prob = prob.astype(jnp.float32) * share
    dprob = dot(block[:, D:], g4, 1, 1)
    ds = (prob * (dprob - rd)).astype(jnp.bfloat16)
    dv = dot(prob.astype(jnp.bfloat16), g4, 1, 0)
    dk = dot(ds, q4, 1, 0) * SCALE
    dq = dot(block[:, :D], ds, 0, 0)
    return dk, dv, dq


def put(out_ref, slot, dk, dv):
    at = pl.ds(pl.multiple_of(slot * ROWS, ROWS), ROWS)
    out_ref[at, :D] = dk.astype(out_ref.dtype)
    out_ref[at, D:] = dv.astype(out_ref.dtype)


def cross_step(slot, core, par_ref, p_ref, st_ref, g4, q4_ref, rd):
    share = st_ref[pl.ds(PEAK + SLOTS + slot - core, 1), :]
    return back_block(par_ref[rows(slot), :], p_ref[rows(slot - core), :], share, g4, q4_ref[...], rd)


def cross_far(place_ref, q4_ref, par_ref, p_ref, g_ref, st_in_ref, out_ref, st_ref):
    core = lax.rem(place_ref[0], 2)
    g4 = g_ref[...]
    rd = st_in_ref[DOT : DOT + 1, :]
    st_ref[DOT : DOT + 1, :] = rd
    st_ref[PEAK:, :] = st_in_ref[PEAK:, :]
    dk, dv, dq = cross_step(1, core, par_ref, p_ref, st_ref, g4, q4_ref, rd)
    put(out_ref, 1, dk, dv)
    st_ref[:D, :] = dq

    @pl.when(core == 1)
    def _():
        out_ref[:ROWS, :] = jnp.zeros((ROWS, 2 * D), out_ref.dtype)

    @pl.when(core == 0)
    def _():
        dk, dv, dq = cross_step(0, core, par_ref, p_ref, st_ref, g4, q4_ref, rd)
        put(out_ref, 0, dk, dv)
        st_ref[:D, :] += dq


def cross_near(place_ref, q4_ref, par_ref, p_ref, g_ref, st_in_ref, out_ref, st_ref):
    core = lax.rem(place_ref[0], 2)
    g4 = g_ref[...]
    rd = st_in_ref[DOT : DOT + 1, :]
    st_ref[DOT : DOT + 1, :] = rd
    st_ref[PEAK:, :] = st_in_ref[PEAK:, :]
    total = st_in_ref[:D, :]
    for slot in (2, 3):
        dk, dv, dq = cross_step(slot, core, par_ref, p_ref, st_ref, g4, q4_ref, rd)
        put(out_ref, slot - 2, dk, dv)
        total = total + dq
    st_ref[:D, :] = total

    @pl.when(core == 0)
    def _():
        out_ref[2 * ROWS :, :] = jnp.zeros((ROWS, 2 * D), out_ref.dtype)

    @pl.when(core == 1)
    def _():
        dk, dv, dq = cross_step(4, core, par_ref, p_ref, st_ref, g4, q4_ref, rd)
        put(out_ref, 2, dk, dv)
        st_ref[:D, :] += dq


def own_kernel(slots, q4_ref, own_ref, near_ref, side_ref, g_ref, st_in_ref, *refs):
    out_ref, st_ref = refs[-2:]
    g4 = g_ref[...]
    rd = st_in_ref[DOT : DOT + 1, :]
    total = st_in_ref[:D, :]
    for i, slot in enumerate(slots):
        at = slot // 2 * ROWS
        prob = (side_ref if slot % 2 else near_ref)[at : at + ROWS, :]
        share = st_in_ref[PEAK + slot : PEAK + slot + 1, :]
        dk, dv, dq = back_block(own_ref[slot * ROWS : (slot + 1) * ROWS, :], prob, share, g4, q4_ref[...], rd)
        out_ref[i * ROWS : (i + 1) * ROWS, :D] = dk
        out_ref[i * ROWS : (i + 1) * ROWS, D:] = dv
        total = total + dq
    if slots[-1] < REACH:
        st_ref[DOT : DOT + 1, :] = rd
        st_ref[PEAK:, :] = st_in_ref[PEAK:, :]
        st_ref[:D, :] = total
    else:
        dq = jnp.transpose(total) * SCALE
        for h in range(HEADS):
            st_ref[:, h * D : (h + 1) * D] = dq[h * ROWS : (h + 1) * ROWS, :].astype(jnp.bfloat16)


def is_upper(place_ref):
    return (lax.rem(lax.div(place_ref[0], 2), 2) == 1).astype(jnp.float32)


def settle_kernel(own_ref, back_ref, keep_ref, send_ref):
    both = own_ref[...] + back_ref[: 2 * ROWS, :].astype(jnp.float32)
    keep_ref[...] = both[:ROWS]
    send_ref[...] = both[ROWS:].astype(jnp.bfloat16)


def relay_kernel(place_ref, far_ref, near_ref, side_ref, eight_ref, four_ref):
    side = side_ref[...].astype(jnp.float32)
    upper = is_upper(place_ref)
    eight_ref[...] = (far_ref[...] + side * upper).astype(jnp.bfloat16)
    four_ref[...] = (near_ref[...] + side * (1 - upper)).astype(jnp.bfloat16)


def gather_kernel(own_ref, back_ref, two_ref, out_ref):
    total = own_ref[...] + back_ref[2 * ROWS :, :].astype(jnp.float32)
    out_ref[...] = total + two_ref[...].astype(jnp.float32)


def finish_kernel(sum_ref, eight_ref, four_ref, k_ref, v_ref):
    total = sum_ref[...] + four_ref[...].astype(jnp.float32) + eight_ref[...].astype(jnp.float32)
    total = total.astype(jnp.bfloat16)
    k_ref[...] = total[:, :D]
    v_ref[...] = total[:, D:]


def vmem(n):
    return [pl.BlockSpec(memory_space=pltpu.VMEM)] * n


def smem(n):
    return [pl.BlockSpec(memory_space=pltpu.SMEM)] * n


def hbm(n):
    return [pl.BlockSpec(memory_space=pltpu.HBM)] * n


def token(n):
    return [pl.BlockSpec(memory_space=pl.ANY)] * n


def moved(x, axis, to):
    return lax.ppermute(x, axis, [(i, to(i)) for i in range(lax.axis_size(axis))])


def turned(x, axis, by):
    count = lax.axis_size(axis)
    return moved(x, axis, lambda i: (i + by) % count)


def shape(rows, cols, dtype):
    return jax.ShapeDtypeStruct((rows, cols), dtype)


def call(name, kernel, outs, ins, args, scratch=(), flops=1):
    one = not isinstance(outs, tuple)
    return pl.pallas_call(
        kernel,
        out_shape=outs,
        in_specs=ins,
        out_specs=vmem(1)[0] if one else tuple(vmem(len(outs))),
        scratch_shapes=list(scratch),
        compiler_params=pltpu.CompilerParams(vmem_limit_bytes=8 * MIB),
        cost_estimate=pl.CostEstimate(flops=flops, bytes_accessed=1, transcendentals=0),
        name=name,
    )(*args)


def local(queries, keys, values, grad_out, out_weight, lengths):
    bf16, f32 = jnp.bfloat16, jnp.float32
    place = lax.axis_index("ctx").astype(jnp.int32).reshape(1)
    head = lax.axis_index("head").astype(jnp.int32).reshape(1)
    dma = pltpu.SemaphoreType.DMA
    pinned = functools.partial(pltpu.with_memory_space_constraint, memory_space=pltpu.HBM)
    state = shape(STATE, LANES, f32)

    first = moved(grad_out, "head", lambda i: i ^ 1)
    right = turned(grad_out, "head", 2)
    left = turned(grad_out, "head", -2)
    kv = jnp.pad(keys, ((0, 0), (0, D))) + jnp.pad(values, ((0, 0), (D, 0)))
    z2 = turned(kv, "ctx", 2 * PLANE)
    z1 = turned(kv, "ctx", PLANE)
    q4, bound, weight = call(
        "load",
        load_kernel,
        (shape(LANES, D, bf16), shape(8, LANES, f32), shape(HEADS * D, 8 * BLOCK, bf16)),
        smem(2) + hbm(3),
        (place, head, pinned(lengths), pinned(queries), pinned(out_weight)),
        [pltpu.SMEM((lengths.shape[0],), jnp.int32), dma((9 + HEADS,))],
    )
    other = call("stage", stage_kernel, shape(ROWS, BLOCK, bf16), vmem(1) + token(1), (first, q4))
    other_right = turned(other, "head", 2)
    other_left = turned(other, "head", -2)
    far = turned(right, "head", 2)
    other_far = turned(other_left, "head", -2)

    gate = call("gate", gate_kernel, shape(8, D, f32), token(4), (other, right, left, q4))
    picked = call(
        "pick_side", pick_kernel, shape(2 * ROWS, 2 * D, bf16), smem(1) + vmem(3) + token(1), (place, z2, z1, kv, gate)
    )
    side = moved(picked, "ctx", lambda i: i ^ 2)
    p_near, st = call(
        "near",
        near_kernel,
        (shape(3 * ROWS, LANES, bf16), state),
        smem(1) + vmem(5) + token(3),
        (place, z2, z1, kv, q4, bound, picked, other_right, other_left),
    )
    own = call("join_slots", join_kernel, shape(SLOTS * ROWS, 2 * D, bf16), vmem(4) + token(1), (z2, z1, kv, side, st))
    par = moved(own, "ctx", lambda i: i ^ 1)

    p_side, st = call(
        "middle",
        middle_kernel,
        (shape(2 * ROWS, LANES, bf16), state),
        smem(1) + vmem(3),
        (place, own, q4, st),
    )
    early = call(
        "project",
        project_kernel,
        shape(ROWS, HEADS * D, f32),
        vmem(8) + token(1),
        (grad_out, other, right, left, other_right, other_left, far, weight, st),
    )
    g4, gt = call(
        "last_projection",
        last_projection,
        (shape(LANES, D, bf16), shape(D, LANES, f32)),
        vmem(3),
        (other_far, weight, early),
        flops=COSTLY,
    )
    p_par, st = call(
        "across", across_kernel, (shape(REACH * ROWS, LANES, bf16), state), smem(1) + vmem(4), (place, par, q4, gt, st)
    )

    far_cross, st = call(
        "cross_far", cross_far, (shape(2 * ROWS, 2 * D, bf16), state), smem(1) + vmem(5), (place, q4, par, p_par, g4, st)
    )
    far_back = moved(far_cross, "ctx", lambda i: i ^ 1)
    near_cross, st = call(
        "cross_near", cross_near, (shape(3 * ROWS, 2 * D, bf16), state), smem(1) + vmem(5), (place, q4, par, p_par, g4, st), flops=FL
    )
    near_back = moved(near_cross, "ctx", lambda i: i ^ 1)
    far_own, st = call(
        "own_far",
        functools.partial(own_kernel, (0, 1)),
        (shape(2 * ROWS, 2 * D, f32), state),
        vmem(6),
        (q4, own, p_near, p_side, g4, st),
        flops=FL,
    )
    far_keep, far_side = call(
        "settle_far", settle_kernel, (shape(ROWS, 2 * D, f32), shape(ROWS, 2 * D, bf16)), vmem(2), (far_own, far_back)
    )
    far_side = moved(far_side, "ctx", lambda i: i ^ 2)
    near_own, st = call(
        "own_near",
        functools.partial(own_kernel, (2, 3)),
        (shape(2 * ROWS, 2 * D, f32), state),
        vmem(6) + token(1),
        (q4, own, p_near, p_side, g4, st, far_keep),
        flops=FL,
    )
    near_keep, by_two = call(
        "settle_near", settle_kernel, (shape(ROWS, 2 * D, f32), shape(ROWS, 2 * D, bf16)), vmem(2), (near_own, near_back)
    )
    by_two = turned(by_two, "ctx", -2)
    to_eight, to_four = call(
        "relay",
        relay_kernel,
        (shape(ROWS, 2 * D, bf16), shape(ROWS, 2 * D, bf16)),
        smem(1) + vmem(3),
        (place, far_keep, near_keep, far_side),
    )
    by_eight = turned(to_eight, "ctx", -2 * PLANE)
    by_four = turned(to_four, "ctx", -PLANE)
    last_own, grad_queries = call(
        "own_last",
        functools.partial(own_kernel, (4,)),
        (shape(ROWS, 2 * D, f32), shape(ROWS, HEADS * D, bf16)),
        vmem(6) + token(2),
        (q4, own, p_near, p_side, g4, st, to_eight, by_two),
        flops=COSTLY,
    )
    partial_sum = call(
        "gather_near", gather_kernel, shape(ROWS, 2 * D, f32), vmem(3), (last_own, near_back, by_two)
    )
    grad_keys, grad_values = call(
        "finish", finish_kernel, (shape(ROWS, D, bf16), shape(ROWS, D, bf16)), vmem(3), (partial_sum, by_eight, by_four)
    )
    return grad_queries, grad_keys, grad_values


def solution(mesh):
    return jax.shard_map(
        local,
        mesh=mesh,
        in_specs=(
            P("ctx", "head"),
            P("ctx", "head"),
            P("ctx", "head"),
            P("ctx", "head"),
            P("head", None),
            P(),
        ),
        out_specs=(P("ctx", "head"), P("ctx", "head"), P("ctx", "head")),
        check_vma=False,
    )
```

```python
import functools

import jax
import jax.numpy as jnp
from jax import lax
from jax.experimental import pallas as pl
from jax.experimental.pallas import tpu as pltpu
from jax.sharding import PartitionSpec as P

D = 128
HEADS = 4
ROWS = 192
LANES = HEADS * ROWS
REACH = 4
SLOTS = REACH + 1
PLANE = 4
BLOCK = 512
MASS, TOP, START, DOT = D, D + 1, D + 2, D + 3
PEAK = D + 8
STATE = PEAK + 16
NEG = -1e30
FLOOR = -1e20
SCALE = D**-0.5
LOG2E = 1.4426950408889634
MIB = 1 << 20
FL = 4 * 10**9
COSTLY = 4 * 10**9


def dot(a, b, ca, cb):
    return lax.dot_general(a, b, (((ca,), (cb,)), ((), ())), preferred_element_type=jnp.float32)


def stack_heads(src, dst):
    for h in range(HEADS):
        dst[h * ROWS : (h + 1) * ROWS, :] = src[:, h * D : (h + 1) * D]


def load_kernel(place_ref, head_ref, len_hbm, q_hbm, w_hbm, q4_ref, bound_ref, w_ref, len_ref, sems):
    head = head_ref[0]
    copies = [pltpu.make_async_copy(len_hbm, len_ref, sems.at[0])]
    sources = (head, source_of(head, 0, True), source_of(head, -2, False), source_of(head, 2, False))
    sources += (source_of(head, -2, True), source_of(head, 2, True), source_of(head, 4, False), source_of(head, 4, True))
    for i, source in enumerate(sources):
        cols = pl.ds(pl.multiple_of(source * BLOCK, BLOCK), BLOCK)
        copies.append(pltpu.make_async_copy(w_hbm.at[:, cols], w_ref.at[:, pl.ds(i * BLOCK, BLOCK)], sems.at[1 + HEADS + i]))
    for h in range(HEADS):
        across, along = pl.ds(h * ROWS, ROWS), pl.ds(h * D, D)
        copies.append(pltpu.make_async_copy(q_hbm.at[:, along], q4_ref.at[across, :], sems.at[1 + h]))
    for copy in copies:
        copy.start()
    lane = lax.broadcasted_iota(jnp.int32, (1, LANES), 1)
    pos = lane + place_ref[0] * ROWS
    for h in range(1, HEADS):
        pos = pos - jnp.where(lane >= h * ROWS, ROWS, 0)
    start = jnp.zeros((1, LANES), jnp.int32)
    end = jnp.int32(0)
    copies[0].wait()
    for d in range(len_ref.shape[0]):
        end = end + len_ref[d]
        start = jnp.where(end <= pos, end, start)
    bound_ref[0:1, :] = pos.astype(jnp.float32)
    bound_ref[1:2, :] = start.astype(jnp.float32)
    for copy in copies[1:]:
        copy.wait()


def stage_kernel(piece_ref, after, out_ref):
    out_ref[...] = piece_ref[...]


def gate_kernel(*refs):
    refs[-1][...] = jnp.zeros(refs[-1].shape, refs[-1].dtype)


def pick_kernel(place_ref, z2_ref, z1_ref, z0_ref, *refs):
    out_ref = refs[-1]
    upper = lax.rem(lax.div(place_ref[0], 2), 2) == 1

    @pl.when(upper)
    def _():
        out_ref[:ROWS, :] = z2_ref[...]
        out_ref[ROWS:, :] = z1_ref[...]

    @pl.when(jnp.logical_not(upper))
    def _():
        out_ref[:ROWS, :] = z1_ref[...]
        out_ref[ROWS:, :] = z0_ref[...]


def join_kernel(z2_ref, z1_ref, z0_ref, side_ref, *refs):
    out_ref = refs[-1]
    parts = (z2_ref[...], side_ref[:ROWS, :], z1_ref[...], side_ref[ROWS:, :], z0_ref[...])
    for m, part in enumerate(parts):
        out_ref[m * ROWS : (m + 1) * ROWS, :] = part


def absorb(block, queries, row, base, start, state, pos=None):
    s = dot(block[:, :D], queries, 1, 1) * (SCALE * LOG2E)
    visible = row >= start - base * ROWS
    if pos is not None:
        visible = visible & (row <= pos - base * ROWS)
    s = jnp.where(visible, s, NEG)
    peak = jnp.maximum(jnp.max(s, axis=0, keepdims=True), FLOOR)
    prob = jnp.exp2(s - peak).astype(jnp.bfloat16)
    mass = jnp.sum(prob.astype(jnp.float32), axis=0, keepdims=True)
    out = dot(block[:, D:], prob, 0, 0)
    if state is None:
        return prob, peak, (out, mass, peak)
    old_out, old_mass, old_peak = state
    top = jnp.maximum(old_peak, peak)
    before, now = jnp.exp2(old_peak - top), jnp.exp2(peak - top)
    return prob, peak, (old_out * before + out * now, old_mass * before + mass * now, top)


def read_state(ref):
    return ref[:D, :], ref[MASS : MASS + 1, :], ref[TOP : TOP + 1, :]


def write_state(ref, state):
    ref[:D, :], ref[MASS : MASS + 1, :], ref[TOP : TOP + 1, :] = state


def put_row(ref, at, value):
    ref[at : at + 1, :] = value


def near_kernel(place_ref, z2_ref, z1_ref, z0_ref, q4_ref, bound_ref, *refs):
    p_ref, st_ref = refs[-2:]
    me = place_ref[0]
    queries = q4_ref[...]
    row = lax.broadcasted_iota(jnp.int32, (ROWS, LANES), 0)
    pos, start = bound_ref[0:1, :].astype(jnp.int32), bound_ref[1:2, :].astype(jnp.int32)
    state = None
    for i, ref in ((2, z0_ref), (1, z1_ref), (0, z2_ref)):
        at = pos if i == 2 else None
        prob, peak, state = absorb(ref[...], queries, row, me - PLANE * (2 - i), start, state, at)
        p_ref[i * ROWS : (i + 1) * ROWS, :] = prob
        put_row(st_ref, PEAK + 2 * i, peak)
    write_state(st_ref, state)
    put_row(st_ref, START, bound_ref[1:2, :])


def project_kernel(*refs):
    pieces, (w_ref, after, acc_ref) = refs[:6], refs[6:]
    acc = None
    for i, piece in enumerate(pieces):
        part = dot(piece[...], w_ref[:, i * BLOCK : (i + 1) * BLOCK], 1, 1)
        acc = part if acc is None else acc + part
    acc_ref[...] = acc


def last_projection(far_ref, piece_ref, w_ref, acc_ref, g4_ref, gt_ref):
    acc = acc_ref[...] + dot(far_ref[...], w_ref[:, 6 * BLOCK : 7 * BLOCK], 1, 1)
    acc = (acc + dot(piece_ref[...], w_ref[:, 7 * BLOCK :], 1, 1)).astype(jnp.bfloat16)
    for h in range(HEADS):
        g4_ref[h * ROWS : (h + 1) * ROWS, :] = acc[:, h * D : (h + 1) * D]
    gt_ref[...] = jnp.transpose(g4_ref[...].astype(jnp.float32))


def rows(i):
    return pl.ds(pl.multiple_of(i * ROWS, ROWS), ROWS)


def source_of(head, by, flip):
    at = lax.rem(head + by + 8, 8)
    return at + 1 - 2 * lax.rem(at, 2) if flip else at


def middle_kernel(place_ref, own_ref, q4_ref, st_in_ref, p_ref, st_ref):
    queries = q4_ref[...]
    row = lax.broadcasted_iota(jnp.int32, (ROWS, LANES), 0)
    start = st_in_ref[START : START + 1, :].astype(jnp.int32)
    state = read_state(st_in_ref)
    st_ref[PEAK:, :] = st_in_ref[PEAK:, :]
    for i in range(2):
        slot = 2 * i + 1
        block = own_ref[slot * ROWS : (slot + 1) * ROWS, :]
        prob, peak, state = absorb(block, queries, row, place_ref[0] + 2 * (slot - REACH), start, state)
        p_ref[i * ROWS : (i + 1) * ROWS, :] = prob
        put_row(st_ref, PEAK + slot, peak)
    write_state(st_ref, state)
    put_row(st_ref, START, st_in_ref[START : START + 1, :])


def across_kernel(place_ref, par_ref, q4_ref, gt_ref, st_in_ref, p_ref, st_ref):
    me = place_ref[0]
    core = lax.rem(me, 2)
    chip = me - core
    queries = q4_ref[...]
    row = lax.broadcasted_iota(jnp.int32, (ROWS, LANES), 0)
    start = st_in_ref[START : START + 1, :].astype(jnp.int32)
    state = read_state(st_in_ref)
    peaks = [st_in_ref[PEAK + m : PEAK + m + 1, :] for m in range(SLOTS)]
    for i in range(REACH):
        slot = i + core
        prob, peak, state = absorb(par_ref[rows(slot), :], queries, row, chip + 1 - core + 2 * (slot - REACH), start, state)
        p_ref[i * ROWS : (i + 1) * ROWS, :] = prob
        peaks.append(peak)
    out, mass, top = state
    put_row(st_ref, DOT, jnp.sum(gt_ref[...] * out, axis=0, keepdims=True) / mass)
    log_total = top + jnp.log2(mass)
    for i, peak in enumerate(peaks):
        put_row(st_ref, PEAK + i, jnp.exp2(peak - log_total))


def back_block(block, prob, share, g4, q4, rd):
    prob = prob.astype(jnp.float32) * share
    dprob = dot(block[:, D:], g4, 1, 1)
    ds = (prob * (dprob - rd)).astype(jnp.bfloat16)
    dv = dot(prob.astype(jnp.bfloat16), g4, 1, 0)
    dk = dot(ds, q4, 1, 0) * SCALE
    dq = dot(block[:, :D], ds, 0, 0)
    return dk, dv, dq


def put(out_ref, slot, dk, dv):
    at = pl.ds(pl.multiple_of(slot * ROWS, ROWS), ROWS)
    out_ref[at, :D] = dk.astype(out_ref.dtype)
    out_ref[at, D:] = dv.astype(out_ref.dtype)


def cross_step(slot, core, par_ref, p_ref, st_ref, g4, q4_ref, rd):
    share = st_ref[pl.ds(PEAK + SLOTS + slot - core, 1), :]
    return back_block(par_ref[rows(slot), :], p_ref[rows(slot - core), :], share, g4, q4_ref[...], rd)


def cross_far(place_ref, q4_ref, par_ref, p_ref, g_ref, st_in_ref, out_ref, st_ref):
    core = lax.rem(place_ref[0], 2)
    g4 = g_ref[...]
    rd = st_in_ref[DOT : DOT + 1, :]
    st_ref[DOT : DOT + 1, :] = rd
    st_ref[PEAK:, :] = st_in_ref[PEAK:, :]
    dk, dv, dq = cross_step(1, core, par_ref, p_ref, st_ref, g4, q4_ref, rd)
    put(out_ref, 1, dk, dv)
    st_ref[:D, :] = dq

    @pl.when(core == 1)
    def _():
        out_ref[:ROWS, :] = jnp.zeros((ROWS, 2 * D), out_ref.dtype)

    @pl.when(core == 0)
    def _():
        dk, dv, dq = cross_step(0, core, par_ref, p_ref, st_ref, g4, q4_ref, rd)
        put(out_ref, 0, dk, dv)
        st_ref[:D, :] += dq


def cross_near(place_ref, q4_ref, par_ref, p_ref, g_ref, st_in_ref, out_ref, st_ref):
    core = lax.rem(place_ref[0], 2)
    g4 = g_ref[...]
    rd = st_in_ref[DOT : DOT + 1, :]
    st_ref[DOT : DOT + 1, :] = rd
    st_ref[PEAK:, :] = st_in_ref[PEAK:, :]
    total = st_in_ref[:D, :]
    for slot in (2, 3):
        dk, dv, dq = cross_step(slot, core, par_ref, p_ref, st_ref, g4, q4_ref, rd)
        put(out_ref, slot - 2, dk, dv)
        total = total + dq
    st_ref[:D, :] = total

    @pl.when(core == 0)
    def _():
        out_ref[2 * ROWS :, :] = jnp.zeros((ROWS, 2 * D), out_ref.dtype)

    @pl.when(core == 1)
    def _():
        dk, dv, dq = cross_step(4, core, par_ref, p_ref, st_ref, g4, q4_ref, rd)
        put(out_ref, 2, dk, dv)
        st_ref[:D, :] += dq


def own_kernel(slots, q4_ref, own_ref, near_ref, side_ref, g_ref, st_in_ref, *refs):
    out_ref, st_ref = refs[-2:]
    g4 = g_ref[...]
    rd = st_in_ref[DOT : DOT + 1, :]
    total = st_in_ref[:D, :]
    for i, slot in enumerate(slots):
        at = slot // 2 * ROWS
        prob = (side_ref if slot % 2 else near_ref)[at : at + ROWS, :]
        share = st_in_ref[PEAK + slot : PEAK + slot + 1, :]
        dk, dv, dq = back_block(own_ref[slot * ROWS : (slot + 1) * ROWS, :], prob, share, g4, q4_ref[...], rd)
        out_ref[i * ROWS : (i + 1) * ROWS, :D] = dk
        out_ref[i * ROWS : (i + 1) * ROWS, D:] = dv
        total = total + dq
    if slots[-1] < REACH:
        st_ref[DOT : DOT + 1, :] = rd
        st_ref[PEAK:, :] = st_in_ref[PEAK:, :]
        st_ref[:D, :] = total
    else:
        dq = jnp.transpose(total) * SCALE
        for h in range(HEADS):
            st_ref[:, h * D : (h + 1) * D] = dq[h * ROWS : (h + 1) * ROWS, :].astype(jnp.bfloat16)


def is_upper(place_ref):
    return (lax.rem(lax.div(place_ref[0], 2), 2) == 1).astype(jnp.float32)


def settle_kernel(own_ref, back_ref, keep_ref, send_ref):
    both = own_ref[...] + back_ref[: 2 * ROWS, :].astype(jnp.float32)
    keep_ref[...] = both[:ROWS]
    send_ref[...] = both[ROWS:].astype(jnp.bfloat16)


def relay_kernel(place_ref, far_ref, near_ref, side_ref, eight_ref, four_ref):
    side = side_ref[...].astype(jnp.float32)
    upper = is_upper(place_ref)
    eight_ref[...] = (far_ref[...] + side * upper).astype(jnp.bfloat16)
    four_ref[...] = (near_ref[...] + side * (1 - upper)).astype(jnp.bfloat16)


def gather_kernel(own_ref, back_ref, two_ref, out_ref):
    total = own_ref[...] + back_ref[2 * ROWS :, :].astype(jnp.float32)
    out_ref[...] = total + two_ref[...].astype(jnp.float32)


def finish_kernel(sum_ref, eight_ref, four_ref, k_ref, v_ref):
    total = sum_ref[...] + four_ref[...].astype(jnp.float32) + eight_ref[...].astype(jnp.float32)
    total = total.astype(jnp.bfloat16)
    k_ref[...] = total[:, :D]
    v_ref[...] = total[:, D:]


def vmem(n):
    return [pl.BlockSpec(memory_space=pltpu.VMEM)] * n


def smem(n):
    return [pl.BlockSpec(memory_space=pltpu.SMEM)] * n


def hbm(n):
    return [pl.BlockSpec(memory_space=pltpu.HBM)] * n


def token(n):
    return [pl.BlockSpec(memory_space=pl.ANY)] * n


def moved(x, axis, to):
    return lax.ppermute(x, axis, [(i, to(i)) for i in range(lax.axis_size(axis))])


def turned(x, axis, by):
    count = lax.axis_size(axis)
    return moved(x, axis, lambda i: (i + by) % count)


def shape(rows, cols, dtype):
    return jax.ShapeDtypeStruct((rows, cols), dtype)


def call(name, kernel, outs, ins, args, scratch=(), flops=1):
    one = not isinstance(outs, tuple)
    return pl.pallas_call(
        kernel,
        out_shape=outs,
        in_specs=ins,
        out_specs=vmem(1)[0] if one else tuple(vmem(len(outs))),
        scratch_shapes=list(scratch),
        compiler_params=pltpu.CompilerParams(vmem_limit_bytes=8 * MIB),
        cost_estimate=pl.CostEstimate(flops=flops, bytes_accessed=1, transcendentals=0),
        name=name,
    )(*args)


def local(queries, keys, values, grad_out, out_weight, lengths):
    bf16, f32 = jnp.bfloat16, jnp.float32
    place = lax.axis_index("ctx").astype(jnp.int32).reshape(1)
    head = lax.axis_index("head").astype(jnp.int32).reshape(1)
    dma = pltpu.SemaphoreType.DMA
    pinned = functools.partial(pltpu.with_memory_space_constraint, memory_space=pltpu.HBM)
    state = shape(STATE, LANES, f32)

    first = moved(grad_out, "head", lambda i: i ^ 1)
    right = turned(grad_out, "head", 2)
    left = turned(grad_out, "head", -2)
    kv = jnp.pad(keys, ((0, 0), (0, D))) + jnp.pad(values, ((0, 0), (D, 0)))
    z2 = turned(kv, "ctx", 2 * PLANE)
    z1 = turned(kv, "ctx", PLANE)
    q4, bound, weight = call(
        "load",
        load_kernel,
        (shape(LANES, D, bf16), shape(8, LANES, f32), shape(HEADS * D, 8 * BLOCK, bf16)),
        smem(2) + hbm(3),
        (place, head, pinned(lengths), pinned(queries), pinned(out_weight)),
        [pltpu.SMEM((lengths.shape[0],), jnp.int32), dma((9 + HEADS,))],
    )
    other = call("stage", stage_kernel, shape(ROWS, BLOCK, bf16), vmem(1) + token(1), (first, q4))
    other_right = turned(other, "head", 2)
    other_left = turned(other, "head", -2)
    far = turned(right, "head", 2)
    other_far = turned(other_left, "head", -2)

    gate = call("gate", gate_kernel, shape(8, D, f32), token(4), (other, right, left, q4))
    picked = call(
        "pick_side", pick_kernel, shape(2 * ROWS, 2 * D, bf16), smem(1) + vmem(3) + token(1), (place, z2, z1, kv, gate)
    )
    side = moved(picked, "ctx", lambda i: i ^ 2)
    p_near, st = call(
        "near",
        near_kernel,
        (shape(3 * ROWS, LANES, bf16), state),
        smem(1) + vmem(5) + token(3),
        (place, z2, z1, kv, q4, bound, picked, other_right, other_left),
    )
    own = call("join_slots", join_kernel, shape(SLOTS * ROWS, 2 * D, bf16), vmem(4) + token(1), (z2, z1, kv, side, st))
    par = moved(own, "ctx", lambda i: i ^ 1)

    p_side, st = call(
        "middle",
        middle_kernel,
        (shape(2 * ROWS, LANES, bf16), state),
        smem(1) + vmem(3),
        (place, own, q4, st),
    )
    early = call(
        "project",
        project_kernel,
        shape(ROWS, HEADS * D, f32),
        vmem(7) + token(1),
        (grad_out, other, right, left, other_right, other_left, weight, st),
    )
    g4, gt = call(
        "last_projection",
        last_projection,
        (shape(LANES, D, bf16), shape(D, LANES, f32)),
        vmem(4),
        (far, other_far, weight, early),
        flops=COSTLY,
    )
    p_par, st = call(
        "across", across_kernel, (shape(REACH * ROWS, LANES, bf16), state), smem(1) + vmem(4), (place, par, q4, gt, st)
    )

    far_cross, st = call(
        "cross_far", cross_far, (shape(2 * ROWS, 2 * D, bf16), state), smem(1) + vmem(5), (place, q4, par, p_par, g4, st)
    )
    far_back = moved(far_cross, "ctx", lambda i: i ^ 1)
    near_cross, st = call(
        "cross_near", cross_near, (shape(3 * ROWS, 2 * D, bf16), state), smem(1) + vmem(5), (place, q4, par, p_par, g4, st), flops=FL
    )
    near_back = moved(near_cross, "ctx", lambda i: i ^ 1)
    far_own, st = call(
        "own_far",
        functools.partial(own_kernel, (0, 1)),
        (shape(2 * ROWS, 2 * D, f32), state),
        vmem(6),
        (q4, own, p_near, p_side, g4, st),
        flops=FL,
    )
    far_keep, far_side = call(
        "settle_far", settle_kernel, (shape(ROWS, 2 * D, f32), shape(ROWS, 2 * D, bf16)), vmem(2), (far_own, far_back)
    )
    far_side = moved(far_side, "ctx", lambda i: i ^ 2)
    near_own, st = call(
        "own_near",
        functools.partial(own_kernel, (2, 3)),
        (shape(2 * ROWS, 2 * D, f32), state),
        vmem(6) + token(1),
        (q4, own, p_near, p_side, g4, st, far_keep),
        flops=FL,
    )
    near_keep, by_two = call(
        "settle_near", settle_kernel, (shape(ROWS, 2 * D, f32), shape(ROWS, 2 * D, bf16)), vmem(2), (near_own, near_back)
    )
    by_two = turned(by_two, "ctx", -2)
    to_eight, to_four = call(
        "relay",
        relay_kernel,
        (shape(ROWS, 2 * D, bf16), shape(ROWS, 2 * D, bf16)),
        smem(1) + vmem(3),
        (place, far_keep, near_keep, far_side),
    )
    by_eight = turned(to_eight, "ctx", -2 * PLANE)
    by_four = turned(to_four, "ctx", -PLANE)
    last_own, grad_queries = call(
        "own_last",
        functools.partial(own_kernel, (4,)),
        (shape(ROWS, 2 * D, f32), shape(ROWS, HEADS * D, bf16)),
        vmem(6) + token(2),
        (q4, own, p_near, p_side, g4, st, to_eight, by_two),
        flops=COSTLY,
    )
    partial_sum = call(
        "gather_near", gather_kernel, shape(ROWS, 2 * D, f32), vmem(3), (last_own, near_back, by_two)
    )
    grad_keys, grad_values = call(
        "finish", finish_kernel, (shape(ROWS, D, bf16), shape(ROWS, D, bf16)), vmem(3), (partial_sum, by_eight, by_four)
    )
    return grad_queries, grad_keys, grad_values


def solution(mesh):
    return jax.shard_map(
        local,
        mesh=mesh,
        in_specs=(
            P("ctx", "head"),
            P("ctx", "head"),
            P("ctx", "head"),
            P("ctx", "head"),
            P("head", None),
            P(),
        ),
        out_specs=(P("ctx", "head"), P("ctx", "head"), P("ctx", "head")),
        check_vma=False,
    )
```

```python
import functools

import jax
import jax.numpy as jnp
from jax import lax
from jax.experimental import pallas as pl
from jax.experimental.pallas import tpu as pltpu
from jax.sharding import PartitionSpec as P

D = 128
HEADS = 4
ROWS = 192
LANES = HEADS * ROWS
REACH = 4
SLOTS = REACH + 1
PLANE = 4
BLOCK = 512
MASS, TOP, START, DOT = D, D + 1, D + 2, D + 3
PEAK = D + 8
STATE = PEAK + 16
NEG = -1e30
FLOOR = -1e20
SCALE = D**-0.5
LOG2E = 1.4426950408889634
MIB = 1 << 20
FL = 4 * 10**9
COSTLY = 4 * 10**9


def dot(a, b, ca, cb):
    return lax.dot_general(a, b, (((ca,), (cb,)), ((), ())), preferred_element_type=jnp.float32)


def stack_heads(src, dst):
    for h in range(HEADS):
        dst[h * ROWS : (h + 1) * ROWS, :] = src[:, h * D : (h + 1) * D]


def load_kernel(place_ref, head_ref, len_hbm, q_hbm, w_hbm, q4_ref, bound_ref, w_ref, len_ref, sems):
    head = head_ref[0]
    copies = [pltpu.make_async_copy(len_hbm, len_ref, sems.at[0])]
    sources = (head, source_of(head, 0, True), source_of(head, -2, False), source_of(head, 2, False))
    sources += (source_of(head, -2, True), source_of(head, 2, True), source_of(head, 4, False), source_of(head, 4, True))
    for i, source in enumerate(sources):
        cols = pl.ds(pl.multiple_of(source * BLOCK, BLOCK), BLOCK)
        copies.append(pltpu.make_async_copy(w_hbm.at[:, cols], w_ref.at[:, pl.ds(i * BLOCK, BLOCK)], sems.at[1 + HEADS + i]))
    for h in range(HEADS):
        across, along = pl.ds(h * ROWS, ROWS), pl.ds(h * D, D)
        copies.append(pltpu.make_async_copy(q_hbm.at[:, along], q4_ref.at[across, :], sems.at[1 + h]))
    for copy in copies:
        copy.start()
    lane = lax.broadcasted_iota(jnp.int32, (1, LANES), 1)
    pos = lane + place_ref[0] * ROWS
    for h in range(1, HEADS):
        pos = pos - jnp.where(lane >= h * ROWS, ROWS, 0)
    start = jnp.zeros((1, LANES), jnp.int32)
    end = jnp.int32(0)
    copies[0].wait()
    for d in range(len_ref.shape[0]):
        end = end + len_ref[d]
        start = jnp.where(end <= pos, end, start)
    bound_ref[0:1, :] = pos.astype(jnp.float32)
    bound_ref[1:2, :] = start.astype(jnp.float32)
    for copy in copies[1:]:
        copy.wait()


def stage_kernel(piece_ref, after, out_ref):
    out_ref[...] = piece_ref[...]


def gate_kernel(*refs):
    refs[-1][...] = jnp.zeros(refs[-1].shape, refs[-1].dtype)


def pick_kernel(place_ref, z2_ref, z1_ref, z0_ref, *refs):
    out_ref = refs[-1]
    upper = lax.rem(lax.div(place_ref[0], 2), 2) == 1

    @pl.when(upper)
    def _():
        out_ref[:ROWS, :] = z2_ref[...]
        out_ref[ROWS:, :] = z1_ref[...]

    @pl.when(jnp.logical_not(upper))
    def _():
        out_ref[:ROWS, :] = z1_ref[...]
        out_ref[ROWS:, :] = z0_ref[...]


def join_kernel(z2_ref, z1_ref, z0_ref, side_ref, *refs):
    out_ref = refs[-1]
    parts = (z2_ref[...], side_ref[:ROWS, :], z1_ref[...], side_ref[ROWS:, :], z0_ref[...])
    for m, part in enumerate(parts):
        out_ref[m * ROWS : (m + 1) * ROWS, :] = part


def absorb(block, queries, row, base, start, state, pos=None):
    s = dot(block[:, :D], queries, 1, 1) * (SCALE * LOG2E)
    visible = row >= start - base * ROWS
    if pos is not None:
        visible = visible & (row <= pos - base * ROWS)
    s = jnp.where(visible, s, NEG)
    peak = jnp.maximum(jnp.max(s, axis=0, keepdims=True), FLOOR)
    prob = jnp.exp2(s - peak).astype(jnp.bfloat16)
    mass = jnp.sum(prob.astype(jnp.float32), axis=0, keepdims=True)
    out = dot(block[:, D:], prob, 0, 0)
    if state is None:
        return prob, peak, (out, mass, peak)
    old_out, old_mass, old_peak = state
    top = jnp.maximum(old_peak, peak)
    before, now = jnp.exp2(old_peak - top), jnp.exp2(peak - top)
    return prob, peak, (old_out * before + out * now, old_mass * before + mass * now, top)


def read_state(ref):
    return ref[:D, :], ref[MASS : MASS + 1, :], ref[TOP : TOP + 1, :]


def write_state(ref, state):
    ref[:D, :], ref[MASS : MASS + 1, :], ref[TOP : TOP + 1, :] = state


def put_row(ref, at, value):
    ref[at : at + 1, :] = value


def near_kernel(place_ref, z2_ref, z1_ref, z0_ref, q4_ref, bound_ref, *refs):
    p_ref, st_ref = refs[-2:]
    me = place_ref[0]
    queries = q4_ref[...]
    row = lax.broadcasted_iota(jnp.int32, (ROWS, LANES), 0)
    pos, start = bound_ref[0:1, :].astype(jnp.int32), bound_ref[1:2, :].astype(jnp.int32)
    state = None
    for i, ref in ((2, z0_ref), (1, z1_ref), (0, z2_ref)):
        at = pos if i == 2 else None
        prob, peak, state = absorb(ref[...], queries, row, me - PLANE * (2 - i), start, state, at)
        p_ref[i * ROWS : (i + 1) * ROWS, :] = prob
        put_row(st_ref, PEAK + 2 * i, peak)
    write_state(st_ref, state)
    put_row(st_ref, START, bound_ref[1:2, :])


def project_kernel(*refs):
    pieces, (w_ref, after, acc_ref) = refs[:7], refs[7:]
    acc = None
    for i, piece in enumerate(pieces):
        part = dot(piece[...], w_ref[:, i * BLOCK : (i + 1) * BLOCK], 1, 1)
        acc = part if acc is None else acc + part
    acc_ref[...] = acc


def last_projection(piece_ref, w_ref, acc_ref, g4_ref, gt_ref):
    acc = (acc_ref[...] + dot(piece_ref[...], w_ref[:, 7 * BLOCK :], 1, 1)).astype(jnp.bfloat16)
    for h in range(HEADS):
        g4_ref[h * ROWS : (h + 1) * ROWS, :] = acc[:, h * D : (h + 1) * D]
    gt_ref[...] = jnp.transpose(g4_ref[...].astype(jnp.float32))


def rows(i):
    return pl.ds(pl.multiple_of(i * ROWS, ROWS), ROWS)


def source_of(head, by, flip):
    at = lax.rem(head + by + 8, 8)
    return at + 1 - 2 * lax.rem(at, 2) if flip else at


def middle_kernel(place_ref, own_ref, q4_ref, st_in_ref, p_ref, st_ref):
    queries = q4_ref[...]
    row = lax.broadcasted_iota(jnp.int32, (ROWS, LANES), 0)
    start = st_in_ref[START : START + 1, :].astype(jnp.int32)
    state = read_state(st_in_ref)
    st_ref[PEAK:, :] = st_in_ref[PEAK:, :]
    for i in range(2):
        slot = 2 * i + 1
        block = own_ref[slot * ROWS : (slot + 1) * ROWS, :]
        prob, peak, state = absorb(block, queries, row, place_ref[0] + 2 * (slot - REACH), start, state)
        p_ref[i * ROWS : (i + 1) * ROWS, :] = prob
        put_row(st_ref, PEAK + slot, peak)
    write_state(st_ref, state)
    put_row(st_ref, START, st_in_ref[START : START + 1, :])


def across_kernel(place_ref, par_ref, q4_ref, gt_ref, st_in_ref, p_ref, st_ref):
    me = place_ref[0]
    core = lax.rem(me, 2)
    chip = me - core
    queries = q4_ref[...]
    row = lax.broadcasted_iota(jnp.int32, (ROWS, LANES), 0)
    start = st_in_ref[START : START + 1, :].astype(jnp.int32)
    state = read_state(st_in_ref)
    peaks = [st_in_ref[PEAK + m : PEAK + m + 1, :] for m in range(SLOTS)]
    for i in range(REACH):
        slot = i + core
        prob, peak, state = absorb(par_ref[rows(slot), :], queries, row, chip + 1 - core + 2 * (slot - REACH), start, state)
        p_ref[i * ROWS : (i + 1) * ROWS, :] = prob
        peaks.append(peak)
    out, mass, top = state
    put_row(st_ref, DOT, jnp.sum(gt_ref[...] * out, axis=0, keepdims=True) / mass)
    log_total = top + jnp.log2(mass)
    for i, peak in enumerate(peaks):
        put_row(st_ref, PEAK + i, jnp.exp2(peak - log_total))


def back_block(block, prob, share, g4, q4, rd):
    prob = prob.astype(jnp.float32) * share
    dprob = dot(block[:, D:], g4, 1, 1)
    ds = (prob * (dprob - rd)).astype(jnp.bfloat16)
    dv = dot(prob.astype(jnp.bfloat16), g4, 1, 0)
    dk = dot(ds, q4, 1, 0) * SCALE
    dq = dot(block[:, :D], ds, 0, 0)
    return dk, dv, dq


def put(out_ref, slot, dk, dv):
    at = pl.ds(pl.multiple_of(slot * ROWS, ROWS), ROWS)
    out_ref[at, :D] = dk.astype(out_ref.dtype)
    out_ref[at, D:] = dv.astype(out_ref.dtype)


def cross_step(slot, core, par_ref, p_ref, st_ref, g4, q4_ref, rd):
    share = st_ref[pl.ds(PEAK + SLOTS + slot - core, 1), :]
    return back_block(par_ref[rows(slot), :], p_ref[rows(slot - core), :], share, g4, q4_ref[...], rd)


def cross_far(place_ref, q4_ref, par_ref, p_ref, g_ref, st_in_ref, out_ref, st_ref):
    core = lax.rem(place_ref[0], 2)
    g4 = g_ref[...]
    rd = st_in_ref[DOT : DOT + 1, :]
    st_ref[DOT : DOT + 1, :] = rd
    st_ref[PEAK:, :] = st_in_ref[PEAK:, :]
    dk, dv, dq = cross_step(1, core, par_ref, p_ref, st_ref, g4, q4_ref, rd)
    put(out_ref, 1, dk, dv)
    st_ref[:D, :] = dq

    @pl.when(core == 1)
    def _():
        out_ref[:ROWS, :] = jnp.zeros((ROWS, 2 * D), out_ref.dtype)

    @pl.when(core == 0)
    def _():
        dk, dv, dq = cross_step(0, core, par_ref, p_ref, st_ref, g4, q4_ref, rd)
        put(out_ref, 0, dk, dv)
        st_ref[:D, :] += dq


def cross_near(place_ref, q4_ref, par_ref, p_ref, g_ref, st_in_ref, out_ref, st_ref):
    core = lax.rem(place_ref[0], 2)
    g4 = g_ref[...]
    rd = st_in_ref[DOT : DOT + 1, :]
    st_ref[DOT : DOT + 1, :] = rd
    st_ref[PEAK:, :] = st_in_ref[PEAK:, :]
    total = st_in_ref[:D, :]
    for slot in (2, 3):
        dk, dv, dq = cross_step(slot, core, par_ref, p_ref, st_ref, g4, q4_ref, rd)
        put(out_ref, slot - 2, dk, dv)
        total = total + dq
    st_ref[:D, :] = total

    @pl.when(core == 0)
    def _():
        out_ref[2 * ROWS :, :] = jnp.zeros((ROWS, 2 * D), out_ref.dtype)

    @pl.when(core == 1)
    def _():
        dk, dv, dq = cross_step(4, core, par_ref, p_ref, st_ref, g4, q4_ref, rd)
        put(out_ref, 2, dk, dv)
        st_ref[:D, :] += dq


def own_kernel(slots, q4_ref, own_ref, near_ref, side_ref, g_ref, st_in_ref, *refs):
    out_ref, st_ref = refs[-2:]
    g4 = g_ref[...]
    rd = st_in_ref[DOT : DOT + 1, :]
    total = st_in_ref[:D, :]
    for i, slot in enumerate(slots):
        at = slot // 2 * ROWS
        prob = (side_ref if slot % 2 else near_ref)[at : at + ROWS, :]
        share = st_in_ref[PEAK + slot : PEAK + slot + 1, :]
        dk, dv, dq = back_block(own_ref[slot * ROWS : (slot + 1) * ROWS, :], prob, share, g4, q4_ref[...], rd)
        out_ref[i * ROWS : (i + 1) * ROWS, :D] = dk
        out_ref[i * ROWS : (i + 1) * ROWS, D:] = dv
        total = total + dq
    if slots[-1] < REACH:
        st_ref[DOT : DOT + 1, :] = rd
        st_ref[PEAK:, :] = st_in_ref[PEAK:, :]
        st_ref[:D, :] = total
    else:
        dq = jnp.transpose(total) * SCALE
        for h in range(HEADS):
            st_ref[:, h * D : (h + 1) * D] = dq[h * ROWS : (h + 1) * ROWS, :].astype(jnp.bfloat16)


def is_upper(place_ref):
    return (lax.rem(lax.div(place_ref[0], 2), 2) == 1).astype(jnp.float32)


def settle_kernel(own_ref, back_ref, keep_ref, send_ref):
    both = own_ref[...] + back_ref[: 2 * ROWS, :].astype(jnp.float32)
    keep_ref[...] = both[:ROWS]
    send_ref[...] = both[ROWS:].astype(jnp.bfloat16)


def relay_kernel(place_ref, far_ref, near_ref, side_ref, eight_ref, four_ref):
    side = side_ref[...].astype(jnp.float32)
    upper = is_upper(place_ref)
    eight_ref[...] = (far_ref[...] + side * upper).astype(jnp.bfloat16)
    four_ref[...] = (near_ref[...] + side * (1 - upper)).astype(jnp.bfloat16)


def gather_kernel(own_ref, back_ref, two_ref, out_ref):
    total = own_ref[...] + back_ref[2 * ROWS :, :].astype(jnp.float32)
    out_ref[...] = total + two_ref[...].astype(jnp.float32)


def finish_kernel(sum_ref, four_ref, eight_ref, k_ref, v_ref):
    total = sum_ref[...] + four_ref[...].astype(jnp.float32) + eight_ref[...].astype(jnp.float32)
    total = total.astype(jnp.bfloat16)
    k_ref[...] = total[:, :D]
    v_ref[...] = total[:, D:]


def vmem(n):
    return [pl.BlockSpec(memory_space=pltpu.VMEM)] * n


def smem(n):
    return [pl.BlockSpec(memory_space=pltpu.SMEM)] * n


def hbm(n):
    return [pl.BlockSpec(memory_space=pltpu.HBM)] * n


def token(n):
    return [pl.BlockSpec(memory_space=pl.ANY)] * n


def moved(x, axis, to):
    return lax.ppermute(x, axis, [(i, to(i)) for i in range(lax.axis_size(axis))])


def turned(x, axis, by):
    count = lax.axis_size(axis)
    return moved(x, axis, lambda i: (i + by) % count)


def shape(rows, cols, dtype):
    return jax.ShapeDtypeStruct((rows, cols), dtype)


def call(name, kernel, outs, ins, args, scratch=(), flops=1):
    one = not isinstance(outs, tuple)
    return pl.pallas_call(
        kernel,
        out_shape=outs,
        in_specs=ins,
        out_specs=vmem(1)[0] if one else tuple(vmem(len(outs))),
        scratch_shapes=list(scratch),
        compiler_params=pltpu.CompilerParams(vmem_limit_bytes=8 * MIB),
        cost_estimate=pl.CostEstimate(flops=flops, bytes_accessed=1, transcendentals=0),
        name=name,
    )(*args)


def local(queries, keys, values, grad_out, out_weight, lengths):
    bf16, f32 = jnp.bfloat16, jnp.float32
    place = lax.axis_index("ctx").astype(jnp.int32).reshape(1)
    head = lax.axis_index("head").astype(jnp.int32).reshape(1)
    dma = pltpu.SemaphoreType.DMA
    pinned = functools.partial(pltpu.with_memory_space_constraint, memory_space=pltpu.HBM)
    state = shape(STATE, LANES, f32)

    first = moved(grad_out, "head", lambda i: i ^ 1)
    right = turned(grad_out, "head", 2)
    left = turned(grad_out, "head", -2)
    kv = jnp.pad(keys, ((0, 0), (0, D))) + jnp.pad(values, ((0, 0), (D, 0)))
    z2 = turned(kv, "ctx", 2 * PLANE)
    z1 = turned(kv, "ctx", PLANE)
    q4, bound, weight = call(
        "load",
        load_kernel,
        (shape(LANES, D, bf16), shape(8, LANES, f32), shape(HEADS * D, 8 * BLOCK, bf16)),
        smem(2) + hbm(3),
        (place, head, pinned(lengths), pinned(queries), pinned(out_weight)),
        [pltpu.SMEM((lengths.shape[0],), jnp.int32), dma((9 + HEADS,))],
    )
    other = call("stage", stage_kernel, shape(ROWS, BLOCK, bf16), vmem(1) + token(1), (first, q4))
    other_right = turned(other, "head", 2)
    other_left = turned(other, "head", -2)
    far = turned(right, "head", 2)
    other_far = turned(other_left, "head", -2)

    gate = call("gate", gate_kernel, shape(8, D, f32), token(4), (other, right, left, q4))
    picked = call(
        "pick_side", pick_kernel, shape(2 * ROWS, 2 * D, bf16), smem(1) + vmem(3) + token(1), (place, z2, z1, kv, gate)
    )
    side = moved(picked, "ctx", lambda i: i ^ 2)
    p_near, st = call(
        "near",
        near_kernel,
        (shape(3 * ROWS, LANES, bf16), state),
        smem(1) + vmem(5) + token(3),
        (place, z2, z1, kv, q4, bound, picked, other_right, other_left),
    )
    own = call("join_slots", join_kernel, shape(SLOTS * ROWS, 2 * D, bf16), vmem(4) + token(1), (z2, z1, kv, side, st))
    par = moved(own, "ctx", lambda i: i ^ 1)

    p_side, st = call(
        "middle",
        middle_kernel,
        (shape(2 * ROWS, LANES, bf16), state),
        smem(1) + vmem(3),
        (place, own, q4, st),
    )
    early = call(
        "project",
        project_kernel,
        shape(ROWS, HEADS * D, f32),
        vmem(8) + token(1),
        (grad_out, other, right, left, other_right, other_left, far, weight, st),
    )
    g4, gt = call(
        "last_projection",
        last_projection,
        (shape(LANES, D, bf16), shape(D, LANES, f32)),
        vmem(3),
        (other_far, weight, early),
        flops=COSTLY,
    )
    p_par, st = call(
        "across", across_kernel, (shape(REACH * ROWS, LANES, bf16), state), smem(1) + vmem(4), (place, par, q4, gt, st)
    )

    far_cross, st = call(
        "cross_far", cross_far, (shape(2 * ROWS, 2 * D, bf16), state), smem(1) + vmem(5), (place, q4, par, p_par, g4, st)
    )
    far_back = moved(far_cross, "ctx", lambda i: i ^ 1)
    near_cross, st = call(
        "cross_near", cross_near, (shape(3 * ROWS, 2 * D, bf16), state), smem(1) + vmem(5), (place, q4, par, p_par, g4, st), flops=FL
    )
    near_back = moved(near_cross, "ctx", lambda i: i ^ 1)
    far_own, st = call(
        "own_far",
        functools.partial(own_kernel, (0, 1)),
        (shape(2 * ROWS, 2 * D, f32), state),
        vmem(6),
        (q4, own, p_near, p_side, g4, st),
        flops=FL,
    )
    far_keep, far_side = call(
        "settle_far", settle_kernel, (shape(ROWS, 2 * D, f32), shape(ROWS, 2 * D, bf16)), vmem(2), (far_own, far_back)
    )
    far_side = moved(far_side, "ctx", lambda i: i ^ 2)
    near_own, st = call(
        "own_near",
        functools.partial(own_kernel, (2, 3)),
        (shape(2 * ROWS, 2 * D, f32), state),
        vmem(6) + token(1),
        (q4, own, p_near, p_side, g4, st, far_keep),
        flops=FL,
    )
    near_keep, by_two = call(
        "settle_near", settle_kernel, (shape(ROWS, 2 * D, f32), shape(ROWS, 2 * D, bf16)), vmem(2), (near_own, near_back)
    )
    by_two = turned(by_two, "ctx", -2)
    to_eight, to_four = call(
        "relay",
        relay_kernel,
        (shape(ROWS, 2 * D, bf16), shape(ROWS, 2 * D, bf16)),
        smem(1) + vmem(3),
        (place, far_keep, near_keep, far_side),
    )
    by_eight = turned(to_eight, "ctx", -2 * PLANE)
    by_four = turned(to_four, "ctx", -PLANE)
    last_own, grad_queries = call(
        "own_last",
        functools.partial(own_kernel, (4,)),
        (shape(ROWS, 2 * D, f32), shape(ROWS, HEADS * D, bf16)),
        vmem(6) + token(2),
        (q4, own, p_near, p_side, g4, st, to_eight, by_two),
        flops=COSTLY,
    )
    partial_sum = call(
        "gather_near", gather_kernel, shape(ROWS, 2 * D, f32), vmem(3), (last_own, near_back, by_two)
    )
    grad_keys, grad_values = call(
        "finish", finish_kernel, (shape(ROWS, D, bf16), shape(ROWS, D, bf16)), vmem(3), (partial_sum, by_four, by_eight)
    )
    return grad_queries, grad_keys, grad_values


def solution(mesh):
    return jax.shard_map(
        local,
        mesh=mesh,
        in_specs=(
            P("ctx", "head"),
            P("ctx", "head"),
            P("ctx", "head"),
            P("ctx", "head"),
            P("head", None),
            P(),
        ),
        out_specs=(P("ctx", "head"), P("ctx", "head"), P("ctx", "head")),
        check_vma=False,
    )
```

```python
import functools

import jax
import jax.numpy as jnp
from jax import lax
from jax.experimental import pallas as pl
from jax.experimental.pallas import tpu as pltpu
from jax.sharding import PartitionSpec as P

D = 128
HEADS = 4
ROWS = 192
LANES = HEADS * ROWS
REACH = 4
SLOTS = REACH + 1
PLANE = 4
BLOCK = 512
MASS, TOP, START, DOT = D, D + 1, D + 2, D + 3
PEAK = D + 8
STATE = PEAK + 16
NEG = -1e30
FLOOR = -1e20
SCALE = D**-0.5
LOG2E = 1.4426950408889634
MIB = 1 << 20
FL = 4 * 10**9
COSTLY = 4 * 10**9


def dot(a, b, ca, cb):
    return lax.dot_general(a, b, (((ca,), (cb,)), ((), ())), preferred_element_type=jnp.float32)


def stack_heads(src, dst):
    for h in range(HEADS):
        dst[h * ROWS : (h + 1) * ROWS, :] = src[:, h * D : (h + 1) * D]


def load_kernel(place_ref, head_ref, len_hbm, q_hbm, w_hbm, q4_ref, bound_ref, w_ref, len_ref, sems):
    head = head_ref[0]
    copies = [pltpu.make_async_copy(len_hbm, len_ref, sems.at[0])]
    sources = (head, source_of(head, 0, True), source_of(head, -2, False), source_of(head, 2, False))
    sources += (source_of(head, -2, True), source_of(head, 2, True), source_of(head, 4, False), source_of(head, 4, True))
    for i, source in enumerate(sources):
        cols = pl.ds(pl.multiple_of(source * BLOCK, BLOCK), BLOCK)
        copies.append(pltpu.make_async_copy(w_hbm.at[:, cols], w_ref.at[:, pl.ds(i * BLOCK, BLOCK)], sems.at[1 + HEADS + i]))
    for h in range(HEADS):
        across, along = pl.ds(h * ROWS, ROWS), pl.ds(h * D, D)
        copies.append(pltpu.make_async_copy(q_hbm.at[:, along], q4_ref.at[across, :], sems.at[1 + h]))
    for copy in copies:
        copy.start()
    lane = lax.broadcasted_iota(jnp.int32, (1, LANES), 1)
    pos = lane + place_ref[0] * ROWS
    for h in range(1, HEADS):
        pos = pos - jnp.where(lane >= h * ROWS, ROWS, 0)
    start = jnp.zeros((1, LANES), jnp.int32)
    end = jnp.int32(0)
    copies[0].wait()
    for d in range(len_ref.shape[0]):
        end = end + len_ref[d]
        start = jnp.where(end <= pos, end, start)
    bound_ref[0:1, :] = pos.astype(jnp.float32)
    bound_ref[1:2, :] = start.astype(jnp.float32)
    for copy in copies[1:]:
        copy.wait()


def pack_kernel(k_hbm, v_hbm, out_ref, sems):
    first = pltpu.make_async_copy(k_hbm, out_ref.at[:, :D], sems.at[0])
    second = pltpu.make_async_copy(v_hbm, out_ref.at[:, D:], sems.at[1])
    first.start()
    second.start()
    first.wait()
    second.wait()


def stage_kernel(piece_ref, after, out_ref):
    out_ref[...] = piece_ref[...]


def gate_kernel(*refs):
    refs[-1][...] = jnp.zeros(refs[-1].shape, refs[-1].dtype)


def pick_kernel(place_ref, z2_ref, z1_ref, z0_ref, *refs):
    out_ref = refs[-1]
    upper = lax.rem(lax.div(place_ref[0], 2), 2) == 1

    @pl.when(upper)
    def _():
        out_ref[:ROWS, :] = z2_ref[...]
        out_ref[ROWS:, :] = z1_ref[...]

    @pl.when(jnp.logical_not(upper))
    def _():
        out_ref[:ROWS, :] = z1_ref[...]
        out_ref[ROWS:, :] = z0_ref[...]


def join_kernel(z2_ref, z1_ref, z0_ref, side_ref, *refs):
    out_ref = refs[-1]
    parts = (z2_ref[...], side_ref[:ROWS, :], z1_ref[...], side_ref[ROWS:, :], z0_ref[...])
    for m, part in enumerate(parts):
        out_ref[m * ROWS : (m + 1) * ROWS, :] = part


def absorb(block, queries, row, base, start, state, pos=None):
    s = dot(block[:, :D], queries, 1, 1) * (SCALE * LOG2E)
    visible = row >= start - base * ROWS
    if pos is not None:
        visible = visible & (row <= pos - base * ROWS)
    s = jnp.where(visible, s, NEG)
    peak = jnp.maximum(jnp.max(s, axis=0, keepdims=True), FLOOR)
    prob = jnp.exp2(s - peak).astype(jnp.bfloat16)
    mass = jnp.sum(prob.astype(jnp.float32), axis=0, keepdims=True)
    out = dot(block[:, D:], prob, 0, 0)
    if state is None:
        return prob, peak, (out, mass, peak)
    old_out, old_mass, old_peak = state
    top = jnp.maximum(old_peak, peak)
    before, now = jnp.exp2(old_peak - top), jnp.exp2(peak - top)
    return prob, peak, (old_out * before + out * now, old_mass * before + mass * now, top)


def read_state(ref):
    return ref[:D, :], ref[MASS : MASS + 1, :], ref[TOP : TOP + 1, :]


def write_state(ref, state):
    ref[:D, :], ref[MASS : MASS + 1, :], ref[TOP : TOP + 1, :] = state


def put_row(ref, at, value):
    ref[at : at + 1, :] = value


def near_kernel(place_ref, z2_ref, z1_ref, z0_ref, q4_ref, bound_ref, *refs):
    p_ref, st_ref = refs[-2:]
    me = place_ref[0]
    queries = q4_ref[...]
    row = lax.broadcasted_iota(jnp.int32, (ROWS, LANES), 0)
    pos, start = bound_ref[0:1, :].astype(jnp.int32), bound_ref[1:2, :].astype(jnp.int32)
    state = None
    for i, ref in ((2, z0_ref), (1, z1_ref), (0, z2_ref)):
        at = pos if i == 2 else None
        prob, peak, state = absorb(ref[...], queries, row, me - PLANE * (2 - i), start, state, at)
        p_ref[i * ROWS : (i + 1) * ROWS, :] = prob
        put_row(st_ref, PEAK + 2 * i, peak)
    write_state(st_ref, state)
    put_row(st_ref, START, bound_ref[1:2, :])


def project_kernel(*refs):
    pieces, (w_ref, after, acc_ref) = refs[:7], refs[7:]
    acc = None
    for i, piece in enumerate(pieces):
        part = dot(piece[...], w_ref[:, i * BLOCK : (i + 1) * BLOCK], 1, 1)
        acc = part if acc is None else acc + part
    acc_ref[...] = acc


def last_projection(piece_ref, w_ref, acc_ref, g4_ref, gt_ref):
    acc = (acc_ref[...] + dot(piece_ref[...], w_ref[:, 7 * BLOCK :], 1, 1)).astype(jnp.bfloat16)
    for h in range(HEADS):
        g4_ref[h * ROWS : (h + 1) * ROWS, :] = acc[:, h * D : (h + 1) * D]
    gt_ref[...] = jnp.transpose(g4_ref[...].astype(jnp.float32))


def rows(i):
    return pl.ds(pl.multiple_of(i * ROWS, ROWS), ROWS)


def source_of(head, by, flip):
    at = lax.rem(head + by + 8, 8)
    return at + 1 - 2 * lax.rem(at, 2) if flip else at


def middle_kernel(place_ref, own_ref, q4_ref, st_in_ref, p_ref, st_ref):
    queries = q4_ref[...]
    row = lax.broadcasted_iota(jnp.int32, (ROWS, LANES), 0)
    start = st_in_ref[START : START + 1, :].astype(jnp.int32)
    state = read_state(st_in_ref)
    st_ref[PEAK:, :] = st_in_ref[PEAK:, :]
    for i in range(2):
        slot = 2 * i + 1
        block = own_ref[slot * ROWS : (slot + 1) * ROWS, :]
        prob, peak, state = absorb(block, queries, row, place_ref[0] + 2 * (slot - REACH), start, state)
        p_ref[i * ROWS : (i + 1) * ROWS, :] = prob
        put_row(st_ref, PEAK + slot, peak)
    write_state(st_ref, state)
    put_row(st_ref, START, st_in_ref[START : START + 1, :])


def across_kernel(place_ref, par_ref, q4_ref, gt_ref, st_in_ref, p_ref, st_ref):
    me = place_ref[0]
    core = lax.rem(me, 2)
    chip = me - core
    queries = q4_ref[...]
    row = lax.broadcasted_iota(jnp.int32, (ROWS, LANES), 0)
    start = st_in_ref[START : START + 1, :].astype(jnp.int32)
    state = read_state(st_in_ref)
    peaks = [st_in_ref[PEAK + m : PEAK + m + 1, :] for m in range(SLOTS)]
    for i in range(REACH):
        slot = i + core
        prob, peak, state = absorb(par_ref[rows(slot), :], queries, row, chip + 1 - core + 2 * (slot - REACH), start, state)
        p_ref[i * ROWS : (i + 1) * ROWS, :] = prob
        peaks.append(peak)
    out, mass, top = state
    put_row(st_ref, DOT, jnp.sum(gt_ref[...] * out, axis=0, keepdims=True) / mass)
    log_total = top + jnp.log2(mass)
    for i, peak in enumerate(peaks):
        put_row(st_ref, PEAK + i, jnp.exp2(peak - log_total))


def back_block(block, prob, share, g4, q4, rd):
    prob = prob.astype(jnp.float32) * share
    dprob = dot(block[:, D:], g4, 1, 1)
    ds = (prob * (dprob - rd)).astype(jnp.bfloat16)
    dv = dot(prob.astype(jnp.bfloat16), g4, 1, 0)
    dk = dot(ds, q4, 1, 0) * SCALE
    dq = dot(block[:, :D], ds, 0, 0)
    return dk, dv, dq


def put(out_ref, slot, dk, dv):
    at = pl.ds(pl.multiple_of(slot * ROWS, ROWS), ROWS)
    out_ref[at, :D] = dk.astype(out_ref.dtype)
    out_ref[at, D:] = dv.astype(out_ref.dtype)


def cross_step(slot, core, par_ref, p_ref, st_ref, g4, q4_ref, rd):
    share = st_ref[pl.ds(PEAK + SLOTS + slot - core, 1), :]
    return back_block(par_ref[rows(slot), :], p_ref[rows(slot - core), :], share, g4, q4_ref[...], rd)


def cross_far(place_ref, q4_ref, par_ref, p_ref, g_ref, st_in_ref, out_ref, st_ref):
    core = lax.rem(place_ref[0], 2)
    g4 = g_ref[...]
    rd = st_in_ref[DOT : DOT + 1, :]
    st_ref[DOT : DOT + 1, :] = rd
    st_ref[PEAK:, :] = st_in_ref[PEAK:, :]
    dk, dv, dq = cross_step(1, core, par_ref, p_ref, st_ref, g4, q4_ref, rd)
    put(out_ref, 1, dk, dv)
    st_ref[:D, :] = dq

    @pl.when(core == 1)
    def _():
        out_ref[:ROWS, :] = jnp.zeros((ROWS, 2 * D), out_ref.dtype)

    @pl.when(core == 0)
    def _():
        dk, dv, dq = cross_step(0, core, par_ref, p_ref, st_ref, g4, q4_ref, rd)
        put(out_ref, 0, dk, dv)
        st_ref[:D, :] += dq


def cross_near(place_ref, q4_ref, par_ref, p_ref, g_ref, st_in_ref, out_ref, st_ref):
    core = lax.rem(place_ref[0], 2)
    g4 = g_ref[...]
    rd = st_in_ref[DOT : DOT + 1, :]
    st_ref[DOT : DOT + 1, :] = rd
    st_ref[PEAK:, :] = st_in_ref[PEAK:, :]
    total = st_in_ref[:D, :]
    for slot in (2, 3):
        dk, dv, dq = cross_step(slot, core, par_ref, p_ref, st_ref, g4, q4_ref, rd)
        put(out_ref, slot - 2, dk, dv)
        total = total + dq
    st_ref[:D, :] = total

    @pl.when(core == 0)
    def _():
        out_ref[2 * ROWS :, :] = jnp.zeros((ROWS, 2 * D), out_ref.dtype)

    @pl.when(core == 1)
    def _():
        dk, dv, dq = cross_step(4, core, par_ref, p_ref, st_ref, g4, q4_ref, rd)
        put(out_ref, 2, dk, dv)
        st_ref[:D, :] += dq


def own_kernel(slots, q4_ref, own_ref, near_ref, side_ref, g_ref, st_in_ref, *refs):
    out_ref, st_ref = refs[-2:]
    g4 = g_ref[...]
    rd = st_in_ref[DOT : DOT + 1, :]
    total = st_in_ref[:D, :]
    for i, slot in enumerate(slots):
        at = slot // 2 * ROWS
        prob = (side_ref if slot % 2 else near_ref)[at : at + ROWS, :]
        share = st_in_ref[PEAK + slot : PEAK + slot + 1, :]
        dk, dv, dq = back_block(own_ref[slot * ROWS : (slot + 1) * ROWS, :], prob, share, g4, q4_ref[...], rd)
        out_ref[i * ROWS : (i + 1) * ROWS, :D] = dk
        out_ref[i * ROWS : (i + 1) * ROWS, D:] = dv
        total = total + dq
    if slots[-1] < REACH:
        st_ref[DOT : DOT + 1, :] = rd
        st_ref[PEAK:, :] = st_in_ref[PEAK:, :]
        st_ref[:D, :] = total
    else:
        dq = jnp.transpose(total) * SCALE
        for h in range(HEADS):
            st_ref[:, h * D : (h + 1) * D] = dq[h * ROWS : (h + 1) * ROWS, :].astype(jnp.bfloat16)


def is_upper(place_ref):
    return (lax.rem(lax.div(place_ref[0], 2), 2) == 1).astype(jnp.float32)


def settle_kernel(own_ref, back_ref, keep_ref, send_ref):
    both = own_ref[...] + back_ref[: 2 * ROWS, :].astype(jnp.float32)
    keep_ref[...] = both[:ROWS]
    send_ref[...] = both[ROWS:].astype(jnp.bfloat16)


def relay_kernel(place_ref, far_ref, near_ref, side_ref, eight_ref, four_ref):
    side = side_ref[...].astype(jnp.float32)
    upper = is_upper(place_ref)
    eight_ref[...] = (far_ref[...] + side * upper).astype(jnp.bfloat16)
    four_ref[...] = (near_ref[...] + side * (1 - upper)).astype(jnp.bfloat16)


def gather_kernel(own_ref, back_ref, two_ref, out_ref):
    total = own_ref[...] + back_ref[2 * ROWS :, :].astype(jnp.float32)
    out_ref[...] = total + two_ref[...].astype(jnp.float32)


def finish_kernel(sum_ref, eight_ref, four_ref, k_ref, v_ref):
    total = sum_ref[...] + four_ref[...].astype(jnp.float32) + eight_ref[...].astype(jnp.float32)
    total = total.astype(jnp.bfloat16)
    k_ref[...] = total[:, :D]
    v_ref[...] = total[:, D:]


def vmem(n):
    return [pl.BlockSpec(memory_space=pltpu.VMEM)] * n


def smem(n):
    return [pl.BlockSpec(memory_space=pltpu.SMEM)] * n


def hbm(n):
    return [pl.BlockSpec(memory_space=pltpu.HBM)] * n


def token(n):
    return [pl.BlockSpec(memory_space=pl.ANY)] * n


def moved(x, axis, to):
    return lax.ppermute(x, axis, [(i, to(i)) for i in range(lax.axis_size(axis))])


def turned(x, axis, by):
    count = lax.axis_size(axis)
    return moved(x, axis, lambda i: (i + by) % count)


def shape(rows, cols, dtype):
    return jax.ShapeDtypeStruct((rows, cols), dtype)


def call(name, kernel, outs, ins, args, scratch=(), flops=1):
    one = not isinstance(outs, tuple)
    return pl.pallas_call(
        kernel,
        out_shape=outs,
        in_specs=ins,
        out_specs=vmem(1)[0] if one else tuple(vmem(len(outs))),
        scratch_shapes=list(scratch),
        compiler_params=pltpu.CompilerParams(vmem_limit_bytes=8 * MIB),
        cost_estimate=pl.CostEstimate(flops=flops, bytes_accessed=1, transcendentals=0),
        name=name,
    )(*args)


def local(queries, keys, values, grad_out, out_weight, lengths):
    bf16, f32 = jnp.bfloat16, jnp.float32
    place = lax.axis_index("ctx").astype(jnp.int32).reshape(1)
    head = lax.axis_index("head").astype(jnp.int32).reshape(1)
    dma = pltpu.SemaphoreType.DMA
    pinned = functools.partial(pltpu.with_memory_space_constraint, memory_space=pltpu.HBM)
    state = shape(STATE, LANES, f32)

    first = moved(grad_out, "head", lambda i: i ^ 1)
    right = turned(grad_out, "head", 2)
    left = turned(grad_out, "head", -2)
    kv = call("pack", pack_kernel, shape(ROWS, 2 * D, bf16), hbm(2), (pinned(keys), pinned(values)), [dma((2,))])
    z2 = turned(kv, "ctx", 2 * PLANE)
    z1 = turned(kv, "ctx", PLANE)
    q4, bound, weight = call(
        "load",
        load_kernel,
        (shape(LANES, D, bf16), shape(8, LANES, f32), shape(HEADS * D, 8 * BLOCK, bf16)),
        smem(2) + hbm(3),
        (place, head, pinned(lengths), pinned(queries), pinned(out_weight)),
        [pltpu.SMEM((lengths.shape[0],), jnp.int32), dma((9 + HEADS,))],
    )
    other = call("stage", stage_kernel, shape(ROWS, BLOCK, bf16), vmem(1) + token(1), (first, q4))
    other_right = turned(other, "head", 2)
    other_left = turned(other, "head", -2)
    far = turned(right, "head", 2)
    other_far = turned(other_left, "head", -2)

    gate = call("gate", gate_kernel, shape(8, D, f32), token(4), (other, right, left, q4))
    picked = call(
        "pick_side", pick_kernel, shape(2 * ROWS, 2 * D, bf16), smem(1) + vmem(3) + token(1), (place, z2, z1, kv, gate)
    )
    side = moved(picked, "ctx", lambda i: i ^ 2)
    p_near, st = call(
        "near",
        near_kernel,
        (shape(3 * ROWS, LANES, bf16), state),
        smem(1) + vmem(5) + token(3),
        (place, z2, z1, kv, q4, bound, picked, other_right, other_left),
    )
    own = call("join_slots", join_kernel, shape(SLOTS * ROWS, 2 * D, bf16), vmem(4) + token(1), (z2, z1, kv, side, st))
    par = moved(own, "ctx", lambda i: i ^ 1)

    p_side, st = call(
        "middle",
        middle_kernel,
        (shape(2 * ROWS, LANES, bf16), state),
        smem(1) + vmem(3),
        (place, own, q4, st),
    )
    early = call(
        "project",
        project_kernel,
        shape(ROWS, HEADS * D, f32),
        vmem(8) + token(1),
        (grad_out, other, right, left, other_right, other_left, far, weight, st),
    )
    g4, gt = call(
        "last_projection",
        last_projection,
        (shape(LANES, D, bf16), shape(D, LANES, f32)),
        vmem(3),
        (other_far, weight, early),
        flops=COSTLY,
    )
    p_par, st = call(
        "across", across_kernel, (shape(REACH * ROWS, LANES, bf16), state), smem(1) + vmem(4), (place, par, q4, gt, st)
    )

    far_cross, st = call(
        "cross_far", cross_far, (shape(2 * ROWS, 2 * D, bf16), state), smem(1) + vmem(5), (place, q4, par, p_par, g4, st)
    )
    far_back = moved(far_cross, "ctx", lambda i: i ^ 1)
    near_cross, st = call(
        "cross_near", cross_near, (shape(3 * ROWS, 2 * D, bf16), state), smem(1) + vmem(5), (place, q4, par, p_par, g4, st), flops=FL
    )
    near_back = moved(near_cross, "ctx", lambda i: i ^ 1)
    far_own, st = call(
        "own_far",
        functools.partial(own_kernel, (0, 1)),
        (shape(2 * ROWS, 2 * D, f32), state),
        vmem(6),
        (q4, own, p_near, p_side, g4, st),
        flops=FL,
    )
    far_keep, far_side = call(
        "settle_far", settle_kernel, (shape(ROWS, 2 * D, f32), shape(ROWS, 2 * D, bf16)), vmem(2), (far_own, far_back)
    )
    far_side = moved(far_side, "ctx", lambda i: i ^ 2)
    near_own, st = call(
        "own_near",
        functools.partial(own_kernel, (2, 3)),
        (shape(2 * ROWS, 2 * D, f32), state),
        vmem(6) + token(1),
        (q4, own, p_near, p_side, g4, st, far_keep),
        flops=FL,
    )
    near_keep, by_two = call(
        "settle_near", settle_kernel, (shape(ROWS, 2 * D, f32), shape(ROWS, 2 * D, bf16)), vmem(2), (near_own, near_back)
    )
    by_two = turned(by_two, "ctx", -2)
    to_eight, to_four = call(
        "relay",
        relay_kernel,
        (shape(ROWS, 2 * D, bf16), shape(ROWS, 2 * D, bf16)),
        smem(1) + vmem(3),
        (place, far_keep, near_keep, far_side),
    )
    by_eight = turned(to_eight, "ctx", -2 * PLANE)
    by_four = turned(to_four, "ctx", -PLANE)
    last_own, grad_queries = call(
        "own_last",
        functools.partial(own_kernel, (4,)),
        (shape(ROWS, 2 * D, f32), shape(ROWS, HEADS * D, bf16)),
        vmem(6) + token(2),
        (q4, own, p_near, p_side, g4, st, to_eight, by_two),
        flops=COSTLY,
    )
    partial_sum = call(
        "gather_near", gather_kernel, shape(ROWS, 2 * D, f32), vmem(3), (last_own, near_back, by_two)
    )
    grad_keys, grad_values = call(
        "finish", finish_kernel, (shape(ROWS, D, bf16), shape(ROWS, D, bf16)), vmem(3), (partial_sum, by_eight, by_four)
    )
    return grad_queries, grad_keys, grad_values


def solution(mesh):
    return jax.shard_map(
        local,
        mesh=mesh,
        in_specs=(
            P("ctx", "head"),
            P("ctx", "head"),
            P("ctx", "head"),
            P("ctx", "head"),
            P("head", None),
            P(),
        ),
        out_specs=(P("ctx", "head"), P("ctx", "head"), P("ctx", "head")),
        check_vma=False,
    )
```
